32 devices in a mesh: region: 2 (over x), dev: 16 (over z, y, core).
Axes of the slice: x: 2, y: 2, z: 4, core: 2. Of those that a mesh axis runs over, the one named last changes fastest.
Arguments:
- positions: float32 [3, 128, 128], P(None, ('region', 'dev')), as said below
- charges: float32 [128, 128], P(('region', 'dev')), may hold values from -3 to 3
- types: int32 [128, 128], P(('region', 'dev')), may hold values from 0 to 5
- pairs: int32 [128, 13], P(('region', 'dev')), may hold values from -1 to 127, as said below
- owner_map: int32 [128], replicated, may hold values from 0 to 127, as said below
Outputs:
- born_radius: float32 [128, 128], P(('region', 'dev'))
- energy: float32 [128, 128], P(('region', 'dev'))
- forces: float32 [3, 128, 128], P(None, ('region', 'dev'))
- born_grad: float32 [128, 128], P(('region', 'dev'))
The draws below stay inside these ranges and needn't reach their ends.
Inputs may be any that keep to these rules, and one draw needn't show every extreme that they name: `pairs`: row g lists cells next to block g's cell; -1 marks an empty slot. The block that owner_map gives for a listed cell differs from g and lies in g's region (blocks r * 64 to (r + 1) * 64 - 1) or in the next region. No pair of blocks is listed twice, in either order. `owner_map`: for each region r, a permutation of the cells r * 64 to (r + 1) * 64 - 1 onto the blocks with the same ids. `positions`: any two atoms are 1.5 or more apart.
All inputs are finite; a program needn't handle non-finite values.
Results may differ from the reference program's by a relative error of at most 0.0003.
Values sent between devices are 32-bit elements; how exact they have to be, the bound alone decides.
No kernel may reach another device: no remote copies, remote signals or barrier semaphores. Data moves between devices by JAX's collectives and lax.ppermute only.
A program may use at most 64 MiB of HBM per device.

```python
import jax
import jax.numpy as jnp
import numpy as np
from jax import lax

BLK_DEV = 4
LAT_X = 4
LAT_Y = 4
LAT_Z = 8
NTYPES = 6
GRID_Y = 4
ATOMS_BLK = 128
GRID_Z = 4
BLOCKS = 128
N_REGION = 2
N_DEV = 16


shell_offsets = np.array([[1, -1, -1], [1, -1, 0], [1, -1, 1], [1, 0, -1], [1, 0, 0], [1, 0, 1], [1, 1, -1], [1, 1, 0], [1, 1, 1], [0, 1, -1], [0, 1, 0], [0, 1, 1], [0, 0, 1]], dtype=np.int32)


lattice_spacing = 3.0


def permute_region(sub_key):
    return jax.random.permutation(sub_key, N_DEV * BLK_DEV).astype(jnp.int32)


def layout(key):
    base_key = jax.random.fold_in(key, 4242)
    region_blocks = N_DEV * BLK_DEV
    permuted = jax.vmap(permute_region)(jax.random.split(base_key, N_REGION))
    region_start = (jnp.arange(N_REGION, dtype=jnp.int32) * region_blocks)[:, None]
    owner_map = (permuted + region_start).reshape(-1)
    cell_count = owner_map.shape[0]
    block_cell = jnp.zeros((cell_count,), jnp.int32).at[owner_map].set(jnp.arange(cell_count, dtype=jnp.int32))
    return (owner_map, block_cell)


def cell_coords(cell_ids):
    region_blocks = N_DEV * BLK_DEV
    region_ids = cell_ids // region_blocks
    local_ids = cell_ids % region_blocks
    cell_x = region_ids * BLK_DEV + local_ids // (GRID_Y * GRID_Z)
    cell_y = local_ids // GRID_Z % GRID_Y
    cell_z = local_ids % GRID_Z
    return (cell_x, cell_y, cell_z)


def cell_number(cell_x, cell_y, cell_z):
    region_ids = cell_x // BLK_DEV
    local_ids = cell_x % BLK_DEV * GRID_Y * GRID_Z + cell_y * GRID_Z + cell_z
    return region_ids * (N_DEV * BLK_DEV) + local_ids


def draw_owner_map(key, part):
    owner_map, block_cell = layout(key)
    return owner_map


def draw_pairs(key, part):
    owner_map, block_cell = layout(key)
    cell_x, cell_y, cell_z = cell_coords(block_cell)
    shift_table = jnp.asarray(shell_offsets, jnp.int32)
    near_x = cell_x[:, None] + shift_table[None, :, 0]
    near_y = cell_y[:, None] + shift_table[None, :, 1]
    near_z = cell_z[:, None] + shift_table[None, :, 2]
    inside = (near_x < N_REGION * BLK_DEV) & (near_y >= 0) & (near_y < GRID_Y) & (near_z >= 0) & (near_z < GRID_Z)
    near_id = cell_number(jnp.minimum(near_x, N_REGION * BLK_DEV - 1), jnp.clip(near_y, 0, GRID_Y - 1), jnp.clip(near_z, 0, GRID_Z - 1))
    return jnp.where(inside, near_id, -1).astype(jnp.int32)


def draw_positions(key, part):
    owner_map, block_cell = layout(key)
    cell_x, cell_y, cell_z = cell_coords(block_cell)
    atom_ids = jnp.arange(ATOMS_BLK, dtype=jnp.int32)
    lat_x = atom_ids // (LAT_Y * LAT_Z)
    lat_y = atom_ids // LAT_Z % LAT_Y
    lat_z = atom_ids % LAT_Z
    coord_x = (cell_x[:, None] * LAT_X + lat_x[None]).astype(jnp.float32) + 0.5
    coord_y = (cell_y[:, None] * LAT_Y + lat_y[None]).astype(jnp.float32) + 0.5
    coord_z = (cell_z[:, None] * LAT_Z + lat_z[None]).astype(jnp.float32) + 0.5
    lattice = jnp.stack([coord_x, coord_y, coord_z]) * lattice_spacing
    noise_key = jax.random.fold_in(key, 977)
    uniform_draw = jax.random.uniform(noise_key, lattice.shape, jnp.float32, -1.0, 1.0)
    jitter = uniform_draw
    return lattice + 0.25 * lattice_spacing * jitter


def set_ends(drawn, key, least, high):
    longest = drawn.shape.index(max(drawn.shape))
    spots = []
    for shift in (0, 1):
        where = [jax.random.randint(jax.random.fold_in(key, axis), (), 0, length) for axis, length in enumerate(drawn.shape)]
        where[longest] = (where[longest] + shift) % drawn.shape[longest]
        spots.append(tuple(where))
    return drawn.at[spots[0]].set(least).at[spots[1]].set(high)


def block_scale(own_key, dims, shards, smallest, top_value):
    def one(position, blocks):
        draws = jax.random.uniform(jax.random.fold_in(jax.random.fold_in(own_key, 6), position), (blocks,), jnp.float32, smallest / len(shards), top_value / len(shards))
        return jnp.repeat(jnp.exp(draws), dims[position] // blocks).reshape((-1,) + (1,) * (len(dims) - position - 1))

    gain = one(*shards[0])
    for cut in shards[1:]:
        gain = gain * one(*cut)
    return gain


def scatter_about(key, dims, spread, bound, shards=(), kind=jnp.bfloat16):
    entries = spread * jax.random.normal(key, dims, jnp.float32)
    if shards:
        entries = entries * block_scale(key, dims, shards, -0.22, 0.18)
    return jnp.clip(entries, -bound, bound).astype(kind)


def setup_inputs(seed: int = 0) -> dict:
    key_of = jax.random.split(jax.random.key(seed), 6)
    return {
        "positions": draw_positions(jax.random.fold_in(key_of[5], 71), 0),
        "charges": scatter_about(key_of[1], (BLOCKS, ATOMS_BLK), 0.6, 3.0, ((0, 32),), jnp.float32),
        "types": set_ends(jax.random.randint(key_of[2], (BLOCKS, ATOMS_BLK), 0, NTYPES), jax.random.fold_in(key_of[2], 1), 0, NTYPES - 1).astype(jnp.int32),
        "pairs": draw_pairs(jax.random.fold_in(key_of[5], 71), 0),
        "owner_map": draw_owner_map(jax.random.fold_in(key_of[5], 71), 0),
    }


type_radii = (1.2, 1.7, 1.55, 1.52, 1.85, 1.8)
type_scales = (0.85, 0.72, 0.79, 0.85, 0.86, 0.96)
radius_offset = 0.09
born_alpha = 1.0
born_beta = 0.8
born_gamma = 4.85
solvent_tau = 1.0 - 1.0 / 78.5

def lookup_types(types):
    shape_tail = (-1,) + (1,) * types.ndim
    type_ids = jnp.arange(len(type_radii), dtype=jnp.int32).reshape(shape_tail)
    one_hot = (types[None] == type_ids).astype(jnp.float32)
    radii_table = jnp.asarray(type_radii, jnp.float32).reshape(shape_tail)
    scale_table = jnp.asarray(type_scales, jnp.float32).reshape(shape_tail)
    intrinsic = lax.optimization_barrier(jnp.sum(one_hot * radii_table, axis=0))
    offset_rho = intrinsic - radius_offset
    scaled_rho = lax.optimization_barrier(jnp.sum(one_hot * scale_table, axis=0)) * offset_rho
    return (intrinsic, offset_rho, scaled_rho)

def descreen(distance, rho_self, scaled_other):
    high_edge = distance + scaled_other
    low_edge = jnp.maximum(rho_self, jnp.abs(distance - scaled_other))
    inv_low = 1.0 / low_edge
    inv_high = 1.0 / high_edge
    inv_dist = 1.0 / distance
    integral = inv_low - inv_high + 0.25 * distance * (inv_high * inv_high - inv_low * inv_low) + 0.5 * inv_dist * jnp.log(low_edge * inv_high) + 0.25 * scaled_other * scaled_other * inv_dist * (inv_low * inv_low - inv_high * inv_high)
    inner_term = jnp.where(rho_self < scaled_other - distance, 2.0 * (1.0 / rho_self - inv_low), 0.0)
    return jnp.where(high_edge > rho_self, 0.5 * (integral + inner_term), 0.0)

def masked_sum(values, keep_mask, reduce_axes):
    return lax.optimization_barrier(jnp.sum(jnp.where(keep_mask, values, 0.0), axis=reduce_axes))

def pair_geometry(home_block, partner_fields, usable):
    slot_count = partner_fields.shape[1]
    atom_count = home_block.shape[-1]
    separation = home_block[:3, None, :, None] - partner_fields[:3, :, None, :]
    squared = lax.optimization_barrier(jnp.sum(separation * separation, axis=0))
    slot_ids = jnp.arange(slot_count, dtype=jnp.int32)[:, None, None]
    atom_ids = jnp.arange(atom_count, dtype=jnp.int32)
    diagonal = (slot_ids == 0) & (atom_ids[:, None] == atom_ids[None, :])[None]
    home_mask = usable[:, None, None] & jnp.logical_not(diagonal)
    partner_mask = home_mask & (slot_ids > 0)
    distance = jnp.sqrt(jnp.where(home_mask, squared, 1.0))
    return (separation, distance, home_mask, partner_mask)

def descreen_tile(home_block, partner_fields, usable):
    separation, distance, home_mask, partner_mask = pair_geometry(home_block, partner_fields, usable)
    home_term = descreen(distance, home_block[3][None, :, None], partner_fields[4][:, None, :])
    partner_term = descreen(distance, partner_fields[3][:, None, :], home_block[4][None, :, None])
    return (masked_sum(home_term, home_mask, (0, 2))[None], masked_sum(partner_term, partner_mask, 1)[None])

def energy_tile(home_block, partner_fields, usable):
    separation, distance, home_mask, partner_mask = pair_geometry(home_block, partner_fields, usable)
    charge_prod = solvent_tau * home_block[3][None, :, None] * partner_fields[3][:, None, :]
    radius_home = home_block[4][None, :, None]
    radius_partner = partner_fields[4][:, None, :]
    radius_prod = radius_home * radius_partner
    squared = distance * distance
    exponent_arg = squared / (4.0 * radius_prod)
    damped = jnp.exp(-exponent_arg)
    denom_sq = squared + radius_prod * damped
    denom_root = jnp.sqrt(denom_sq)
    inv_cube = 1.0 / (denom_root * denom_sq)
    pair_energy = -0.5 * charge_prod / denom_root
    pull_coef = -charge_prod * (1.0 - 0.25 * damped) * inv_cube
    grad_common = 0.5 * charge_prod * damped * (1.0 + exponent_arg) * inv_cube
    home_sum = jnp.stack([masked_sum(pull_coef * separation[0], home_mask, (0, 2)), masked_sum(pull_coef * separation[1], home_mask, (0, 2)), masked_sum(pull_coef * separation[2], home_mask, (0, 2)), masked_sum(pair_energy, home_mask, (0, 2)), masked_sum(grad_common * radius_partner, home_mask, (0, 2))])
    other_sum = jnp.stack([masked_sum(-pull_coef * separation[0], partner_mask, 1), masked_sum(-pull_coef * separation[1], partner_mask, 1), masked_sum(-pull_coef * separation[2], partner_mask, 1), masked_sum(pair_energy, partner_mask, 1), masked_sum(grad_common * radius_home, partner_mask, 1)])
    return (home_sum, other_sum)

def sweep(fields, partner_ids, live_slot, tile_fn, field_count):
    block_count = fields.shape[1]
    first_ok = jnp.zeros((1,), jnp.int32) == 0

    def visit(totals, block_index):
        home_block = jnp.take(fields, block_index, axis=1)
        targets = jnp.take(partner_ids, block_index, axis=0)
        usable = jnp.concatenate([first_ok, jnp.take(live_slot, block_index, axis=0)])
        partner_fields = jnp.concatenate([home_block[:, None], jnp.take(fields, targets, axis=1)], axis=1)
        home_sum, other_sum = tile_fn(home_block, partner_fields, usable)
        totals = totals.at[:, block_index].add(home_sum)
        totals = totals.at[:, targets].add(other_sum[:, 1:])
        return (totals, None)
    initial = jnp.zeros((field_count, block_count, fields.shape[2]), jnp.float32)
    totals, unused = lax.scan(visit, initial, jnp.arange(block_count, dtype=jnp.int32))
    return totals

def reference(positions, charges, types, pairs, owner_map):
    intrinsic, offset_rho, scaled_rho = lookup_types(types)
    live_slot = pairs >= 0
    partner_ids = owner_map[jnp.maximum(pairs, 0)]
    first_fields = jnp.concatenate([positions, offset_rho[None], scaled_rho[None]], axis=0)
    descreen_sum = sweep(first_fields, partner_ids, live_slot, descreen_tile, 1)[0]
    psi_value = descreen_sum * offset_rho
    shaped = born_alpha * psi_value - born_beta * psi_value * psi_value + born_gamma * psi_value * psi_value * psi_value
    born_radius = 1.0 / (1.0 / offset_rho - jnp.tanh(shaped) / intrinsic)
    second = jnp.concatenate([positions, charges[None], born_radius[None]], axis=0)
    totals = sweep(second, partner_ids, live_slot, energy_tile, 5)
    charge_sq = solvent_tau * charges * charges
    energy = totals[3] - 0.5 * charge_sq / born_radius
    born_grad = totals[4] + 0.5 * charge_sq / (born_radius * born_radius)
    return (born_radius, energy, totals[:3], born_grad)
```

```python
import functools

import jax
import jax.numpy as jnp
from jax import lax
from jax.experimental import pallas as pl
from jax.experimental.pallas import tpu as pltpu
from jax.sharding import PartitionSpec as P

type_radii = (1.2, 1.7, 1.55, 1.52, 1.85, 1.8)
type_scales = (0.85, 0.72, 0.79, 0.85, 0.86, 0.96)
radius_offset = 0.09
born_alpha = 1.0
born_beta = 0.8
born_gamma = 4.85
solvent_tau = 1.0 - 1.0 / 78.5

ROW_X, ROW_Y, ROW_Z, ROW_TYPE, ROW_CHARGE, ROW_PARTNER, ROW_COUNT = range(7)
STEP = 32
LANES = 128


def window_regions(region_count):
    return (region_count, True) if region_count <= 3 else (3, False)


def gather_window(payload):
    regions = lax.axis_size("region")
    if window_regions(regions)[1]:
        return lax.all_gather(payload, ("region", "dev"), axis=0)
    here = lax.all_gather(payload, "dev", axis=0)
    below = lax.ppermute(here, "region", [(i, i + 1) for i in range(regions - 1)])
    above = lax.ppermute(here, "region", [(i + 1, i) for i in range(regions - 1)])
    return jnp.concatenate([below, here, above], axis=0)


def by_type(types, table):
    value = jnp.full(types.shape, table[0], jnp.float32)
    for index in range(1, len(table)):
        value = jnp.where(types == index, jnp.float32(table[index]), value)
    return value


def type_fields(types):
    intrinsic = by_type(types, type_radii)
    rho = intrinsic - radius_offset
    return intrinsic, rho, by_type(types, type_scales) * rho


def spread_columns(rows, columns_ref):
    count, atoms = rows.shape
    padded = jnp.concatenate([rows, jnp.zeros((LANES - count, atoms), jnp.float32)], axis=0)
    turned = padded.T
    for index in range(count):
        columns_ref[index] = jnp.broadcast_to(turned[:, index : index + 1], (atoms, LANES))


def lane_sums(columns, count):
    atoms = columns[0].shape[0]
    lane = lax.broadcasted_iota(jnp.int32, (atoms, LANES), 1)
    packed = jnp.zeros((atoms, LANES), jnp.float32)
    for index, column in enumerate(columns):
        packed = jnp.where(lane == index, jnp.sum(column, axis=1, keepdims=True), packed)
    return packed.T[:count]


def descreen(squared, rho, inv_rho, scaled, scaled_sq):
    inv_dist = lax.rsqrt(squared)
    distance = squared * inv_dist
    high = distance + scaled
    gap = distance - scaled
    low = jnp.maximum(rho, jnp.abs(gap))
    inv_both = pl.reciprocal(low * high)
    inv_low = high * inv_both
    inv_high = low * inv_both
    quarter = 0.25 * inv_dist
    curve = (squared - scaled_sq) * quarter
    body = (0.5 * (inv_low - inv_high)) * (1.0 - (inv_low + inv_high) * curve)
    body = body + jnp.log(low * inv_high) * quarter
    body = body + jnp.where(rho < -gap, inv_rho - inv_low, 0.0)
    return jnp.where(high > rho, body, 0.0)


def neighbour_lists(partner_ref, own_partner_ref, first_own, blocks, table_ref):
    window = partner_ref.shape[0]
    tiles = window // LANES
    ids = jnp.concatenate(
        [partner_ref[i * LANES : (i + 1) * LANES, :].T[:16] for i in range(tiles)], axis=1
    )
    lane = lax.broadcasted_iota(jnp.int32, (1, window), 1)
    rows = []
    for block in range(blocks):
        own = (first_own + block + 1).astype(jnp.float32)
        listed_by = jnp.max(jnp.where(ids == own, 1.0, 0.0), axis=0, keepdims=True)
        for slot in range(own_partner_ref.shape[1]):
            listed_by = jnp.where(lane == own_partner_ref[block, slot] - 1, 1.0, listed_by)
        rows.append(listed_by)
    spare = (-blocks) % 8
    linked = jnp.concatenate(rows + [jnp.zeros((spare, window), jnp.float32)] * (spare > 0), axis=0)
    before = lax.broadcasted_iota(jnp.int32, (window, window), 0)
    after = lax.broadcasted_iota(jnp.int32, (window, window), 1)
    ramp = jnp.where(before <= after, 1.0, 0.0).astype(jnp.bfloat16)
    rank = jnp.dot(linked.astype(jnp.bfloat16), ramp, preferred_element_type=jnp.float32)
    place = jnp.where(linked > 0.0, rank - 1.0, -1.0).astype(jnp.int32)
    total = jnp.sum(linked, axis=1, keepdims=True).astype(jnp.int32)
    tile_lane = lax.broadcasted_iota(jnp.int32, (LANES, LANES), 1)
    tile_row = lax.broadcasted_iota(jnp.int32, (LANES, LANES), 0)
    for out_tile in range(tiles):
        packed = jnp.zeros((LANES, LANES), jnp.float32)
        for block in range(blocks):
            found = jnp.zeros((LANES, LANES), jnp.float32)
            for in_tile in range(tiles):
                part = place[block : block + 1, in_tile * LANES : (in_tile + 1) * LANES]
                hit = part == tile_row + out_tile * LANES
                found = found + jnp.where(hit, (tile_lane + in_tile * LANES).astype(jnp.float32), 0.0)
            packed = jnp.where(tile_lane == block, jnp.sum(found, axis=1, keepdims=True), packed)
        table_ref[0:blocks, out_tile * LANES : (out_tile + 1) * LANES] = packed.T[:blocks].astype(jnp.int32)
    for block in range(blocks):
        table_ref[blocks + block : blocks + block + 1, :] = jnp.broadcast_to(
            total[block : block + 1], (1, window)
        )


def radii_kernel(
    blocks,
    first_ref,
    own_partner_ref,
    positions_ref,
    types_ref,
    fields_ref,
    window_types_ref,
    partner_ref,
    radii_ref,
    table_ref,
    columns_ref,
    scaled_ref,
    scaled_sq_ref,
    total_ref,
    lists_ref,
    lists_sem,
):
    atoms = types_ref.shape[1]
    neighbour_lists(partner_ref, own_partner_ref, first_ref[0], blocks, table_ref)
    move = pltpu.make_async_copy(table_ref, lists_ref, lists_sem)
    move.start()
    _, _, scaled = type_fields(window_types_ref[...])
    scaled_ref[...] = scaled
    scaled_sq_ref[...] = scaled * scaled
    intrinsic, rho, own_scaled = type_fields(types_ref[...])
    rows = [positions_ref[axis] for axis in range(3)] + [rho, 1.0 / rho]
    spread_columns(jnp.concatenate(rows, axis=0), columns_ref)
    move.wait()

    def pair_step(block, start, partner):
        step = pl.ds(start, STEP)
        x, y, z, s, s2 = partner
        dx = columns_ref[block, step, :] - x
        dy = columns_ref[blocks + block, step, :] - y
        dz = columns_ref[2 * blocks + block, step, :] - z
        squared = dx * dx + dy * dy + dz * dz
        return squared, columns_ref[3 * blocks + block, step, :], columns_ref[4 * blocks + block, step, :], s, s2

    for block in range(blocks):
        own = (
            positions_ref[0, block : block + 1, :],
            positions_ref[1, block : block + 1, :],
            positions_ref[2, block : block + 1, :],
            own_scaled[block : block + 1],
            own_scaled[block : block + 1] * own_scaled[block : block + 1],
        )
        for start in range(0, atoms, STEP):
            squared, r, ir, s, s2 = pair_step(block, start, own)
            same = lax.broadcasted_iota(jnp.int32, (STEP, LANES), 0) + start == lax.broadcasted_iota(
                jnp.int32, (STEP, LANES), 1
            )
            term = descreen(jnp.where(same, 1.0, squared), r, ir, s, s2)
            total_ref[block, start : start + STEP, :] = jnp.where(same, 0.0, term)

        def visit(index, carry, block=block):
            other = lists_ref[block, index]
            base = (other // blocks) * (ROW_COUNT * blocks) + other % blocks
            partner = tuple(
                fields_ref[pl.ds(base + row * blocks, 1), :] for row in (ROW_X, ROW_Y, ROW_Z)
            ) + (scaled_ref[pl.ds(other, 1), :], scaled_sq_ref[pl.ds(other, 1), :])
            for start in range(0, atoms, STEP):
                total_ref[block, start : start + STEP, :] += descreen(*pair_step(block, start, partner))
            return carry

        lax.fori_loop(0, lists_ref[blocks + block, 0], visit, 0)
    descreened = lane_sums([total_ref[block] for block in range(blocks)], blocks)
    psi = descreened * rho
    shaped = born_alpha * psi - born_beta * psi * psi + born_gamma * psi * psi * psi
    radii_ref[...] = 1.0 / (1.0 / rho - jnp.tanh(shaped) / intrinsic)


def energy_kernel(
    blocks,
    lists_ref,
    positions_ref,
    charges_ref,
    own_radii_ref,
    fields_ref,
    radii_ref,
    energy_ref,
    forces_ref,
    grad_ref,
    columns_ref,
    decay_ref,
    total_ref,
):
    atoms = charges_ref.shape[1]
    decay_ref[...] = 1.0 / radii_ref[...]
    own_radii = own_radii_ref[...]
    own_decay = 1.0 / own_radii
    rows = [positions_ref[axis] for axis in range(3)] + [own_radii, -0.25 * own_decay]
    spread_columns(jnp.concatenate(rows, axis=0), columns_ref)

    def pair_terms(block, start, partner, same=None):
        step = pl.ds(start, STEP)
        x, y, z, charge, radius, decay = partner
        dx = columns_ref[block, step, :] - x
        dy = columns_ref[blocks + block, step, :] - y
        dz = columns_ref[2 * blocks + block, step, :] - z
        squared = dx * dx + dy * dy + dz * dz
        if same is not None:
            squared = jnp.where(same, 1.0, squared)
        power = squared * (columns_ref[4 * blocks + block, step, :] * decay)
        damped = jnp.exp(power)
        blend = (columns_ref[3 * blocks + block, step, :] * radius) * damped
        inv_root = lax.rsqrt(squared + blend)
        if same is not None:
            charge = jnp.where(same, 0.0, charge)
        potential = charge * inv_root
        cubed = potential * (inv_root * inv_root)
        pull = cubed * (1.0 - 0.25 * damped)
        return (pull * dx, pull * dy, pull * dz, potential, cubed * blend * (1.0 - power))

    for block in range(blocks):
        own = tuple(positions_ref[axis, block : block + 1, :] for axis in range(3)) + (
            charges_ref[block : block + 1, :],
            own_radii[block : block + 1],
            own_decay[block : block + 1],
        )
        for start in range(0, atoms, STEP):
            same = lax.broadcasted_iota(jnp.int32, (STEP, LANES), 0) + start == lax.broadcasted_iota(
                jnp.int32, (STEP, LANES), 1
            )
            for term, value in enumerate(pair_terms(block, start, own, same)):
                total_ref[term * blocks + block, start : start + STEP, :] = value

        def visit(index, carry, block=block):
            other = lists_ref[block, index]
            base = (other // blocks) * (ROW_COUNT * blocks) + other % blocks
            partner = tuple(
                fields_ref[pl.ds(base + row * blocks, 1), :] for row in (ROW_X, ROW_Y, ROW_Z, ROW_CHARGE)
            ) + (radii_ref[pl.ds(other, 1), :], decay_ref[pl.ds(other, 1), :])
            for start in range(0, atoms, STEP):
                for term, value in enumerate(pair_terms(block, start, partner)):
                    total_ref[term * blocks + block, start : start + STEP, :] += value
            return carry

        lax.fori_loop(0, lists_ref[blocks + block, 0], visit, 0)
    sums = lane_sums([total_ref[index] for index in range(5 * blocks)], 5 * blocks)
    charges = charges_ref[...]
    scale = solvent_tau * charges
    for axis in range(3):
        forces_ref[axis] = -scale * sums[axis * blocks : (axis + 1) * blocks]
    own_energy = 0.5 * scale * charges * own_decay
    energy_ref[...] = -0.5 * scale * sums[3 * blocks : 4 * blocks] - own_energy
    grad_ref[...] = (0.5 * scale * sums[4 * blocks : 5 * blocks] + own_energy) * own_decay


def shards(positions, charges, types, pairs, owner_map):
    _, blocks, atoms = positions.shape
    regions = lax.axis_size("region")
    region_devices = lax.axis_size("dev")
    kept_regions, whole = window_regions(regions)
    window = kept_regions * region_devices * blocks
    padded = -(-window // LANES) * LANES
    region_here = lax.axis_index("region")
    first_window = 0 if whole else (region_here - 1) * region_devices * blocks
    first_own = (region_here * region_devices + lax.axis_index("dev")) * blocks

    partners = jnp.where(pairs >= 0, owner_map[jnp.maximum(pairs, 0)] + 1, 0)
    partner_row = jnp.pad(partners.astype(jnp.float32), ((0, 0), (0, atoms - pairs.shape[1])))
    payload = jnp.concatenate(
        [positions, types.astype(jnp.float32)[None], charges[None], partner_row[None]], axis=0
    )
    gathered = gather_window(payload)
    window_types = gathered[:, ROW_TYPE].reshape(window, atoms)
    window_partners = gathered[:, ROW_PARTNER].reshape(window, atoms)
    if padded > window:
        window_partners = jnp.pad(window_partners, ((0, padded - window), (0, 0)))
    fields = gathered.reshape(window * ROW_COUNT, atoms)
    own_place = jnp.maximum(partners - first_window, 0) * (partners > 0)

    vmem = pl.BlockSpec(memory_space=pltpu.VMEM)
    smem = pl.BlockSpec(memory_space=pltpu.SMEM)
    table = jax.ShapeDtypeStruct((-(-2 * blocks // 8) * 8, padded), jnp.int32)
    own_radii, lists = pl.pallas_call(
        functools.partial(radii_kernel, blocks),
        out_shape=(jax.ShapeDtypeStruct((blocks, atoms), jnp.float32), table),
        in_specs=[smem, smem] + [vmem] * 5,
        out_specs=(vmem, vmem),
        scratch_shapes=[
            pltpu.VMEM((5 * blocks, atoms, LANES), jnp.float32),
            pltpu.VMEM((window, atoms), jnp.float32),
            pltpu.VMEM((window, atoms), jnp.float32),
            pltpu.VMEM((blocks, atoms, LANES), jnp.float32),
            pltpu.SMEM(table.shape, jnp.int32),
            pltpu.SemaphoreType.DMA(()),
        ],
        compiler_params=pltpu.CompilerParams(vmem_limit_bytes=40 * 1024 * 1024),
    )(
        jnp.full((1,), first_own, jnp.int32),
        own_place,
        positions,
        types,
        fields,
        window_types,
        window_partners,
    )
    window_radii = gather_window(own_radii).reshape(window, atoms)
    block_out = jax.ShapeDtypeStruct((blocks, atoms), jnp.float32)
    energy, forces, grad = pl.pallas_call(
        functools.partial(energy_kernel, blocks),
        out_shape=(block_out, jax.ShapeDtypeStruct((3, blocks, atoms), jnp.float32), block_out),
        in_specs=[smem] + [vmem] * 5,
        out_specs=(vmem, vmem, vmem),
        scratch_shapes=[
            pltpu.VMEM((5 * blocks, atoms, LANES), jnp.float32),
            pltpu.VMEM((window, atoms), jnp.float32),
            pltpu.VMEM((5 * blocks, atoms, LANES), jnp.float32),
        ],
        compiler_params=pltpu.CompilerParams(vmem_limit_bytes=40 * 1024 * 1024),
    )(lists, positions, charges, own_radii, fields, window_radii)
    return own_radii, energy, forces, grad


def solution(mesh):
    placed = (
        P(None, ("region", "dev"), None),
        P(("region", "dev"), None),
        P(("region", "dev"), None),
        P(("region", "dev"), None),
        P(),
    )
    return jax.shard_map(
        shards,
        mesh=mesh,
        in_specs=placed,
        out_specs=(
            P(("region", "dev"), None),
            P(("region", "dev"), None),
            P(None, ("region", "dev"), None),
            P(("region", "dev"), None),
        ),
        check_vma=False,
    )
```

```python
import functools

import jax
import jax.numpy as jnp
from jax import lax
from jax.experimental import pallas as pl
from jax.experimental.pallas import tpu as pltpu
from jax.sharding import PartitionSpec as P

type_radii = (1.2, 1.7, 1.55, 1.52, 1.85, 1.8)
type_scales = (0.85, 0.72, 0.79, 0.85, 0.86, 0.96)
radius_offset = 0.09
born_alpha = 1.0
born_beta = 0.8
born_gamma = 4.85
solvent_tau = 1.0 - 1.0 / 78.5

ROW_X, ROW_Y, ROW_Z, ROW_TYPE, ROW_CHARGE, ROW_PARTNER, ROW_COUNT = range(7)
STEP = 32
LANES = 128


def window_regions(region_count):
    return (region_count, True) if region_count <= 3 else (3, False)


def sent_to_all(payload, axes):
    copies = jnp.broadcast_to(payload, (lax.axis_size(axes),) + payload.shape)
    return lax.all_to_all(copies, axes, split_axis=0, concat_axis=0, tiled=True)


def gather_window(payload):
    regions = lax.axis_size("region")
    if window_regions(regions)[1]:
        return sent_to_all(payload, ("region", "dev"))
    here = sent_to_all(payload, "dev")
    below = lax.ppermute(here, "region", [(i, i + 1) for i in range(regions - 1)])
    above = lax.ppermute(here, "region", [(i + 1, i) for i in range(regions - 1)])
    return jnp.concatenate([below, here, above], axis=0)


def by_type(types, table):
    value = jnp.full(types.shape, table[0], jnp.float32)
    for index in range(1, len(table)):
        value = jnp.where(types == index, jnp.float32(table[index]), value)
    return value


def type_fields(types):
    intrinsic = by_type(types, type_radii)
    rho = intrinsic - radius_offset
    return intrinsic, rho, by_type(types, type_scales) * rho


def spread_columns(rows, columns_ref):
    count, atoms = rows.shape
    padded = jnp.concatenate([rows, jnp.zeros((LANES - count, atoms), jnp.float32)], axis=0)
    turned = padded.T
    for index in range(count):
        columns_ref[index] = jnp.broadcast_to(turned[:, index : index + 1], (atoms, LANES))


def lane_sums(columns, count):
    atoms = columns[0].shape[0]
    lane = lax.broadcasted_iota(jnp.int32, (atoms, LANES), 1)
    packed = jnp.zeros((atoms, LANES), jnp.float32)
    for index, column in enumerate(columns):
        packed = jnp.where(lane == index, jnp.sum(column, axis=1, keepdims=True), packed)
    return packed.T[:count]


def descreen(squared, rho, inv_rho, scaled, scaled_sq):
    inv_dist = lax.rsqrt(squared)
    distance = squared * inv_dist
    high = distance + scaled
    gap = distance - scaled
    low = jnp.maximum(rho, jnp.abs(gap))
    inv_both = pl.reciprocal(low * high)
    inv_low = high * inv_both
    inv_high = low * inv_both
    quarter = 0.25 * inv_dist
    curve = (squared - scaled_sq) * quarter
    body = (0.5 * (inv_low - inv_high)) * (1.0 - (inv_low + inv_high) * curve)
    body = body + jnp.log(low * inv_high) * quarter
    body = body + jnp.where(rho < -gap, inv_rho - inv_low, 0.0)
    return jnp.where(high > rho, body, 0.0)


def neighbour_lists(partner_ref, own_partner_ref, first_own, blocks, table_ref):
    window = partner_ref.shape[0]
    tiles = window // LANES
    ids = jnp.concatenate(
        [partner_ref[i * LANES : (i + 1) * LANES, :].T[:16] for i in range(tiles)], axis=1
    )
    lane = lax.broadcasted_iota(jnp.int32, (1, window), 1)
    rows = []
    for block in range(blocks):
        own = (first_own + block + 1).astype(jnp.float32)
        listed_by = jnp.max(jnp.where(ids == own, 1.0, 0.0), axis=0, keepdims=True)
        for slot in range(own_partner_ref.shape[1]):
            listed_by = jnp.where(lane == own_partner_ref[block, slot] - 1, 1.0, listed_by)
        rows.append(listed_by)
    spare = (-blocks) % 8
    linked = jnp.concatenate(rows + [jnp.zeros((spare, window), jnp.float32)] * (spare > 0), axis=0)
    before = lax.broadcasted_iota(jnp.int32, (window, window), 0)
    after = lax.broadcasted_iota(jnp.int32, (window, window), 1)
    ramp = jnp.where(before <= after, 1.0, 0.0).astype(jnp.bfloat16)
    rank = jnp.dot(linked.astype(jnp.bfloat16), ramp, preferred_element_type=jnp.float32)
    place = jnp.where(linked > 0.0, rank - 1.0, -1.0).astype(jnp.int32)
    total = jnp.sum(linked, axis=1, keepdims=True).astype(jnp.int32)
    tile_lane = lax.broadcasted_iota(jnp.int32, (LANES, LANES), 1)
    tile_row = lax.broadcasted_iota(jnp.int32, (LANES, LANES), 0)
    for out_tile in range(tiles):
        packed = jnp.zeros((LANES, LANES), jnp.float32)
        for block in range(blocks):
            found = jnp.zeros((LANES, LANES), jnp.float32)
            for in_tile in range(tiles):
                part = place[block : block + 1, in_tile * LANES : (in_tile + 1) * LANES]
                hit = part == tile_row + out_tile * LANES
                found = found + jnp.where(hit, (tile_lane + in_tile * LANES).astype(jnp.float32), 0.0)
            packed = jnp.where(tile_lane == block, jnp.sum(found, axis=1, keepdims=True), packed)
        table_ref[0:blocks, out_tile * LANES : (out_tile + 1) * LANES] = packed.T[:blocks].astype(jnp.int32)
    for block in range(blocks):
        table_ref[blocks + block : blocks + block + 1, :] = jnp.broadcast_to(
            total[block : block + 1], (1, window)
        )


def radii_kernel(
    blocks,
    first_ref,
    own_partner_ref,
    positions_ref,
    types_ref,
    fields_ref,
    window_types_ref,
    partner_ref,
    radii_ref,
    table_ref,
    columns_ref,
    scaled_ref,
    scaled_sq_ref,
    total_ref,
    lists_ref,
    lists_sem,
):
    atoms = types_ref.shape[1]
    neighbour_lists(partner_ref, own_partner_ref, first_ref[0], blocks, table_ref)
    move = pltpu.make_async_copy(table_ref, lists_ref, lists_sem)
    move.start()
    _, _, scaled = type_fields(window_types_ref[...])
    scaled_ref[...] = scaled
    scaled_sq_ref[...] = scaled * scaled
    intrinsic, rho, own_scaled = type_fields(types_ref[...])
    rows = [positions_ref[axis] for axis in range(3)] + [rho, 1.0 / rho]
    spread_columns(jnp.concatenate(rows, axis=0), columns_ref)
    move.wait()

    def pair_step(block, start, partner):
        step = pl.ds(start, STEP)
        x, y, z, s, s2 = partner
        dx = columns_ref[block, step, :] - x
        dy = columns_ref[blocks + block, step, :] - y
        dz = columns_ref[2 * blocks + block, step, :] - z
        squared = dx * dx + dy * dy + dz * dz
        return squared, columns_ref[3 * blocks + block, step, :], columns_ref[4 * blocks + block, step, :], s, s2

    for block in range(blocks):
        own = (
            positions_ref[0, block : block + 1, :],
            positions_ref[1, block : block + 1, :],
            positions_ref[2, block : block + 1, :],
            own_scaled[block : block + 1],
            own_scaled[block : block + 1] * own_scaled[block : block + 1],
        )
        for start in range(0, atoms, STEP):
            squared, r, ir, s, s2 = pair_step(block, start, own)
            same = lax.broadcasted_iota(jnp.int32, (STEP, LANES), 0) + start == lax.broadcasted_iota(
                jnp.int32, (STEP, LANES), 1
            )
            term = descreen(jnp.where(same, 1.0, squared), r, ir, s, s2)
            total_ref[block, start : start + STEP, :] = jnp.where(same, 0.0, term)

        def visit(index, carry, block=block):
            other = lists_ref[block, index]
            base = (other // blocks) * (ROW_COUNT * blocks) + other % blocks
            partner = tuple(
                fields_ref[pl.ds(base + row * blocks, 1), :] for row in (ROW_X, ROW_Y, ROW_Z)
            ) + (scaled_ref[pl.ds(other, 1), :], scaled_sq_ref[pl.ds(other, 1), :])
            for start in range(0, atoms, STEP):
                total_ref[block, start : start + STEP, :] += descreen(*pair_step(block, start, partner))
            return carry

        lax.fori_loop(0, lists_ref[blocks + block, 0], visit, 0)
    descreened = lane_sums([total_ref[block] for block in range(blocks)], blocks)
    psi = descreened * rho
    shaped = born_alpha * psi - born_beta * psi * psi + born_gamma * psi * psi * psi
    radii_ref[...] = 1.0 / (1.0 / rho - jnp.tanh(shaped) / intrinsic)


def energy_kernel(
    blocks,
    lists_ref,
    positions_ref,
    charges_ref,
    own_radii_ref,
    fields_ref,
    radii_ref,
    energy_ref,
    forces_ref,
    grad_ref,
    columns_ref,
    decay_ref,
    total_ref,
):
    atoms = charges_ref.shape[1]
    decay_ref[...] = 1.0 / radii_ref[...]
    own_radii = own_radii_ref[...]
    own_decay = 1.0 / own_radii
    rows = [positions_ref[axis] for axis in range(3)] + [own_radii, -0.25 * own_decay]
    spread_columns(jnp.concatenate(rows, axis=0), columns_ref)

    def pair_terms(block, start, partner, same=None):
        step = pl.ds(start, STEP)
        x, y, z, charge, radius, decay = partner
        dx = columns_ref[block, step, :] - x
        dy = columns_ref[blocks + block, step, :] - y
        dz = columns_ref[2 * blocks + block, step, :] - z
        squared = dx * dx + dy * dy + dz * dz
        if same is not None:
            squared = jnp.where(same, 1.0, squared)
        power = squared * (columns_ref[4 * blocks + block, step, :] * decay)
        damped = jnp.exp(power)
        blend = (columns_ref[3 * blocks + block, step, :] * radius) * damped
        inv_root = lax.rsqrt(squared + blend)
        if same is not None:
            charge = jnp.where(same, 0.0, charge)
        potential = charge * inv_root
        cubed = potential * (inv_root * inv_root)
        pull = cubed * (1.0 - 0.25 * damped)
        return (pull * dx, pull * dy, pull * dz, potential, cubed * blend * (1.0 - power))

    for block in range(blocks):
        own = tuple(positions_ref[axis, block : block + 1, :] for axis in range(3)) + (
            charges_ref[block : block + 1, :],
            own_radii[block : block + 1],
            own_decay[block : block + 1],
        )
        for start in range(0, atoms, STEP):
            same = lax.broadcasted_iota(jnp.int32, (STEP, LANES), 0) + start == lax.broadcasted_iota(
                jnp.int32, (STEP, LANES), 1
            )
            for term, value in enumerate(pair_terms(block, start, own, same)):
                total_ref[term * blocks + block, start : start + STEP, :] = value

        def visit(index, carry, block=block):
            other = lists_ref[block, index]
            base = (other // blocks) * (ROW_COUNT * blocks) + other % blocks
            partner = tuple(
                fields_ref[pl.ds(base + row * blocks, 1), :] for row in (ROW_X, ROW_Y, ROW_Z, ROW_CHARGE)
            ) + (radii_ref[pl.ds(other, 1), :], decay_ref[pl.ds(other, 1), :])
            for start in range(0, atoms, STEP):
                for term, value in enumerate(pair_terms(block, start, partner)):
                    total_ref[term * blocks + block, start : start + STEP, :] += value
            return carry

        lax.fori_loop(0, lists_ref[blocks + block, 0], visit, 0)
    sums = lane_sums([total_ref[index] for index in range(5 * blocks)], 5 * blocks)
    charges = charges_ref[...]
    scale = solvent_tau * charges
    for axis in range(3):
        forces_ref[axis] = -scale * sums[axis * blocks : (axis + 1) * blocks]
    own_energy = 0.5 * scale * charges * own_decay
    energy_ref[...] = -0.5 * scale * sums[3 * blocks : 4 * blocks] - own_energy
    grad_ref[...] = (0.5 * scale * sums[4 * blocks : 5 * blocks] + own_energy) * own_decay


def shards(positions, charges, types, pairs, owner_map):
    _, blocks, atoms = positions.shape
    regions = lax.axis_size("region")
    region_devices = lax.axis_size("dev")
    kept_regions, whole = window_regions(regions)
    window = kept_regions * region_devices * blocks
    padded = -(-window // LANES) * LANES
    region_here = lax.axis_index("region")
    first_window = 0 if whole else (region_here - 1) * region_devices * blocks
    first_own = (region_here * region_devices + lax.axis_index("dev")) * blocks

    partners = jnp.where(pairs >= 0, owner_map[jnp.maximum(pairs, 0)] + 1, 0)
    partner_row = jnp.pad(partners.astype(jnp.float32), ((0, 0), (0, atoms - pairs.shape[1])))
    payload = jnp.concatenate(
        [positions, types.astype(jnp.float32)[None], charges[None], partner_row[None]], axis=0
    )
    gathered = gather_window(payload)
    window_types = gathered[:, ROW_TYPE].reshape(window, atoms)
    window_partners = gathered[:, ROW_PARTNER].reshape(window, atoms)
    if padded > window:
        window_partners = jnp.pad(window_partners, ((0, padded - window), (0, 0)))
    fields = gathered.reshape(window * ROW_COUNT, atoms)
    own_place = jnp.maximum(partners - first_window, 0) * (partners > 0)

    vmem = pl.BlockSpec(memory_space=pltpu.VMEM)
    smem = pl.BlockSpec(memory_space=pltpu.SMEM)
    table = jax.ShapeDtypeStruct((-(-2 * blocks // 8) * 8, padded), jnp.int32)
    own_radii, lists = pl.pallas_call(
        functools.partial(radii_kernel, blocks),
        out_shape=(jax.ShapeDtypeStruct((blocks, atoms), jnp.float32), table),
        in_specs=[smem, smem] + [vmem] * 5,
        out_specs=(vmem, vmem),
        scratch_shapes=[
            pltpu.VMEM((5 * blocks, atoms, LANES), jnp.float32),
            pltpu.VMEM((window, atoms), jnp.float32),
            pltpu.VMEM((window, atoms), jnp.float32),
            pltpu.VMEM((blocks, atoms, LANES), jnp.float32),
            pltpu.SMEM(table.shape, jnp.int32),
            pltpu.SemaphoreType.DMA(()),
        ],
        compiler_params=pltpu.CompilerParams(vmem_limit_bytes=40 * 1024 * 1024),
    )(
        jnp.full((1,), first_own, jnp.int32),
        own_place,
        positions,
        types,
        fields,
        window_types,
        window_partners,
    )
    window_radii = gather_window(own_radii).reshape(window, atoms)
    block_out = jax.ShapeDtypeStruct((blocks, atoms), jnp.float32)
    energy, forces, grad = pl.pallas_call(
        functools.partial(energy_kernel, blocks),
        out_shape=(block_out, jax.ShapeDtypeStruct((3, blocks, atoms), jnp.float32), block_out),
        in_specs=[smem] + [vmem] * 5,
        out_specs=(vmem, vmem, vmem),
        scratch_shapes=[
            pltpu.VMEM((5 * blocks, atoms, LANES), jnp.float32),
            pltpu.VMEM((window, atoms), jnp.float32),
            pltpu.VMEM((5 * blocks, atoms, LANES), jnp.float32),
        ],
        compiler_params=pltpu.CompilerParams(vmem_limit_bytes=40 * 1024 * 1024),
    )(lists, positions, charges, own_radii, fields, window_radii)
    return own_radii, energy, forces, grad


def solution(mesh):
    placed = (
        P(None, ("region", "dev"), None),
        P(("region", "dev"), None),
        P(("region", "dev"), None),
        P(("region", "dev"), None),
        P(),
    )
    return jax.shard_map(
        shards,
        mesh=mesh,
        in_specs=placed,
        out_specs=(
            P(("region", "dev"), None),
            P(("region", "dev"), None),
            P(None, ("region", "dev"), None),
            P(("region", "dev"), None),
        ),
        check_vma=False,
    )
```

```python
import functools

import jax
import jax.numpy as jnp
from jax import lax
from jax.experimental import pallas as pl
from jax.experimental.pallas import tpu as pltpu
from jax.sharding import PartitionSpec as P

type_radii = (1.2, 1.7, 1.55, 1.52, 1.85, 1.8)
type_scales = (0.85, 0.72, 0.79, 0.85, 0.86, 0.96)
radius_offset = 0.09
born_alpha = 1.0
born_beta = 0.8
born_gamma = 4.85
solvent_tau = 1.0 - 1.0 / 78.5

ROW_X, ROW_Y, ROW_Z, ROW_TYPE, ROW_CHARGE, ROW_PARTNER, ROW_COUNT = range(7)
LANES = 128
STEP = 32
CHUNK = 32
EMPTY_SLOT = -1.0e6
FAR_AWAY = 1.0e15

scaled_values = [scale * (radius - radius_offset) for radius, scale in zip(type_radii, type_scales)]
short_range = 1.01 * max(
    max(scaled_values) - (min(type_radii) - radius_offset),
    (max(type_radii) - radius_offset) - min(scaled_values),
    0.5,
)


def window_regions(region_count):
    return (region_count, True) if region_count <= 3 else (3, False)


def exchange_axes():
    return ("region", "dev") if window_regions(lax.axis_size("region"))[1] else ("dev",)


def gather_window(copies):
    here = lax.all_to_all(copies, exchange_axes(), split_axis=0, concat_axis=0, tiled=True)
    regions = lax.axis_size("region")
    if window_regions(regions)[1]:
        return here
    below = lax.ppermute(here, "region", [(i, i + 1) for i in range(regions - 1)])
    above = lax.ppermute(here, "region", [(i + 1, i) for i in range(regions - 1)])
    return jnp.concatenate([below, here, above], axis=0)


def by_type(types, table):
    value = jnp.full(types.shape, table[0], jnp.float32)
    for index in range(1, len(table)):
        value = jnp.where(types == index, jnp.float32(table[index]), value)
    return value


def type_fields(types):
    intrinsic = by_type(types, type_radii)
    rho = intrinsic - radius_offset
    return intrinsic, rho, by_type(types, type_scales) * rho


def turned(rows):
    count, width = rows.shape
    if count < LANES:
        rows = jnp.concatenate([rows, jnp.zeros((LANES - count, width), rows.dtype)], axis=0)
    return rows.T


def spread(columns, index):
    return jnp.broadcast_to(columns[:, index : index + 1], (columns.shape[0], LANES))


def lane_sums(arrays, count):
    atoms = arrays[0].shape[0]
    lane = lax.broadcasted_iota(jnp.int32, (atoms, LANES), 1)
    packed = jnp.zeros((atoms, LANES), jnp.float32)
    for index, array in enumerate(arrays):
        packed = jnp.where(lane == index, jnp.sum(array, axis=1, keepdims=True), packed)
    return packed.T[:count]


def fields_kernel(positions_ref, types_ref, charges_ref, pairs_ref, owner_ref, copies_ref):
    copy_count, _, blocks, atoms = copies_ref.shape
    slot = lax.broadcasted_iota(jnp.int32, (1, atoms), 1)
    partners = []
    for block in range(blocks):
        row = jnp.full((1, atoms), EMPTY_SLOT, jnp.float32)
        for index in range(pairs_ref.shape[1]):
            cell = pairs_ref[block, index]
            partner = jnp.where(cell >= 0, owner_ref[jnp.maximum(cell, 0)] + 1, int(EMPTY_SLOT))
            row = jnp.where(slot == index, partner.astype(jnp.float32), row)
        partners.append(row)
    rows = [positions_ref[axis] for axis in range(3)]
    rows += [types_ref[...].astype(jnp.float32), charges_ref[...], jnp.concatenate(partners, axis=0)]
    for copy in range(copy_count):
        for index, row in enumerate(rows):
            copies_ref[copy, index] = row


def descreen(squared, rho, scaled):
    inv_dist = lax.rsqrt(squared)
    share = scaled * inv_dist
    inner = 0.25 - share
    high = 0.25 + share
    low = jnp.maximum(rho * inv_dist, inner)
    inv_low = pltpu.reciprocal(low, approx=True)
    ratio = low * pltpu.reciprocal(high, approx=True)
    curve = (1.0 - ratio) + inner * (ratio - high * inv_low)
    return (inv_low * curve + 2.0 * jnp.log(ratio)) * inv_dist


def descreen_any(squared, rho, scaled):
    rho, scaled = 4.0 * rho, 4.0 * scaled
    inv_dist = lax.rsqrt(squared)
    distance = squared * inv_dist
    high = distance + scaled
    gap = distance - scaled
    low = jnp.maximum(rho, jnp.abs(gap))
    inv_low = 1.0 / low
    inv_high = 1.0 / high
    quarter = 0.25 * inv_dist
    curve = (squared - scaled * scaled) * quarter
    body = (0.5 * (inv_low - inv_high)) * (1.0 - (inv_low + inv_high) * curve)
    body = body + jnp.log(low * inv_high) * quarter
    body = body + jnp.where(rho < -gap, 1.0 / rho - inv_low, 0.0)
    return jnp.where(high > rho, 8.0 * body, 0.0)


def neighbour_lists(partner_ref, first_home, home_id, first_window, homes, slots, filler, table_ref):
    window = partner_ref.shape[0]
    tiles = [slice(start, start + LANES) for start in range(0, window, LANES)]
    depth = -(-slots // 8) * 8
    ids = jnp.concatenate([partner_ref[tile, :].T[:depth] for tile in tiles], axis=1)
    lists = turned(partner_ref[pl.ds(first_home, homes), :])[:depth]
    lane = lax.broadcasted_iota(jnp.int32, (depth, window), 1)
    lane_id = (lane + (first_window + 1)).astype(jnp.float32)
    rows = []
    for home in range(homes):
        own = (home_id + home + 1).astype(jnp.float32)
        linked = (ids == own) | (lane_id == lists[:, home : home + 1])
        rows.append(jnp.max(jnp.where(linked, 1.0, 0.0), axis=0, keepdims=True))
    linked = jnp.concatenate(rows, axis=0)
    before = lax.broadcasted_iota(jnp.int32, (window, window), 0)
    after = lax.broadcasted_iota(jnp.int32, (window, window), 1)
    ramp = jnp.where(before <= after, 1.0, 0.0).astype(jnp.bfloat16)
    rank = jnp.dot(linked.astype(jnp.bfloat16), ramp, preferred_element_type=jnp.float32)
    place = jnp.where(linked > 0.0, rank - 1.0, -1.0)
    total = jnp.sum(linked, axis=1, keepdims=True)
    columns = [turned(place[:, tile]) for tile in tiles]
    spot = lax.broadcasted_iota(jnp.int32, (LANES, LANES), 1).astype(jnp.float32)
    name = lax.broadcasted_iota(jnp.int32, (LANES, LANES), 0).astype(jnp.float32)
    for tile in tiles:
        for home in range(homes):
            found = jnp.zeros((LANES, LANES), jnp.float32)
            for other, column in zip(tiles, columns):
                hit = column[:, home : home + 1] == spot + float(tile.start)
                found = found + jnp.where(hit, name + float(other.start), 0.0)
            row = jnp.sum(found, axis=0, keepdims=True)
            past = spot[:1] + float(tile.start) >= total[home : home + 1]
            table_ref[home : home + 1, tile] = jnp.where(past, float(filler), row).astype(jnp.int32)
    table_ref[homes : 2 * homes, :] = jnp.broadcast_to(total, (homes, window)).astype(jnp.int32)


def radii_kernel(
    blocks,
    slots,
    place_ref,
    x_ref,
    y_ref,
    z_ref,
    types_ref,
    partner_ref,
    copies_ref,
    table_ref,
    columns_ref,
    window_ref,
    total_ref,
    turned_ref,
    packed_ref,
    near_ref,
    lists_ref,
    lists_sem,
):
    _, homes, chunk, _ = columns_ref.shape
    window = types_ref.shape[0]
    parts = homes // blocks
    together = max(1, LANES // chunk)
    first_home = pl.multiple_of(place_ref[0], homes)
    first_atom = pl.multiple_of(place_ref[3], chunk)
    neighbour_lists(partner_ref, first_home, place_ref[1], place_ref[2], homes, slots, window, table_ref)
    move = pltpu.make_async_copy(table_ref, lists_ref, lists_sem)
    move.start()

    _, _, scaled = type_fields(types_ref[...])
    for index, field in enumerate((x_ref[...], y_ref[...], z_ref[...], 0.25 * scaled)):
        window_ref[index, 0:window, :] = field
        window_ref[index, window : window + 8, :] = jnp.full((8, LANES), 0.0 if index else FAR_AWAY, jnp.float32)

    home_rows = [ref[pl.ds(first_home, homes), :] for ref in (types_ref, x_ref, y_ref, z_ref)]
    turned_ref[...] = turned(jnp.concatenate(home_rows, axis=0))
    columns = turned_ref[pl.ds(first_atom, chunk), :]
    intrinsic, rho, _ = type_fields(columns)
    for home in range(homes):
        columns_ref[0, home] = spread(0.25 * rho, home)
        for index in range(1, 4):
            columns_ref[index, home] = spread(columns, index * homes + home)

    def pair_distance(home, partner, start):
        step = pl.ds(start, STEP)
        dx = columns_ref[1, home, step, :] - window_ref[0, pl.ds(partner, 1), :]
        dy = columns_ref[2, home, step, :] - window_ref[1, pl.ds(partner, 1), :]
        dz = columns_ref[3, home, step, :] - window_ref[2, pl.ds(partner, 1), :]
        return dx * dx + dy * dy + dz * dz

    def sweep(integral):
        near_ref[...] = jnp.full((STEP, LANES), FAR_AWAY, jnp.float32)

        def own_pairs(turn, carry):
            for index in range(together):
                home = turn * together + index
                for start in range(0, chunk, STEP):
                    row = lax.broadcasted_iota(jnp.int32, (STEP, LANES), 0) + (first_atom + start)
                    same = row == lax.broadcasted_iota(jnp.int32, (STEP, LANES), 1)
                    squared = jnp.where(same, FAR_AWAY, pair_distance(home, first_home + home, start))
                    term = integral(
                        squared,
                        columns_ref[0, home, pl.ds(start, STEP), :],
                        window_ref[3, pl.ds(first_home + home, 1), :],
                    )
                    total_ref[home, pl.ds(start, STEP), :] = jnp.where(same, 0.0, term)
                    near_ref[...] = jnp.minimum(near_ref[...], squared)
            return carry

        lax.fori_loop(0, homes // together, own_pairs, 0)
        lane = lax.broadcasted_iota(jnp.int32, (chunk, LANES), 1)

        def one_home(home, packed):
            def visit(turn, carry):
                sums, nearest = list(carry[0]), carry[1]
                for index in range(together):
                    partner = lists_ref[home, turn * together + index]
                    scaled = window_ref[3, pl.ds(partner, 1), :]
                    for place, start in enumerate(range(0, chunk, STEP)):
                        squared = pair_distance(home, partner, start)
                        nearest = jnp.minimum(nearest, squared)
                        rho = columns_ref[0, home, pl.ds(start, STEP), :]
                        sums[place] = sums[place] + integral(squared, rho, scaled)
                return tuple(sums), nearest

            turns = (lists_ref[homes + home, 0] + (together - 1)) // together
            begin = tuple(total_ref[home, pl.ds(start, STEP), :] for start in range(0, chunk, STEP))
            sums, nearest = lax.fori_loop(0, turns, visit, (begin, near_ref[...]))
            near_ref[...] = nearest
            sums = jnp.concatenate([jnp.sum(part, axis=1, keepdims=True) for part in sums], axis=0)
            return jnp.where(lane == home, sums, packed)

        packed_ref[...] = lax.fori_loop(0, homes, one_home, jnp.zeros((chunk, LANES), jnp.float32))

    move.wait()
    sweep(descreen)

    @pl.when(jnp.min(near_ref[...]) < short_range * short_range)
    def _():
        sweep(descreen_any)

    psi = (0.125 * packed_ref[...]) * rho
    shaped = born_alpha * psi - born_beta * psi * psi + born_gamma * psi * psi * psi
    radii = 1.0 / (1.0 / rho - jnp.tanh(shaped) / intrinsic)

    if chunk < LANES:
        radii = jnp.concatenate([radii, jnp.zeros((LANES - chunk, LANES), jnp.float32)], axis=0)
    turned_ref[...] = radii.T
    lane = lax.broadcasted_iota(jnp.int32, (blocks, LANES), 1)
    sent = turned_ref[pl.ds(0, blocks, stride=parts), :]
    for index in range(1, parts):
        rows = pltpu.roll(turned_ref[pl.ds(index, blocks, stride=parts), :], index * chunk, 1)
        sent = jnp.where(lane >= index * chunk, rows, sent)
    for copy in range(copies_ref.shape[0]):
        copies_ref[copy] = sent


def energy_kernel(
    blocks,
    parts,
    place_ref,
    lists_ref,
    positions_ref,
    charges_ref,
    fields_ref,
    gathered_ref,
    own_radii_ref,
    energy_ref,
    forces_ref,
    grad_ref,
    columns_ref,
    radii_ref,
    decay_ref,
    total_ref,
):
    atoms = charges_ref.shape[1]
    devices = gathered_ref.shape[0]
    window = devices * blocks
    part_rows = window // parts
    chunk = atoms // parts
    first_own, list_row = place_ref[0], place_ref[1]

    lane = lax.broadcasted_iota(jnp.int32, (part_rows, LANES), 1)
    if parts == 1:
        radii_ref[...] = gathered_ref[...].reshape(window, atoms)
    else:
        pieces = [
            gathered_ref[pl.ds(part, devices // parts, stride=parts)].reshape(part_rows, atoms)
            for part in range(parts)
        ]
        for place in range(parts):
            whole = pieces[0] if place == 0 else pltpu.roll(pieces[0], (parts - place) * chunk, 1)
            for part in range(1, parts):
                shift = (part - place) % parts
                piece = pieces[part] if shift == 0 else pltpu.roll(pieces[part], shift * chunk, 1)
                whole = jnp.where(lane >= part * chunk, piece, whole)
            radii_ref[place * part_rows : (place + 1) * part_rows, :] = whole
    decay_ref[...] = 1.0 / radii_ref[...]

    def radii_row(block):
        return pl.ds((block % parts) * part_rows + block // parts, 1)

    for block in range(blocks):
        own_radii_ref[block : block + 1, :] = radii_ref[radii_row(first_own + block), :]
    own_radii = own_radii_ref[...]
    own_decay = 1.0 / own_radii
    rows = [positions_ref[axis] for axis in range(3)] + [own_radii, -0.25 * own_decay]
    columns = turned(jnp.concatenate(rows, axis=0))
    for index in range(5 * blocks):
        columns_ref[index] = spread(columns, index)

    def pair_terms(block, start, partner, same=None):
        step = pl.ds(start, STEP)
        x, y, z, charge, radius, decay = partner
        dx = columns_ref[block, step, :] - x
        dy = columns_ref[blocks + block, step, :] - y
        dz = columns_ref[2 * blocks + block, step, :] - z
        squared = dx * dx + dy * dy + dz * dz
        if same is not None:
            squared = jnp.where(same, 1.0, squared)
        power = squared * (columns_ref[4 * blocks + block, step, :] * decay)
        damped = jnp.exp(power)
        blend = (columns_ref[3 * blocks + block, step, :] * radius) * damped
        inv_root = lax.rsqrt(squared + blend)
        if same is not None:
            charge = jnp.where(same, 0.0, charge)
        potential = charge * inv_root
        cubed = potential * (inv_root * inv_root)
        pull = cubed * (1.0 - 0.25 * damped)
        return (pull * dx, pull * dy, pull * dz, potential, cubed * blend * (1.0 - power))

    for block in range(blocks):
        own = tuple(positions_ref[axis, block : block + 1, :] for axis in range(3)) + (
            charges_ref[block : block + 1, :],
            own_radii[block : block + 1],
            own_decay[block : block + 1],
        )
        for start in range(0, atoms, STEP):
            same = lax.broadcasted_iota(jnp.int32, (STEP, LANES), 0) + start == lax.broadcasted_iota(
                jnp.int32, (STEP, LANES), 1
            )
            for term, value in enumerate(pair_terms(block, start, own, same)):
                total_ref[term * blocks + block, start : start + STEP, :] = value

        def visit(index, carry, block=block):
            other = lists_ref[list_row + block, index]
            base = (other // blocks) * (ROW_COUNT * blocks) + other % blocks
            row = radii_row(other)
            partner = tuple(
                fields_ref[pl.ds(base + field * blocks, 1), :] for field in (ROW_X, ROW_Y, ROW_Z, ROW_CHARGE)
            ) + (radii_ref[row, :], decay_ref[row, :])
            for start in range(0, atoms, STEP):
                for term, value in enumerate(pair_terms(block, start, partner)):
                    total_ref[term * blocks + block, start : start + STEP, :] += value
            return carry

        lax.fori_loop(0, lists_ref[parts * blocks + list_row + block, 0], visit, 0)
    sums = lane_sums([total_ref[index] for index in range(5 * blocks)], 5 * blocks)
    charges = charges_ref[...]
    scale = solvent_tau * charges
    for axis in range(3):
        forces_ref[axis] = -scale * sums[axis * blocks : (axis + 1) * blocks]
    own_energy = 0.5 * scale * charges * own_decay
    energy_ref[...] = -0.5 * scale * sums[3 * blocks : 4 * blocks] - own_energy
    grad_ref[...] = (0.5 * scale * sums[4 * blocks : 5 * blocks] + own_energy) * own_decay


def shards(positions, charges, types, pairs, owner_map):
    _, blocks, atoms = positions.shape
    regions = lax.axis_size("region")
    region_devices = lax.axis_size("dev")
    kept_regions, whole = window_regions(regions)
    devices = kept_regions * region_devices
    window = devices * blocks
    region_here = lax.axis_index("region")
    device_here = lax.axis_index("dev")
    first_window = 0 if whole else (region_here - 1) * region_devices * blocks

    parts = atoms // CHUNK
    while region_devices % parts or 4 * parts * blocks > LANES:
        parts //= 2
    homes = parts * blocks
    chunk = atoms // parts
    part_here = device_here % parts
    home_id = (region_here * region_devices + device_here - part_here) * blocks
    first_home = home_id - first_window

    vmem = pl.BlockSpec(memory_space=pltpu.VMEM)
    smem = pl.BlockSpec(memory_space=pltpu.SMEM)
    params = pltpu.CompilerParams(vmem_limit_bytes=40 * 1024 * 1024)
    copy_count = lax.axis_size(exchange_axes())
    gathered = gather_window(
        pl.pallas_call(
            fields_kernel,
            out_shape=jax.ShapeDtypeStruct((copy_count, ROW_COUNT, blocks, atoms), jnp.float32),
            in_specs=[vmem, vmem, vmem, smem, smem],
            out_specs=vmem,
            compiler_params=params,
        )(positions, types, charges, pairs, owner_map)
    )
    x, y, z, window_types, window_partners = (
        gathered[:, row].reshape(window, atoms) for row in (ROW_X, ROW_Y, ROW_Z, ROW_TYPE, ROW_PARTNER)
    )
    if window % LANES:
        window_partners = jnp.pad(window_partners, ((0, -window % LANES), (0, 0)))
    table = jax.ShapeDtypeStruct((2 * homes, window_partners.shape[0]), jnp.int32)
    place = jnp.stack([first_home, home_id, jnp.int32(first_window), part_here * chunk])
    copies, lists = pl.pallas_call(
        functools.partial(radii_kernel, blocks, pairs.shape[1]),
        out_shape=(jax.ShapeDtypeStruct((copy_count, blocks, atoms), jnp.float32), table),
        in_specs=[smem] + [vmem] * 5,
        out_specs=(vmem, vmem),
        scratch_shapes=[
            pltpu.VMEM((4, homes, chunk, LANES), jnp.float32),
            pltpu.VMEM((4, window + 8, atoms), jnp.float32),
            pltpu.VMEM((homes, chunk, LANES), jnp.float32),
            pltpu.VMEM((LANES, LANES), jnp.float32),
            pltpu.VMEM((chunk, LANES), jnp.float32),
            pltpu.VMEM((STEP, LANES), jnp.float32),
            pltpu.SMEM(table.shape, jnp.int32),
            pltpu.SemaphoreType.DMA(()),
        ],
        compiler_params=params,
    )(place, x, y, z, window_types, window_partners)
    block_out = jax.ShapeDtypeStruct((blocks, atoms), jnp.float32)
    own_place = jnp.stack([first_home + part_here * blocks, part_here * blocks])
    own_radii, energy, forces, grad = pl.pallas_call(
        functools.partial(energy_kernel, blocks, parts),
        out_shape=(block_out, block_out, jax.ShapeDtypeStruct((3, blocks, atoms), jnp.float32), block_out),
        in_specs=[smem, smem] + [vmem] * 4,
        out_specs=(vmem, vmem, vmem, vmem),
        scratch_shapes=[
            pltpu.VMEM((5 * blocks, atoms, LANES), jnp.float32),
            pltpu.VMEM((window, atoms), jnp.float32),
            pltpu.VMEM((window, atoms), jnp.float32),
            pltpu.VMEM((5 * blocks, atoms, LANES), jnp.float32),
        ],
        compiler_params=params,
    )(own_place, lists, positions, charges, gathered.reshape(window * ROW_COUNT, atoms), gather_window(copies))
    return own_radii, energy, forces, grad


def solution(mesh):
    placed = (
        P(None, ("region", "dev"), None),
        P(("region", "dev"), None),
        P(("region", "dev"), None),
        P(("region", "dev"), None),
        P(),
    )
    return jax.shard_map(
        shards,
        mesh=mesh,
        in_specs=placed,
        out_specs=(
            P(("region", "dev"), None),
            P(("region", "dev"), None),
            P(None, ("region", "dev"), None),
            P(("region", "dev"), None),
        ),
        check_vma=False,
    )
```

```python
import functools

import jax
import jax.numpy as jnp
from jax import lax
from jax.experimental import pallas as pl
from jax.experimental.pallas import tpu as pltpu
from jax.sharding import PartitionSpec as P

type_radii = (1.2, 1.7, 1.55, 1.52, 1.85, 1.8)
type_scales = (0.85, 0.72, 0.79, 0.85, 0.86, 0.96)
radius_offset = 0.09
born_alpha = 1.0
born_beta = 0.8
born_gamma = 4.85
solvent_tau = 1.0 - 1.0 / 78.5

ROW_X, ROW_Y, ROW_Z, ROW_TYPE, ROW_CHARGE, ROW_PARTNER, ROW_COUNT = range(7)
LANES = 128
SUBLANES = 8
STEP = 4
CHUNK = 32
ITEMS = 4
EMPTY_SLOT = -1.0e6
FAR_AWAY = 1.0e15

scaled_values = [scale * (radius - radius_offset) for radius, scale in zip(type_radii, type_scales)]
short_range = 1.01 * max(
    max(scaled_values) - (min(type_radii) - radius_offset),
    (max(type_radii) - radius_offset) - min(scaled_values),
    0.5,
)


def window_regions(region_count):
    return (region_count, True) if region_count <= 3 else (3, False)


def exchange_axes():
    return ("region", "dev") if window_regions(lax.axis_size("region"))[1] else ("dev",)


def gather_window(copies):
    here = lax.all_to_all(copies, exchange_axes(), split_axis=0, concat_axis=0, tiled=True)
    regions = lax.axis_size("region")
    if window_regions(regions)[1]:
        return here
    below = lax.ppermute(here, "region", [(i, i + 1) for i in range(regions - 1)])
    above = lax.ppermute(here, "region", [(i + 1, i) for i in range(regions - 1)])
    return jnp.concatenate([below, here, above], axis=0)


def by_type(types, table):
    value = jnp.full(types.shape, table[0], jnp.float32)
    for index in range(1, len(table)):
        value = jnp.where(types == index, jnp.float32(table[index]), value)
    return value


def type_fields(types):
    intrinsic = by_type(types, type_radii)
    rho = intrinsic - radius_offset
    return intrinsic, rho, by_type(types, type_scales) * rho


def turned(rows):
    count, width = rows.shape
    if count < LANES:
        rows = jnp.concatenate([rows, jnp.zeros((LANES - count, width), rows.dtype)], axis=0)
    return rows.T


def spread(columns, index):
    count = columns.shape[0]
    wide = jnp.broadcast_to(columns[:, index : index + 1], (count, LANES))
    return wide.reshape(count // SUBLANES, SUBLANES, LANES)


def row_of(ref, field, row):
    return ref[field, pl.ds(row, SUBLANES, stride=0), :][None]


def diagonal(groups, first_atom):
    shape = (groups, SUBLANES, LANES)
    row = lax.broadcasted_iota(jnp.int32, shape, 0) * SUBLANES + lax.broadcasted_iota(jnp.int32, shape, 1)
    return row + first_atom == lax.broadcasted_iota(jnp.int32, shape, 2)


def lane_total(array):
    return jnp.sum(array.reshape(-1, LANES), axis=1, keepdims=True)


def lane_sums(arrays, count):
    atoms = arrays[0].shape[0] * SUBLANES
    lane = lax.broadcasted_iota(jnp.int32, (atoms, LANES), 1)
    packed = jnp.zeros((atoms, LANES), jnp.float32)
    for index, array in enumerate(arrays):
        packed = jnp.where(lane == index, lane_total(array), packed)
    return packed.T[:count]


def fields_kernel(blocks, atoms, *refs):
    inputs, copies_ref, here, sems = refs[:5], refs[5], refs[6:11], refs[11]
    moves = [pltpu.make_async_copy(src, dst, sems.at[i]) for i, (src, dst) in enumerate(zip(inputs, here))]
    for move in moves:
        move.start()
    for move in moves:
        move.wait()
    positions_ref, types_ref, charges_ref, pairs_ref, owner_ref = here
    slot = lax.broadcasted_iota(jnp.int32, (1, atoms), 1)
    partners = []
    for block in range(blocks):
        row = jnp.full((1, atoms), EMPTY_SLOT, jnp.float32)
        for index in range(pairs_ref.shape[1]):
            cell = pairs_ref[block, index]
            partner = jnp.where(cell >= 0, owner_ref[jnp.maximum(cell, 0)] + 1, int(EMPTY_SLOT))
            row = jnp.where(slot == index, partner.astype(jnp.float32), row)
        partners.append(row)
    rows = [positions_ref[axis] for axis in range(3)]
    rows += [types_ref[...].astype(jnp.float32), charges_ref[...], jnp.concatenate(partners, axis=0)]
    for copy in range(copies_ref.shape[0]):
        for index, row in enumerate(rows):
            copies_ref[copy, index] = row


def descreen(squared, rho, scaled):
    inv_dist = lax.rsqrt(squared)
    share = scaled * inv_dist
    inner = 0.25 - share
    high = 0.25 + share
    low = jnp.maximum(rho * inv_dist, inner)
    inv_low = pltpu.reciprocal(low, approx=True)
    ratio = low * pltpu.reciprocal(high, approx=True)
    curve = (1.0 - ratio) + inner * (ratio - high * inv_low)
    return (inv_low * curve + 2.0 * jnp.log(ratio)) * inv_dist


def descreen_any(squared, rho, scaled):
    rho, scaled = 4.0 * rho, 4.0 * scaled
    inv_dist = lax.rsqrt(squared)
    distance = squared * inv_dist
    high = distance + scaled
    gap = distance - scaled
    low = jnp.maximum(rho, jnp.abs(gap))
    inv_low = 1.0 / low
    inv_high = 1.0 / high
    quarter = 0.25 * inv_dist
    curve = (squared - scaled * scaled) * quarter
    body = (0.5 * (inv_low - inv_high)) * (1.0 - (inv_low + inv_high) * curve)
    body = body + jnp.log(low * inv_high) * quarter
    body = body + jnp.where(rho < -gap, 1.0 / rho - inv_low, 0.0)
    return jnp.where(high > rho, 8.0 * body, 0.0)


def neighbour_lists(partner_ref, first_home, home_id, first_window, homes, slots, filler, table_ref):
    window = partner_ref.shape[0]
    tiles = [slice(start, start + LANES) for start in range(0, window, LANES)]
    depth = -(-slots // 8) * 8
    ids = jnp.concatenate([partner_ref[tile, :].T[:depth] for tile in tiles], axis=1)
    lists = turned(partner_ref[pl.ds(first_home, homes), :])[:depth]
    lane = lax.broadcasted_iota(jnp.int32, (depth, window), 1)
    lane_id = (lane + (first_window + 1)).astype(jnp.float32)
    rows = []
    for home in range(homes):
        own = (home_id + home + 1).astype(jnp.float32)
        linked = (ids == own) | (lane_id == lists[:, home : home + 1])
        rows.append(jnp.max(jnp.where(linked, 1.0, 0.0), axis=0, keepdims=True))
    linked = jnp.concatenate(rows, axis=0)
    before = lax.broadcasted_iota(jnp.int32, (window, window), 0)
    after = lax.broadcasted_iota(jnp.int32, (window, window), 1)
    ramp = jnp.where(before <= after, 1.0, 0.0).astype(jnp.bfloat16)
    rank = jnp.dot(linked.astype(jnp.bfloat16), ramp, preferred_element_type=jnp.float32)
    place = jnp.where(linked > 0.0, rank - 1.0, -1.0)
    total = jnp.sum(linked, axis=1, keepdims=True)
    columns = [turned(place[:, tile]) for tile in tiles]
    spot = lax.broadcasted_iota(jnp.int32, (LANES, LANES), 1).astype(jnp.float32)
    name = lax.broadcasted_iota(jnp.int32, (LANES, LANES), 0).astype(jnp.float32)
    for tile in tiles:
        for home in range(homes):
            found = jnp.zeros((LANES, LANES), jnp.float32)
            for other, column in zip(tiles, columns):
                hit = column[:, home : home + 1] == spot + float(tile.start)
                found = found + jnp.where(hit, name + float(other.start), 0.0)
            row = jnp.sum(found, axis=0, keepdims=True)
            past = spot[:1] + float(tile.start) >= total[home : home + 1]
            table_ref[home : home + 1, tile] = jnp.where(past, float(filler), row).astype(jnp.int32)
    table_ref[homes : 2 * homes, :] = jnp.broadcast_to(total, (homes, window)).astype(jnp.int32)
    table_ref[2 * homes :, :] = jnp.full((SUBLANES, window), filler, jnp.int32)


def radii_kernel(
    blocks,
    slots,
    place_ref,
    x_ref,
    y_ref,
    z_ref,
    types_ref,
    partner_ref,
    copies_ref,
    table_ref,
    columns_ref,
    window_ref,
    total_ref,
    turned_ref,
    packed_ref,
    near_ref,
    lists_ref,
    items_ref,
    lists_sem,
):
    _, homes, groups, _, _ = columns_ref.shape
    chunk = groups * SUBLANES
    window = types_ref.shape[0]
    parts = homes // blocks
    together = max(1, LANES // chunk)
    first_home = pl.multiple_of(place_ref[0], homes)
    first_atom = pl.multiple_of(place_ref[3], chunk)
    neighbour_lists(partner_ref, first_home, place_ref[1], place_ref[2], homes, slots, window, table_ref)
    move = pltpu.make_async_copy(table_ref, lists_ref, lists_sem)
    move.start()

    _, _, scaled = type_fields(types_ref[...])
    for index, field in enumerate((x_ref[...], y_ref[...], z_ref[...], 0.25 * scaled)):
        window_ref[index, 0:window, :] = field
        window_ref[index, window : window + SUBLANES, :] = jnp.full(
            (SUBLANES, LANES), 0.0 if index else FAR_AWAY, jnp.float32
        )

    home_rows = [ref[pl.ds(first_home, homes), :] for ref in (types_ref, x_ref, y_ref, z_ref)]
    turned_ref[...] = turned(jnp.concatenate(home_rows, axis=0))
    columns = turned_ref[pl.ds(first_atom, chunk), :]
    intrinsic, rho, _ = type_fields(columns)
    for home in range(homes):
        columns_ref[0, home] = spread(0.25 * rho, home)
        for index in range(1, 4):
            columns_ref[index, home] = spread(columns, index * homes + home)

    def pair_distance(home, step, rows):
        dx = columns_ref[1, home, step] - rows[0]
        dy = columns_ref[2, home, step] - rows[1]
        dz = columns_ref[3, home, step] - rows[2]
        return dx * dx + dy * dy + dz * dz

    steps = [pl.ds(start, STEP) for start in range(0, groups, STEP)]

    shift = (lists_ref.shape[1] - 1).bit_length()
    usual = 8

    def list_items(home, filled):
        turns = (lists_ref[homes + home, 0] + (together - 1)) // together

        def put(index, carry):
            items_ref[filled + index] = (home << shift) + index * together
            return carry

        for index in range(usual):
            put(index, 0)
        lax.fori_loop(usual, turns, put, 0)
        return filled + turns

    def sweep(integral, item_count):
        near_ref[...] = jnp.full(near_ref.shape, FAR_AWAY, jnp.float32)
        own_together = min(homes, 2 * together)

        def own_pairs(turn, carry):
            for index in range(own_together):
                home = turn * own_together + index
                rows = [row_of(window_ref, field, first_home + home) for field in range(4)]
                for start, step in zip(range(0, groups, STEP), steps):
                    same = diagonal(STEP, first_atom + start * SUBLANES)
                    squared = jnp.where(same, FAR_AWAY, pair_distance(home, step, rows))
                    term = integral(squared, columns_ref[0, home, step], rows[3])
                    total_ref[home, step] = jnp.where(same, 0.0, term)
                    near_ref[...] = jnp.minimum(near_ref[...], squared)
            return carry

        lax.fori_loop(0, homes // own_together, own_pairs, 0)

        def visit(turn, nearest):
            sums = []
            for index in range(ITEMS):
                item = items_ref[turn * ITEMS + index]
                line, entry = item >> shift, item & ((1 << shift) - 1)
                home = jnp.minimum(line, homes - 1)
                parts_of = [None] * len(steps)
                for other in range(together):
                    partner = lists_ref[line, entry + other]
                    rows = [row_of(window_ref, field, partner) for field in range(4)]
                    for place, step in enumerate(steps):
                        squared = pair_distance(home, step, rows)
                        nearest = jnp.minimum(nearest, squared)
                        term = integral(squared, columns_ref[0, home, step], rows[3])
                        parts_of[place] = term if other == 0 else parts_of[place] + term
                sums.append((home, parts_of))
            for home, parts_of in sums:
                for part, step in zip(parts_of, steps):
                    total_ref[home, step] += part
            return nearest

        near_ref[...] = lax.fori_loop(0, (item_count + (ITEMS - 1)) // ITEMS, visit, near_ref[...])
        lane = lax.broadcasted_iota(jnp.int32, (chunk, LANES), 1)
        packed = jnp.zeros((chunk, LANES), jnp.float32)
        for home in range(homes):
            packed = jnp.where(lane == home, lane_total(total_ref[home]), packed)
        packed_ref[...] = packed

    move.wait()
    item_count = lax.fori_loop(0, homes, list_items, 0)
    for index in range(ITEMS):
        items_ref[item_count + index] = (2 * homes) << shift
    sweep(descreen, item_count)

    @pl.when(jnp.min(near_ref[...]) < short_range * short_range)
    def _():
        sweep(descreen_any, item_count)

    psi = (0.125 * packed_ref[...]) * rho
    shaped = born_alpha * psi - born_beta * psi * psi + born_gamma * psi * psi * psi
    radii = 1.0 / (1.0 / rho - jnp.tanh(shaped) / intrinsic)

    if chunk < LANES:
        radii = jnp.concatenate([radii, jnp.zeros((LANES - chunk, LANES), jnp.float32)], axis=0)
    turned_ref[...] = radii.T
    lane = lax.broadcasted_iota(jnp.int32, (blocks, LANES), 1)
    sent = turned_ref[pl.ds(0, blocks, stride=parts), :]
    for index in range(1, parts):
        rows = pltpu.roll(turned_ref[pl.ds(index, blocks, stride=parts), :], index * chunk, 1)
        sent = jnp.where(lane >= index * chunk, rows, sent)
    for copy in range(copies_ref.shape[0]):
        copies_ref[copy] = sent


def energy_kernel(
    blocks,
    parts,
    place_ref,
    lists_ref,
    positions_ref,
    charges_ref,
    x_ref,
    y_ref,
    z_ref,
    window_charges_ref,
    gathered_ref,
    own_radii_ref,
    energy_ref,
    forces_ref,
    grad_ref,
    columns_ref,
    window_ref,
    total_ref,
):
    atoms = charges_ref.shape[1]
    devices = gathered_ref.shape[0]
    window = devices * blocks
    part_rows = window // parts
    chunk = atoms // parts
    groups = atoms // SUBLANES
    first_own, list_row = place_ref[0], place_ref[1]

    for index, ref in enumerate((x_ref, y_ref, z_ref, window_charges_ref)):
        window_ref[index, 0:window, :] = ref[...]
    lane = lax.broadcasted_iota(jnp.int32, (part_rows, LANES), 1)
    pieces = [
        gathered_ref[pl.ds(part, devices // parts, stride=parts)].reshape(part_rows, atoms)
        for part in range(parts)
    ]
    for place in range(parts):
        whole = pieces[0] if place == 0 else pltpu.roll(pieces[0], (parts - place) * chunk, 1)
        for part in range(1, parts):
            shift = (part - place) % parts
            piece = pieces[part] if shift == 0 else pltpu.roll(pieces[part], shift * chunk, 1)
            whole = jnp.where(lane >= part * chunk, piece, whole)
        window_ref[4, pl.ds(place, part_rows, stride=parts), :] = whole
        window_ref[5, pl.ds(place, part_rows, stride=parts), :] = 1.0 / whole

    for block in range(blocks):
        own_radii_ref[block : block + 1, :] = window_ref[4, pl.ds(first_own + block, 1), :]
    own_radii = own_radii_ref[...]
    own_decay = 1.0 / own_radii
    rows = [positions_ref[axis] for axis in range(3)] + [own_radii, -0.25 * own_decay]
    columns = turned(jnp.concatenate(rows, axis=0))
    for index in range(5 * blocks):
        columns_ref[index] = spread(columns, index)

    def pair_terms(block, step, rows, same=None):
        x, y, z, charge, radius, decay = rows
        dx = columns_ref[block, step] - x
        dy = columns_ref[blocks + block, step] - y
        dz = columns_ref[2 * blocks + block, step] - z
        squared = dx * dx + dy * dy + dz * dz
        if same is not None:
            squared = jnp.where(same, 1.0, squared)
            charge = jnp.where(same, 0.0, charge)
        power = squared * (columns_ref[4 * blocks + block, step] * decay)
        damped = jnp.exp(power)
        blend = (columns_ref[3 * blocks + block, step] * radius) * damped
        inv_root = lax.rsqrt(squared + blend)
        potential = charge * inv_root
        cubed = potential * (inv_root * inv_root)
        pull = cubed * (1.0 - 0.25 * damped)
        return (pull * dx, pull * dy, pull * dz, potential, cubed * blend * (1.0 - power))

    for block in range(blocks):
        rows = [row_of(window_ref, field, first_own + block) for field in range(6)]
        for start in range(0, groups, STEP):
            step = pl.ds(start, STEP)
            terms = pair_terms(block, step, rows, diagonal(STEP, start * SUBLANES))
            for term, value in enumerate(terms):
                total_ref[term * blocks + block, step] = value

        def visit(count, first, index, carry, block=block):
            partners = []
            for other in range(count):
                partner = lists_ref[list_row + block, first + index * count + other]
                partners.append([row_of(window_ref, field, partner) for field in range(6)])
            for start in range(0, groups, STEP):
                step = pl.ds(start, STEP)
                sums = [total_ref[term * blocks + block, step] for term in range(5)]
                for rows in partners:
                    sums = [total + value for total, value in zip(sums, pair_terms(block, step, rows))]
                for term, value in enumerate(sums):
                    total_ref[term * blocks + block, step] = value
            return carry

        left = lists_ref[parts * blocks + list_row + block, 0]
        first = 0
        for count in (4, 2, 1):
            turns = left // count
            lax.fori_loop(0, turns, functools.partial(visit, count, first), 0)
            first = first + turns * count
            left = left - turns * count
    sums = lane_sums([total_ref[index] for index in range(5 * blocks)], 5 * blocks)
    charges = charges_ref[...]
    scale = solvent_tau * charges
    for axis in range(3):
        forces_ref[axis] = -scale * sums[axis * blocks : (axis + 1) * blocks]
    own_energy = 0.5 * scale * charges * own_decay
    energy_ref[...] = -0.5 * scale * sums[3 * blocks : 4 * blocks] - own_energy
    grad_ref[...] = (0.5 * scale * sums[4 * blocks : 5 * blocks] + own_energy) * own_decay


def shards(positions, charges, types, pairs, owner_map):
    _, blocks, atoms = positions.shape
    regions = lax.axis_size("region")
    region_devices = lax.axis_size("dev")
    kept_regions, whole = window_regions(regions)
    devices = kept_regions * region_devices
    window = devices * blocks
    region_here = lax.axis_index("region")
    device_here = lax.axis_index("dev")
    first_window = 0 if whole else (region_here - 1) * region_devices * blocks

    parts = atoms // CHUNK
    while region_devices % parts or 4 * parts * blocks > LANES:
        parts //= 2
    homes = parts * blocks
    chunk = atoms // parts
    part_here = device_here % parts
    home_id = (region_here * region_devices + device_here - part_here) * blocks
    first_home = home_id - first_window

    vmem = pl.BlockSpec(memory_space=pltpu.VMEM)
    smem = pl.BlockSpec(memory_space=pltpu.SMEM)
    params = pltpu.CompilerParams(vmem_limit_bytes=40 * 1024 * 1024)
    copy_count = lax.axis_size(exchange_axes())
    gathered = gather_window(
        pl.pallas_call(
            functools.partial(fields_kernel, blocks, atoms),
            out_shape=jax.ShapeDtypeStruct((copy_count, ROW_COUNT, blocks, atoms), jnp.float32),
            in_specs=[pl.BlockSpec(memory_space=pltpu.HBM)] * 5,
            out_specs=vmem,
            scratch_shapes=[
                pltpu.VMEM(positions.shape, positions.dtype),
                pltpu.VMEM(types.shape, types.dtype),
                pltpu.VMEM(charges.shape, charges.dtype),
                pltpu.SMEM(pairs.shape, pairs.dtype),
                pltpu.SMEM(owner_map.shape, owner_map.dtype),
                pltpu.SemaphoreType.DMA((5,)),
            ],
            compiler_params=params,
        )(positions, types, charges, pairs, owner_map)
    )
    x, y, z, window_types, window_charges, window_partners = (
        gathered[:, row].reshape(window, atoms) for row in range(ROW_COUNT)
    )
    if window % LANES:
        window_partners = jnp.pad(window_partners, ((0, -window % LANES), (0, 0)))
    table = jax.ShapeDtypeStruct((2 * homes + SUBLANES, window_partners.shape[0]), jnp.int32)
    place = jnp.stack([first_home, home_id, jnp.int32(first_window), part_here * chunk])
    copies, lists = pl.pallas_call(
        functools.partial(radii_kernel, blocks, pairs.shape[1]),
        out_shape=(jax.ShapeDtypeStruct((copy_count, blocks, atoms), jnp.float32), table),
        in_specs=[smem] + [vmem] * 5,
        out_specs=(vmem, vmem),
        scratch_shapes=[
            pltpu.VMEM((4, homes, chunk // SUBLANES, SUBLANES, LANES), jnp.float32),
            pltpu.VMEM((4, window + SUBLANES, atoms), jnp.float32),
            pltpu.VMEM((homes, chunk // SUBLANES, SUBLANES, LANES), jnp.float32),
            pltpu.VMEM((LANES, LANES), jnp.float32),
            pltpu.VMEM((chunk, LANES), jnp.float32),
            pltpu.VMEM((STEP, SUBLANES, LANES), jnp.float32),
            pltpu.SMEM(table.shape, jnp.int32),
            pltpu.SMEM((homes * (table.shape[1] // max(1, LANES // chunk) + 1) + 64,), jnp.int32),
            pltpu.SemaphoreType.DMA(()),
        ],
        compiler_params=params,
    )(place, x, y, z, window_types, window_partners)
    block_out = jax.ShapeDtypeStruct((blocks, atoms), jnp.float32)
    own_place = jnp.stack([first_home + part_here * blocks, part_here * blocks])
    own_radii, energy, forces, grad = pl.pallas_call(
        functools.partial(energy_kernel, blocks, parts),
        out_shape=(block_out, block_out, jax.ShapeDtypeStruct((3, blocks, atoms), jnp.float32), block_out),
        in_specs=[smem, smem] + [vmem] * 7,
        out_specs=(vmem, vmem, vmem, vmem),
        scratch_shapes=[
            pltpu.VMEM((5 * blocks, atoms // SUBLANES, SUBLANES, LANES), jnp.float32),
            pltpu.VMEM((6, window + SUBLANES, atoms), jnp.float32),
            pltpu.VMEM((5 * blocks, atoms // SUBLANES, SUBLANES, LANES), jnp.float32),
        ],
        compiler_params=params,
    )(own_place, lists, positions, charges, x, y, z, window_charges, gather_window(copies))
    return own_radii, energy, forces, grad


def solution(mesh):
    placed = (
        P(None, ("region", "dev"), None),
        P(("region", "dev"), None),
        P(("region", "dev"), None),
        P(("region", "dev"), None),
        P(),
    )
    return jax.shard_map(
        shards,
        mesh=mesh,
        in_specs=placed,
        out_specs=(
            P(("region", "dev"), None),
            P(("region", "dev"), None),
            P(None, ("region", "dev"), None),
            P(("region", "dev"), None),
        ),
        check_vma=False,
    )
```

```python
import functools

import jax
import jax.numpy as jnp
from jax import lax
from jax.experimental import pallas as pl
from jax.experimental.pallas import tpu as pltpu
from jax.sharding import PartitionSpec as P

type_radii = (1.2, 1.7, 1.55, 1.52, 1.85, 1.8)
type_scales = (0.85, 0.72, 0.79, 0.85, 0.86, 0.96)
radius_offset = 0.09
born_alpha = 1.0
born_beta = 0.8
born_gamma = 4.85
solvent_tau = 1.0 - 1.0 / 78.5

ROW_X, ROW_Y, ROW_Z, ROW_TYPE, ROW_CHARGE, ROW_PARTNER, ROW_COUNT = range(7)
LANES = 128
SUBLANES = 8
STEP = 2
CHUNK = 32
ITEMS = 4
EMPTY_SLOT = -1.0e6
FAR_AWAY = 1.0e15

scaled_values = [scale * (radius - radius_offset) for radius, scale in zip(type_radii, type_scales)]
short_range = 1.01 * max(
    max(scaled_values) - (min(type_radii) - radius_offset),
    (max(type_radii) - radius_offset) - min(scaled_values),
    0.5,
)


def window_regions(region_count):
    return (region_count, True) if region_count <= 3 else (3, False)


def exchange_axes():
    return ("region", "dev") if window_regions(lax.axis_size("region"))[1] else ("dev",)


def gather_window(copies):
    here = lax.all_to_all(copies, exchange_axes(), split_axis=0, concat_axis=0, tiled=True)
    regions = lax.axis_size("region")
    if window_regions(regions)[1]:
        return here
    below = lax.ppermute(here, "region", [(i, i + 1) for i in range(regions - 1)])
    above = lax.ppermute(here, "region", [(i + 1, i) for i in range(regions - 1)])
    return jnp.concatenate([below, here, above], axis=0)


def by_type(types, table):
    value = jnp.full(types.shape, table[0], jnp.float32)
    for index in range(1, len(table)):
        value = jnp.where(types == index, jnp.float32(table[index]), value)
    return value


def type_fields(types):
    intrinsic = by_type(types, type_radii)
    rho = intrinsic - radius_offset
    return intrinsic, rho, by_type(types, type_scales) * rho


def turned(rows):
    count, width = rows.shape
    if count < LANES:
        rows = jnp.concatenate([rows, jnp.zeros((LANES - count, width), rows.dtype)], axis=0)
    return rows.T


def spread(columns, index):
    count = columns.shape[0]
    wide = jnp.broadcast_to(columns[:, index : index + 1], (count, LANES))
    return wide.reshape(count // SUBLANES, SUBLANES, LANES)


def row_of(ref, field, row):
    return ref[field, pl.ds(row, SUBLANES, stride=0), :][None]


def diagonal(groups, first_atom):
    shape = (groups, SUBLANES, LANES)
    row = lax.broadcasted_iota(jnp.int32, shape, 0) * SUBLANES + lax.broadcasted_iota(jnp.int32, shape, 1)
    return row + first_atom == lax.broadcasted_iota(jnp.int32, shape, 2)


def lane_total(array):
    return jnp.sum(array.reshape(-1, LANES), axis=1, keepdims=True)


def lane_sums(arrays, count):
    atoms = arrays[0].shape[0] * SUBLANES
    lane = lax.broadcasted_iota(jnp.int32, (atoms, LANES), 1)
    packed = jnp.zeros((atoms, LANES), jnp.float32)
    for index, array in enumerate(arrays):
        packed = jnp.where(lane == index, lane_total(array), packed)
    return packed.T[:count]


def fields_kernel(blocks, atoms, *refs):
    inputs, copies_ref, here, sems = refs[:5], refs[5], refs[6:11], refs[11]
    moves = [pltpu.make_async_copy(src, dst, sems.at[i]) for i, (src, dst) in enumerate(zip(inputs, here))]
    for move in moves:
        move.start()
    for move in moves:
        move.wait()
    positions_ref, types_ref, charges_ref, pairs_ref, owner_ref = here
    slot = lax.broadcasted_iota(jnp.int32, (1, atoms), 1)
    partners = []
    for block in range(blocks):
        row = jnp.full((1, atoms), EMPTY_SLOT, jnp.float32)
        for index in range(pairs_ref.shape[1]):
            cell = pairs_ref[block, index]
            partner = jnp.where(cell >= 0, owner_ref[jnp.maximum(cell, 0)] + 1, int(EMPTY_SLOT))
            row = jnp.where(slot == index, partner.astype(jnp.float32), row)
        partners.append(row)
    rows = [positions_ref[axis] for axis in range(3)]
    rows += [types_ref[...].astype(jnp.float32), charges_ref[...], jnp.concatenate(partners, axis=0)]
    for copy in range(copies_ref.shape[0]):
        for index, row in enumerate(rows):
            copies_ref[copy, index] = row


def descreen(squared, rho, scaled):
    inv_dist = lax.rsqrt(squared)
    share = scaled * inv_dist
    inner = 0.25 - share
    high = 0.25 + share
    low = jnp.maximum(rho * inv_dist, inner)
    inv_low = pltpu.reciprocal(low, approx=True)
    ratio = low * pltpu.reciprocal(high, approx=True)
    curve = (1.0 - ratio) + inner * (ratio - high * inv_low)
    return (inv_low * curve + 2.0 * jnp.log(ratio)) * inv_dist


def descreen_any(squared, rho, scaled):
    rho, scaled = 4.0 * rho, 4.0 * scaled
    inv_dist = lax.rsqrt(squared)
    distance = squared * inv_dist
    high = distance + scaled
    gap = distance - scaled
    low = jnp.maximum(rho, jnp.abs(gap))
    inv_low = 1.0 / low
    inv_high = 1.0 / high
    quarter = 0.25 * inv_dist
    curve = (squared - scaled * scaled) * quarter
    body = (0.5 * (inv_low - inv_high)) * (1.0 - (inv_low + inv_high) * curve)
    body = body + jnp.log(low * inv_high) * quarter
    body = body + jnp.where(rho < -gap, 1.0 / rho - inv_low, 0.0)
    return jnp.where(high > rho, 8.0 * body, 0.0)


def neighbour_lists(partner_ref, first_home, home_id, first_window, homes, slots, filler, table_ref):
    window = partner_ref.shape[0]
    tiles = [slice(start, start + LANES) for start in range(0, window, LANES)]
    depth = -(-slots // 8) * 8
    ids = jnp.concatenate([partner_ref[tile, :].T[:depth] for tile in tiles], axis=1)
    lists = turned(partner_ref[pl.ds(first_home, homes), :])[:depth]
    lane = lax.broadcasted_iota(jnp.int32, (depth, window), 1)
    lane_id = (lane + (first_window + 1)).astype(jnp.float32)
    rows = []
    for home in range(homes):
        own = (home_id + home + 1).astype(jnp.float32)
        linked = (ids == own) | (lane_id == lists[:, home : home + 1])
        rows.append(jnp.max(jnp.where(linked, 1.0, 0.0), axis=0, keepdims=True))
    linked = jnp.concatenate(rows, axis=0)
    before = lax.broadcasted_iota(jnp.int32, (window, window), 0)
    after = lax.broadcasted_iota(jnp.int32, (window, window), 1)
    ramp = jnp.where(before <= after, 1.0, 0.0).astype(jnp.bfloat16)
    rank = jnp.dot(linked.astype(jnp.bfloat16), ramp, preferred_element_type=jnp.float32)
    place = jnp.where(linked > 0.0, rank - 1.0, -1.0)
    total = jnp.sum(linked, axis=1, keepdims=True)
    columns = [turned(place[:, tile]) for tile in tiles]
    spot = lax.broadcasted_iota(jnp.int32, (LANES, LANES), 1).astype(jnp.float32)
    name = lax.broadcasted_iota(jnp.int32, (LANES, LANES), 0).astype(jnp.float32)
    for tile in tiles:
        for home in range(homes):
            found = jnp.zeros((LANES, LANES), jnp.float32)
            for other, column in zip(tiles, columns):
                hit = column[:, home : home + 1] == spot + float(tile.start)
                found = found + jnp.where(hit, name + float(other.start), 0.0)
            row = jnp.sum(found, axis=0, keepdims=True)
            past = spot[:1] + float(tile.start) >= total[home : home + 1]
            table_ref[home : home + 1, tile] = jnp.where(past, float(filler), row).astype(jnp.int32)
    table_ref[homes : 2 * homes, :] = jnp.broadcast_to(total, (homes, window)).astype(jnp.int32)
    table_ref[2 * homes :, :] = jnp.full((SUBLANES, window), filler, jnp.int32)


def radii_kernel(
    blocks,
    slots,
    place_ref,
    x_ref,
    y_ref,
    z_ref,
    types_ref,
    partner_ref,
    copies_ref,
    table_ref,
    columns_ref,
    window_ref,
    total_ref,
    turned_ref,
    packed_ref,
    near_ref,
    lists_ref,
    items_ref,
    lists_sem,
):
    _, homes, groups, _, _ = columns_ref.shape
    chunk = groups * SUBLANES
    window = types_ref.shape[0]
    parts = homes // blocks
    together = max(1, LANES // chunk)
    first_home = pl.multiple_of(place_ref[0], homes)
    first_atom = pl.multiple_of(place_ref[3], chunk)
    neighbour_lists(partner_ref, first_home, place_ref[1], place_ref[2], homes, slots, window, table_ref)
    move = pltpu.make_async_copy(table_ref, lists_ref, lists_sem)
    move.start()

    _, _, scaled = type_fields(types_ref[...])
    for index, field in enumerate((x_ref[...], y_ref[...], z_ref[...], 0.25 * scaled)):
        window_ref[index, 0:window, :] = field
        window_ref[index, window : window + SUBLANES, :] = jnp.full(
            (SUBLANES, LANES), 0.0 if index else FAR_AWAY, jnp.float32
        )

    home_rows = [ref[pl.ds(first_home, homes), :] for ref in (types_ref, x_ref, y_ref, z_ref)]
    turned_ref[...] = turned(jnp.concatenate(home_rows, axis=0))
    columns = turned_ref[pl.ds(first_atom, chunk), :]
    intrinsic, rho, _ = type_fields(columns)
    for home in range(homes):
        columns_ref[0, home] = spread(0.25 * rho, home)
        for index in range(1, 4):
            columns_ref[index, home] = spread(columns, index * homes + home)

    def pair_distance(home, step, rows):
        dx = columns_ref[1, home, step] - rows[0]
        dy = columns_ref[2, home, step] - rows[1]
        dz = columns_ref[3, home, step] - rows[2]
        return dx * dx + dy * dy + dz * dz

    steps = [pl.ds(start, STEP) for start in range(0, groups, STEP)]

    shift = (lists_ref.shape[1] - 1).bit_length()
    usual = 8

    def list_items(home, filled):
        turns = (lists_ref[homes + home, 0] + (together - 1)) // together

        def put(index, carry):
            items_ref[filled + index] = (home << shift) + index * together
            return carry

        for index in range(usual):
            put(index, 0)
        lax.fori_loop(usual, turns, put, 0)
        return filled + turns

    def sweep(integral, item_count):
        near_ref[...] = jnp.full(near_ref.shape, FAR_AWAY, jnp.float32)
        own_together = min(homes, 2 * together)

        def own_pairs(turn, carry):
            for index in range(own_together):
                home = turn * own_together + index
                rows = [row_of(window_ref, field, first_home + home) for field in range(4)]
                for start, step in zip(range(0, groups, STEP), steps):
                    same = diagonal(STEP, first_atom + start * SUBLANES)
                    squared = jnp.where(same, FAR_AWAY, pair_distance(home, step, rows))
                    term = integral(squared, columns_ref[0, home, step], rows[3])
                    total_ref[home, step] = jnp.where(same, 0.0, term)
                    near_ref[...] = jnp.minimum(near_ref[...], squared)
            return carry

        lax.fori_loop(0, homes // own_together, own_pairs, 0)

        def visit(turn, nearest):
            sums = []
            for index in range(ITEMS):
                item = items_ref[turn * ITEMS + index]
                line, entry = item >> shift, item & ((1 << shift) - 1)
                home = jnp.minimum(line, homes - 1)
                parts_of = [None] * len(steps)
                for other in range(together):
                    partner = lists_ref[line, entry + other]
                    rows = [row_of(window_ref, field, partner) for field in range(4)]
                    for place, step in enumerate(steps):
                        squared = pair_distance(home, step, rows)
                        nearest = jnp.minimum(nearest, squared)
                        term = integral(squared, columns_ref[0, home, step], rows[3])
                        parts_of[place] = term if other == 0 else parts_of[place] + term
                sums.append((home, parts_of))
            for home, parts_of in sums:
                for part, step in zip(parts_of, steps):
                    total_ref[home, step] += part
            return nearest

        near_ref[...] = lax.fori_loop(0, (item_count + (ITEMS - 1)) // ITEMS, visit, near_ref[...])
        lane = lax.broadcasted_iota(jnp.int32, (chunk, LANES), 1)
        packed = jnp.zeros((chunk, LANES), jnp.float32)
        for home in range(homes):
            packed = jnp.where(lane == home, lane_total(total_ref[home]), packed)
        packed_ref[...] = packed

    move.wait()
    item_count = lax.fori_loop(0, homes, list_items, 0)
    for index in range(ITEMS):
        items_ref[item_count + index] = (2 * homes) << shift
    sweep(descreen, item_count)

    @pl.when(jnp.min(near_ref[...]) < short_range * short_range)
    def _():
        sweep(descreen_any, item_count)

    psi = (0.125 * packed_ref[...]) * rho
    shaped = born_alpha * psi - born_beta * psi * psi + born_gamma * psi * psi * psi
    radii = 1.0 / (1.0 / rho - jnp.tanh(shaped) / intrinsic)

    if chunk < LANES:
        radii = jnp.concatenate([radii, jnp.zeros((LANES - chunk, LANES), jnp.float32)], axis=0)
    turned_ref[...] = radii.T
    lane = lax.broadcasted_iota(jnp.int32, (blocks, LANES), 1)
    sent = turned_ref[pl.ds(0, blocks, stride=parts), :]
    for index in range(1, parts):
        rows = pltpu.roll(turned_ref[pl.ds(index, blocks, stride=parts), :], index * chunk, 1)
        sent = jnp.where(lane >= index * chunk, rows, sent)
    for copy in range(copies_ref.shape[0]):
        copies_ref[copy] = sent


def energy_kernel(
    blocks,
    parts,
    place_ref,
    lists_ref,
    positions_ref,
    charges_ref,
    x_ref,
    y_ref,
    z_ref,
    window_charges_ref,
    gathered_ref,
    own_radii_ref,
    energy_ref,
    forces_ref,
    grad_ref,
    columns_ref,
    window_ref,
    total_ref,
):
    atoms = charges_ref.shape[1]
    devices = gathered_ref.shape[0]
    window = devices * blocks
    part_rows = window // parts
    chunk = atoms // parts
    groups = atoms // SUBLANES
    first_own, list_row = place_ref[0], place_ref[1]

    for index, ref in enumerate((x_ref, y_ref, z_ref, window_charges_ref)):
        window_ref[index, 0:window, :] = ref[...]
    lane = lax.broadcasted_iota(jnp.int32, (part_rows, LANES), 1)
    pieces = [
        gathered_ref[pl.ds(part, devices // parts, stride=parts)].reshape(part_rows, atoms)
        for part in range(parts)
    ]
    for place in range(parts):
        whole = pieces[0] if place == 0 else pltpu.roll(pieces[0], (parts - place) * chunk, 1)
        for part in range(1, parts):
            shift = (part - place) % parts
            piece = pieces[part] if shift == 0 else pltpu.roll(pieces[part], shift * chunk, 1)
            whole = jnp.where(lane >= part * chunk, piece, whole)
        window_ref[4, pl.ds(place, part_rows, stride=parts), :] = whole

    for block in range(blocks):
        own_radii_ref[block : block + 1, :] = window_ref[4, pl.ds(first_own + block, 1), :]
    own_radii = own_radii_ref[...]
    own_decay = 1.0 / own_radii
    rows = [positions_ref[axis] for axis in range(3)] + [-4.0 * own_radii]
    columns = turned(jnp.concatenate(rows, axis=0))
    for index in range(4 * blocks):
        columns_ref[index] = spread(columns, index)

    def pair_terms(block, step, rows, same=None):
        x, y, z, charge, radius = rows
        dx = columns_ref[block, step] - x
        dy = columns_ref[blocks + block, step] - y
        dz = columns_ref[2 * blocks + block, step] - z
        squared = dx * dx + dy * dy + dz * dz
        if same is not None:
            squared = jnp.where(same, 1.0, squared)
            charge = jnp.where(same, 0.0, charge)
        spread_sq = columns_ref[3 * blocks + block, step] * radius
        power = squared * pltpu.reciprocal(spread_sq, approx=True)
        quarter = 0.25 * jnp.exp(power)
        blend = spread_sq * quarter
        inv_root = lax.rsqrt(squared - blend)
        potential = charge * inv_root
        cubed = potential * (inv_root * inv_root)
        pull = cubed * (1.0 - quarter)
        return (pull * dx, pull * dy, pull * dz, potential, cubed * blend * (1.0 - power))

    for block in range(blocks):
        rows = [row_of(window_ref, field, first_own + block) for field in range(5)]
        for start in range(0, groups, STEP):
            step = pl.ds(start, STEP)
            terms = pair_terms(block, step, rows, diagonal(STEP, start * SUBLANES))
            for term, value in enumerate(terms):
                total_ref[term * blocks + block, step] = value

        def visit(count, first, index, carry, block=block):
            partners = []
            for other in range(count):
                partner = lists_ref[list_row + block, first + index * count + other]
                partners.append([row_of(window_ref, field, partner) for field in range(5)])
            for start in range(0, groups, STEP):
                step = pl.ds(start, STEP)
                sums = [total_ref[term * blocks + block, step] for term in range(5)]
                for rows in partners:
                    sums = [total + value for total, value in zip(sums, pair_terms(block, step, rows))]
                for term, value in enumerate(sums):
                    total_ref[term * blocks + block, step] = value
            return carry

        left = lists_ref[parts * blocks + list_row + block, 0]
        first = 0
        for count in (4, 2, 1):
            turns = left // count
            lax.fori_loop(0, turns, functools.partial(visit, count, first), 0)
            first = first + turns * count
            left = left - turns * count
    sums = lane_sums([total_ref[index] for index in range(5 * blocks)], 5 * blocks)
    charges = charges_ref[...]
    scale = solvent_tau * charges
    for axis in range(3):
        forces_ref[axis] = -scale * sums[axis * blocks : (axis + 1) * blocks]
    own_energy = 0.5 * scale * charges * own_decay
    energy_ref[...] = -0.5 * scale * sums[3 * blocks : 4 * blocks] - own_energy
    grad_ref[...] = (own_energy - 0.5 * scale * sums[4 * blocks : 5 * blocks]) * own_decay


def shards(positions, charges, types, pairs, owner_map):
    _, blocks, atoms = positions.shape
    regions = lax.axis_size("region")
    region_devices = lax.axis_size("dev")
    kept_regions, whole = window_regions(regions)
    devices = kept_regions * region_devices
    window = devices * blocks
    region_here = lax.axis_index("region")
    device_here = lax.axis_index("dev")
    first_window = 0 if whole else (region_here - 1) * region_devices * blocks

    parts = atoms // CHUNK
    while region_devices % parts or 4 * parts * blocks > LANES:
        parts //= 2
    homes = parts * blocks
    chunk = atoms // parts
    part_here = device_here % parts
    home_id = (region_here * region_devices + device_here - part_here) * blocks
    first_home = home_id - first_window

    vmem = pl.BlockSpec(memory_space=pltpu.VMEM)
    smem = pl.BlockSpec(memory_space=pltpu.SMEM)
    params = pltpu.CompilerParams(vmem_limit_bytes=40 * 1024 * 1024)
    copy_count = lax.axis_size(exchange_axes())
    gathered = gather_window(
        pl.pallas_call(
            functools.partial(fields_kernel, blocks, atoms),
            out_shape=jax.ShapeDtypeStruct((copy_count, ROW_COUNT, blocks, atoms), jnp.float32),
            in_specs=[pl.BlockSpec(memory_space=pltpu.HBM)] * 5,
            out_specs=vmem,
            scratch_shapes=[
                pltpu.VMEM(positions.shape, positions.dtype),
                pltpu.VMEM(types.shape, types.dtype),
                pltpu.VMEM(charges.shape, charges.dtype),
                pltpu.SMEM(pairs.shape, pairs.dtype),
                pltpu.SMEM(owner_map.shape, owner_map.dtype),
                pltpu.SemaphoreType.DMA((5,)),
            ],
        )(positions, types, charges, pairs, owner_map)
    )
    x, y, z, window_types, window_charges, window_partners = (
        gathered[:, row].reshape(window, atoms) for row in range(ROW_COUNT)
    )
    if window % LANES:
        window_partners = jnp.pad(window_partners, ((0, -window % LANES), (0, 0)))
    table = jax.ShapeDtypeStruct((2 * homes + SUBLANES, window_partners.shape[0]), jnp.int32)
    place = jnp.stack([first_home, home_id, jnp.int32(first_window), part_here * chunk])
    copies, lists = pl.pallas_call(
        functools.partial(radii_kernel, blocks, pairs.shape[1]),
        out_shape=(jax.ShapeDtypeStruct((copy_count, blocks, atoms), jnp.float32), table),
        in_specs=[smem] + [vmem] * 5,
        out_specs=(vmem, vmem),
        scratch_shapes=[
            pltpu.VMEM((4, homes, chunk // SUBLANES, SUBLANES, LANES), jnp.float32),
            pltpu.VMEM((4, window + SUBLANES, atoms), jnp.float32),
            pltpu.VMEM((homes, chunk // SUBLANES, SUBLANES, LANES), jnp.float32),
            pltpu.VMEM((LANES, LANES), jnp.float32),
            pltpu.VMEM((chunk, LANES), jnp.float32),
            pltpu.VMEM((STEP, SUBLANES, LANES), jnp.float32),
            pltpu.SMEM(table.shape, jnp.int32),
            pltpu.SMEM((homes * (table.shape[1] // max(1, LANES // chunk) + 1) + 64,), jnp.int32),
            pltpu.SemaphoreType.DMA(()),
        ],
        compiler_params=params,
    )(place, x, y, z, window_types, window_partners)
    block_out = jax.ShapeDtypeStruct((blocks, atoms), jnp.float32)
    own_place = jnp.stack([first_home + part_here * blocks, part_here * blocks])
    own_radii, energy, forces, grad = pl.pallas_call(
        functools.partial(energy_kernel, blocks, parts),
        out_shape=(block_out, block_out, jax.ShapeDtypeStruct((3, blocks, atoms), jnp.float32), block_out),
        in_specs=[smem, smem] + [vmem] * 7,
        out_specs=(vmem, vmem, vmem, vmem),
        scratch_shapes=[
            pltpu.VMEM((4 * blocks, atoms // SUBLANES, SUBLANES, LANES), jnp.float32),
            pltpu.VMEM((5, window + SUBLANES, atoms), jnp.float32),
            pltpu.VMEM((5 * blocks, atoms // SUBLANES, SUBLANES, LANES), jnp.float32),
        ],
        compiler_params=params,
    )(own_place, lists, positions, charges, x, y, z, window_charges, gather_window(copies))
    return own_radii, energy, forces, grad


def solution(mesh):
    placed = (
        P(None, ("region", "dev"), None),
        P(("region", "dev"), None),
        P(("region", "dev"), None),
        P(("region", "dev"), None),
        P(),
    )
    return jax.shard_map(
        shards,
        mesh=mesh,
        in_specs=placed,
        out_specs=(
            P(("region", "dev"), None),
            P(("region", "dev"), None),
            P(None, ("region", "dev"), None),
            P(("region", "dev"), None),
        ),
        check_vma=False,
    )
```

```python
import functools

import jax
import jax.numpy as jnp
from jax import lax
from jax.experimental import pallas as pl
from jax.experimental.pallas import tpu as pltpu
from jax.sharding import PartitionSpec as P

type_radii = (1.2, 1.7, 1.55, 1.52, 1.85, 1.8)
type_scales = (0.85, 0.72, 0.79, 0.85, 0.86, 0.96)
radius_offset = 0.09
born_alpha = 1.0
born_beta = 0.8
born_gamma = 4.85
solvent_tau = 1.0 - 1.0 / 78.5

ROW_X, ROW_Y, ROW_Z, ROW_TYPE, ROW_CHARGE, ROW_PARTNER, ROW_COUNT = range(7)
WINDOW_X, WINDOW_Y, WINDOW_Z, WINDOW_SCALED, WINDOW_CHARGE, WINDOW_COUNT = range(6)
LANES = 128
SUBLANES = 8
STEP = 4
ENERGY_STEP = 2
CHUNK = 32
ITEMS = 4
EMPTY_SLOT = -1.0e6
FAR_AWAY = 1.0e15

scaled_values = [scale * (radius - radius_offset) for radius, scale in zip(type_radii, type_scales)]
short_range = 1.01 * max(
    max(scaled_values) - (min(type_radii) - radius_offset),
    (max(type_radii) - radius_offset) - min(scaled_values),
    0.5,
)


def window_regions(region_count):
    return (region_count, True) if region_count <= 3 else (3, False)


def exchange_axes():
    return ("region", "dev") if window_regions(lax.axis_size("region"))[1] else ("dev",)


def sent_directly(copies):
    return lax.all_to_all(copies, exchange_axes(), split_axis=0, concat_axis=0, tiled=True)


def near_count(device_count):
    return next(count for count in (4, 2, 1) if device_count % count == 0)


def sent_in_stages(copies):
    count = lax.axis_size("dev")
    near = near_count(count)
    far = count // near
    lines = [[line + near * step for step in range(far)] for line in range(near)]
    lined = lax.all_to_all(copies, "dev", split_axis=0, concat_axis=0, axis_index_groups=lines, tiled=True)
    axes = exchange_axes()
    regions = lax.axis_size(axes) // count
    planes = [
        [region * count + step * near + line for region in range(regions) for line in range(near)]
        for step in range(far)
    ]
    copies = jnp.broadcast_to(lined, (regions * near,) + lined.shape)
    return lax.all_to_all(copies, axes, split_axis=0, concat_axis=0, axis_index_groups=planes, tiled=True)


def with_other_regions(here):
    regions = lax.axis_size("region")
    if window_regions(regions)[1]:
        return here
    below = lax.ppermute(here, "region", [(i, i + 1) for i in range(regions - 1)])
    above = lax.ppermute(here, "region", [(i + 1, i) for i in range(regions - 1)])
    return jnp.concatenate([below, here, above], axis=0)


def by_type(types, table):
    value = jnp.full(types.shape, table[0], jnp.float32)
    for index in range(1, len(table)):
        value = jnp.where(types == index, jnp.float32(table[index]), value)
    return value


def type_fields(types):
    intrinsic = by_type(types, type_radii)
    rho = intrinsic - radius_offset
    return intrinsic, rho, by_type(types, type_scales) * rho


def turned(rows):
    count, width = rows.shape
    if count < LANES:
        rows = jnp.concatenate([rows, jnp.zeros((LANES - count, width), rows.dtype)], axis=0)
    return rows.T


def spread(columns, index):
    count = columns.shape[0]
    wide = jnp.broadcast_to(columns[:, index : index + 1], (count, LANES))
    return wide.reshape(count // SUBLANES, SUBLANES, LANES)


def row_of(ref, field, row):
    return ref[field, pl.ds(row, SUBLANES, stride=0), :][None]


def diagonal(groups, first_atom):
    shape = (groups, SUBLANES, LANES)
    row = lax.broadcasted_iota(jnp.int32, shape, 0) * SUBLANES + lax.broadcasted_iota(jnp.int32, shape, 1)
    return row + first_atom == lax.broadcasted_iota(jnp.int32, shape, 2)


def lane_total(array):
    return jnp.sum(array.reshape(-1, LANES), axis=1, keepdims=True)


def lane_sums(arrays, count):
    atoms = arrays[0].shape[0] * SUBLANES
    lane = lax.broadcasted_iota(jnp.int32, (atoms, LANES), 1)
    packed = jnp.zeros((atoms, LANES), jnp.float32)
    for index, array in enumerate(arrays):
        packed = jnp.where(lane == index, lane_total(array), packed)
    return packed.T[:count]


def fields_kernel(blocks, atoms, *refs):
    inputs, copies_ref, here, sems = refs[:5], refs[5], refs[6:11], refs[11]
    moves = [pltpu.make_async_copy(src, dst, sems.at[i]) for i, (src, dst) in enumerate(zip(inputs, here))]
    for move in moves:
        move.start()
    for move in moves:
        move.wait()
    positions_ref, types_ref, charges_ref, pairs_ref, owner_ref = here
    slot = lax.broadcasted_iota(jnp.int32, (1, atoms), 1)
    partners = []
    for block in range(blocks):
        row = jnp.full((1, atoms), EMPTY_SLOT, jnp.float32)
        for index in range(pairs_ref.shape[1]):
            cell = pairs_ref[block, index]
            partner = jnp.where(cell >= 0, owner_ref[jnp.maximum(cell, 0)] + 1, int(EMPTY_SLOT))
            row = jnp.where(slot == index, partner.astype(jnp.float32), row)
        partners.append(row)
    rows = [positions_ref[axis] for axis in range(3)]
    rows += [types_ref[...].astype(jnp.float32), charges_ref[...], jnp.concatenate(partners, axis=0)]
    for copy in range(copies_ref.shape[0]):
        for index, row in enumerate(rows):
            copies_ref[copy, index] = row


def descreen(squared, rho, scaled):
    inv_dist = lax.rsqrt(squared)
    share = scaled * inv_dist
    inner = 0.25 - share
    high = 0.25 + share
    low = jnp.maximum(rho * inv_dist, inner)
    inv_low = pltpu.reciprocal(low, approx=True)
    ratio = low * pltpu.reciprocal(high, approx=True)
    curve = (1.0 - ratio) + inner * (ratio - high * inv_low)
    return (inv_low * curve + 2.0 * jnp.log(ratio)) * inv_dist


def descreen_any(squared, rho, scaled):
    rho, scaled = 4.0 * rho, 4.0 * scaled
    inv_dist = lax.rsqrt(squared)
    distance = squared * inv_dist
    high = distance + scaled
    gap = distance - scaled
    low = jnp.maximum(rho, jnp.abs(gap))
    inv_low = 1.0 / low
    inv_high = 1.0 / high
    quarter = 0.25 * inv_dist
    curve = (squared - scaled * scaled) * quarter
    body = (0.5 * (inv_low - inv_high)) * (1.0 - (inv_low + inv_high) * curve)
    body = body + jnp.log(low * inv_high) * quarter
    body = body + jnp.where(rho < -gap, 1.0 / rho - inv_low, 0.0)
    return jnp.where(high > rho, 8.0 * body, 0.0)


def neighbour_lists(partner_ref, first_home, home_id, first_window, homes, slots, filler, table_ref):
    window = partner_ref.shape[0]
    tiles = [slice(start, start + LANES) for start in range(0, window, LANES)]
    depth = -(-slots // 8) * 8
    ids = jnp.concatenate([partner_ref[tile, :].T[:depth] for tile in tiles], axis=1)
    lists = turned(partner_ref[pl.ds(first_home, homes), :])[:depth]
    lane = lax.broadcasted_iota(jnp.int32, (depth, window), 1)
    lane_id = (lane + (first_window + 1)).astype(jnp.float32)
    rows = []
    for home in range(homes):
        own = (home_id + home + 1).astype(jnp.float32)
        linked = (ids == own) | (lane_id == lists[:, home : home + 1])
        rows.append(jnp.max(jnp.where(linked, 1.0, 0.0), axis=0, keepdims=True))
    linked = jnp.concatenate(rows, axis=0)
    before = lax.broadcasted_iota(jnp.int32, (window, window), 0)
    after = lax.broadcasted_iota(jnp.int32, (window, window), 1)
    ramp = jnp.where(before <= after, 1.0, 0.0).astype(jnp.bfloat16)
    rank = jnp.dot(linked.astype(jnp.bfloat16), ramp, preferred_element_type=jnp.float32)
    place = jnp.where(linked > 0.0, rank - 1.0, -1.0)
    total = jnp.sum(linked, axis=1, keepdims=True)
    columns = [turned(place[:, tile]) for tile in tiles]
    spot = lax.broadcasted_iota(jnp.int32, (LANES, LANES), 1).astype(jnp.float32)
    name = lax.broadcasted_iota(jnp.int32, (LANES, LANES), 0).astype(jnp.float32)
    for tile in tiles:
        for home in range(homes):
            found = jnp.zeros((LANES, LANES), jnp.float32)
            for other, column in zip(tiles, columns):
                hit = column[:, home : home + 1] == spot + float(tile.start)
                found = found + jnp.where(hit, name + float(other.start), 0.0)
            row = jnp.sum(found, axis=0, keepdims=True)
            past = spot[:1] + float(tile.start) >= total[home : home + 1]
            table_ref[home : home + 1, tile] = jnp.where(past, float(filler), row).astype(jnp.int32)
    table_ref[homes : 2 * homes, :] = jnp.broadcast_to(total, (homes, window)).astype(jnp.int32)
    table_ref[2 * homes :, :] = jnp.full((SUBLANES, window), filler, jnp.int32)


def radii_kernel(
    blocks,
    slots,
    order,
    place_ref,
    arrived_ref,
    copies_ref,
    table_ref,
    window_ref,
    columns_ref,
    types_ref,
    partner_ref,
    total_ref,
    turned_ref,
    packed_ref,
    near_ref,
    lists_ref,
    items_ref,
    lists_sem,
):
    _, homes, groups, _, _ = columns_ref.shape
    chunk = groups * SUBLANES
    window = types_ref.shape[0]
    parts = homes // blocks
    together = max(1, LANES // chunk)
    first_home = pl.multiple_of(place_ref[0], homes)
    first_atom = pl.multiple_of(place_ref[3], chunk)

    tables = [window_ref.at[WINDOW_X], window_ref.at[WINDOW_Y], window_ref.at[WINDOW_Z]]
    tables += [types_ref, window_ref.at[WINDOW_CHARGE], partner_ref]
    for place, device in enumerate(order):
        for field, table in enumerate(tables):
            rows = arrived_ref[place, field * blocks : (field + 1) * blocks, :]
            table[device * blocks : (device + 1) * blocks, :] = rows
    if partner_ref.shape[0] > window:
        spare = (partner_ref.shape[0] - window, LANES)
        partner_ref[window:, :] = jnp.full(spare, EMPTY_SLOT, jnp.float32)
    neighbour_lists(partner_ref, first_home, place_ref[1], place_ref[2], homes, slots, window, table_ref)
    move = pltpu.make_async_copy(table_ref, lists_ref, lists_sem)
    move.start()

    _, _, scaled = type_fields(types_ref[...])
    window_ref[WINDOW_SCALED, 0:window, :] = 0.25 * scaled
    for field in range(WINDOW_COUNT):
        filler = FAR_AWAY if field == WINDOW_X else 0.0
        window_ref[field, window : window + SUBLANES, :] = jnp.full((SUBLANES, LANES), filler, jnp.float32)

    home_rows = [window_ref[field, pl.ds(first_home, homes), :] for field in range(3)]
    turned_ref[...] = turned(jnp.concatenate([types_ref[pl.ds(first_home, homes), :]] + home_rows, axis=0))
    columns = turned_ref[pl.ds(first_atom, chunk), :]
    intrinsic, rho, _ = type_fields(columns)
    for home in range(homes):
        columns_ref[0, home] = spread(0.25 * rho, home)
        for index in range(1, 4):
            columns_ref[index, home] = spread(columns, index * homes + home)

    def pair_distance(home, step, rows):
        dx = columns_ref[1, home, step] - rows[0]
        dy = columns_ref[2, home, step] - rows[1]
        dz = columns_ref[3, home, step] - rows[2]
        return dx * dx + dy * dy + dz * dz

    steps = [pl.ds(start, STEP) for start in range(0, groups, STEP)]

    shift = (lists_ref.shape[1] - 1).bit_length()
    usual = 8

    def list_items(home, filled):
        turns = (lists_ref[homes + home, 0] + (together - 1)) // together

        def put(index, carry):
            items_ref[filled + index] = (home << shift) + index * together
            return carry

        for index in range(usual):
            put(index, 0)
        lax.fori_loop(usual, turns, put, 0)
        return filled + turns

    def sweep(integral, item_count):
        near_ref[...] = jnp.full(near_ref.shape, FAR_AWAY, jnp.float32)
        own_together = min(homes, 2 * together)

        def own_pairs(turn, carry):
            for index in range(own_together):
                home = turn * own_together + index
                rows = [row_of(window_ref, field, first_home + home) for field in range(4)]
                for start, step in zip(range(0, groups, STEP), steps):
                    same = diagonal(STEP, first_atom + start * SUBLANES)
                    squared = jnp.where(same, FAR_AWAY, pair_distance(home, step, rows))
                    term = integral(squared, columns_ref[0, home, step], rows[3])
                    total_ref[home, step] = jnp.where(same, 0.0, term)
                    near_ref[...] = jnp.minimum(near_ref[...], squared)
            return carry

        lax.fori_loop(0, homes // own_together, own_pairs, 0)

        def visit(turn, nearest):
            sums = []
            for index in range(ITEMS):
                item = items_ref[turn * ITEMS + index]
                line, entry = item >> shift, item & ((1 << shift) - 1)
                home = jnp.minimum(line, homes - 1)
                parts_of = [None] * len(steps)
                for other in range(together):
                    partner = lists_ref[line, entry + other]
                    rows = [row_of(window_ref, field, partner) for field in range(4)]
                    for place, step in enumerate(steps):
                        squared = pair_distance(home, step, rows)
                        nearest = jnp.minimum(nearest, squared)
                        term = integral(squared, columns_ref[0, home, step], rows[3])
                        parts_of[place] = term if other == 0 else parts_of[place] + term
                sums.append((home, parts_of))
            for home, parts_of in sums:
                for part, step in zip(parts_of, steps):
                    total_ref[home, step] += part
            return nearest

        near_ref[...] = lax.fori_loop(0, (item_count + (ITEMS - 1)) // ITEMS, visit, near_ref[...])
        lane = lax.broadcasted_iota(jnp.int32, (chunk, LANES), 1)
        packed = jnp.zeros((chunk, LANES), jnp.float32)
        for home in range(homes):
            packed = jnp.where(lane == home, lane_total(total_ref[home]), packed)
        packed_ref[...] = packed

    move.wait()
    item_count = lax.fori_loop(0, homes, list_items, 0)
    for index in range(ITEMS):
        items_ref[item_count + index] = (2 * homes) << shift
    sweep(descreen, item_count)

    @pl.when(jnp.min(near_ref[...]) < short_range * short_range)
    def _():
        sweep(descreen_any, item_count)

    psi = (0.125 * packed_ref[...]) * rho
    shaped = born_alpha * psi - born_beta * psi * psi + born_gamma * psi * psi * psi
    radii = 1.0 / (1.0 / rho - jnp.tanh(shaped) / intrinsic)

    if chunk < LANES:
        radii = jnp.concatenate([radii, jnp.zeros((LANES - chunk, LANES), jnp.float32)], axis=0)
    turned_ref[...] = radii.T
    lane = lax.broadcasted_iota(jnp.int32, (blocks, LANES), 1)
    sent = turned_ref[pl.ds(0, blocks, stride=parts), :]
    for index in range(1, parts):
        rows = pltpu.roll(turned_ref[pl.ds(index, blocks, stride=parts), :], index * chunk, 1)
        sent = jnp.where(lane >= index * chunk, rows, sent)
    for copy in range(copies_ref.shape[0]):
        copies_ref[copy] = sent


def energy_kernel(
    parts,
    place_ref,
    lists_ref,
    window_ref,
    gathered_ref,
    own_radii_ref,
    energy_ref,
    forces_ref,
    grad_ref,
    columns_ref,
    radii_ref,
    total_ref,
):
    devices, blocks, atoms = gathered_ref.shape
    window = devices * blocks
    part_rows = window // parts
    chunk = atoms // parts
    groups = atoms // SUBLANES
    first_own, list_row = place_ref[0], place_ref[1]

    lane = lax.broadcasted_iota(jnp.int32, (part_rows, LANES), 1)
    pieces = [
        gathered_ref[pl.ds(part, devices // parts, stride=parts)].reshape(part_rows, atoms)
        for part in range(parts)
    ]
    for place in range(parts):
        whole = pieces[0] if place == 0 else pltpu.roll(pieces[0], (parts - place) * chunk, 1)
        for part in range(1, parts):
            shift = (part - place) % parts
            piece = pieces[part] if shift == 0 else pltpu.roll(pieces[part], shift * chunk, 1)
            whole = jnp.where(lane >= part * chunk, piece, whole)
        radii_ref[0, pl.ds(place, part_rows, stride=parts), :] = whole

    radii_ref[0, window : window + SUBLANES, :] = jnp.ones((SUBLANES, LANES), jnp.float32)
    fields = [(window_ref, field) for field in (WINDOW_X, WINDOW_Y, WINDOW_Z, WINDOW_CHARGE)] + [(radii_ref, 0)]
    own = [
        jnp.concatenate([ref[field, pl.ds(first_own + block, 1), :] for block in range(blocks)], axis=0)
        for ref, field in fields
    ]
    charges, own_radii = own[3], own[4]
    own_radii_ref[...] = own_radii
    own_decay = 1.0 / own_radii
    columns = turned(jnp.concatenate(own[:3] + [-4.0 * own_radii], axis=0))
    for index in range(4 * blocks):
        columns_ref[index] = spread(columns, index)

    def pair_terms(block, step, rows, same=None):
        x, y, z, charge, radius = rows
        dx = columns_ref[block, step] - x
        dy = columns_ref[blocks + block, step] - y
        dz = columns_ref[2 * blocks + block, step] - z
        squared = dx * dx + dy * dy + dz * dz
        if same is not None:
            squared = jnp.where(same, 1.0, squared)
            charge = jnp.where(same, 0.0, charge)
        spread_sq = columns_ref[3 * blocks + block, step] * radius
        power = squared * pltpu.reciprocal(spread_sq, approx=True)
        quarter = 0.25 * jnp.exp(power)
        blend = spread_sq * quarter
        inv_root = lax.rsqrt(squared - blend)
        potential = charge * inv_root
        cubed = potential * (inv_root * inv_root)
        pull = cubed * (1.0 - quarter)
        return (pull * dx, pull * dy, pull * dz, potential, cubed * blend * (1.0 - power))

    for block in range(blocks):
        rows = [row_of(ref, field, first_own + block) for ref, field in fields]
        for start in range(0, groups, ENERGY_STEP):
            step = pl.ds(start, ENERGY_STEP)
            terms = pair_terms(block, step, rows, diagonal(ENERGY_STEP, start * SUBLANES))
            for term, value in enumerate(terms):
                total_ref[term * blocks + block, step] = value

        def visit(count, first, index, carry, block=block):
            partners = []
            for other in range(count):
                partner = lists_ref[list_row + block, first + index * count + other]
                partners.append([row_of(ref, field, partner) for ref, field in fields])
            for start in range(0, groups, ENERGY_STEP):
                step = pl.ds(start, ENERGY_STEP)
                sums = [total_ref[term * blocks + block, step] for term in range(5)]
                for rows in partners:
                    sums = [total + value for total, value in zip(sums, pair_terms(block, step, rows))]
                for term, value in enumerate(sums):
                    total_ref[term * blocks + block, step] = value
            return carry

        left = lists_ref[parts * blocks + list_row + block, 0]
        first = 0
        for count in (4, 2, 1):
            turns = left // count
            lax.fori_loop(0, turns, functools.partial(visit, count, first), 0)
            first = first + turns * count
            left = left - turns * count
    sums = lane_sums([total_ref[index] for index in range(5 * blocks)], 5 * blocks)
    scale = solvent_tau * charges
    for axis in range(3):
        forces_ref[axis] = -scale * sums[axis * blocks : (axis + 1) * blocks]
    own_energy = 0.5 * scale * charges * own_decay
    energy_ref[...] = -0.5 * scale * sums[3 * blocks : 4 * blocks] - own_energy
    grad_ref[...] = (own_energy - 0.5 * scale * sums[4 * blocks : 5 * blocks]) * own_decay


def shards(positions, charges, types, pairs, owner_map):
    _, blocks, atoms = positions.shape
    regions = lax.axis_size("region")
    region_devices = lax.axis_size("dev")
    kept_regions, whole = window_regions(regions)
    devices = kept_regions * region_devices
    window = devices * blocks
    region_here = lax.axis_index("region")
    device_here = lax.axis_index("dev")
    first_window = 0 if whole else (region_here - 1) * region_devices * blocks

    parts = atoms // CHUNK
    while region_devices % parts or 4 * parts * blocks > LANES:
        parts //= 2
    homes = parts * blocks
    chunk = atoms // parts
    part_here = device_here % parts
    home_id = (region_here * region_devices + device_here - part_here) * blocks
    first_home = home_id - first_window

    vmem = pl.BlockSpec(memory_space=pltpu.VMEM)
    smem = pl.BlockSpec(memory_space=pltpu.SMEM)
    params = pltpu.CompilerParams(vmem_limit_bytes=40 * 1024 * 1024)
    copy_count = lax.axis_size(exchange_axes())
    line_count = region_devices // near_count(region_devices)
    arrived = sent_in_stages(
        pl.pallas_call(
            functools.partial(fields_kernel, blocks, atoms),
            out_shape=jax.ShapeDtypeStruct((line_count, ROW_COUNT, blocks, atoms), jnp.float32),
            in_specs=[pl.BlockSpec(memory_space=pltpu.HBM)] * 5,
            out_specs=vmem,
            scratch_shapes=[
                pltpu.VMEM(positions.shape, positions.dtype),
                pltpu.VMEM(types.shape, types.dtype),
                pltpu.VMEM(charges.shape, charges.dtype),
                pltpu.SMEM(pairs.shape, pairs.dtype),
                pltpu.SMEM(owner_map.shape, owner_map.dtype),
                pltpu.SemaphoreType.DMA((5,)),
            ],
        )(positions, types, charges, pairs, owner_map)
    )
    arrived = with_other_regions(arrived).reshape(devices, ROW_COUNT * blocks, atoms)
    near = near_count(region_devices)
    order = [
        region * region_devices + step * near + line
        for region in range(kept_regions)
        for line in range(near)
        for step in range(line_count)
    ]
    padded = -(-window // LANES) * LANES
    table = jax.ShapeDtypeStruct((2 * homes + SUBLANES, padded), jnp.int32)
    place = jnp.stack([first_home, home_id, jnp.int32(first_window), part_here * chunk])
    fields = jax.ShapeDtypeStruct((WINDOW_COUNT, window + SUBLANES, atoms), jnp.float32)
    copies, lists, window_fields = pl.pallas_call(
        functools.partial(radii_kernel, blocks, pairs.shape[1], order),
        out_shape=(jax.ShapeDtypeStruct((copy_count, blocks, atoms), jnp.float32), table, fields),
        in_specs=[smem, vmem],
        out_specs=(vmem, vmem, vmem),
        scratch_shapes=[
            pltpu.VMEM((4, homes, chunk // SUBLANES, SUBLANES, LANES), jnp.float32),
            pltpu.VMEM((window, atoms), jnp.float32),
            pltpu.VMEM((padded, atoms), jnp.float32),
            pltpu.VMEM((homes, chunk // SUBLANES, SUBLANES, LANES), jnp.float32),
            pltpu.VMEM((LANES, LANES), jnp.float32),
            pltpu.VMEM((chunk, LANES), jnp.float32),
            pltpu.VMEM((STEP, SUBLANES, LANES), jnp.float32),
            pltpu.SMEM(table.shape, jnp.int32),
            pltpu.SMEM((homes * (table.shape[1] // max(1, LANES // chunk) + 1) + 64,), jnp.int32),
            pltpu.SemaphoreType.DMA(()),
        ],
        compiler_params=params,
    )(place, arrived)
    block_out = jax.ShapeDtypeStruct((blocks, atoms), jnp.float32)
    own_place = jnp.stack([first_home + part_here * blocks, part_here * blocks])
    own_radii, energy, forces, grad = pl.pallas_call(
        functools.partial(energy_kernel, parts),
        out_shape=(block_out, block_out, jax.ShapeDtypeStruct((3, blocks, atoms), jnp.float32), block_out),
        in_specs=[smem, smem, vmem, vmem],
        out_specs=(vmem, vmem, vmem, vmem),
        scratch_shapes=[
            pltpu.VMEM((4 * blocks, atoms // SUBLANES, SUBLANES, LANES), jnp.float32),
            pltpu.VMEM((1, window + SUBLANES, atoms), jnp.float32),
            pltpu.VMEM((5 * blocks, atoms // SUBLANES, SUBLANES, LANES), jnp.float32),
        ],
        compiler_params=params,
    )(own_place, lists, window_fields, with_other_regions(sent_directly(copies)))
    return own_radii, energy, forces, grad


def solution(mesh):
    placed = (
        P(None, ("region", "dev"), None),
        P(("region", "dev"), None),
        P(("region", "dev"), None),
        P(("region", "dev"), None),
        P(),
    )
    return jax.shard_map(
        shards,
        mesh=mesh,
        in_specs=placed,
        out_specs=(
            P(("region", "dev"), None),
            P(("region", "dev"), None),
            P(None, ("region", "dev"), None),
            P(("region", "dev"), None),
        ),
        check_vma=False,
    )
```

```python
import functools

import jax
import jax.numpy as jnp
from jax import lax
from jax.experimental import pallas as pl
from jax.experimental.pallas import tpu as pltpu
from jax.sharding import PartitionSpec as P

type_radii = (1.2, 1.7, 1.55, 1.52, 1.85, 1.8)
type_scales = (0.85, 0.72, 0.79, 0.85, 0.86, 0.96)
radius_offset = 0.09
born_alpha = 1.0
born_beta = 0.8
born_gamma = 4.85
solvent_tau = 1.0 - 1.0 / 78.5

ROW_X, ROW_Y, ROW_Z, ROW_TYPE, ROW_CHARGE, ROW_PARTNER, ROW_COUNT = range(7)
WINDOW_X, WINDOW_Y, WINDOW_Z, WINDOW_SCALED, WINDOW_CHARGE, WINDOW_COUNT = range(6)
LANES = 128
SUBLANES = 8
STEP = 4
ENERGY_STEP = 2
CHUNK = 32
ITEMS = 4
EMPTY_SLOT = -1.0e6
FAR_AWAY = 1.0e15

scaled_values = [scale * (radius - radius_offset) for radius, scale in zip(type_radii, type_scales)]
short_range = 1.01 * max(
    max(scaled_values) - (min(type_radii) - radius_offset),
    (max(type_radii) - radius_offset) - min(scaled_values),
    0.5,
)


def window_regions(region_count):
    return (region_count, True) if region_count <= 3 else (3, False)


def exchange_axes():
    return ("region", "dev") if window_regions(lax.axis_size("region"))[1] else ("dev",)


def sent_directly(copies):
    return lax.all_to_all(copies, exchange_axes(), split_axis=0, concat_axis=0, tiled=True)


def twin_count(device_count):
    return 2 - device_count % 2


def sent_to_both_twins(copies):
    count = lax.axis_size("dev")
    twins = twin_count(count)
    axes = exchange_axes()
    regions = lax.axis_size(axes) // count
    alike = [list(range(parity, regions * count, twins)) for parity in range(twins)]
    here = lax.all_to_all(copies, axes, split_axis=0, concat_axis=0, axis_index_groups=alike, tiled=True)
    if twins == 1:
        return [here]
    return [here, lax.ppermute(here, "dev", [(i, i ^ 1) for i in range(count)])]


def with_other_regions(here):
    regions = lax.axis_size("region")
    if window_regions(regions)[1]:
        return here
    below = lax.ppermute(here, "region", [(i, i + 1) for i in range(regions - 1)])
    above = lax.ppermute(here, "region", [(i + 1, i) for i in range(regions - 1)])
    return jnp.concatenate([below, here, above], axis=0)


def by_type(types, table):
    value = jnp.full(types.shape, table[0], jnp.float32)
    for index in range(1, len(table)):
        value = jnp.where(types == index, jnp.float32(table[index]), value)
    return value


def type_fields(types):
    intrinsic = by_type(types, type_radii)
    rho = intrinsic - radius_offset
    return intrinsic, rho, by_type(types, type_scales) * rho


def turned(rows):
    count, width = rows.shape
    if count < LANES:
        rows = jnp.concatenate([rows, jnp.zeros((LANES - count, width), rows.dtype)], axis=0)
    return rows.T


def spread(columns, index):
    count = columns.shape[0]
    wide = jnp.broadcast_to(columns[:, index : index + 1], (count, LANES))
    return wide.reshape(count // SUBLANES, SUBLANES, LANES)


def row_of(ref, field, row):
    return ref[field, pl.ds(row, SUBLANES, stride=0), :][None]


def diagonal(groups, first_atom):
    shape = (groups, SUBLANES, LANES)
    row = lax.broadcasted_iota(jnp.int32, shape, 0) * SUBLANES + lax.broadcasted_iota(jnp.int32, shape, 1)
    return row + first_atom == lax.broadcasted_iota(jnp.int32, shape, 2)


def lane_total(array):
    return jnp.sum(array.reshape(-1, LANES), axis=1, keepdims=True)


def lane_sums(arrays, count):
    atoms = arrays[0].shape[0] * SUBLANES
    lane = lax.broadcasted_iota(jnp.int32, (atoms, LANES), 1)
    packed = jnp.zeros((atoms, LANES), jnp.float32)
    for index, array in enumerate(arrays):
        packed = jnp.where(lane == index, lane_total(array), packed)
    return packed.T[:count]


def fields_kernel(blocks, atoms, *refs):
    inputs, copies_ref, here, sems = refs[:5], refs[5], refs[6:11], refs[11]
    moves = [pltpu.make_async_copy(src, dst, sems.at[i]) for i, (src, dst) in enumerate(zip(inputs, here))]
    for move in moves:
        move.start()
    for move in moves:
        move.wait()
    positions_ref, types_ref, charges_ref, pairs_ref, owner_ref = here
    slot = lax.broadcasted_iota(jnp.int32, (1, atoms), 1)
    partners = []
    for block in range(blocks):
        row = jnp.full((1, atoms), EMPTY_SLOT, jnp.float32)
        for index in range(pairs_ref.shape[1]):
            cell = pairs_ref[block, index]
            partner = jnp.where(cell >= 0, owner_ref[jnp.maximum(cell, 0)] + 1, int(EMPTY_SLOT))
            row = jnp.where(slot == index, partner.astype(jnp.float32), row)
        partners.append(row)
    rows = [positions_ref[axis] for axis in range(3)]
    rows += [types_ref[...].astype(jnp.float32), charges_ref[...], jnp.concatenate(partners, axis=0)]
    for copy in range(copies_ref.shape[0]):
        for index, row in enumerate(rows):
            copies_ref[copy, index] = row


def descreen(squared, rho, scaled):
    inv_dist = lax.rsqrt(squared)
    share = scaled * inv_dist
    inner = 0.25 - share
    high = 0.25 + share
    low = jnp.maximum(rho * inv_dist, inner)
    inv_both = pltpu.reciprocal(low * high, approx=True)
    inv_low = high * inv_both
    ratio = low * (low * inv_both)
    curve = (1.0 - ratio) + inner * (ratio - high * inv_low)
    return (inv_low * curve + 2.0 * jnp.log(ratio)) * inv_dist


def descreen_any(squared, rho, scaled):
    rho, scaled = 4.0 * rho, 4.0 * scaled
    inv_dist = lax.rsqrt(squared)
    distance = squared * inv_dist
    high = distance + scaled
    gap = distance - scaled
    low = jnp.maximum(rho, jnp.abs(gap))
    inv_low = 1.0 / low
    inv_high = 1.0 / high
    quarter = 0.25 * inv_dist
    curve = (squared - scaled * scaled) * quarter
    body = (0.5 * (inv_low - inv_high)) * (1.0 - (inv_low + inv_high) * curve)
    body = body + jnp.log(low * inv_high) * quarter
    body = body + jnp.where(rho < -gap, 1.0 / rho - inv_low, 0.0)
    return jnp.where(high > rho, 8.0 * body, 0.0)


def neighbour_lists(partner_ref, first_home, home_id, first_window, homes, slots, filler, table_ref):
    window = partner_ref.shape[0]
    tiles = [slice(start, start + LANES) for start in range(0, window, LANES)]
    depth = -(-slots // 8) * 8
    ids = jnp.concatenate([partner_ref[tile, :].T[:depth] for tile in tiles], axis=1)
    lists = turned(partner_ref[pl.ds(first_home, homes), :])[:depth]
    lane = lax.broadcasted_iota(jnp.int32, (depth, window), 1)
    lane_id = (lane + (first_window + 1)).astype(jnp.float32)
    rows = []
    for home in range(homes):
        own = (home_id + home + 1).astype(jnp.float32)
        linked = (ids == own) | (lane_id == lists[:, home : home + 1])
        rows.append(jnp.max(jnp.where(linked, 1.0, 0.0), axis=0, keepdims=True))
    linked = jnp.concatenate(rows, axis=0)
    before = lax.broadcasted_iota(jnp.int32, (window, window), 0)
    after = lax.broadcasted_iota(jnp.int32, (window, window), 1)
    ramp = jnp.where(before <= after, 1.0, 0.0).astype(jnp.bfloat16)
    rank = jnp.dot(linked.astype(jnp.bfloat16), ramp, preferred_element_type=jnp.float32)
    place = jnp.where(linked > 0.0, rank - 1.0, -1.0)
    total = jnp.sum(linked, axis=1, keepdims=True)
    columns = [turned(place[:, tile]) for tile in tiles]
    spot = lax.broadcasted_iota(jnp.int32, (LANES, LANES), 1).astype(jnp.float32)
    name = lax.broadcasted_iota(jnp.int32, (LANES, LANES), 0).astype(jnp.float32)
    for tile in tiles:
        for home in range(homes):
            found = jnp.zeros((LANES, LANES), jnp.float32)
            for other, column in zip(tiles, columns):
                hit = column[:, home : home + 1] == spot + float(tile.start)
                found = found + jnp.where(hit, name + float(other.start), 0.0)
            row = jnp.sum(found, axis=0, keepdims=True)
            past = spot[:1] + float(tile.start) >= total[home : home + 1]
            table_ref[home : home + 1, tile] = jnp.where(past, float(filler), row).astype(jnp.int32)
    table_ref[homes : 2 * homes, :] = jnp.broadcast_to(total, (homes, window)).astype(jnp.int32)
    table_ref[2 * homes :, :] = jnp.full((SUBLANES, window), filler, jnp.int32)


def radii_kernel(
    blocks,
    slots,
    twins,
    place_ref,
    *refs,
):
    arrived_refs, refs = refs[:twins], refs[twins:]
    copies_ref, table_ref, window_ref, columns_ref, types_ref, partner_ref, total_ref, *refs = refs
    turned_ref, packed_ref, near_ref, lists_ref, items_ref, lists_sem = refs
    _, homes, groups, _, _ = columns_ref.shape
    chunk = groups * SUBLANES
    window = types_ref.shape[0]
    parts = homes // blocks
    together = max(1, LANES // chunk)
    first_home = pl.multiple_of(place_ref[0], homes)
    first_atom = pl.multiple_of(place_ref[3], chunk)

    tables = [window_ref.at[WINDOW_X], window_ref.at[WINDOW_Y], window_ref.at[WINDOW_Z]]
    tables += [types_ref, window_ref.at[WINDOW_CHARGE], partner_ref]
    odd = place_ref[4] == 1
    for place in range(arrived_refs[0].shape[0]):
        for field, table in enumerate(tables):
            rows = [ref[place, field * blocks : (field + 1) * blocks, :] for ref in arrived_refs]
            if twins == 2:
                rows = [jnp.where(odd, rows[1], rows[0]), jnp.where(odd, rows[0], rows[1])]
            first = place * twins * blocks
            table[first : first + twins * blocks, :] = jnp.concatenate(rows, axis=0)
    if partner_ref.shape[0] > window:
        spare = (partner_ref.shape[0] - window, LANES)
        partner_ref[window:, :] = jnp.full(spare, EMPTY_SLOT, jnp.float32)
    neighbour_lists(partner_ref, first_home, place_ref[1], place_ref[2], homes, slots, window, table_ref)
    move = pltpu.make_async_copy(table_ref, lists_ref, lists_sem)
    move.start()

    _, _, scaled = type_fields(types_ref[...])
    window_ref[WINDOW_SCALED, 0:window, :] = 0.25 * scaled
    for field in range(WINDOW_COUNT):
        filler = FAR_AWAY if field == WINDOW_X else 0.0
        window_ref[field, window : window + SUBLANES, :] = jnp.full((SUBLANES, LANES), filler, jnp.float32)

    home_rows = [window_ref[field, pl.ds(first_home, homes), :] for field in range(3)]
    turned_ref[...] = turned(jnp.concatenate([types_ref[pl.ds(first_home, homes), :]] + home_rows, axis=0))
    columns = turned_ref[pl.ds(first_atom, chunk), :]
    intrinsic, rho, _ = type_fields(columns)
    for home in range(homes):
        columns_ref[0, home] = spread(0.25 * rho, home)
        for index in range(1, 4):
            columns_ref[index, home] = spread(columns, index * homes + home)

    def pair_distance(home, step, rows):
        dx = columns_ref[1, home, step] - rows[0]
        dy = columns_ref[2, home, step] - rows[1]
        dz = columns_ref[3, home, step] - rows[2]
        return dx * dx + dy * dy + dz * dz

    steps = [pl.ds(start, STEP) for start in range(0, groups, STEP)]

    shift = (lists_ref.shape[1] - 1).bit_length()
    usual = 8

    def list_items(home, filled):
        turns = (lists_ref[homes + home, 0] + (together - 1)) // together

        def put(index, carry):
            items_ref[filled + index] = (home << shift) + index * together
            return carry

        for index in range(usual):
            put(index, 0)
        lax.fori_loop(usual, turns, put, 0)
        return filled + turns

    def sweep(integral, item_count):
        near_ref[...] = jnp.full(near_ref.shape, FAR_AWAY, jnp.float32)
        own_together = min(homes, 2 * together)

        def own_pairs(turn, carry):
            for index in range(own_together):
                home = turn * own_together + index
                rows = [row_of(window_ref, field, first_home + home) for field in range(4)]
                for start, step in zip(range(0, groups, STEP), steps):
                    same = diagonal(STEP, first_atom + start * SUBLANES)
                    squared = jnp.where(same, FAR_AWAY, pair_distance(home, step, rows))
                    term = integral(squared, columns_ref[0, home, step], rows[3])
                    total_ref[home, step] = jnp.where(same, 0.0, term)
                    near_ref[...] = jnp.minimum(near_ref[...], squared)
            return carry

        lax.fori_loop(0, homes // own_together, own_pairs, 0)

        def visit(turn, nearest):
            sums = []
            for index in range(ITEMS):
                item = items_ref[turn * ITEMS + index]
                line, entry = item >> shift, item & ((1 << shift) - 1)
                home = jnp.minimum(line, homes - 1)
                parts_of = [None] * len(steps)
                for other in range(together):
                    partner = lists_ref[line, entry + other]
                    rows = [row_of(window_ref, field, partner) for field in range(4)]
                    for place, step in enumerate(steps):
                        squared = pair_distance(home, step, rows)
                        nearest = jnp.minimum(nearest, squared)
                        term = integral(squared, columns_ref[0, home, step], rows[3])
                        parts_of[place] = term if other == 0 else parts_of[place] + term
                sums.append((home, parts_of))
            for home, parts_of in sums:
                for part, step in zip(parts_of, steps):
                    total_ref[home, step] += part
            return nearest

        near_ref[...] = lax.fori_loop(0, (item_count + (ITEMS - 1)) // ITEMS, visit, near_ref[...])
        lane = lax.broadcasted_iota(jnp.int32, (chunk, LANES), 1)
        packed = jnp.zeros((chunk, LANES), jnp.float32)
        for home in range(homes):
            packed = jnp.where(lane == home, lane_total(total_ref[home]), packed)
        packed_ref[...] = packed

    move.wait()
    item_count = lax.fori_loop(0, homes, list_items, 0)
    for index in range(ITEMS):
        items_ref[item_count + index] = (2 * homes) << shift
    sweep(descreen, item_count)

    @pl.when(jnp.min(near_ref[...]) < short_range * short_range)
    def _():
        sweep(descreen_any, item_count)

    psi = (0.125 * packed_ref[...]) * rho
    shaped = born_alpha * psi - born_beta * psi * psi + born_gamma * psi * psi * psi
    radii = 1.0 / (1.0 / rho - jnp.tanh(shaped) / intrinsic)

    if chunk < LANES:
        radii = jnp.concatenate([radii, jnp.zeros((LANES - chunk, LANES), jnp.float32)], axis=0)
    turned_ref[...] = radii.T
    lane = lax.broadcasted_iota(jnp.int32, (blocks, LANES), 1)
    sent = turned_ref[pl.ds(0, blocks, stride=parts), :]
    for index in range(1, parts):
        rows = pltpu.roll(turned_ref[pl.ds(index, blocks, stride=parts), :], index * chunk, 1)
        sent = jnp.where(lane >= index * chunk, rows, sent)
    for copy in range(copies_ref.shape[0]):
        copies_ref[copy] = sent


def energy_kernel(
    parts,
    place_ref,
    lists_ref,
    window_ref,
    gathered_ref,
    own_radii_ref,
    energy_ref,
    forces_ref,
    grad_ref,
    columns_ref,
    radii_ref,
    total_ref,
):
    devices, blocks, atoms = gathered_ref.shape
    window = devices * blocks
    part_rows = window // parts
    chunk = atoms // parts
    groups = atoms // SUBLANES
    first_own, list_row = place_ref[0], place_ref[1]

    lane = lax.broadcasted_iota(jnp.int32, (part_rows, LANES), 1)
    pieces = [
        gathered_ref[pl.ds(part, devices // parts, stride=parts)].reshape(part_rows, atoms)
        for part in range(parts)
    ]
    for place in range(parts):
        whole = pieces[0] if place == 0 else pltpu.roll(pieces[0], (parts - place) * chunk, 1)
        for part in range(1, parts):
            shift = (part - place) % parts
            piece = pieces[part] if shift == 0 else pltpu.roll(pieces[part], shift * chunk, 1)
            whole = jnp.where(lane >= part * chunk, piece, whole)
        radii_ref[0, pl.ds(place, part_rows, stride=parts), :] = whole

    radii_ref[0, window : window + SUBLANES, :] = jnp.ones((SUBLANES, LANES), jnp.float32)
    fields = [(window_ref, field) for field in (WINDOW_X, WINDOW_Y, WINDOW_Z, WINDOW_CHARGE)] + [(radii_ref, 0)]
    own = [
        jnp.concatenate([ref[field, pl.ds(first_own + block, 1), :] for block in range(blocks)], axis=0)
        for ref, field in fields
    ]
    charges, own_radii = own[3], own[4]
    own_radii_ref[...] = own_radii
    own_decay = 1.0 / own_radii
    columns = turned(jnp.concatenate(own[:3] + [-4.0 * own_radii], axis=0))
    for index in range(4 * blocks):
        columns_ref[index] = spread(columns, index)

    def pair_terms(block, step, rows, same=None):
        x, y, z, charge, radius = rows
        dx = columns_ref[block, step] - x
        dy = columns_ref[blocks + block, step] - y
        dz = columns_ref[2 * blocks + block, step] - z
        squared = dx * dx + dy * dy + dz * dz
        if same is not None:
            squared = jnp.where(same, 1.0, squared)
            charge = jnp.where(same, 0.0, charge)
        spread_sq = columns_ref[3 * blocks + block, step] * radius
        power = squared * pltpu.reciprocal(spread_sq, approx=True)
        quarter = 0.25 * jnp.exp(power)
        blend = spread_sq * quarter
        inv_root = lax.rsqrt(squared - blend)
        potential = charge * inv_root
        cubed = potential * (inv_root * inv_root)
        pull = cubed * (1.0 - quarter)
        return (pull * dx, pull * dy, pull * dz, potential, cubed * blend * (1.0 - power))

    for block in range(blocks):
        rows = [row_of(ref, field, first_own + block) for ref, field in fields]
        for start in range(0, groups, ENERGY_STEP):
            step = pl.ds(start, ENERGY_STEP)
            terms = pair_terms(block, step, rows, diagonal(ENERGY_STEP, start * SUBLANES))
            for term, value in enumerate(terms):
                total_ref[term * blocks + block, step] = value

        def visit(count, first, index, carry, block=block):
            partners = []
            for other in range(count):
                partner = lists_ref[list_row + block, first + index * count + other]
                partners.append([row_of(ref, field, partner) for ref, field in fields])
            for start in range(0, groups, ENERGY_STEP):
                step = pl.ds(start, ENERGY_STEP)
                sums = [total_ref[term * blocks + block, step] for term in range(5)]
                for rows in partners:
                    sums = [total + value for total, value in zip(sums, pair_terms(block, step, rows))]
                for term, value in enumerate(sums):
                    total_ref[term * blocks + block, step] = value
            return carry

        left = lists_ref[parts * blocks + list_row + block, 0]
        first = 0
        for count in (4, 2, 1):
            turns = left // count
            lax.fori_loop(0, turns, functools.partial(visit, count, first), 0)
            first = first + turns * count
            left = left - turns * count
    sums = lane_sums([total_ref[index] for index in range(5 * blocks)], 5 * blocks)
    scale = solvent_tau * charges
    for axis in range(3):
        forces_ref[axis] = -scale * sums[axis * blocks : (axis + 1) * blocks]
    own_energy = 0.5 * scale * charges * own_decay
    energy_ref[...] = -0.5 * scale * sums[3 * blocks : 4 * blocks] - own_energy
    grad_ref[...] = (own_energy - 0.5 * scale * sums[4 * blocks : 5 * blocks]) * own_decay


def shards(positions, charges, types, pairs, owner_map):
    _, blocks, atoms = positions.shape
    regions = lax.axis_size("region")
    region_devices = lax.axis_size("dev")
    kept_regions, whole = window_regions(regions)
    devices = kept_regions * region_devices
    window = devices * blocks
    region_here = lax.axis_index("region")
    device_here = lax.axis_index("dev")
    first_window = 0 if whole else (region_here - 1) * region_devices * blocks

    parts = atoms // CHUNK
    while region_devices % parts or 4 * parts * blocks > LANES:
        parts //= 2
    homes = parts * blocks
    chunk = atoms // parts
    part_here = device_here % parts
    home_id = (region_here * region_devices + device_here - part_here) * blocks
    first_home = home_id - first_window

    vmem = pl.BlockSpec(memory_space=pltpu.VMEM)
    smem = pl.BlockSpec(memory_space=pltpu.SMEM)
    params = pltpu.CompilerParams(vmem_limit_bytes=40 * 1024 * 1024)
    copy_count = lax.axis_size(exchange_axes())
    twins = twin_count(region_devices)
    arrived = sent_to_both_twins(
        pl.pallas_call(
            functools.partial(fields_kernel, blocks, atoms),
            out_shape=jax.ShapeDtypeStruct((copy_count // twins, ROW_COUNT, blocks, atoms), jnp.float32),
            in_specs=[pl.BlockSpec(memory_space=pltpu.HBM)] * 5,
            out_specs=vmem,
            scratch_shapes=[
                pltpu.VMEM(positions.shape, positions.dtype),
                pltpu.VMEM(types.shape, types.dtype),
                pltpu.VMEM(charges.shape, charges.dtype),
                pltpu.SMEM(pairs.shape, pairs.dtype),
                pltpu.SMEM(owner_map.shape, owner_map.dtype),
                pltpu.SemaphoreType.DMA((5,)),
            ],
        )(positions, types, charges, pairs, owner_map)
    )
    arrived = [with_other_regions(part).reshape(devices // twins, ROW_COUNT * blocks, atoms) for part in arrived]
    padded = -(-window // LANES) * LANES
    table = jax.ShapeDtypeStruct((2 * homes + SUBLANES, padded), jnp.int32)
    place = jnp.stack([first_home, home_id, jnp.int32(first_window), part_here * chunk, device_here % twins])
    fields = jax.ShapeDtypeStruct((WINDOW_COUNT, window + SUBLANES, atoms), jnp.float32)
    copies, lists, window_fields = pl.pallas_call(
        functools.partial(radii_kernel, blocks, pairs.shape[1], twins),
        out_shape=(jax.ShapeDtypeStruct((copy_count, blocks, atoms), jnp.float32), table, fields),
        in_specs=[smem] + [vmem] * twins,
        out_specs=(vmem, vmem, vmem),
        scratch_shapes=[
            pltpu.VMEM((4, homes, chunk // SUBLANES, SUBLANES, LANES), jnp.float32),
            pltpu.VMEM((window, atoms), jnp.float32),
            pltpu.VMEM((padded, atoms), jnp.float32),
            pltpu.VMEM((homes, chunk // SUBLANES, SUBLANES, LANES), jnp.float32),
            pltpu.VMEM((LANES, LANES), jnp.float32),
            pltpu.VMEM((chunk, LANES), jnp.float32),
            pltpu.VMEM((STEP, SUBLANES, LANES), jnp.float32),
            pltpu.SMEM(table.shape, jnp.int32),
            pltpu.SMEM((homes * (table.shape[1] // max(1, LANES // chunk) + 1) + 64,), jnp.int32),
            pltpu.SemaphoreType.DMA(()),
        ],
        compiler_params=params,
    )(place, *arrived)
    block_out = jax.ShapeDtypeStruct((blocks, atoms), jnp.float32)
    own_place = jnp.stack([first_home + part_here * blocks, part_here * blocks])
    own_radii, energy, forces, grad = pl.pallas_call(
        functools.partial(energy_kernel, parts),
        out_shape=(block_out, block_out, jax.ShapeDtypeStruct((3, blocks, atoms), jnp.float32), block_out),
        in_specs=[smem, smem, vmem, vmem],
        out_specs=(vmem, vmem, vmem, vmem),
        scratch_shapes=[
            pltpu.VMEM((4 * blocks, atoms // SUBLANES, SUBLANES, LANES), jnp.float32),
            pltpu.VMEM((1, window + SUBLANES, atoms), jnp.float32),
            pltpu.VMEM((5 * blocks, atoms // SUBLANES, SUBLANES, LANES), jnp.float32),
        ],
        compiler_params=params,
    )(own_place, lists, window_fields, with_other_regions(sent_directly(copies)))
    return own_radii, energy, forces, grad


def solution(mesh):
    placed = (
        P(None, ("region", "dev"), None),
        P(("region", "dev"), None),
        P(("region", "dev"), None),
        P(("region", "dev"), None),
        P(),
    )
    return jax.shard_map(
        shards,
        mesh=mesh,
        in_specs=placed,
        out_specs=(
            P(("region", "dev"), None),
            P(("region", "dev"), None),
            P(None, ("region", "dev"), None),
            P(("region", "dev"), None),
        ),
        check_vma=False,
    )
```

```python
import functools

import jax
import jax.numpy as jnp
from jax import lax
from jax.experimental import pallas as pl
from jax.experimental.pallas import tpu as pltpu
from jax.sharding import PartitionSpec as P

type_radii = (1.2, 1.7, 1.55, 1.52, 1.85, 1.8)
type_scales = (0.85, 0.72, 0.79, 0.85, 0.86, 0.96)
radius_offset = 0.09
born_alpha = 1.0
born_beta = 0.8
born_gamma = 4.85
solvent_tau = 1.0 - 1.0 / 78.5

ROW_X, ROW_Y, ROW_Z, ROW_TYPE, ROW_CHARGE, ROW_PARTNER, ROW_COUNT = range(7)
WINDOW_X, WINDOW_Y, WINDOW_Z, WINDOW_SCALED, WINDOW_CHARGE, WINDOW_COUNT = range(6)
LANES = 128
SUBLANES = 8
STEP = 4
ENERGY_STEP = 2
CHUNK = 32
LIST_ROWS = 32
ITEMS = 4
EMPTY_SLOT = -1.0e6
FAR_AWAY = 1.0e15

scaled_values = [scale * (radius - radius_offset) for radius, scale in zip(type_radii, type_scales)]
short_range = 1.01 * max(
    max(scaled_values) - (min(type_radii) - radius_offset),
    (max(type_radii) - radius_offset) - min(scaled_values),
    0.5,
)


def window_regions(region_count):
    return (region_count, True) if region_count <= 3 else (3, False)


def exchange_axes():
    return ("region", "dev") if window_regions(lax.axis_size("region"))[1] else ("dev",)


def twin_count(device_count):
    return 2 - device_count % 2


def sent_to_both_twins(copies):
    count = lax.axis_size("dev")
    twins = twin_count(count)
    axes = exchange_axes()
    regions = lax.axis_size(axes) // count
    alike = [list(range(parity, regions * count, twins)) for parity in range(twins)]
    here = lax.all_to_all(copies, axes, split_axis=0, concat_axis=0, axis_index_groups=alike, tiled=True)
    if twins == 1:
        return [here]
    return [here, lax.ppermute(here, "dev", [(i, i ^ 1) for i in range(count)])]


def with_other_regions(here):
    regions = lax.axis_size("region")
    if window_regions(regions)[1]:
        return here
    below = lax.ppermute(here, "region", [(i, i + 1) for i in range(regions - 1)])
    above = lax.ppermute(here, "region", [(i + 1, i) for i in range(regions - 1)])
    return jnp.concatenate([below, here, above], axis=0)


def by_type(types, table):
    value = jnp.full(types.shape, table[0], jnp.float32)
    for index in range(1, len(table)):
        value = jnp.where(types == index, jnp.float32(table[index]), value)
    return value


def type_fields(types):
    intrinsic = by_type(types, type_radii)
    rho = intrinsic - radius_offset
    return intrinsic, rho, by_type(types, type_scales) * rho


def turned(rows):
    count, width = rows.shape
    if count < LANES:
        rows = jnp.concatenate([rows, jnp.zeros((LANES - count, width), rows.dtype)], axis=0)
    return rows.T


def spread(columns, index):
    count = columns.shape[0]
    wide = jnp.broadcast_to(columns[:, index : index + 1], (count, LANES))
    return wide.reshape(count // SUBLANES, SUBLANES, LANES)


def row_of(ref, field, row):
    return ref[field, pl.ds(row, SUBLANES, stride=0), :][None]


def diagonal(groups, first_atom):
    shape = (groups, SUBLANES, LANES)
    row = lax.broadcasted_iota(jnp.int32, shape, 0) * SUBLANES + lax.broadcasted_iota(jnp.int32, shape, 1)
    return row + first_atom == lax.broadcasted_iota(jnp.int32, shape, 2)


def lane_total(array):
    return jnp.sum(array.reshape(-1, LANES), axis=1, keepdims=True)


def lane_sums(arrays, count):
    atoms = arrays[0].shape[0] * SUBLANES
    lane = lax.broadcasted_iota(jnp.int32, (atoms, LANES), 1)
    packed = jnp.zeros((atoms, LANES), jnp.float32)
    for index, array in enumerate(arrays):
        packed = jnp.where(lane == index, lane_total(array), packed)
    return packed.T[:count]


def fields_kernel(blocks, atoms, *refs):
    inputs, copies_ref, here, sems = refs[:5], refs[5], refs[6:11], refs[11]
    moves = [pltpu.make_async_copy(src, dst, sems.at[i]) for i, (src, dst) in enumerate(zip(inputs, here))]
    for move in moves:
        move.start()
    for move in moves:
        move.wait()
    positions_ref, types_ref, charges_ref, pairs_ref, owner_ref = here
    slot = lax.broadcasted_iota(jnp.int32, (1, atoms), 1)
    partners = []
    for block in range(blocks):
        row = jnp.full((1, atoms), EMPTY_SLOT, jnp.float32)
        for index in range(pairs_ref.shape[1]):
            cell = pairs_ref[block, index]
            partner = jnp.where(cell >= 0, owner_ref[jnp.maximum(cell, 0)] + 1, int(EMPTY_SLOT))
            row = jnp.where(slot == index, partner.astype(jnp.float32), row)
        partners.append(row)
    rows = [positions_ref[axis] for axis in range(3)]
    rows += [types_ref[...].astype(jnp.float32), charges_ref[...], jnp.concatenate(partners, axis=0)]
    for copy in range(copies_ref.shape[0]):
        for index, row in enumerate(rows):
            copies_ref[copy, index] = row


def descreen(squared, rho, scaled):
    inv_dist = lax.rsqrt(squared)
    share = scaled * inv_dist
    inner = 0.25 - share
    high = 0.25 + share
    low = jnp.maximum(rho * inv_dist, inner)
    inv_low = pltpu.reciprocal(low, approx=True)
    ratio = low * pltpu.reciprocal(high, approx=True)
    curve = (1.0 - ratio) + inner * (ratio - high * inv_low)
    return (inv_low * curve + 2.0 * jnp.log(ratio)) * inv_dist


def descreen_any(squared, rho, scaled):
    rho, scaled = 4.0 * rho, 4.0 * scaled
    inv_dist = lax.rsqrt(squared)
    distance = squared * inv_dist
    high = distance + scaled
    gap = distance - scaled
    low = jnp.maximum(rho, jnp.abs(gap))
    inv_low = 1.0 / low
    inv_high = 1.0 / high
    quarter = 0.25 * inv_dist
    curve = (squared - scaled * scaled) * quarter
    body = (0.5 * (inv_low - inv_high)) * (1.0 - (inv_low + inv_high) * curve)
    body = body + jnp.log(low * inv_high) * quarter
    body = body + jnp.where(rho < -gap, 1.0 / rho - inv_low, 0.0)
    return jnp.where(high > rho, 8.0 * body, 0.0)


def neighbour_lists(partner_ref, first_home, home_id, first_window, homes, slots, filler, table_ref):
    window = partner_ref.shape[0]
    tiles = [slice(start, start + LANES) for start in range(0, window, LANES)]
    depth = -(-slots // SUBLANES) * SUBLANES
    ids = jnp.concatenate([partner_ref[tile, :].T[:depth] for tile in tiles], axis=1)
    lists = turned(partner_ref[pl.ds(first_home, homes), :])[:depth]
    lane = lax.broadcasted_iota(jnp.int32, (depth, window), 1)
    lane_id = (lane + (first_window + 1)).astype(jnp.float32)
    rows = []
    for home in range(homes):
        own = (home_id + home + 1).astype(jnp.float32)
        linked = (ids == own) | (lane_id == lists[:, home : home + 1])
        rows.append(jnp.max(jnp.where(linked, 1.0, 0.0), axis=0, keepdims=True))
    linked = jnp.concatenate(rows, axis=0)
    before = lax.broadcasted_iota(jnp.int32, (window, window), 0)
    after = lax.broadcasted_iota(jnp.int32, (window, window), 1)
    ramp = jnp.where(before <= after, 1.0, 0.0).astype(jnp.bfloat16)
    rank = jnp.dot(linked.astype(jnp.bfloat16), ramp, preferred_element_type=jnp.float32)
    place = jnp.where(linked > 0.0, rank, 0.0)
    total = jnp.sum(linked, axis=1, keepdims=True)
    name = lax.broadcasted_iota(jnp.int32, (LIST_ROWS, window), 1).astype(jnp.float32)
    spot = lax.broadcasted_iota(jnp.int32, (LIST_ROWS, window), 0).astype(jnp.float32)
    own_lane = lax.broadcasted_iota(jnp.int32, (LIST_ROWS, LANES), 1)

    def some_rows(start):
        first = jnp.asarray(start + 1).astype(jnp.float32)
        packed = jnp.zeros((LIST_ROWS, LANES), jnp.float32)
        for home in range(homes):
            hit = place[home : home + 1] == spot + first
            found = jnp.sum(jnp.where(hit, name - float(filler), 0.0), axis=1, keepdims=True)
            packed = jnp.where(own_lane == home, found, packed)
        rows = pl.ds(pl.multiple_of(SUBLANES + start, SUBLANES), LIST_ROWS)
        table_ref[rows, :] = packed.astype(jnp.int32) + filler

    counts = jnp.zeros((SUBLANES, LANES), jnp.float32)
    lane = lax.broadcasted_iota(jnp.int32, (SUBLANES, LANES), 1)
    for home in range(homes):
        counts = jnp.where(lane == home, total[home : home + 1], counts)
    longest = jnp.max(total)
    table_ref[0:SUBLANES, :] = jnp.where(lane == LANES - 1, longest, counts).astype(jnp.int32)
    some_rows(0)

    def more_rows(turn, carry):
        some_rows(turn * LIST_ROWS)
        return carry

    lax.fori_loop(1, (longest.astype(jnp.int32) + (LIST_ROWS - 1)) // LIST_ROWS, more_rows, 0)


def move_lists(table_ref, lists_ref, sem, when_wanted):
    usual = pl.ds(0, SUBLANES + LIST_ROWS)
    move = pltpu.make_async_copy(table_ref.at[usual], lists_ref.at[usual], sem)
    move.start()
    when_wanted()
    move.wait()
    rows = lists_ref.shape[0] - (SUBLANES + LIST_ROWS)
    if rows > 0:

        @pl.when(lists_ref[0, LANES - 1] > LIST_ROWS)
        def _():
            rest = pl.ds(SUBLANES + LIST_ROWS, rows)
            more = pltpu.make_async_copy(table_ref.at[rest], lists_ref.at[rest], sem)
            more.start()
            more.wait()


def device_place(blocks, parts, whole):
    region, device = lax.axis_index("region"), lax.axis_index("dev")
    region_blocks = lax.axis_size("dev") * blocks
    first_window = 0 if whole else (region - 1) * region_blocks
    first_own = region * region_blocks + device * blocks
    part = lax.rem(device, parts)
    return first_window, first_own - part * blocks, first_own, part


def radii_kernel(
    blocks,
    slots,
    twins,
    whole,
    *refs,
):
    arrived_refs, refs = refs[:twins], refs[twins:]
    copies_ref, table_ref, window_ref, columns_ref, types_ref, partner_ref, total_ref, *refs = refs
    turned_ref, packed_ref, near_ref, lists_ref, items_ref, lists_sem = refs
    _, homes, groups, _, _ = columns_ref.shape
    chunk = groups * SUBLANES
    window = types_ref.shape[0]
    parts = homes // blocks
    together = max(1, LANES // chunk)
    first_window, home_id, _, part = device_place(blocks, parts, whole)
    first_home = pl.multiple_of(home_id - first_window, homes)
    first_atom = pl.multiple_of(part * chunk, chunk)

    tables = [window_ref.at[WINDOW_X], window_ref.at[WINDOW_Y], window_ref.at[WINDOW_Z]]
    tables += [types_ref, window_ref.at[WINDOW_CHARGE], partner_ref]
    odd = lax.rem(lax.axis_index("dev"), 2) == 1
    for place in range(arrived_refs[0].shape[0]):
        for field, table in enumerate(tables):
            rows = [ref[place, field * blocks : (field + 1) * blocks, :] for ref in arrived_refs]
            if twins == 2:
                rows = [jnp.where(odd, rows[1], rows[0]), jnp.where(odd, rows[0], rows[1])]
            first = place * twins * blocks
            table[first : first + twins * blocks, :] = jnp.concatenate(rows, axis=0)
    if partner_ref.shape[0] > window:
        spare = (partner_ref.shape[0] - window, LANES)
        partner_ref[window:, :] = jnp.full(spare, EMPTY_SLOT, jnp.float32)
    def scaled_radii():
        _, _, scaled = type_fields(types_ref[...])
        window_ref[WINDOW_SCALED, 0:window, :] = 0.25 * scaled
        for field in range(WINDOW_COUNT):
            filler = FAR_AWAY if field == WINDOW_X else 0.0
            window_ref[field, window : window + SUBLANES, :] = jnp.full((SUBLANES, LANES), filler, jnp.float32)

    def home_columns():
        scaled_radii()
        home_rows = [window_ref[field, pl.ds(first_home, homes), :] for field in range(3)]
        turned_ref[...] = turned(jnp.concatenate([types_ref[pl.ds(first_home, homes), :]] + home_rows, axis=0))
        columns = turned_ref[pl.ds(first_atom, chunk), :]
        _, rho, _ = type_fields(columns)
        for home in range(homes):
            columns_ref[0, home] = spread(0.25 * rho, home)
            for index in range(1, 4):
                columns_ref[index, home] = spread(columns, index * homes + home)

    neighbour_lists(partner_ref, first_home, home_id, first_window, homes, slots, window, table_ref)
    move_lists(table_ref, lists_ref, lists_sem, home_columns)
    intrinsic, rho, _ = type_fields(turned_ref[pl.ds(first_atom, chunk), :])

    def pair_distance(home, step, rows):
        dx = columns_ref[1, home, step] - rows[0]
        dy = columns_ref[2, home, step] - rows[1]
        dz = columns_ref[3, home, step] - rows[2]
        return dx * dx + dy * dy + dz * dz

    steps = [pl.ds(start, STEP) for start in range(0, groups, STEP)]

    shift = lists_ref.shape[0].bit_length()
    usual = 8

    def list_items(home, filled):
        turns = (lists_ref[0, home] + (together - 1)) // together

        def put(index, carry):
            items_ref[filled + index] = (home << shift) + index * together
            return carry

        for index in range(usual):
            put(index, 0)
        lax.fori_loop(usual, turns, put, 0)
        return filled + turns

    def sweep(integral, item_count):
        near_ref[...] = jnp.full(near_ref.shape, FAR_AWAY, jnp.float32)
        own_together = min(homes, 2 * together)

        def own_pairs(turn, carry):
            for index in range(own_together):
                home = turn * own_together + index
                rows = [row_of(window_ref, field, first_home + home) for field in range(4)]
                for start, step in zip(range(0, groups, STEP), steps):
                    same = diagonal(STEP, first_atom + start * SUBLANES)
                    squared = jnp.where(same, FAR_AWAY, pair_distance(home, step, rows))
                    term = integral(squared, columns_ref[0, home, step], rows[3])
                    total_ref[home, step] = jnp.where(same, 0.0, term)
                    near_ref[...] = jnp.minimum(near_ref[...], squared)
            return carry

        lax.fori_loop(0, homes // own_together, own_pairs, 0)

        def visit(turn, nearest):
            sums = []
            for index in range(ITEMS):
                item = items_ref[turn * ITEMS + index]
                line, entry = item >> shift, item & ((1 << shift) - 1)
                home = jnp.minimum(line, homes - 1)
                parts_of = [None] * len(steps)
                for other in range(together):
                    partner = lists_ref[SUBLANES + entry + other, line]
                    rows = [row_of(window_ref, field, partner) for field in range(4)]
                    for place, step in enumerate(steps):
                        squared = pair_distance(home, step, rows)
                        nearest = jnp.minimum(nearest, squared)
                        term = integral(squared, columns_ref[0, home, step], rows[3])
                        parts_of[place] = term if other == 0 else parts_of[place] + term
                sums.append((home, parts_of))
            for home, parts_of in sums:
                for part, step in zip(parts_of, steps):
                    total_ref[home, step] += part
            return nearest

        near_ref[...] = lax.fori_loop(0, (item_count + (ITEMS - 1)) // ITEMS, visit, near_ref[...])
        lane = lax.broadcasted_iota(jnp.int32, (chunk, LANES), 1)
        packed = jnp.zeros((chunk, LANES), jnp.float32)
        for home in range(homes):
            packed = jnp.where(lane == home, lane_total(total_ref[home]), packed)
        packed_ref[...] = packed

    item_count = lax.fori_loop(0, homes, list_items, 0)
    for index in range(ITEMS):
        items_ref[item_count + index] = homes << shift
    sweep(descreen, item_count)

    @pl.when(jnp.min(near_ref[...]) < short_range * short_range)
    def _():
        sweep(descreen_any, item_count)

    psi = (0.125 * packed_ref[...]) * rho
    shaped = born_alpha * psi - born_beta * psi * psi + born_gamma * psi * psi * psi
    radii = 1.0 / (1.0 / rho - jnp.tanh(shaped) / intrinsic)

    if chunk < LANES:
        radii = jnp.concatenate([radii, jnp.zeros((LANES - chunk, LANES), jnp.float32)], axis=0)
    turned_ref[...] = radii.T
    lane = lax.broadcasted_iota(jnp.int32, (blocks, LANES), 1)
    sent = turned_ref[pl.ds(0, blocks, stride=parts), :]
    for index in range(1, parts):
        rows = pltpu.roll(turned_ref[pl.ds(index, blocks, stride=parts), :], index * chunk, 1)
        sent = jnp.where(lane >= index * chunk, rows, sent)
    for copy in range(copies_ref.shape[0]):
        copies_ref[copy] = sent


def energy_kernel(
    parts,
    twins,
    whole,
    table_ref,
    window_ref,
    *refs,
):
    arrived_refs, refs = refs[:twins], refs[twins:]
    own_radii_ref, energy_ref, forces_ref, grad_ref, columns_ref, radii_ref, total_ref, *refs = refs
    gathered_ref, lists_ref, lists_sem = refs
    devices, blocks, atoms = gathered_ref.shape
    window = devices * blocks
    part_rows = window // parts
    chunk = atoms // parts
    groups = atoms // SUBLANES
    first_window, _, own_id, part_here = device_place(blocks, parts, whole)
    first_own, list_lane = own_id - first_window, part_here * blocks
    fields = [(window_ref, field) for field in (WINDOW_X, WINDOW_Y, WINDOW_Z, WINDOW_CHARGE)] + [(radii_ref, 0)]
    odd = lax.rem(lax.axis_index("dev"), 2) == 1

    def unpack():
        for place in range(arrived_refs[0].shape[0]):
            rows = [ref[place] for ref in arrived_refs]
            if twins == 2:
                rows = [jnp.where(odd, rows[1], rows[0]), jnp.where(odd, rows[0], rows[1])]
            for twin, row in enumerate(rows):
                gathered_ref[place * twins + twin] = row
        lane = lax.broadcasted_iota(jnp.int32, (part_rows, LANES), 1)
        pieces = [
            gathered_ref[pl.ds(part, devices // parts, stride=parts)].reshape(part_rows, atoms)
            for part in range(parts)
        ]
        for place in range(parts):
            whole_rows = pieces[0] if place == 0 else pltpu.roll(pieces[0], (parts - place) * chunk, 1)
            for part in range(1, parts):
                shift = (part - place) % parts
                piece = pieces[part] if shift == 0 else pltpu.roll(pieces[part], shift * chunk, 1)
                whole_rows = jnp.where(lane >= part * chunk, piece, whole_rows)
            radii_ref[0, pl.ds(place, part_rows, stride=parts), :] = whole_rows
        radii_ref[0, window : window + SUBLANES, :] = jnp.ones((SUBLANES, LANES), jnp.float32)

    def own_rows(ref, field):
        return jnp.concatenate([ref[field, pl.ds(first_own + block, 1), :] for block in range(blocks)], axis=0)

    def pair_terms(block, step, rows, same=None):
        x, y, z, charge, radius = rows
        dx = columns_ref[block, step] - x
        dy = columns_ref[blocks + block, step] - y
        dz = columns_ref[2 * blocks + block, step] - z
        squared = dx * dx + dy * dy + dz * dz
        if same is not None:
            squared = jnp.where(same, 1.0, squared)
            charge = jnp.where(same, 0.0, charge)
        spread_sq = columns_ref[3 * blocks + block, step] * radius
        power = squared * pltpu.reciprocal(spread_sq, approx=True)
        quarter = 0.25 * jnp.exp(power)
        blend = spread_sq * quarter
        inv_root = lax.rsqrt(squared - blend)
        potential = charge * inv_root
        cubed = potential * (inv_root * inv_root)
        pull = cubed * (1.0 - quarter)
        return (pull * dx, pull * dy, pull * dz, potential, cubed * blend * (1.0 - power))

    def own_pairs():
        unpack()
        own_radii = own_rows(radii_ref, 0)
        own_radii_ref[...] = own_radii
        own = [own_rows(window_ref, field) for field in (WINDOW_X, WINDOW_Y, WINDOW_Z)]
        columns = turned(jnp.concatenate(own + [-4.0 * own_radii], axis=0))
        for index in range(4 * blocks):
            columns_ref[index] = spread(columns, index)
        for block in range(blocks):
            rows = [row_of(ref, field, first_own + block) for ref, field in fields]
            for start in range(0, groups, ENERGY_STEP):
                step = pl.ds(start, ENERGY_STEP)
                terms = pair_terms(block, step, rows, diagonal(ENERGY_STEP, start * SUBLANES))
                for term, value in enumerate(terms):
                    total_ref[term * blocks + block, step] = value

    move_lists(table_ref, lists_ref, lists_sem, own_pairs)
    for block in range(blocks):

        def visit(count, first, index, carry, block=block):
            partners = []
            for other in range(count):
                partner = lists_ref[SUBLANES + first + index * count + other, list_lane + block]
                partners.append([row_of(ref, field, partner) for ref, field in fields])
            for start in range(0, groups, ENERGY_STEP):
                step = pl.ds(start, ENERGY_STEP)
                sums = [total_ref[term * blocks + block, step] for term in range(5)]
                for rows in partners:
                    sums = [total + value for total, value in zip(sums, pair_terms(block, step, rows))]
                for term, value in enumerate(sums):
                    total_ref[term * blocks + block, step] = value
            return carry

        left = lists_ref[0, list_lane + block]
        first = 0
        for count in (4, 2, 1):
            turns = left // count
            lax.fori_loop(0, turns, functools.partial(visit, count, first), 0)
            first = first + turns * count
            left = left - turns * count
    sums = lane_sums([total_ref[index] for index in range(5 * blocks)], 5 * blocks)
    charges = own_rows(window_ref, WINDOW_CHARGE)
    own_decay = 1.0 / own_radii_ref[...]
    scale = solvent_tau * charges
    for axis in range(3):
        forces_ref[axis] = -scale * sums[axis * blocks : (axis + 1) * blocks]
    own_energy = 0.5 * scale * charges * own_decay
    energy_ref[...] = -0.5 * scale * sums[3 * blocks : 4 * blocks] - own_energy
    grad_ref[...] = (own_energy - 0.5 * scale * sums[4 * blocks : 5 * blocks]) * own_decay


def shards(positions, charges, types, pairs, owner_map):
    _, blocks, atoms = positions.shape
    regions = lax.axis_size("region")
    region_devices = lax.axis_size("dev")
    kept_regions, whole = window_regions(regions)
    devices = kept_regions * region_devices
    window = devices * blocks
    parts = atoms // CHUNK
    while region_devices % parts or 4 * parts * blocks > LANES:
        parts //= 2
    homes = parts * blocks
    chunk = atoms // parts

    vmem = pl.BlockSpec(memory_space=pltpu.VMEM)
    params = pltpu.CompilerParams(vmem_limit_bytes=40 * 1024 * 1024)
    copy_count = lax.axis_size(exchange_axes())
    twins = twin_count(region_devices)
    arrived = sent_to_both_twins(
        pl.pallas_call(
            functools.partial(fields_kernel, blocks, atoms),
            out_shape=jax.ShapeDtypeStruct((copy_count // twins, ROW_COUNT, blocks, atoms), jnp.float32),
            in_specs=[pl.BlockSpec(memory_space=pltpu.HBM)] * 5,
            out_specs=vmem,
            scratch_shapes=[
                pltpu.VMEM(positions.shape, positions.dtype),
                pltpu.VMEM(types.shape, types.dtype),
                pltpu.VMEM(charges.shape, charges.dtype),
                pltpu.SMEM(pairs.shape, pairs.dtype),
                pltpu.SMEM(owner_map.shape, owner_map.dtype),
                pltpu.SemaphoreType.DMA((5,)),
            ],
        )(positions, types, charges, pairs, owner_map)
    )
    arrived = [with_other_regions(part).reshape(devices // twins, ROW_COUNT * blocks, atoms) for part in arrived]
    padded = -(-window // LANES) * LANES
    table = jax.ShapeDtypeStruct((SUBLANES + padded, LANES), jnp.int32)
    fields = jax.ShapeDtypeStruct((WINDOW_COUNT, window + SUBLANES, atoms), jnp.float32)
    copies, lists, window_fields = pl.pallas_call(
        functools.partial(radii_kernel, blocks, pairs.shape[1], twins, whole),
        out_shape=(jax.ShapeDtypeStruct((copy_count // twins, blocks, atoms), jnp.float32), table, fields),
        in_specs=[vmem] * twins,
        out_specs=(vmem, vmem, vmem),
        scratch_shapes=[
            pltpu.VMEM((4, homes, chunk // SUBLANES, SUBLANES, LANES), jnp.float32),
            pltpu.VMEM((window, atoms), jnp.float32),
            pltpu.VMEM((padded, atoms), jnp.float32),
            pltpu.VMEM((homes, chunk // SUBLANES, SUBLANES, LANES), jnp.float32),
            pltpu.VMEM((LANES, LANES), jnp.float32),
            pltpu.VMEM((chunk, LANES), jnp.float32),
            pltpu.VMEM((STEP, SUBLANES, LANES), jnp.float32),
            pltpu.SMEM(table.shape, jnp.int32),
            pltpu.SMEM((homes * (padded // max(1, LANES // chunk) + 1) + 64,), jnp.int32),
            pltpu.SemaphoreType.DMA(()),
        ],
        compiler_params=params,
    )(*arrived)
    block_out = jax.ShapeDtypeStruct((blocks, atoms), jnp.float32)
    window_radii = [
        with_other_regions(part).reshape(devices // twins, blocks, atoms) for part in sent_to_both_twins(copies)
    ]
    own_radii, energy, forces, grad = pl.pallas_call(
        functools.partial(energy_kernel, parts, twins, whole),
        out_shape=(block_out, block_out, jax.ShapeDtypeStruct((3, blocks, atoms), jnp.float32), block_out),
        in_specs=[pl.BlockSpec(memory_space=pl.ANY), vmem] + [vmem] * twins,
        out_specs=(vmem, vmem, vmem, vmem),
        scratch_shapes=[
            pltpu.VMEM((4 * blocks, atoms // SUBLANES, SUBLANES, LANES), jnp.float32),
            pltpu.VMEM((1, window + SUBLANES, atoms), jnp.float32),
            pltpu.VMEM((5 * blocks, atoms // SUBLANES, SUBLANES, LANES), jnp.float32),
            pltpu.VMEM((devices, blocks, atoms), jnp.float32),
            pltpu.SMEM(table.shape, jnp.int32),
            pltpu.SemaphoreType.DMA(()),
        ],
        compiler_params=params,
    )(lists, window_fields, *window_radii)
    return own_radii, energy, forces, grad


def solution(mesh):
    placed = (
        P(None, ("region", "dev"), None),
        P(("region", "dev"), None),
        P(("region", "dev"), None),
        P(("region", "dev"), None),
        P(),
    )
    return jax.shard_map(
        shards,
        mesh=mesh,
        in_specs=placed,
        out_specs=(
            P(("region", "dev"), None),
            P(("region", "dev"), None),
            P(None, ("region", "dev"), None),
            P(("region", "dev"), None),
        ),
        check_vma=False,
    )
```

```python
import functools

import jax
import jax.numpy as jnp
from jax import lax
from jax.experimental import pallas as pl
from jax.experimental.pallas import tpu as pltpu
from jax.sharding import PartitionSpec as P

type_radii = (1.2, 1.7, 1.55, 1.52, 1.85, 1.8)
type_scales = (0.85, 0.72, 0.79, 0.85, 0.86, 0.96)
radius_offset = 0.09
born_alpha = 1.0
born_beta = 0.8
born_gamma = 4.85
solvent_tau = 1.0 - 1.0 / 78.5

ROW_X, ROW_Y, ROW_Z, ROW_TYPE, ROW_CHARGE, ROW_PARTNER, ROW_COUNT = range(7)
WINDOW_X, WINDOW_Y, WINDOW_Z, WINDOW_SCALED, WINDOW_CHARGE, WINDOW_COUNT = range(6)
LANES = 128
SUBLANES = 8
STEP = 4
ENERGY_STEP = 2
CHUNK = 32
LIST_ROWS = 32
ITEMS = 8
EMPTY_SLOT = -1.0e6
FAR_AWAY = 1.0e15

scaled_values = [scale * (radius - radius_offset) for radius, scale in zip(type_radii, type_scales)]
short_range = 1.01 * max(
    max(scaled_values) - (min(type_radii) - radius_offset),
    (max(type_radii) - radius_offset) - min(scaled_values),
    0.5,
)


def window_regions(region_count):
    return (region_count, True) if region_count <= 3 else (3, False)


def exchange_axes():
    return ("region", "dev") if window_regions(lax.axis_size("region"))[1] else ("dev",)


def twin_count(device_count):
    return 2 - device_count % 2


def sent_to_both_twins(copies):
    count = lax.axis_size("dev")
    twins = twin_count(count)
    axes = exchange_axes()
    regions = lax.axis_size(axes) // count
    alike = [list(range(parity, regions * count, twins)) for parity in range(twins)]
    here = lax.all_to_all(copies, axes, split_axis=0, concat_axis=0, axis_index_groups=alike, tiled=True)
    if twins == 1:
        return [here]
    return [here, lax.ppermute(here, "dev", [(i, i ^ 1) for i in range(count)])]


def line_shape(device_count):
    twins = twin_count(device_count)
    near = 2 - device_count // twins % 2
    return device_count // (twins * near), near, twins


def gathered_by_lines(payload):
    count = lax.axis_size("dev")
    far, near, twins = line_shape(count)
    step = near * twins
    lines = [[line + step * place for place in range(far)] for line in range(step)]
    lined = lax.all_gather(payload, "dev", axis=0, axis_index_groups=lines)
    axes = exchange_axes()
    regions = lax.axis_size(axes) // count
    planes = [
        [region * count + place * step + line * twins + twin for region in range(regions) for line in range(near)]
        for place in range(far)
        for twin in range(twins)
    ]
    here = lax.all_gather(lined, axes, axis=0, axis_index_groups=planes)
    if twins == 1:
        return [here]
    return [here, lax.ppermute(here, "dev", [(i, i ^ 1) for i in range(count)])]


def with_other_regions(here):
    regions = lax.axis_size("region")
    if window_regions(regions)[1]:
        return here
    below = lax.ppermute(here, "region", [(i, i + 1) for i in range(regions - 1)])
    above = lax.ppermute(here, "region", [(i + 1, i) for i in range(regions - 1)])
    return jnp.concatenate([below, here, above], axis=0)


def by_type(types, table):
    value = jnp.full(types.shape, table[0], jnp.float32)
    for index in range(1, len(table)):
        value = jnp.where(types == index, jnp.float32(table[index]), value)
    return value


def type_fields(types):
    intrinsic = by_type(types, type_radii)
    rho = intrinsic - radius_offset
    return intrinsic, rho, by_type(types, type_scales) * rho


def turned(rows):
    count, width = rows.shape
    if count < LANES:
        rows = jnp.concatenate([rows, jnp.zeros((LANES - count, width), rows.dtype)], axis=0)
    return rows.T


def spread(columns, index):
    count = columns.shape[0]
    wide = jnp.broadcast_to(columns[:, index : index + 1], (count, LANES))
    return wide.reshape(count // SUBLANES, SUBLANES, LANES)


def row_of(ref, field, row):
    return ref[field, pl.ds(row, SUBLANES, stride=0), :][None]


def diagonal(groups, first_atom):
    shape = (groups, SUBLANES, LANES)
    row = lax.broadcasted_iota(jnp.int32, shape, 0) * SUBLANES + lax.broadcasted_iota(jnp.int32, shape, 1)
    return row + first_atom == lax.broadcasted_iota(jnp.int32, shape, 2)


def lane_total(array):
    return jnp.sum(array.reshape(-1, LANES), axis=1, keepdims=True)


def lane_sums(arrays, count):
    atoms = arrays[0].shape[0] * SUBLANES
    lane = lax.broadcasted_iota(jnp.int32, (atoms, LANES), 1)
    packed = jnp.zeros((atoms, LANES), jnp.float32)
    for index, array in enumerate(arrays):
        packed = jnp.where(lane == index, lane_total(array), packed)
    return packed.T[:count]


def fields_kernel(blocks, atoms, *refs):
    inputs, copies_ref, here, sems = refs[:5], refs[5], refs[6:11], refs[11]
    moves = [pltpu.make_async_copy(src, dst, sems.at[i]) for i, (src, dst) in enumerate(zip(inputs, here))]
    for move in moves:
        move.start()
    for move in moves:
        move.wait()
    positions_ref, types_ref, charges_ref, pairs_ref, owner_ref = here
    slot = lax.broadcasted_iota(jnp.int32, (1, atoms), 1)
    partners = []
    for block in range(blocks):
        row = jnp.full((1, atoms), EMPTY_SLOT, jnp.float32)
        for index in range(pairs_ref.shape[1]):
            cell = pairs_ref[block, index]
            partner = jnp.where(cell >= 0, owner_ref[jnp.maximum(cell, 0)] + 1, int(EMPTY_SLOT))
            row = jnp.where(slot == index, partner.astype(jnp.float32), row)
        partners.append(row)
    rows = [positions_ref[axis] for axis in range(3)]
    rows += [types_ref[...].astype(jnp.float32), charges_ref[...], jnp.concatenate(partners, axis=0)]
    for copy in range(copies_ref.shape[0]):
        for index, row in enumerate(rows):
            copies_ref[copy, index] = row


def descreen(squared, rho, scaled):
    inv_dist = lax.rsqrt(squared)
    share = scaled * inv_dist
    inner = 0.25 - share
    high = 0.25 + share
    low = jnp.maximum(rho * inv_dist, inner)
    inv_low = pltpu.reciprocal(low, approx=True)
    ratio = low * pltpu.reciprocal(high, approx=True)
    curve = (1.0 - ratio) + inner * (ratio - high * inv_low)
    return (inv_low * curve + 2.0 * jnp.log(ratio)) * inv_dist


def descreen_any(squared, rho, scaled):
    rho, scaled = 4.0 * rho, 4.0 * scaled
    inv_dist = lax.rsqrt(squared)
    distance = squared * inv_dist
    high = distance + scaled
    gap = distance - scaled
    low = jnp.maximum(rho, jnp.abs(gap))
    inv_low = 1.0 / low
    inv_high = 1.0 / high
    quarter = 0.25 * inv_dist
    curve = (squared - scaled * scaled) * quarter
    body = (0.5 * (inv_low - inv_high)) * (1.0 - (inv_low + inv_high) * curve)
    body = body + jnp.log(low * inv_high) * quarter
    body = body + jnp.where(rho < -gap, 1.0 / rho - inv_low, 0.0)
    return jnp.where(high > rho, 8.0 * body, 0.0)


def neighbour_lists(partner_ref, first_home, home_id, first_window, homes, slots, filler, table_ref):
    window = partner_ref.shape[0]
    tiles = [slice(start, start + LANES) for start in range(0, window, LANES)]
    depth = -(-slots // SUBLANES) * SUBLANES
    ids = jnp.concatenate([partner_ref[tile, :].T[:depth] for tile in tiles], axis=1)
    lists = turned(partner_ref[pl.ds(first_home, homes), :])[:depth]
    lane = lax.broadcasted_iota(jnp.int32, (depth, window), 1)
    lane_id = (lane + (first_window + 1)).astype(jnp.float32)
    rows = []
    for home in range(homes):
        own = (home_id + home + 1).astype(jnp.float32)
        linked = (ids == own) | (lane_id == lists[:, home : home + 1])
        rows.append(jnp.max(jnp.where(linked, 1.0, 0.0), axis=0, keepdims=True))
    linked = jnp.concatenate(rows, axis=0)
    before = lax.broadcasted_iota(jnp.int32, (window, window), 0)
    after = lax.broadcasted_iota(jnp.int32, (window, window), 1)
    ramp = jnp.where(before <= after, 1.0, 0.0).astype(jnp.bfloat16)
    rank = jnp.dot(linked.astype(jnp.bfloat16), ramp, preferred_element_type=jnp.float32)
    place = jnp.where(linked > 0.0, rank, 0.0)
    total = jnp.sum(linked, axis=1, keepdims=True)
    name = lax.broadcasted_iota(jnp.int32, (LIST_ROWS, window), 1).astype(jnp.float32)
    spot = lax.broadcasted_iota(jnp.int32, (LIST_ROWS, window), 0).astype(jnp.float32)
    own_lane = lax.broadcasted_iota(jnp.int32, (LIST_ROWS, LANES), 1)

    def some_rows(start):
        first = jnp.asarray(start + 1).astype(jnp.float32)
        packed = jnp.zeros((LIST_ROWS, LANES), jnp.float32)
        for home in range(homes):
            hit = place[home : home + 1] == spot + first
            found = jnp.sum(jnp.where(hit, name - float(filler), 0.0), axis=1, keepdims=True)
            packed = jnp.where(own_lane == home, found, packed)
        rows = pl.ds(pl.multiple_of(SUBLANES + start, SUBLANES), LIST_ROWS)
        table_ref[rows, :] = packed.astype(jnp.int32) + filler

    counts = jnp.zeros((SUBLANES, LANES), jnp.float32)
    lane = lax.broadcasted_iota(jnp.int32, (SUBLANES, LANES), 1)
    for home in range(homes):
        counts = jnp.where(lane == home, total[home : home + 1], counts)
    longest = jnp.max(total)
    table_ref[0:SUBLANES, :] = jnp.where(lane == LANES - 1, longest, counts).astype(jnp.int32)
    some_rows(0)

    def more_rows(turn, carry):
        some_rows(turn * LIST_ROWS)
        return carry

    lax.fori_loop(1, (longest.astype(jnp.int32) + (LIST_ROWS - 1)) // LIST_ROWS, more_rows, 0)


def move_lists(table_ref, lists_ref, sem, when_wanted):
    usual = pl.ds(0, SUBLANES + LIST_ROWS)
    move = pltpu.make_async_copy(table_ref.at[usual], lists_ref.at[usual], sem)
    move.start()
    when_wanted()
    move.wait()
    rows = lists_ref.shape[0] - (SUBLANES + LIST_ROWS)
    if rows > 0:

        @pl.when(lists_ref[0, LANES - 1] > LIST_ROWS)
        def _():
            rest = pl.ds(SUBLANES + LIST_ROWS, rows)
            more = pltpu.make_async_copy(table_ref.at[rest], lists_ref.at[rest], sem)
            more.start()
            more.wait()


def device_place(blocks, parts, whole):
    region, device = lax.axis_index("region"), lax.axis_index("dev")
    region_blocks = lax.axis_size("dev") * blocks
    first_window = 0 if whole else (region - 1) * region_blocks
    first_own = region * region_blocks + device * blocks
    part = lax.rem(device, parts)
    return first_window, first_own - part * blocks, first_own, part


def radii_kernel(
    blocks,
    slots,
    twins,
    whole,
    *refs,
):
    arrived_refs, refs = refs[:twins], refs[twins:]
    sent_ref, table_ref, window_ref, columns_ref, types_ref, partner_ref, total_ref, *refs = refs
    turned_ref, packed_ref, near_ref, lists_ref, items_ref, lists_sem = refs
    _, homes, groups, _, _ = columns_ref.shape
    chunk = groups * SUBLANES
    window = types_ref.shape[0]
    parts = homes // blocks
    together = max(1, LANES // chunk)
    first_window, home_id, _, part = device_place(blocks, parts, whole)
    first_home = pl.multiple_of(home_id - first_window, homes)
    first_atom = pl.multiple_of(part * chunk, chunk)

    tables = [window_ref.at[WINDOW_X], window_ref.at[WINDOW_Y], window_ref.at[WINDOW_Z]]
    tables += [types_ref, window_ref.at[WINDOW_CHARGE], partner_ref]
    odd = lax.rem(lax.axis_index("dev"), 2) == 1
    for place in range(arrived_refs[0].shape[0]):
        for field, table in enumerate(tables):
            rows = [ref[place, field * blocks : (field + 1) * blocks, :] for ref in arrived_refs]
            if twins == 2:
                rows = [jnp.where(odd, rows[1], rows[0]), jnp.where(odd, rows[0], rows[1])]
            first = place * twins * blocks
            table[first : first + twins * blocks, :] = jnp.concatenate(rows, axis=0)
    if partner_ref.shape[0] > window:
        spare = (partner_ref.shape[0] - window, LANES)
        partner_ref[window:, :] = jnp.full(spare, EMPTY_SLOT, jnp.float32)
    def scaled_radii():
        _, _, scaled = type_fields(types_ref[...])
        window_ref[WINDOW_SCALED, 0:window, :] = 0.25 * scaled
        for field in range(WINDOW_COUNT):
            filler = FAR_AWAY if field == WINDOW_X else 0.0
            window_ref[field, window : window + SUBLANES, :] = jnp.full((SUBLANES, LANES), filler, jnp.float32)

    def home_columns():
        scaled_radii()
        home_rows = [window_ref[field, pl.ds(first_home, homes), :] for field in range(3)]
        turned_ref[...] = turned(jnp.concatenate([types_ref[pl.ds(first_home, homes), :]] + home_rows, axis=0))
        columns = turned_ref[pl.ds(first_atom, chunk), :]
        _, rho, _ = type_fields(columns)
        for home in range(homes):
            columns_ref[0, home] = spread(0.25 * rho, home)
            for index in range(1, 4):
                columns_ref[index, home] = spread(columns, index * homes + home)

    neighbour_lists(partner_ref, first_home, home_id, first_window, homes, slots, window, table_ref)
    move_lists(table_ref, lists_ref, lists_sem, home_columns)
    intrinsic, rho, _ = type_fields(turned_ref[pl.ds(first_atom, chunk), :])

    def pair_distance(home, step, rows):
        dx = columns_ref[1, home, step] - rows[0]
        dy = columns_ref[2, home, step] - rows[1]
        dz = columns_ref[3, home, step] - rows[2]
        return dx * dx + dy * dy + dz * dz

    steps = [pl.ds(start, STEP) for start in range(0, groups, STEP)]

    shift = lists_ref.shape[0].bit_length()
    usual = 8

    def list_items(home, filled):
        turns = (lists_ref[0, home] + (together - 1)) // together

        def put(index, carry):
            items_ref[filled + index] = (home << shift) + index * together
            return carry

        for index in range(usual):
            put(index, 0)
        lax.fori_loop(usual, turns, put, 0)
        return filled + turns

    def sweep(integral, item_count):
        near_ref[...] = jnp.full(near_ref.shape, FAR_AWAY, jnp.float32)
        own_together = min(homes, 2 * together)

        def own_pairs(turn, carry):
            for index in range(own_together):
                home = turn * own_together + index
                rows = [row_of(window_ref, field, first_home + home) for field in range(4)]
                for start, step in zip(range(0, groups, STEP), steps):
                    same = diagonal(STEP, first_atom + start * SUBLANES)
                    squared = jnp.where(same, FAR_AWAY, pair_distance(home, step, rows))
                    term = integral(squared, columns_ref[0, home, step], rows[3])
                    total_ref[home, step] = jnp.where(same, 0.0, term)
                    near_ref[...] = jnp.minimum(near_ref[...], squared)
            return carry

        lax.fori_loop(0, homes // own_together, own_pairs, 0)

        def visit(turn, nearest):
            sums = []
            for index in range(ITEMS):
                item = items_ref[turn * ITEMS + index]
                line, entry = item >> shift, item & ((1 << shift) - 1)
                home = jnp.minimum(line, homes - 1)
                parts_of = [None] * len(steps)
                for other in range(together):
                    partner = lists_ref[SUBLANES + entry + other, line]
                    rows = [row_of(window_ref, field, partner) for field in range(4)]
                    for place, step in enumerate(steps):
                        squared = pair_distance(home, step, rows)
                        nearest = jnp.minimum(nearest, squared)
                        term = integral(squared, columns_ref[0, home, step], rows[3])
                        parts_of[place] = term if other == 0 else parts_of[place] + term
                sums.append((home, parts_of))
            for home, parts_of in sums:
                for part, step in zip(parts_of, steps):
                    total_ref[home, step] += part
            return nearest

        near_ref[...] = lax.fori_loop(0, (item_count + (ITEMS - 1)) // ITEMS, visit, near_ref[...])
        lane = lax.broadcasted_iota(jnp.int32, (chunk, LANES), 1)
        packed = jnp.zeros((chunk, LANES), jnp.float32)
        for home in range(homes):
            packed = jnp.where(lane == home, lane_total(total_ref[home]), packed)
        packed_ref[...] = packed

    item_count = lax.fori_loop(0, homes, list_items, 0)
    for index in range(ITEMS):
        items_ref[item_count + index] = homes << shift
    sweep(descreen, item_count)

    @pl.when(jnp.min(near_ref[...]) < short_range * short_range)
    def _():
        sweep(descreen_any, item_count)

    psi = (0.125 * packed_ref[...]) * rho
    shaped = born_alpha * psi - born_beta * psi * psi + born_gamma * psi * psi * psi
    radii = 1.0 / (1.0 / rho - jnp.tanh(shaped) / intrinsic)

    if chunk < LANES:
        radii = jnp.concatenate([radii, jnp.zeros((LANES - chunk, LANES), jnp.float32)], axis=0)
    turned_ref[...] = radii.T
    lane = lax.broadcasted_iota(jnp.int32, (blocks, LANES), 1)
    sent = turned_ref[pl.ds(0, blocks, stride=parts), :]
    for index in range(1, parts):
        rows = pltpu.roll(turned_ref[pl.ds(index, blocks, stride=parts), :], index * chunk, 1)
        sent = jnp.where(lane >= index * chunk, rows, sent)
    sent_ref[...] = sent


def energy_kernel(
    parts,
    twins,
    order,
    whole,
    table_ref,
    window_ref,
    *refs,
):
    arrived_refs, refs = refs[:twins], refs[twins:]
    own_radii_ref, energy_ref, forces_ref, grad_ref, columns_ref, radii_ref, total_ref, *refs = refs
    gathered_ref, lists_ref, lists_sem = refs
    devices, blocks, atoms = gathered_ref.shape
    window = devices * blocks
    part_rows = window // parts
    chunk = atoms // parts
    groups = atoms // SUBLANES
    first_window, _, own_id, part_here = device_place(blocks, parts, whole)
    first_own, list_lane = own_id - first_window, part_here * blocks
    fields = [(window_ref, field) for field in (WINDOW_X, WINDOW_Y, WINDOW_Z, WINDOW_CHARGE)] + [(radii_ref, 0)]
    odd = lax.rem(lax.axis_index("dev"), 2) == 1

    def unpack():
        for index, place in enumerate(order):
            rows = [ref[index] for ref in arrived_refs]
            if twins == 2:
                rows = [jnp.where(odd, rows[1], rows[0]), jnp.where(odd, rows[0], rows[1])]
            for twin, row in enumerate(rows):
                gathered_ref[place * twins + twin] = row
        lane = lax.broadcasted_iota(jnp.int32, (part_rows, LANES), 1)
        pieces = [
            gathered_ref[pl.ds(part, devices // parts, stride=parts)].reshape(part_rows, atoms)
            for part in range(parts)
        ]
        for place in range(parts):
            whole_rows = pieces[0] if place == 0 else pltpu.roll(pieces[0], (parts - place) * chunk, 1)
            for part in range(1, parts):
                shift = (part - place) % parts
                piece = pieces[part] if shift == 0 else pltpu.roll(pieces[part], shift * chunk, 1)
                whole_rows = jnp.where(lane >= part * chunk, piece, whole_rows)
            radii_ref[0, pl.ds(place, part_rows, stride=parts), :] = whole_rows
        radii_ref[0, window : window + SUBLANES, :] = jnp.ones((SUBLANES, LANES), jnp.float32)

    def own_rows(ref, field):
        return jnp.concatenate([ref[field, pl.ds(first_own + block, 1), :] for block in range(blocks)], axis=0)

    def pair_terms(block, step, rows, same=None):
        x, y, z, charge, radius = rows
        dx = columns_ref[block, step] - x
        dy = columns_ref[blocks + block, step] - y
        dz = columns_ref[2 * blocks + block, step] - z
        squared = dx * dx + dy * dy + dz * dz
        if same is not None:
            squared = jnp.where(same, 1.0, squared)
            charge = jnp.where(same, 0.0, charge)
        spread_sq = columns_ref[3 * blocks + block, step] * radius
        power = squared * pltpu.reciprocal(spread_sq, approx=True)
        quarter = 0.25 * jnp.exp(power)
        blend = spread_sq * quarter
        inv_root = lax.rsqrt(squared - blend)
        potential = charge * inv_root
        cubed = potential * (inv_root * inv_root)
        pull = cubed * (1.0 - quarter)
        return (pull * dx, pull * dy, pull * dz, potential, cubed * blend * (1.0 - power))

    def own_pairs():
        unpack()
        own_radii = own_rows(radii_ref, 0)
        own_radii_ref[...] = own_radii
        own = [own_rows(window_ref, field) for field in (WINDOW_X, WINDOW_Y, WINDOW_Z)]
        columns = turned(jnp.concatenate(own + [-4.0 * own_radii], axis=0))
        for index in range(4 * blocks):
            columns_ref[index] = spread(columns, index)
        for block in range(blocks):
            rows = [row_of(ref, field, first_own + block) for ref, field in fields]
            for start in range(0, groups, ENERGY_STEP):
                step = pl.ds(start, ENERGY_STEP)
                terms = pair_terms(block, step, rows, diagonal(ENERGY_STEP, start * SUBLANES))
                for term, value in enumerate(terms):
                    total_ref[term * blocks + block, step] = value

    move_lists(table_ref, lists_ref, lists_sem, own_pairs)
    for block in range(blocks):

        def visit(count, first, index, carry, block=block):
            partners = []
            for other in range(count):
                partner = lists_ref[SUBLANES + first + index * count + other, list_lane + block]
                partners.append([row_of(ref, field, partner) for ref, field in fields])
            for start in range(0, groups, ENERGY_STEP):
                step = pl.ds(start, ENERGY_STEP)
                sums = [total_ref[term * blocks + block, step] for term in range(5)]
                for rows in partners:
                    sums = [total + value for total, value in zip(sums, pair_terms(block, step, rows))]
                for term, value in enumerate(sums):
                    total_ref[term * blocks + block, step] = value
            return carry

        left = lists_ref[0, list_lane + block]
        first = 0
        for count in (4, 2, 1):
            turns = left // count
            lax.fori_loop(0, turns, functools.partial(visit, count, first), 0)
            first = first + turns * count
            left = left - turns * count
    sums = lane_sums([total_ref[index] for index in range(5 * blocks)], 5 * blocks)
    charges = own_rows(window_ref, WINDOW_CHARGE)
    own_decay = 1.0 / own_radii_ref[...]
    scale = solvent_tau * charges
    for axis in range(3):
        forces_ref[axis] = -scale * sums[axis * blocks : (axis + 1) * blocks]
    own_energy = 0.5 * scale * charges * own_decay
    energy_ref[...] = -0.5 * scale * sums[3 * blocks : 4 * blocks] - own_energy
    grad_ref[...] = (own_energy - 0.5 * scale * sums[4 * blocks : 5 * blocks]) * own_decay


def shards(positions, charges, types, pairs, owner_map):
    _, blocks, atoms = positions.shape
    regions = lax.axis_size("region")
    region_devices = lax.axis_size("dev")
    kept_regions, whole = window_regions(regions)
    devices = kept_regions * region_devices
    window = devices * blocks
    parts = atoms // CHUNK
    while region_devices % parts or 4 * parts * blocks > LANES:
        parts //= 2
    homes = parts * blocks
    chunk = atoms // parts

    vmem = pl.BlockSpec(memory_space=pltpu.VMEM)
    params = pltpu.CompilerParams(vmem_limit_bytes=40 * 1024 * 1024)
    copy_count = lax.axis_size(exchange_axes())
    twins = twin_count(region_devices)
    arrived = sent_to_both_twins(
        pl.pallas_call(
            functools.partial(fields_kernel, blocks, atoms),
            out_shape=jax.ShapeDtypeStruct((copy_count // twins, ROW_COUNT, blocks, atoms), jnp.float32),
            in_specs=[pl.BlockSpec(memory_space=pltpu.HBM)] * 5,
            out_specs=vmem,
            scratch_shapes=[
                pltpu.VMEM(positions.shape, positions.dtype),
                pltpu.VMEM(types.shape, types.dtype),
                pltpu.VMEM(charges.shape, charges.dtype),
                pltpu.SMEM(pairs.shape, pairs.dtype),
                pltpu.SMEM(owner_map.shape, owner_map.dtype),
                pltpu.SemaphoreType.DMA((5,)),
            ],
        )(positions, types, charges, pairs, owner_map)
    )
    arrived = [with_other_regions(part).reshape(devices // twins, ROW_COUNT * blocks, atoms) for part in arrived]
    padded = -(-window // LANES) * LANES
    table = jax.ShapeDtypeStruct((SUBLANES + padded, LANES), jnp.int32)
    fields = jax.ShapeDtypeStruct((WINDOW_COUNT, window + SUBLANES, atoms), jnp.float32)
    sent, lists, window_fields = pl.pallas_call(
        functools.partial(radii_kernel, blocks, pairs.shape[1], twins, whole),
        out_shape=(jax.ShapeDtypeStruct((blocks, atoms), jnp.float32), table, fields),
        in_specs=[vmem] * twins,
        out_specs=(vmem, vmem, vmem),
        scratch_shapes=[
            pltpu.VMEM((4, homes, chunk // SUBLANES, SUBLANES, LANES), jnp.float32),
            pltpu.VMEM((window, atoms), jnp.float32),
            pltpu.VMEM((padded, atoms), jnp.float32),
            pltpu.VMEM((homes, chunk // SUBLANES, SUBLANES, LANES), jnp.float32),
            pltpu.VMEM((LANES, LANES), jnp.float32),
            pltpu.VMEM((chunk, LANES), jnp.float32),
            pltpu.VMEM((STEP, SUBLANES, LANES), jnp.float32),
            pltpu.SMEM(table.shape, jnp.int32),
            pltpu.SMEM((homes * (padded // max(1, LANES // chunk) + 1) + 64,), jnp.int32),
            pltpu.SemaphoreType.DMA(()),
        ],
        compiler_params=params,
    )(*arrived)
    block_out = jax.ShapeDtypeStruct((blocks, atoms), jnp.float32)
    far, near, _ = line_shape(region_devices)
    order = [
        (region * far + place) * near + line
        for region in range(kept_regions)
        for line in range(near)
        for place in range(far)
    ]
    window_radii = [
        with_other_regions(part).reshape(devices // twins, blocks, atoms) for part in gathered_by_lines(sent)
    ]
    own_radii, energy, forces, grad = pl.pallas_call(
        functools.partial(energy_kernel, parts, twins, order, whole),
        out_shape=(block_out, block_out, jax.ShapeDtypeStruct((3, blocks, atoms), jnp.float32), block_out),
        in_specs=[pl.BlockSpec(memory_space=pl.ANY), vmem] + [vmem] * twins,
        out_specs=(vmem, vmem, vmem, vmem),
        scratch_shapes=[
            pltpu.VMEM((4 * blocks, atoms // SUBLANES, SUBLANES, LANES), jnp.float32),
            pltpu.VMEM((1, window + SUBLANES, atoms), jnp.float32),
            pltpu.VMEM((5 * blocks, atoms // SUBLANES, SUBLANES, LANES), jnp.float32),
            pltpu.VMEM((devices, blocks, atoms), jnp.float32),
            pltpu.SMEM(table.shape, jnp.int32),
            pltpu.SemaphoreType.DMA(()),
        ],
        compiler_params=params,
    )(lists, window_fields, *window_radii)
    return own_radii, energy, forces, grad


def solution(mesh):
    placed = (
        P(None, ("region", "dev"), None),
        P(("region", "dev"), None),
        P(("region", "dev"), None),
        P(("region", "dev"), None),
        P(),
    )
    return jax.shard_map(
        shards,
        mesh=mesh,
        in_specs=placed,
        out_specs=(
            P(("region", "dev"), None),
            P(("region", "dev"), None),
            P(None, ("region", "dev"), None),
            P(("region", "dev"), None),
        ),
        check_vma=False,
    )
```

```python
import functools

import jax
import jax.numpy as jnp
from jax import lax
from jax.experimental import pallas as pl
from jax.experimental.pallas import tpu as pltpu
from jax.sharding import PartitionSpec as P

type_radii = (1.2, 1.7, 1.55, 1.52, 1.85, 1.8)
type_scales = (0.85, 0.72, 0.79, 0.85, 0.86, 0.96)
radius_offset = 0.09
born_alpha = 1.0
born_beta = 0.8
born_gamma = 4.85
solvent_tau = 1.0 - 1.0 / 78.5

ROW_X, ROW_Y, ROW_Z, ROW_TYPE, ROW_CHARGE, ROW_PARTNER, ROW_COUNT = range(7)
WINDOW_X, WINDOW_Y, WINDOW_Z, WINDOW_SCALED, WINDOW_CHARGE, WINDOW_COUNT = range(6)
LANES = 128
SUBLANES = 8
STEP = 4
ENERGY_STEP = 2
CHUNK = 32
LIST_ROWS = 32
ITEMS = 4
EMPTY_SLOT = -1.0e6
FAR_AWAY = 1.0e15

scaled_values = [scale * (radius - radius_offset) for radius, scale in zip(type_radii, type_scales)]
short_range = 1.01 * max(
    max(scaled_values) - (min(type_radii) - radius_offset),
    (max(type_radii) - radius_offset) - min(scaled_values),
    0.5,
)


def window_regions(region_count):
    return (region_count, True) if region_count <= 3 else (3, False)


def exchange_axes():
    return ("region", "dev") if window_regions(lax.axis_size("region"))[1] else ("dev",)


def sent_directly(copies):
    return lax.all_to_all(copies, exchange_axes(), split_axis=0, concat_axis=0, tiled=True)


def twin_count(device_count):
    return 2 - device_count % 2


def sent_to_both_twins(copies):
    count = lax.axis_size("dev")
    twins = twin_count(count)
    axes = exchange_axes()
    regions = lax.axis_size(axes) // count
    alike = [list(range(parity, regions * count, twins)) for parity in range(twins)]
    here = lax.all_to_all(copies, axes, split_axis=0, concat_axis=0, axis_index_groups=alike, tiled=True)
    if twins == 1:
        return [here]
    return [here, lax.ppermute(here, "dev", [(i, i ^ 1) for i in range(count)])]


def with_other_regions(here):
    regions = lax.axis_size("region")
    if window_regions(regions)[1]:
        return here
    below = lax.ppermute(here, "region", [(i, i + 1) for i in range(regions - 1)])
    above = lax.ppermute(here, "region", [(i + 1, i) for i in range(regions - 1)])
    return jnp.concatenate([below, here, above], axis=0)


def by_type(types, table):
    value = jnp.full(types.shape, table[0], jnp.float32)
    for index in range(1, len(table)):
        value = jnp.where(types == index, jnp.float32(table[index]), value)
    return value


def type_fields(types):
    intrinsic = by_type(types, type_radii)
    rho = intrinsic - radius_offset
    return intrinsic, rho, by_type(types, type_scales) * rho


def turned(rows):
    count, width = rows.shape
    if count < LANES:
        rows = jnp.concatenate([rows, jnp.zeros((LANES - count, width), rows.dtype)], axis=0)
    return rows.T


def spread(columns, index):
    count = columns.shape[0]
    wide = jnp.broadcast_to(columns[:, index : index + 1], (count, LANES))
    return wide.reshape(count // SUBLANES, SUBLANES, LANES)


def row_of(ref, field, row):
    return ref[field, pl.ds(row, SUBLANES, stride=0), :][None]


def diagonal(groups, first_atom):
    shape = (groups, SUBLANES, LANES)
    row = lax.broadcasted_iota(jnp.int32, shape, 0) * SUBLANES + lax.broadcasted_iota(jnp.int32, shape, 1)
    return row + first_atom == lax.broadcasted_iota(jnp.int32, shape, 2)


def lane_total(array):
    return jnp.sum(array.reshape(-1, LANES), axis=1, keepdims=True)


def lane_sums(arrays, count):
    atoms = arrays[0].shape[0] * SUBLANES
    lane = lax.broadcasted_iota(jnp.int32, (atoms, LANES), 1)
    packed = jnp.zeros((atoms, LANES), jnp.float32)
    for index, array in enumerate(arrays):
        packed = jnp.where(lane == index, lane_total(array), packed)
    return packed.T[:count]


def fields_kernel(blocks, atoms, *refs):
    inputs, copies_ref, here, sems = refs[:5], refs[5], refs[6:11], refs[11]
    moves = [pltpu.make_async_copy(src, dst, sems.at[i]) for i, (src, dst) in enumerate(zip(inputs, here))]
    for move in moves:
        move.start()
    for move in moves:
        move.wait()
    positions_ref, types_ref, charges_ref, pairs_ref, owner_ref = here
    slot = lax.broadcasted_iota(jnp.int32, (1, atoms), 1)
    partners = []
    for block in range(blocks):
        row = jnp.full((1, atoms), EMPTY_SLOT, jnp.float32)
        for index in range(pairs_ref.shape[1]):
            cell = pairs_ref[block, index]
            partner = jnp.where(cell >= 0, owner_ref[jnp.maximum(cell, 0)] + 1, int(EMPTY_SLOT))
            row = jnp.where(slot == index, partner.astype(jnp.float32), row)
        partners.append(row)
    rows = [positions_ref[axis] for axis in range(3)]
    rows += [types_ref[...].astype(jnp.float32), charges_ref[...], jnp.concatenate(partners, axis=0)]
    for copy in range(copies_ref.shape[0]):
        for index, row in enumerate(rows):
            copies_ref[copy, index] = row


def descreen(squared, rho, scaled):
    inv_dist = lax.rsqrt(squared)
    share = scaled * inv_dist
    inner = 0.25 - share
    high = 0.25 + share
    low = jnp.maximum(rho * inv_dist, inner)
    inv_low = pltpu.reciprocal(low, approx=True)
    ratio = low * pltpu.reciprocal(high, approx=True)
    curve = (1.0 - ratio) + inner * (ratio - high * inv_low)
    return (inv_low * curve + 2.0 * jnp.log(ratio)) * inv_dist


def descreen_any(squared, rho, scaled):
    rho, scaled = 4.0 * rho, 4.0 * scaled
    inv_dist = lax.rsqrt(squared)
    distance = squared * inv_dist
    high = distance + scaled
    gap = distance - scaled
    low = jnp.maximum(rho, jnp.abs(gap))
    inv_low = 1.0 / low
    inv_high = 1.0 / high
    quarter = 0.25 * inv_dist
    curve = (squared - scaled * scaled) * quarter
    body = (0.5 * (inv_low - inv_high)) * (1.0 - (inv_low + inv_high) * curve)
    body = body + jnp.log(low * inv_high) * quarter
    body = body + jnp.where(rho < -gap, 1.0 / rho - inv_low, 0.0)
    return jnp.where(high > rho, 8.0 * body, 0.0)


def neighbour_lists(partner_ref, first_home, home_id, first_window, homes, slots, filler, table_ref):
    window = partner_ref.shape[0]
    tiles = [slice(start, start + LANES) for start in range(0, window, LANES)]
    depth = -(-slots // SUBLANES) * SUBLANES
    ids = jnp.concatenate([partner_ref[tile, :].T[:depth] for tile in tiles], axis=1)
    lists = turned(partner_ref[pl.ds(first_home, homes), :])[:depth]
    lane = lax.broadcasted_iota(jnp.int32, (depth, window), 1)
    lane_id = (lane + (first_window + 1)).astype(jnp.float32)
    rows = []
    for home in range(homes):
        own = (home_id + home + 1).astype(jnp.float32)
        linked = (ids == own) | (lane_id == lists[:, home : home + 1])
        rows.append(jnp.max(jnp.where(linked, 1.0, 0.0), axis=0, keepdims=True))
    linked = jnp.concatenate(rows, axis=0)
    before = lax.broadcasted_iota(jnp.int32, (window, window), 0)
    after = lax.broadcasted_iota(jnp.int32, (window, window), 1)
    ramp = jnp.where(before <= after, 1.0, 0.0).astype(jnp.bfloat16)
    rank = jnp.dot(linked.astype(jnp.bfloat16), ramp, preferred_element_type=jnp.float32)
    place = jnp.where(linked > 0.0, rank, 0.0)
    total = jnp.sum(linked, axis=1, keepdims=True)
    name = lax.broadcasted_iota(jnp.int32, (LIST_ROWS, window), 1).astype(jnp.float32)
    spot = lax.broadcasted_iota(jnp.int32, (LIST_ROWS, window), 0).astype(jnp.float32)
    own_lane = lax.broadcasted_iota(jnp.int32, (LIST_ROWS, LANES), 1)

    def some_rows(start):
        first = jnp.asarray(start + 1).astype(jnp.float32)
        packed = jnp.zeros((LIST_ROWS, LANES), jnp.float32)
        for home in range(homes):
            hit = place[home : home + 1] == spot + first
            found = jnp.sum(jnp.where(hit, name - float(filler), 0.0), axis=1, keepdims=True)
            packed = jnp.where(own_lane == home, found, packed)
        rows = pl.ds(pl.multiple_of(SUBLANES + start, SUBLANES), LIST_ROWS)
        table_ref[rows, :] = packed.astype(jnp.int32) + filler

    counts = jnp.zeros((SUBLANES, LANES), jnp.float32)
    lane = lax.broadcasted_iota(jnp.int32, (SUBLANES, LANES), 1)
    for home in range(homes):
        counts = jnp.where(lane == home, total[home : home + 1], counts)
    longest = jnp.max(total)
    table_ref[0:SUBLANES, :] = jnp.where(lane == LANES - 1, longest, counts).astype(jnp.int32)
    some_rows(0)

    def more_rows(turn, carry):
        some_rows(turn * LIST_ROWS)
        return carry

    lax.fori_loop(1, (longest.astype(jnp.int32) + (LIST_ROWS - 1)) // LIST_ROWS, more_rows, 0)


def move_lists(table_ref, lists_ref, sem, when_wanted):
    usual = pl.ds(0, SUBLANES + LIST_ROWS)
    move = pltpu.make_async_copy(table_ref.at[usual], lists_ref.at[usual], sem)
    move.start()
    when_wanted()
    move.wait()
    rows = lists_ref.shape[0] - (SUBLANES + LIST_ROWS)
    if rows > 0:

        @pl.when(lists_ref[0, LANES - 1] > LIST_ROWS)
        def _():
            rest = pl.ds(SUBLANES + LIST_ROWS, rows)
            more = pltpu.make_async_copy(table_ref.at[rest], lists_ref.at[rest], sem)
            more.start()
            more.wait()


def device_place(blocks, parts, whole):
    region, device = lax.axis_index("region"), lax.axis_index("dev")
    region_blocks = lax.axis_size("dev") * blocks
    first_window = 0 if whole else (region - 1) * region_blocks
    first_own = region * region_blocks + device * blocks
    part = lax.rem(device, parts)
    return first_window, first_own - part * blocks, first_own, part


def radii_kernel(
    blocks,
    slots,
    twins,
    whole,
    *refs,
):
    arrived_refs, refs = refs[:twins], refs[twins:]
    copies_ref, table_ref, window_ref, columns_ref, types_ref, partner_ref, total_ref, *refs = refs
    turned_ref, packed_ref, near_ref, lists_ref, items_ref, lists_sem = refs
    _, homes, groups, _, _ = columns_ref.shape
    chunk = groups * SUBLANES
    window = types_ref.shape[0]
    parts = homes // blocks
    together = max(1, LANES // chunk)
    first_window, home_id, _, part = device_place(blocks, parts, whole)
    first_home = pl.multiple_of(home_id - first_window, homes)
    first_atom = pl.multiple_of(part * chunk, chunk)

    tables = [window_ref.at[WINDOW_X], window_ref.at[WINDOW_Y], window_ref.at[WINDOW_Z]]
    tables += [types_ref, window_ref.at[WINDOW_CHARGE], partner_ref]
    odd = lax.rem(lax.axis_index("dev"), 2) == 1
    for place in range(arrived_refs[0].shape[0]):
        for field, table in enumerate(tables):
            rows = [ref[place, field * blocks : (field + 1) * blocks, :] for ref in arrived_refs]
            if twins == 2:
                rows = [jnp.where(odd, rows[1], rows[0]), jnp.where(odd, rows[0], rows[1])]
            first = place * twins * blocks
            table[first : first + twins * blocks, :] = jnp.concatenate(rows, axis=0)
    if partner_ref.shape[0] > window:
        spare = (partner_ref.shape[0] - window, LANES)
        partner_ref[window:, :] = jnp.full(spare, EMPTY_SLOT, jnp.float32)
    def scaled_radii():
        _, _, scaled = type_fields(types_ref[...])
        window_ref[WINDOW_SCALED, 0:window, :] = 0.25 * scaled
        for field in range(WINDOW_COUNT):
            filler = FAR_AWAY if field == WINDOW_X else 0.0
            window_ref[field, window : window + SUBLANES, :] = jnp.full((SUBLANES, LANES), filler, jnp.float32)

    def home_columns():
        scaled_radii()
        home_rows = [window_ref[field, pl.ds(first_home, homes), :] for field in range(3)]
        turned_ref[...] = turned(jnp.concatenate([types_ref[pl.ds(first_home, homes), :]] + home_rows, axis=0))
        columns = turned_ref[pl.ds(first_atom, chunk), :]
        _, rho, _ = type_fields(columns)
        for home in range(homes):
            columns_ref[0, home] = spread(0.25 * rho, home)
            for index in range(1, 4):
                columns_ref[index, home] = spread(columns, index * homes + home)

    neighbour_lists(partner_ref, first_home, home_id, first_window, homes, slots, window, table_ref)
    move_lists(table_ref, lists_ref, lists_sem, home_columns)
    intrinsic, rho, _ = type_fields(turned_ref[pl.ds(first_atom, chunk), :])

    def pair_distance(home, step, rows):
        dx = columns_ref[1, home, step] - rows[0]
        dy = columns_ref[2, home, step] - rows[1]
        dz = columns_ref[3, home, step] - rows[2]
        return dx * dx + dy * dy + dz * dz

    steps = [pl.ds(start, STEP) for start in range(0, groups, STEP)]

    shift = lists_ref.shape[0].bit_length()
    usual = 8

    def list_items(home, filled):
        turns = (lists_ref[0, home] + (together - 1)) // together

        def put(index, carry):
            items_ref[filled + index] = (home << shift) + index * together
            return carry

        for index in range(usual):
            put(index, 0)
        lax.fori_loop(usual, turns, put, 0)
        return filled + turns

    def sweep(integral, item_count):
        near_ref[...] = jnp.full(near_ref.shape, FAR_AWAY, jnp.float32)
        own_together = min(homes, 2 * together)

        def own_pairs(turn, carry):
            for index in range(own_together):
                home = turn * own_together + index
                rows = [row_of(window_ref, field, first_home + home) for field in range(4)]
                for start, step in zip(range(0, groups, STEP), steps):
                    same = diagonal(STEP, first_atom + start * SUBLANES)
                    squared = jnp.where(same, FAR_AWAY, pair_distance(home, step, rows))
                    term = integral(squared, columns_ref[0, home, step], rows[3])
                    total_ref[home, step] = jnp.where(same, 0.0, term)
                    near_ref[...] = jnp.minimum(near_ref[...], squared)
            return carry

        lax.fori_loop(0, homes // own_together, own_pairs, 0)

        def visit(turn, nearest):
            sums = []
            for index in range(ITEMS):
                item = items_ref[turn * ITEMS + index]
                line, entry = item >> shift, item & ((1 << shift) - 1)
                home = jnp.minimum(line, homes - 1)
                parts_of = [None] * len(steps)
                for other in range(together):
                    partner = lists_ref[SUBLANES + entry + other, line]
                    rows = [row_of(window_ref, field, partner) for field in range(4)]
                    for place, step in enumerate(steps):
                        squared = pair_distance(home, step, rows)
                        nearest = jnp.minimum(nearest, squared)
                        term = integral(squared, columns_ref[0, home, step], rows[3])
                        parts_of[place] = term if other == 0 else parts_of[place] + term
                sums.append((home, parts_of))
            for home, parts_of in sums:
                for part, step in zip(parts_of, steps):
                    total_ref[home, step] += part
            return nearest

        near_ref[...] = lax.fori_loop(0, (item_count + (ITEMS - 1)) // ITEMS, visit, near_ref[...])
        lane = lax.broadcasted_iota(jnp.int32, (chunk, LANES), 1)
        packed = jnp.zeros((chunk, LANES), jnp.float32)
        for home in range(homes):
            packed = jnp.where(lane == home, lane_total(total_ref[home]), packed)
        packed_ref[...] = packed

    item_count = lax.fori_loop(0, homes, list_items, 0)
    for index in range(ITEMS):
        items_ref[item_count + index] = homes << shift
    sweep(descreen, item_count)

    @pl.when(jnp.min(near_ref[...]) < short_range * short_range)
    def _():
        sweep(descreen_any, item_count)

    psi = (0.125 * packed_ref[...]) * rho
    shaped = born_alpha * psi - born_beta * psi * psi + born_gamma * psi * psi * psi
    radii = 1.0 / (1.0 / rho - jnp.tanh(shaped) / intrinsic)

    if chunk < LANES:
        radii = jnp.concatenate([radii, jnp.zeros((LANES - chunk, LANES), jnp.float32)], axis=0)
    turned_ref[...] = radii.T
    lane = lax.broadcasted_iota(jnp.int32, (blocks, LANES), 1)
    sent = turned_ref[pl.ds(0, blocks, stride=parts), :]
    for index in range(1, parts):
        rows = pltpu.roll(turned_ref[pl.ds(index, blocks, stride=parts), :], index * chunk, 1)
        sent = jnp.where(lane >= index * chunk, rows, sent)
    for copy in range(copies_ref.shape[0]):
        copies_ref[copy] = sent


def energy_kernel(
    parts,
    whole,
    table_ref,
    window_ref,
    gathered_ref,
    own_radii_ref,
    energy_ref,
    forces_ref,
    grad_ref,
    columns_ref,
    radii_ref,
    total_ref,
    lists_ref,
    lists_sem,
):
    devices, blocks, atoms = gathered_ref.shape
    window = devices * blocks
    part_rows = window // parts
    chunk = atoms // parts
    groups = atoms // SUBLANES
    first_window, _, own_id, part_here = device_place(blocks, parts, whole)
    first_own, list_lane = own_id - first_window, part_here * blocks
    fields = [(window_ref, field) for field in (WINDOW_X, WINDOW_Y, WINDOW_Z, WINDOW_CHARGE)] + [(radii_ref, 0)]

    def unpack():
        lane = lax.broadcasted_iota(jnp.int32, (part_rows, LANES), 1)
        pieces = [
            gathered_ref[pl.ds(part, devices // parts, stride=parts)].reshape(part_rows, atoms)
            for part in range(parts)
        ]
        for place in range(parts):
            whole_rows = pieces[0] if place == 0 else pltpu.roll(pieces[0], (parts - place) * chunk, 1)
            for part in range(1, parts):
                shift = (part - place) % parts
                piece = pieces[part] if shift == 0 else pltpu.roll(pieces[part], shift * chunk, 1)
                whole_rows = jnp.where(lane >= part * chunk, piece, whole_rows)
            radii_ref[0, pl.ds(place, part_rows, stride=parts), :] = whole_rows
        radii_ref[0, window : window + SUBLANES, :] = jnp.ones((SUBLANES, LANES), jnp.float32)

    def own_rows(ref, field):
        return jnp.concatenate([ref[field, pl.ds(first_own + block, 1), :] for block in range(blocks)], axis=0)

    def pair_terms(block, step, rows, same=None):
        x, y, z, charge, radius = rows
        dx = columns_ref[block, step] - x
        dy = columns_ref[blocks + block, step] - y
        dz = columns_ref[2 * blocks + block, step] - z
        squared = dx * dx + dy * dy + dz * dz
        if same is not None:
            squared = jnp.where(same, 1.0, squared)
            charge = jnp.where(same, 0.0, charge)
        spread_sq = columns_ref[3 * blocks + block, step] * radius
        power = squared * pltpu.reciprocal(spread_sq, approx=True)
        quarter = 0.25 * jnp.exp(power)
        blend = spread_sq * quarter
        inv_root = lax.rsqrt(squared - blend)
        potential = charge * inv_root
        cubed = potential * (inv_root * inv_root)
        pull = cubed * (1.0 - quarter)
        return (pull * dx, pull * dy, pull * dz, potential, cubed * blend * (1.0 - power))

    def own_pairs():
        unpack()
        own_radii = own_rows(radii_ref, 0)
        own_radii_ref[...] = own_radii
        own = [own_rows(window_ref, field) for field in (WINDOW_X, WINDOW_Y, WINDOW_Z)]
        columns = turned(jnp.concatenate(own + [-4.0 * own_radii], axis=0))
        for index in range(4 * blocks):
            columns_ref[index] = spread(columns, index)

        def own_block(block, carry):
            rows = [row_of(ref, field, first_own + block) for ref, field in fields]
            for start in range(0, groups, ENERGY_STEP):
                step = pl.ds(start, ENERGY_STEP)
                terms = pair_terms(block, step, rows, diagonal(ENERGY_STEP, start * SUBLANES))
                for term, value in enumerate(terms):
                    total_ref[term * blocks + block, step] = value
            return carry

        lax.fori_loop(0, blocks, own_block, 0)

    move_lists(table_ref, lists_ref, lists_sem, own_pairs)

    def one_block(block, carry):
        def visit(count, first, index, carry):
            partners = []
            for other in range(count):
                partner = lists_ref[SUBLANES + first + index * count + other, list_lane + block]
                partners.append([row_of(ref, field, partner) for ref, field in fields])
            for start in range(0, groups, ENERGY_STEP):
                step = pl.ds(start, ENERGY_STEP)
                sums = [total_ref[term * blocks + block, step] for term in range(5)]
                for rows in partners:
                    sums = [total + value for total, value in zip(sums, pair_terms(block, step, rows))]
                for term, value in enumerate(sums):
                    total_ref[term * blocks + block, step] = value
            return carry

        left = lists_ref[0, list_lane + block]
        first = 0
        for count in (4, 2, 1):
            turns = left // count
            lax.fori_loop(0, turns, functools.partial(visit, count, first), 0)
            first = first + turns * count
            left = left - turns * count
        return carry

    lax.fori_loop(0, blocks, one_block, 0)
    sums = lane_sums([total_ref[index] for index in range(5 * blocks)], 5 * blocks)
    charges = own_rows(window_ref, WINDOW_CHARGE)
    own_decay = 1.0 / own_radii_ref[...]
    scale = solvent_tau * charges
    for axis in range(3):
        forces_ref[axis] = -scale * sums[axis * blocks : (axis + 1) * blocks]
    own_energy = 0.5 * scale * charges * own_decay
    energy_ref[...] = -0.5 * scale * sums[3 * blocks : 4 * blocks] - own_energy
    grad_ref[...] = (own_energy - 0.5 * scale * sums[4 * blocks : 5 * blocks]) * own_decay


def shards(positions, charges, types, pairs, owner_map):
    _, blocks, atoms = positions.shape
    regions = lax.axis_size("region")
    region_devices = lax.axis_size("dev")
    kept_regions, whole = window_regions(regions)
    devices = kept_regions * region_devices
    window = devices * blocks
    parts = atoms // CHUNK
    while region_devices % parts or 4 * parts * blocks > LANES:
        parts //= 2
    homes = parts * blocks
    chunk = atoms // parts

    vmem = pl.BlockSpec(memory_space=pltpu.VMEM)
    params = pltpu.CompilerParams(vmem_limit_bytes=40 * 1024 * 1024)
    copy_count = lax.axis_size(exchange_axes())
    twins = twin_count(region_devices)
    arrived = sent_to_both_twins(
        pl.pallas_call(
            functools.partial(fields_kernel, blocks, atoms),
            out_shape=jax.ShapeDtypeStruct((copy_count // twins, ROW_COUNT, blocks, atoms), jnp.float32),
            in_specs=[pl.BlockSpec(memory_space=pltpu.HBM)] * 5,
            out_specs=vmem,
            scratch_shapes=[
                pltpu.VMEM(positions.shape, positions.dtype),
                pltpu.VMEM(types.shape, types.dtype),
                pltpu.VMEM(charges.shape, charges.dtype),
                pltpu.SMEM(pairs.shape, pairs.dtype),
                pltpu.SMEM(owner_map.shape, owner_map.dtype),
                pltpu.SemaphoreType.DMA((5,)),
            ],
        )(positions, types, charges, pairs, owner_map)
    )
    arrived = [with_other_regions(part).reshape(devices // twins, ROW_COUNT * blocks, atoms) for part in arrived]
    padded = -(-window // LANES) * LANES
    table = jax.ShapeDtypeStruct((SUBLANES + padded, LANES), jnp.int32)
    fields = jax.ShapeDtypeStruct((WINDOW_COUNT, window + SUBLANES, atoms), jnp.float32)
    copies, lists, window_fields = pl.pallas_call(
        functools.partial(radii_kernel, blocks, pairs.shape[1], twins, whole),
        out_shape=(jax.ShapeDtypeStruct((copy_count, blocks, atoms), jnp.float32), table, fields),
        in_specs=[vmem] * twins,
        out_specs=(vmem, vmem, vmem),
        scratch_shapes=[
            pltpu.VMEM((4, homes, chunk // SUBLANES, SUBLANES, LANES), jnp.float32),
            pltpu.VMEM((window, atoms), jnp.float32),
            pltpu.VMEM((padded, atoms), jnp.float32),
            pltpu.VMEM((homes, chunk // SUBLANES, SUBLANES, LANES), jnp.float32),
            pltpu.VMEM((LANES, LANES), jnp.float32),
            pltpu.VMEM((chunk, LANES), jnp.float32),
            pltpu.VMEM((STEP, SUBLANES, LANES), jnp.float32),
            pltpu.SMEM(table.shape, jnp.int32),
            pltpu.SMEM((homes * (padded // max(1, LANES // chunk) + 1) + 64,), jnp.int32),
            pltpu.SemaphoreType.DMA(()),
        ],
        compiler_params=params,
    )(*arrived)
    block_out = jax.ShapeDtypeStruct((blocks, atoms), jnp.float32)
    window_radii = with_other_regions(sent_directly(copies))
    own_radii, energy, forces, grad = pl.pallas_call(
        functools.partial(energy_kernel, parts, whole),
        out_shape=(block_out, block_out, jax.ShapeDtypeStruct((3, blocks, atoms), jnp.float32), block_out),
        in_specs=[pl.BlockSpec(memory_space=pl.ANY), vmem, vmem],
        out_specs=(vmem, vmem, vmem, vmem),
        scratch_shapes=[
            pltpu.VMEM((4 * blocks, atoms // SUBLANES, SUBLANES, LANES), jnp.float32),
            pltpu.VMEM((1, window + SUBLANES, atoms), jnp.float32),
            pltpu.VMEM((5 * blocks, atoms // SUBLANES, SUBLANES, LANES), jnp.float32),
            pltpu.SMEM(table.shape, jnp.int32),
            pltpu.SemaphoreType.DMA(()),
        ],
        compiler_params=params,
    )(lists, window_fields, window_radii)
    return own_radii, energy, forces, grad


def solution(mesh):
    placed = (
        P(None, ("region", "dev"), None),
        P(("region", "dev"), None),
        P(("region", "dev"), None),
        P(("region", "dev"), None),
        P(),
    )
    return jax.shard_map(
        shards,
        mesh=mesh,
        in_specs=placed,
        out_specs=(
            P(("region", "dev"), None),
            P(("region", "dev"), None),
            P(None, ("region", "dev"), None),
            P(("region", "dev"), None),
        ),
        check_vma=False,
    )
```

```python
import functools

import jax
import jax.numpy as jnp
from jax import lax
from jax.experimental import pallas as pl
from jax.experimental.pallas import tpu as pltpu
from jax.sharding import PartitionSpec as P

type_radii = (1.2, 1.7, 1.55, 1.52, 1.85, 1.8)
type_scales = (0.85, 0.72, 0.79, 0.85, 0.86, 0.96)
radius_offset = 0.09
born_alpha = 1.0
born_beta = 0.8
born_gamma = 4.85
solvent_tau = 1.0 - 1.0 / 78.5

ROW_X, ROW_Y, ROW_Z, ROW_TYPE, ROW_CHARGE, ROW_PARTNER, ROW_COUNT = range(7)
WINDOW_X, WINDOW_Y, WINDOW_Z, WINDOW_SCALED, WINDOW_CHARGE, WINDOW_COUNT = range(6)
LANES = 128
SUBLANES = 8
STEP = 4
ENERGY_STEP = 2
CHUNK = 32
LIST_ROWS = 32
ITEMS = 4
EMPTY_SLOT = -1.0e6
FAR_AWAY = 1.0e15

scaled_values = [scale * (radius - radius_offset) for radius, scale in zip(type_radii, type_scales)]
short_range = 1.01 * max(
    max(scaled_values) - (min(type_radii) - radius_offset),
    (max(type_radii) - radius_offset) - min(scaled_values),
    0.5,
)


def window_regions(region_count):
    return (region_count, True) if region_count <= 3 else (3, False)


def exchange_axes():
    return ("region", "dev") if window_regions(lax.axis_size("region"))[1] else ("dev",)


def sent_directly(copies):
    return lax.all_to_all(copies, exchange_axes(), split_axis=0, concat_axis=0, tiled=True)


def twin_count(device_count):
    return 2 - device_count % 2


def sent_to_both_twins(copies):
    count = lax.axis_size("dev")
    twins = twin_count(count)
    axes = exchange_axes()
    regions = lax.axis_size(axes) // count
    alike = [list(range(parity, regions * count, twins)) for parity in range(twins)]
    here = lax.all_to_all(copies, axes, split_axis=0, concat_axis=0, axis_index_groups=alike, tiled=True)
    if twins == 1:
        return [here]
    return [here, lax.ppermute(here, "dev", [(i, i ^ 1) for i in range(count)])]


def with_other_regions(here):
    regions = lax.axis_size("region")
    if window_regions(regions)[1]:
        return here
    below = lax.ppermute(here, "region", [(i, i + 1) for i in range(regions - 1)])
    above = lax.ppermute(here, "region", [(i + 1, i) for i in range(regions - 1)])
    return jnp.concatenate([below, here, above], axis=0)


def by_type(types, table):
    value = jnp.full(types.shape, table[0], jnp.float32)
    for index in range(1, len(table)):
        value = jnp.where(types == index, jnp.float32(table[index]), value)
    return value


def type_fields(types):
    intrinsic = by_type(types, type_radii)
    rho = intrinsic - radius_offset
    return intrinsic, rho, by_type(types, type_scales) * rho


def turned(rows):
    count, width = rows.shape
    if count < LANES:
        rows = jnp.concatenate([rows, jnp.zeros((LANES - count, width), rows.dtype)], axis=0)
    return rows.T


def spread(columns, index):
    count = columns.shape[0]
    wide = jnp.broadcast_to(columns[:, index : index + 1], (count, LANES))
    return wide.reshape(count // SUBLANES, SUBLANES, LANES)


def row_of(ref, field, row):
    return ref[field, pl.ds(row, SUBLANES, stride=0), :][None]


def diagonal(groups, first_atom):
    shape = (groups, SUBLANES, LANES)
    row = lax.broadcasted_iota(jnp.int32, shape, 0) * SUBLANES + lax.broadcasted_iota(jnp.int32, shape, 1)
    return row + first_atom == lax.broadcasted_iota(jnp.int32, shape, 2)


def lane_total(array):
    return jnp.sum(array.reshape(-1, LANES), axis=1, keepdims=True)


def lane_sums(arrays, count):
    atoms = arrays[0].shape[0] * SUBLANES
    lane = lax.broadcasted_iota(jnp.int32, (atoms, LANES), 1)
    packed = jnp.zeros((atoms, LANES), jnp.float32)
    for index, array in enumerate(arrays):
        packed = jnp.where(lane == index, lane_total(array), packed)
    return packed.T[:count]


def fields_kernel(blocks, atoms, *refs):
    inputs, copies_ref, here, payload_ref, sems, out_sems = refs[:5], refs[5], refs[6:11], refs[11], refs[12], refs[13]
    moves = [pltpu.make_async_copy(src, dst, sems.at[i]) for i, (src, dst) in enumerate(zip(inputs, here))]
    for move in moves:
        move.start()
    for move in moves:
        move.wait()
    positions_ref, types_ref, charges_ref, pairs_ref, owner_ref = here
    payload_ref[ROW_X : ROW_Z + 1] = positions_ref[...]
    payload_ref[ROW_TYPE] = types_ref[...].astype(jnp.float32)
    payload_ref[ROW_CHARGE] = charges_ref[...]

    def send(first, count, turn):
        rows = pl.ds(first, count)
        sent = []
        for copy in range(copies_ref.shape[0]):
            move = pltpu.make_async_copy(payload_ref.at[rows], copies_ref.at[copy, rows], out_sems.at[turn, copy])
            move.start()
            sent.append(move)
        return sent

    moves = send(0, ROW_PARTNER, 0)
    slot = lax.broadcasted_iota(jnp.int32, (1, atoms), 1)
    partners = []
    for block in range(blocks):
        row = jnp.full((1, atoms), EMPTY_SLOT, jnp.float32)
        for index in range(pairs_ref.shape[1]):
            cell = pairs_ref[block, index]
            partner = jnp.where(cell >= 0, owner_ref[jnp.maximum(cell, 0)] + 1, int(EMPTY_SLOT))
            row = jnp.where(slot == index, partner.astype(jnp.float32), row)
        partners.append(row)
    payload_ref[ROW_PARTNER] = jnp.concatenate(partners, axis=0)
    for move in moves + send(ROW_PARTNER, 1, 1):
        move.wait()


def descreen(squared, rho, scaled):
    inv_dist = lax.rsqrt(squared)
    share = scaled * inv_dist
    inner = 0.25 - share
    high = 0.25 + share
    low = jnp.maximum(rho * inv_dist, inner)
    inv_low = pltpu.reciprocal(low, approx=True)
    ratio = low * pltpu.reciprocal(high, approx=True)
    curve = (1.0 - ratio) + inner * (ratio - high * inv_low)
    return (inv_low * curve + 2.0 * jnp.log(ratio)) * inv_dist


def descreen_any(squared, rho, scaled):
    rho, scaled = 4.0 * rho, 4.0 * scaled
    inv_dist = lax.rsqrt(squared)
    distance = squared * inv_dist
    high = distance + scaled
    gap = distance - scaled
    low = jnp.maximum(rho, jnp.abs(gap))
    inv_low = 1.0 / low
    inv_high = 1.0 / high
    quarter = 0.25 * inv_dist
    curve = (squared - scaled * scaled) * quarter
    body = (0.5 * (inv_low - inv_high)) * (1.0 - (inv_low + inv_high) * curve)
    body = body + jnp.log(low * inv_high) * quarter
    body = body + jnp.where(rho < -gap, 1.0 / rho - inv_low, 0.0)
    return jnp.where(high > rho, 8.0 * body, 0.0)


def neighbour_lists(partner_ref, first_home, home_id, first_window, homes, slots, filler, table_ref):
    window = partner_ref.shape[0]
    tiles = [slice(start, start + LANES) for start in range(0, window, LANES)]
    depth = -(-slots // SUBLANES) * SUBLANES
    ids = jnp.concatenate([partner_ref[tile, :].T[:depth] for tile in tiles], axis=1)
    lists = turned(partner_ref[pl.ds(first_home, homes), :])[:depth]
    lane = lax.broadcasted_iota(jnp.int32, (depth, window), 1)
    lane_id = (lane + (first_window + 1)).astype(jnp.float32)
    rows = []
    for home in range(homes):
        own = (home_id + home + 1).astype(jnp.float32)
        linked = (ids == own) | (lane_id == lists[:, home : home + 1])
        rows.append(jnp.max(jnp.where(linked, 1.0, 0.0), axis=0, keepdims=True))
    linked = jnp.concatenate(rows, axis=0)
    before = lax.broadcasted_iota(jnp.int32, (window, window), 0)
    after = lax.broadcasted_iota(jnp.int32, (window, window), 1)
    ramp = jnp.where(before <= after, 1.0, 0.0).astype(jnp.bfloat16)
    rank = jnp.dot(linked.astype(jnp.bfloat16), ramp, preferred_element_type=jnp.float32)
    place = jnp.where(linked > 0.0, rank, 0.0)
    total = jnp.sum(linked, axis=1, keepdims=True)
    name = lax.broadcasted_iota(jnp.int32, (LIST_ROWS, window), 1).astype(jnp.float32)
    spot = lax.broadcasted_iota(jnp.int32, (LIST_ROWS, window), 0).astype(jnp.float32)
    own_lane = lax.broadcasted_iota(jnp.int32, (LIST_ROWS, LANES), 1)

    def some_rows(start):
        first = jnp.asarray(start + 1).astype(jnp.float32)
        packed = jnp.zeros((LIST_ROWS, LANES), jnp.float32)
        for home in range(homes):
            hit = place[home : home + 1] == spot + first
            found = jnp.sum(jnp.where(hit, name - float(filler), 0.0), axis=1, keepdims=True)
            packed = jnp.where(own_lane == home, found, packed)
        rows = pl.ds(pl.multiple_of(SUBLANES + start, SUBLANES), LIST_ROWS)
        table_ref[rows, :] = packed.astype(jnp.int32) + filler

    counts = jnp.zeros((SUBLANES, LANES), jnp.float32)
    lane = lax.broadcasted_iota(jnp.int32, (SUBLANES, LANES), 1)
    for home in range(homes):
        counts = jnp.where(lane == home, total[home : home + 1], counts)
    longest = jnp.max(total)
    table_ref[0:SUBLANES, :] = jnp.where(lane == LANES - 1, longest, counts).astype(jnp.int32)
    some_rows(0)

    def more_rows(turn, carry):
        some_rows(turn * LIST_ROWS)
        return carry

    lax.fori_loop(1, (longest.astype(jnp.int32) + (LIST_ROWS - 1)) // LIST_ROWS, more_rows, 0)


def move_lists(table_ref, lists_ref, sem, when_wanted):
    usual = pl.ds(0, SUBLANES + LIST_ROWS)
    move = pltpu.make_async_copy(table_ref.at[usual], lists_ref.at[usual], sem)
    move.start()
    when_wanted()
    move.wait()
    rows = lists_ref.shape[0] - (SUBLANES + LIST_ROWS)
    if rows > 0:

        @pl.when(lists_ref[0, LANES - 1] > LIST_ROWS)
        def _():
            rest = pl.ds(SUBLANES + LIST_ROWS, rows)
            more = pltpu.make_async_copy(table_ref.at[rest], lists_ref.at[rest], sem)
            more.start()
            more.wait()


def device_place(blocks, parts, whole):
    region, device = lax.axis_index("region"), lax.axis_index("dev")
    region_blocks = lax.axis_size("dev") * blocks
    first_window = 0 if whole else (region - 1) * region_blocks
    first_own = region * region_blocks + device * blocks
    part = lax.rem(device, parts)
    return first_window, first_own - part * blocks, first_own, part


def radii_kernel(
    blocks,
    slots,
    twins,
    whole,
    *refs,
):
    arrived_refs, refs = refs[:twins], refs[twins:]
    copies_ref, table_ref, window_ref, columns_ref, types_ref, partner_ref, total_ref, *refs = refs
    turned_ref, packed_ref, near_ref, lists_ref, items_ref, lists_sem = refs
    _, homes, groups, _, _ = columns_ref.shape
    chunk = groups * SUBLANES
    window = types_ref.shape[0]
    parts = homes // blocks
    together = max(1, LANES // chunk)
    first_window, home_id, _, part = device_place(blocks, parts, whole)
    first_home = pl.multiple_of(home_id - first_window, homes)
    first_atom = pl.multiple_of(part * chunk, chunk)

    tables = [window_ref.at[WINDOW_X], window_ref.at[WINDOW_Y], window_ref.at[WINDOW_Z]]
    tables += [types_ref, window_ref.at[WINDOW_CHARGE], partner_ref]
    odd = lax.rem(lax.axis_index("dev"), 2) == 1
    for place in range(arrived_refs[0].shape[0]):
        for field, table in enumerate(tables):
            rows = [ref[place, field * blocks : (field + 1) * blocks, :] for ref in arrived_refs]
            if twins == 2:
                rows = [jnp.where(odd, rows[1], rows[0]), jnp.where(odd, rows[0], rows[1])]
            first = place * twins * blocks
            table[first : first + twins * blocks, :] = jnp.concatenate(rows, axis=0)
    if partner_ref.shape[0] > window:
        spare = (partner_ref.shape[0] - window, LANES)
        partner_ref[window:, :] = jnp.full(spare, EMPTY_SLOT, jnp.float32)
    def scaled_radii():
        _, _, scaled = type_fields(types_ref[...])
        window_ref[WINDOW_SCALED, 0:window, :] = 0.25 * scaled
        for field in range(WINDOW_COUNT):
            filler = FAR_AWAY if field == WINDOW_X else 0.0
            window_ref[field, window : window + SUBLANES, :] = jnp.full((SUBLANES, LANES), filler, jnp.float32)

    def home_columns():
        scaled_radii()
        home_rows = [window_ref[field, pl.ds(first_home, homes), :] for field in range(3)]
        turned_ref[...] = turned(jnp.concatenate([types_ref[pl.ds(first_home, homes), :]] + home_rows, axis=0))
        columns = turned_ref[pl.ds(first_atom, chunk), :]
        _, rho, _ = type_fields(columns)
        for home in range(homes):
            columns_ref[0, home] = spread(0.25 * rho, home)
            for index in range(1, 4):
                columns_ref[index, home] = spread(columns, index * homes + home)

    def pair_distance(home, step, rows):
        dx = columns_ref[1, home, step] - rows[0]
        dy = columns_ref[2, home, step] - rows[1]
        dz = columns_ref[3, home, step] - rows[2]
        return dx * dx + dy * dy + dz * dz

    steps = [pl.ds(start, STEP) for start in range(0, groups, STEP)]

    shift = lists_ref.shape[0].bit_length()
    usual = 8

    def list_items(home, filled):
        turns = (lists_ref[0, home] + (together - 1)) // together

        def put(index, carry):
            items_ref[filled + index] = (home << shift) + index * together
            return carry

        for index in range(usual):
            put(index, 0)
        lax.fori_loop(usual, turns, put, 0)
        return filled + turns

    def own_sweep(integral):
        near_ref[...] = jnp.full(near_ref.shape, FAR_AWAY, jnp.float32)
        own_together = min(homes, 2 * together)

        def own_pairs(turn, carry):
            for index in range(own_together):
                home = turn * own_together + index
                rows = [row_of(window_ref, field, first_home + home) for field in range(4)]
                for start, step in zip(range(0, groups, STEP), steps):
                    same = diagonal(STEP, first_atom + start * SUBLANES)
                    squared = jnp.where(same, FAR_AWAY, pair_distance(home, step, rows))
                    term = integral(squared, columns_ref[0, home, step], rows[3])
                    total_ref[home, step] = jnp.where(same, 0.0, term)
                    near_ref[...] = jnp.minimum(near_ref[...], squared)
            return carry

        lax.fori_loop(0, homes // own_together, own_pairs, 0)

    def sweep(integral, item_count):
        def visit(turn, nearest):
            sums = []
            for index in range(ITEMS):
                item = items_ref[turn * ITEMS + index]
                line, entry = item >> shift, item & ((1 << shift) - 1)
                home = jnp.minimum(line, homes - 1)
                parts_of = [None] * len(steps)
                for other in range(together):
                    partner = lists_ref[SUBLANES + entry + other, line]
                    rows = [row_of(window_ref, field, partner) for field in range(4)]
                    for place, step in enumerate(steps):
                        squared = pair_distance(home, step, rows)
                        nearest = jnp.minimum(nearest, squared)
                        term = integral(squared, columns_ref[0, home, step], rows[3])
                        parts_of[place] = term if other == 0 else parts_of[place] + term
                sums.append((home, parts_of))
            for home, parts_of in sums:
                for part, step in zip(parts_of, steps):
                    total_ref[home, step] += part
            return nearest

        near_ref[...] = lax.fori_loop(0, (item_count + (ITEMS - 1)) // ITEMS, visit, near_ref[...])
        lane = lax.broadcasted_iota(jnp.int32, (chunk, LANES), 1)
        packed = jnp.zeros((chunk, LANES), jnp.float32)
        for home in range(homes):
            packed = jnp.where(lane == home, lane_total(total_ref[home]), packed)
        packed_ref[...] = packed

    def meanwhile():
        home_columns()
        own_sweep(descreen)

    neighbour_lists(partner_ref, first_home, home_id, first_window, homes, slots, window, table_ref)
    move_lists(table_ref, lists_ref, lists_sem, meanwhile)
    intrinsic, rho, _ = type_fields(turned_ref[pl.ds(first_atom, chunk), :])
    item_count = lax.fori_loop(0, homes, list_items, 0)
    for index in range(ITEMS):
        items_ref[item_count + index] = homes << shift
    sweep(descreen, item_count)

    @pl.when(jnp.min(near_ref[...]) < short_range * short_range)
    def _():
        own_sweep(descreen_any)
        sweep(descreen_any, item_count)

    psi = (0.125 * packed_ref[...]) * rho
    shaped = born_alpha * psi - born_beta * psi * psi + born_gamma * psi * psi * psi
    radii = 1.0 / (1.0 / rho - jnp.tanh(shaped) / intrinsic)

    if chunk < LANES:
        radii = jnp.concatenate([radii, jnp.zeros((LANES - chunk, LANES), jnp.float32)], axis=0)
    turned_ref[...] = radii.T
    lane = lax.broadcasted_iota(jnp.int32, (blocks, LANES), 1)
    sent = turned_ref[pl.ds(0, blocks, stride=parts), :]
    for index in range(1, parts):
        rows = pltpu.roll(turned_ref[pl.ds(index, blocks, stride=parts), :], index * chunk, 1)
        sent = jnp.where(lane >= index * chunk, rows, sent)
    for copy in range(copies_ref.shape[0]):
        copies_ref[copy] = sent


def energy_kernel(
    parts,
    whole,
    table_ref,
    window_ref,
    gathered_ref,
    own_radii_ref,
    energy_ref,
    forces_ref,
    grad_ref,
    columns_ref,
    radii_ref,
    total_ref,
    lists_ref,
    lists_sem,
):
    devices, blocks, atoms = gathered_ref.shape
    window = devices * blocks
    part_rows = window // parts
    chunk = atoms // parts
    groups = atoms // SUBLANES
    first_window, _, own_id, part_here = device_place(blocks, parts, whole)
    first_own, list_lane = own_id - first_window, part_here * blocks
    fields = [(window_ref, field) for field in (WINDOW_X, WINDOW_Y, WINDOW_Z, WINDOW_CHARGE)] + [(radii_ref, 0)]

    def unpack():
        lane = lax.broadcasted_iota(jnp.int32, (part_rows, LANES), 1)
        pieces = [
            gathered_ref[pl.ds(part, devices // parts, stride=parts)].reshape(part_rows, atoms)
            for part in range(parts)
        ]
        for place in range(parts):
            whole_rows = pieces[0] if place == 0 else pltpu.roll(pieces[0], (parts - place) * chunk, 1)
            for part in range(1, parts):
                shift = (part - place) % parts
                piece = pieces[part] if shift == 0 else pltpu.roll(pieces[part], shift * chunk, 1)
                whole_rows = jnp.where(lane >= part * chunk, piece, whole_rows)
            radii_ref[0, pl.ds(place, part_rows, stride=parts), :] = whole_rows
        radii_ref[0, window : window + SUBLANES, :] = jnp.ones((SUBLANES, LANES), jnp.float32)

    def own_rows(ref, field):
        return jnp.concatenate([ref[field, pl.ds(first_own + block, 1), :] for block in range(blocks)], axis=0)

    def pair_terms(block, step, rows, same=None):
        x, y, z, charge, radius = rows
        dx = columns_ref[block, step] - x
        dy = columns_ref[blocks + block, step] - y
        dz = columns_ref[2 * blocks + block, step] - z
        squared = dx * dx + dy * dy + dz * dz
        if same is not None:
            squared = jnp.where(same, 1.0, squared)
            charge = jnp.where(same, 0.0, charge)
        spread_sq = columns_ref[3 * blocks + block, step] * radius
        power = squared * pltpu.reciprocal(spread_sq, approx=True)
        quarter = 0.25 * jnp.exp(power)
        root_sq = squared - spread_sq * quarter
        inv_root = lax.rsqrt(root_sq)
        potential = charge * inv_root
        pull = (potential * pltpu.reciprocal(root_sq, approx=True)) * (1.0 - quarter)
        return (pull * dx, pull * dy, pull * dz, potential, pull * squared)

    def own_pairs():
        unpack()
        own_radii = own_rows(radii_ref, 0)
        own_radii_ref[...] = own_radii
        own = [own_rows(window_ref, field) for field in (WINDOW_X, WINDOW_Y, WINDOW_Z)]
        columns = turned(jnp.concatenate(own + [-4.0 * own_radii], axis=0))
        for index in range(4 * blocks):
            columns_ref[index] = spread(columns, index)
        for block in range(blocks):
            rows = [row_of(ref, field, first_own + block) for ref, field in fields]
            for start in range(0, groups, ENERGY_STEP):
                step = pl.ds(start, ENERGY_STEP)
                terms = pair_terms(block, step, rows, diagonal(ENERGY_STEP, start * SUBLANES))
                for term, value in enumerate(terms):
                    total_ref[term * blocks + block, step] = value

    move_lists(table_ref, lists_ref, lists_sem, own_pairs)
    for block in range(blocks):

        def visit(count, first, index, carry, block=block):
            partners = []
            for other in range(count):
                partner = lists_ref[SUBLANES + first + index * count + other, list_lane + block]
                partners.append([row_of(ref, field, partner) for ref, field in fields])
            for start in range(0, groups, ENERGY_STEP):
                step = pl.ds(start, ENERGY_STEP)
                sums = [total_ref[term * blocks + block, step] for term in range(5)]
                for rows in partners:
                    sums = [total + value for total, value in zip(sums, pair_terms(block, step, rows))]
                for term, value in enumerate(sums):
                    total_ref[term * blocks + block, step] = value
            return carry

        left = lists_ref[0, list_lane + block]
        first = 0
        for count in (4, 2, 1):
            turns = left // count
            lax.fori_loop(0, turns, functools.partial(visit, count, first), 0)
            first = first + turns * count
            left = left - turns * count
    sums = lane_sums([total_ref[index] for index in range(5 * blocks)], 5 * blocks)
    charges = own_rows(window_ref, WINDOW_CHARGE)
    own_decay = 1.0 / own_radii_ref[...]
    scale = solvent_tau * charges
    for axis in range(3):
        forces_ref[axis] = -scale * sums[axis * blocks : (axis + 1) * blocks]
    own_energy = 0.5 * scale * charges * own_decay
    energy_ref[...] = -0.5 * scale * sums[3 * blocks : 4 * blocks] - own_energy
    radial = sums[3 * blocks : 4 * blocks] - sums[4 * blocks : 5 * blocks]
    grad_ref[...] = (own_energy + 0.5 * scale * radial) * own_decay


def shards(positions, charges, types, pairs, owner_map):
    _, blocks, atoms = positions.shape
    regions = lax.axis_size("region")
    region_devices = lax.axis_size("dev")
    kept_regions, whole = window_regions(regions)
    devices = kept_regions * region_devices
    window = devices * blocks
    parts = atoms // CHUNK
    while region_devices % parts or 4 * parts * blocks > LANES:
        parts //= 2
    homes = parts * blocks
    chunk = atoms // parts

    vmem = pl.BlockSpec(memory_space=pltpu.VMEM)
    params = pltpu.CompilerParams(vmem_limit_bytes=40 * 1024 * 1024)
    copy_count = lax.axis_size(exchange_axes())
    twins = twin_count(region_devices)
    arrived = sent_to_both_twins(
        pl.pallas_call(
            functools.partial(fields_kernel, blocks, atoms),
            out_shape=jax.ShapeDtypeStruct((copy_count // twins, ROW_COUNT, blocks, atoms), jnp.float32),
            in_specs=[pl.BlockSpec(memory_space=pltpu.HBM)] * 5,
            out_specs=pl.BlockSpec(memory_space=pltpu.HBM),
            scratch_shapes=[
                pltpu.VMEM(positions.shape, positions.dtype),
                pltpu.VMEM(types.shape, types.dtype),
                pltpu.VMEM(charges.shape, charges.dtype),
                pltpu.SMEM(pairs.shape, pairs.dtype),
                pltpu.SMEM(owner_map.shape, owner_map.dtype),
                pltpu.VMEM((ROW_COUNT, blocks, atoms), jnp.float32),
                pltpu.SemaphoreType.DMA((5,)),
                pltpu.SemaphoreType.DMA((2, copy_count // twins)),
            ],
        )(positions, types, charges, pairs, owner_map)
    )
    arrived = [with_other_regions(part).reshape(devices // twins, ROW_COUNT * blocks, atoms) for part in arrived]
    padded = -(-window // LANES) * LANES
    table = jax.ShapeDtypeStruct((SUBLANES + padded, LANES), jnp.int32)
    fields = jax.ShapeDtypeStruct((WINDOW_COUNT, window + SUBLANES, atoms), jnp.float32)
    copies, lists, window_fields = pl.pallas_call(
        functools.partial(radii_kernel, blocks, pairs.shape[1], twins, whole),
        out_shape=(jax.ShapeDtypeStruct((copy_count, blocks, atoms), jnp.float32), table, fields),
        in_specs=[vmem] * twins,
        out_specs=(vmem, vmem, vmem),
        scratch_shapes=[
            pltpu.VMEM((4, homes, chunk // SUBLANES, SUBLANES, LANES), jnp.float32),
            pltpu.VMEM((window, atoms), jnp.float32),
            pltpu.VMEM((padded, atoms), jnp.float32),
            pltpu.VMEM((homes, chunk // SUBLANES, SUBLANES, LANES), jnp.float32),
            pltpu.VMEM((LANES, LANES), jnp.float32),
            pltpu.VMEM((chunk, LANES), jnp.float32),
            pltpu.VMEM((STEP, SUBLANES, LANES), jnp.float32),
            pltpu.SMEM(table.shape, jnp.int32),
            pltpu.SMEM((homes * (padded // max(1, LANES // chunk) + 1) + 64,), jnp.int32),
            pltpu.SemaphoreType.DMA(()),
        ],
        compiler_params=params,
    )(*arrived)
    block_out = jax.ShapeDtypeStruct((blocks, atoms), jnp.float32)
    window_radii = with_other_regions(sent_directly(copies))
    own_radii, energy, forces, grad = pl.pallas_call(
        functools.partial(energy_kernel, parts, whole),
        out_shape=(block_out, block_out, jax.ShapeDtypeStruct((3, blocks, atoms), jnp.float32), block_out),
        in_specs=[pl.BlockSpec(memory_space=pl.ANY), vmem, vmem],
        out_specs=(vmem, vmem, vmem, vmem),
        scratch_shapes=[
            pltpu.VMEM((4 * blocks, atoms // SUBLANES, SUBLANES, LANES), jnp.float32),
            pltpu.VMEM((1, window + SUBLANES, atoms), jnp.float32),
            pltpu.VMEM((5 * blocks, atoms // SUBLANES, SUBLANES, LANES), jnp.float32),
            pltpu.SMEM(table.shape, jnp.int32),
            pltpu.SemaphoreType.DMA(()),
        ],
        compiler_params=params,
    )(lists, window_fields, window_radii)
    return own_radii, energy, forces, grad


def solution(mesh):
    placed = (
        P(None, ("region", "dev"), None),
        P(("region", "dev"), None),
        P(("region", "dev"), None),
        P(("region", "dev"), None),
        P(),
    )
    return jax.shard_map(
        shards,
        mesh=mesh,
        in_specs=placed,
        out_specs=(
            P(("region", "dev"), None),
            P(("region", "dev"), None),
            P(None, ("region", "dev"), None),
            P(("region", "dev"), None),
        ),
        check_vma=False,
    )
```

```python
import functools

import jax
import jax.numpy as jnp
from jax import lax
from jax.experimental import pallas as pl
from jax.experimental.pallas import tpu as pltpu
from jax.sharding import PartitionSpec as P

type_radii = (1.2, 1.7, 1.55, 1.52, 1.85, 1.8)
type_scales = (0.85, 0.72, 0.79, 0.85, 0.86, 0.96)
radius_offset = 0.09
born_alpha = 1.0
born_beta = 0.8
born_gamma = 4.85
solvent_tau = 1.0 - 1.0 / 78.5

ROW_X, ROW_Y, ROW_Z, ROW_TYPE, ROW_CHARGE, ROW_PARTNER, ROW_COUNT = range(7)
WINDOW_X, WINDOW_Y, WINDOW_Z, WINDOW_SCALED, WINDOW_CHARGE, WINDOW_COUNT = range(6)
LANES = 128
SUBLANES = 8
STEP = 4
ENERGY_STEP = 2
CHUNK = 32
LIST_ROWS = 32
ITEMS = 4
EMPTY_SLOT = -1.0e6
FAR_AWAY = 1.0e15

scaled_values = [scale * (radius - radius_offset) for radius, scale in zip(type_radii, type_scales)]
short_range = 1.01 * max(
    max(scaled_values) - (min(type_radii) - radius_offset),
    (max(type_radii) - radius_offset) - min(scaled_values),
    0.5,
)


def window_regions(region_count):
    return (region_count, True) if region_count <= 3 else (3, False)


def exchange_axes():
    return ("region", "dev") if window_regions(lax.axis_size("region"))[1] else ("dev",)


def sent_directly(copies):
    return lax.all_to_all(copies, exchange_axes(), split_axis=0, concat_axis=0, tiled=True)


def twin_count(device_count):
    return 2 - device_count % 2


def sent_to_both_twins(copies):
    count = lax.axis_size("dev")
    twins = twin_count(count)
    axes = exchange_axes()
    regions = lax.axis_size(axes) // count
    alike = [list(range(parity, regions * count, twins)) for parity in range(twins)]
    here = lax.all_to_all(copies, axes, split_axis=0, concat_axis=0, axis_index_groups=alike, tiled=True)
    if twins == 1:
        return [here]
    return [here, lax.ppermute(here, "dev", [(i, i ^ 1) for i in range(count)])]


def with_other_regions(here):
    regions = lax.axis_size("region")
    if window_regions(regions)[1]:
        return here
    below = lax.ppermute(here, "region", [(i, i + 1) for i in range(regions - 1)])
    above = lax.ppermute(here, "region", [(i + 1, i) for i in range(regions - 1)])
    return jnp.concatenate([below, here, above], axis=0)


def by_type(types, table):
    value = jnp.full(types.shape, table[0], jnp.float32)
    for index in range(1, len(table)):
        value = jnp.where(types == index, jnp.float32(table[index]), value)
    return value


def type_fields(types):
    intrinsic = by_type(types, type_radii)
    rho = intrinsic - radius_offset
    return intrinsic, rho, by_type(types, type_scales) * rho


def turned(rows):
    count, width = rows.shape
    if count < LANES:
        rows = jnp.concatenate([rows, jnp.zeros((LANES - count, width), rows.dtype)], axis=0)
    return rows.T


def spread(columns, index):
    count = columns.shape[0]
    wide = jnp.broadcast_to(columns[:, index : index + 1], (count, LANES))
    return wide.reshape(count // SUBLANES, SUBLANES, LANES)


def row_of(ref, field, row):
    return ref[field, pl.ds(row, SUBLANES, stride=0), :][None]


def diagonal(groups, first_atom):
    shape = (groups, SUBLANES, LANES)
    row = lax.broadcasted_iota(jnp.int32, shape, 0) * SUBLANES + lax.broadcasted_iota(jnp.int32, shape, 1)
    return row + first_atom == lax.broadcasted_iota(jnp.int32, shape, 2)


def lane_total(array):
    return jnp.sum(array.reshape(-1, LANES), axis=1, keepdims=True)


def lane_sums(arrays, count):
    atoms = arrays[0].shape[0] * SUBLANES
    lane = lax.broadcasted_iota(jnp.int32, (atoms, LANES), 1)
    packed = jnp.zeros((atoms, LANES), jnp.float32)
    for index, array in enumerate(arrays):
        packed = jnp.where(lane == index, lane_total(array), packed)
    return packed.T[:count]


def fields_kernel(blocks, atoms, *refs):
    inputs, copies_ref, here, sems = refs[:5], refs[5], refs[6:11], refs[11]
    moves = [pltpu.make_async_copy(src, dst, sems.at[i]) for i, (src, dst) in enumerate(zip(inputs, here))]
    for move in moves:
        move.start()
    for move in moves:
        move.wait()
    positions_ref, types_ref, charges_ref, pairs_ref, owner_ref = here
    slot = lax.broadcasted_iota(jnp.int32, (1, atoms), 1)
    partners = []
    for block in range(blocks):
        row = jnp.full((1, atoms), EMPTY_SLOT, jnp.float32)
        for index in range(pairs_ref.shape[1]):
            cell = pairs_ref[block, index]
            partner = jnp.where(cell >= 0, owner_ref[jnp.maximum(cell, 0)] + 1, int(EMPTY_SLOT))
            row = jnp.where(slot == index, partner.astype(jnp.float32), row)
        partners.append(row)
    rows = [positions_ref[axis] for axis in range(3)]
    rows += [types_ref[...].astype(jnp.float32), charges_ref[...], jnp.concatenate(partners, axis=0)]
    for copy in range(copies_ref.shape[0]):
        for index, row in enumerate(rows):
            copies_ref[copy, index] = row


def descreen(squared, rho, scaled):
    inv_dist = lax.rsqrt(squared)
    share = scaled * inv_dist
    inner = 0.25 - share
    high = 0.25 + share
    low = jnp.maximum(rho * inv_dist, inner)
    inv_low = pltpu.reciprocal(low, approx=True)
    ratio = low * pltpu.reciprocal(high, approx=True)
    curve = (1.0 - ratio) + inner * (ratio - high * inv_low)
    return (inv_low * curve + 2.0 * jnp.log(ratio)) * inv_dist


def descreen_any(squared, rho, scaled):
    rho, scaled = 4.0 * rho, 4.0 * scaled
    inv_dist = lax.rsqrt(squared)
    distance = squared * inv_dist
    high = distance + scaled
    gap = distance - scaled
    low = jnp.maximum(rho, jnp.abs(gap))
    inv_low = 1.0 / low
    inv_high = 1.0 / high
    quarter = 0.25 * inv_dist
    curve = (squared - scaled * scaled) * quarter
    body = (0.5 * (inv_low - inv_high)) * (1.0 - (inv_low + inv_high) * curve)
    body = body + jnp.log(low * inv_high) * quarter
    body = body + jnp.where(rho < -gap, 1.0 / rho - inv_low, 0.0)
    return jnp.where(high > rho, 8.0 * body, 0.0)


def neighbour_lists(partner_ref, first_home, home_id, first_window, homes, slots, filler, table_ref):
    window = partner_ref.shape[0]
    tiles = [slice(start, start + LANES) for start in range(0, window, LANES)]
    depth = -(-slots // SUBLANES) * SUBLANES
    ids = jnp.concatenate([partner_ref[tile, :].T[:depth] for tile in tiles], axis=1)
    lists = turned(partner_ref[pl.ds(first_home, homes), :])[:depth]
    lane = lax.broadcasted_iota(jnp.int32, (depth, window), 1)
    lane_id = (lane + (first_window + 1)).astype(jnp.float32)
    rows = []
    for home in range(homes):
        own = (home_id + home + 1).astype(jnp.float32)
        linked = (ids == own) | (lane_id == lists[:, home : home + 1])
        rows.append(jnp.max(jnp.where(linked, 1.0, 0.0), axis=0, keepdims=True))
    linked = jnp.concatenate(rows, axis=0)
    before = lax.broadcasted_iota(jnp.int32, (window, window), 0)
    after = lax.broadcasted_iota(jnp.int32, (window, window), 1)
    ramp = jnp.where(before <= after, 1.0, 0.0).astype(jnp.bfloat16)
    rank = jnp.dot(linked.astype(jnp.bfloat16), ramp, preferred_element_type=jnp.float32)
    place = jnp.where(linked > 0.0, rank, 0.0)
    total = jnp.sum(linked, axis=1, keepdims=True)
    name = lax.broadcasted_iota(jnp.int32, (LIST_ROWS, window), 1).astype(jnp.float32)
    spot = lax.broadcasted_iota(jnp.int32, (LIST_ROWS, window), 0).astype(jnp.float32)
    own_lane = lax.broadcasted_iota(jnp.int32, (LIST_ROWS, LANES), 1)

    def some_rows(start):
        first = jnp.asarray(start + 1).astype(jnp.float32)
        packed = jnp.zeros((LIST_ROWS, LANES), jnp.float32)
        for home in range(homes):
            hit = place[home : home + 1] == spot + first
            found = jnp.sum(jnp.where(hit, name - float(filler), 0.0), axis=1, keepdims=True)
            packed = jnp.where(own_lane == home, found, packed)
        rows = pl.ds(pl.multiple_of(SUBLANES + start, SUBLANES), LIST_ROWS)
        table_ref[rows, :] = packed.astype(jnp.int32) + filler

    counts = jnp.zeros((SUBLANES, LANES), jnp.float32)
    lane = lax.broadcasted_iota(jnp.int32, (SUBLANES, LANES), 1)
    for home in range(homes):
        counts = jnp.where(lane == home, total[home : home + 1], counts)
    longest = jnp.max(total)
    table_ref[0:SUBLANES, :] = jnp.where(lane == LANES - 1, longest, counts).astype(jnp.int32)
    some_rows(0)

    def more_rows(turn, carry):
        some_rows(turn * LIST_ROWS)
        return carry

    lax.fori_loop(1, (longest.astype(jnp.int32) + (LIST_ROWS - 1)) // LIST_ROWS, more_rows, 0)


def move_lists(table_ref, lists_ref, sem, when_wanted):
    usual = pl.ds(0, SUBLANES + LIST_ROWS)
    move = pltpu.make_async_copy(table_ref.at[usual], lists_ref.at[usual], sem)
    move.start()
    when_wanted()
    move.wait()
    rows = lists_ref.shape[0] - (SUBLANES + LIST_ROWS)
    if rows > 0:

        @pl.when(lists_ref[0, LANES - 1] > LIST_ROWS)
        def _():
            rest = pl.ds(SUBLANES + LIST_ROWS, rows)
            more = pltpu.make_async_copy(table_ref.at[rest], lists_ref.at[rest], sem)
            more.start()
            more.wait()


def device_place(blocks, parts, whole):
    region, device = lax.axis_index("region"), lax.axis_index("dev")
    region_blocks = lax.axis_size("dev") * blocks
    first_window = 0 if whole else (region - 1) * region_blocks
    first_own = region * region_blocks + device * blocks
    part = lax.rem(device, parts)
    return first_window, first_own - part * blocks, first_own, part


def radii_kernel(
    blocks,
    slots,
    twins,
    whole,
    *refs,
):
    arrived_refs, refs = refs[:twins], refs[twins:]
    copies_ref, table_ref, window_ref, columns_ref, types_ref, partner_ref, total_ref, *refs = refs
    turned_ref, packed_ref, near_ref, lists_ref, items_ref, lists_sem = refs
    _, homes, groups, _, _ = columns_ref.shape
    chunk = groups * SUBLANES
    window = types_ref.shape[0]
    parts = homes // blocks
    together = max(1, LANES // chunk)
    first_window, home_id, _, part = device_place(blocks, parts, whole)
    first_home = pl.multiple_of(home_id - first_window, homes)
    first_atom = pl.multiple_of(part * chunk, chunk)

    tables = [window_ref.at[WINDOW_X], window_ref.at[WINDOW_Y], window_ref.at[WINDOW_Z]]
    tables += [types_ref, window_ref.at[WINDOW_CHARGE], partner_ref]
    odd = lax.rem(lax.axis_index("dev"), 2) == 1
    for place in range(arrived_refs[0].shape[0]):
        for field, table in enumerate(tables):
            rows = [ref[place, field * blocks : (field + 1) * blocks, :] for ref in arrived_refs]
            if twins == 2:
                rows = [jnp.where(odd, rows[1], rows[0]), jnp.where(odd, rows[0], rows[1])]
            first = place * twins * blocks
            table[first : first + twins * blocks, :] = jnp.concatenate(rows, axis=0)
    if partner_ref.shape[0] > window:
        spare = (partner_ref.shape[0] - window, LANES)
        partner_ref[window:, :] = jnp.full(spare, EMPTY_SLOT, jnp.float32)
    def scaled_radii():
        _, _, scaled = type_fields(types_ref[...])
        window_ref[WINDOW_SCALED, 0:window, :] = 0.25 * scaled
        for field in range(WINDOW_COUNT):
            filler = FAR_AWAY if field == WINDOW_X else 0.0
            window_ref[field, window : window + SUBLANES, :] = jnp.full((SUBLANES, LANES), filler, jnp.float32)

    def home_columns():
        scaled_radii()
        home_rows = [window_ref[field, pl.ds(first_home, homes), :] for field in range(3)]
        turned_ref[...] = turned(jnp.concatenate([types_ref[pl.ds(first_home, homes), :]] + home_rows, axis=0))
        columns = turned_ref[pl.ds(first_atom, chunk), :]
        _, rho, _ = type_fields(columns)
        for home in range(homes):
            columns_ref[0, home] = spread(0.25 * rho, home)
            for index in range(1, 4):
                columns_ref[index, home] = spread(columns, index * homes + home)

    def pair_distance(home, step, rows):
        dx = columns_ref[1, home, step] - rows[0]
        dy = columns_ref[2, home, step] - rows[1]
        dz = columns_ref[3, home, step] - rows[2]
        return dx * dx + dy * dy + dz * dz

    steps = [pl.ds(start, STEP) for start in range(0, groups, STEP)]

    shift = lists_ref.shape[0].bit_length()
    usual = 8

    def list_items(home, filled):
        turns = (lists_ref[0, home] + (together - 1)) // together

        def put(index, carry):
            items_ref[filled + index] = (home << shift) + index * together
            return carry

        for index in range(usual):
            put(index, 0)
        lax.fori_loop(usual, turns, put, 0)
        return filled + turns

    def own_sweep(integral):
        near_ref[...] = jnp.full(near_ref.shape, FAR_AWAY, jnp.float32)
        own_together = min(homes, 2 * together)

        def own_pairs(turn, carry):
            for index in range(own_together):
                home = turn * own_together + index
                rows = [row_of(window_ref, field, first_home + home) for field in range(4)]
                for start, step in zip(range(0, groups, STEP), steps):
                    same = diagonal(STEP, first_atom + start * SUBLANES)
                    squared = jnp.where(same, FAR_AWAY, pair_distance(home, step, rows))
                    term = integral(squared, columns_ref[0, home, step], rows[3])
                    total_ref[home, step] = jnp.where(same, 0.0, term)
                    near_ref[...] = jnp.minimum(near_ref[...], squared)
            return carry

        lax.fori_loop(0, homes // own_together, own_pairs, 0)

    def sweep(integral, item_count):
        def visit(turn, nearest):
            sums = []
            for index in range(ITEMS):
                item = items_ref[turn * ITEMS + index]
                line, entry = item >> shift, item & ((1 << shift) - 1)
                home = jnp.minimum(line, homes - 1)
                parts_of = [None] * len(steps)
                for other in range(together):
                    partner = lists_ref[SUBLANES + entry + other, line]
                    rows = [row_of(window_ref, field, partner) for field in range(4)]
                    for place, step in enumerate(steps):
                        squared = pair_distance(home, step, rows)
                        nearest = jnp.minimum(nearest, squared)
                        term = integral(squared, columns_ref[0, home, step], rows[3])
                        parts_of[place] = term if other == 0 else parts_of[place] + term
                sums.append((home, parts_of))
            for home, parts_of in sums:
                for part, step in zip(parts_of, steps):
                    total_ref[home, step] += part
            return nearest

        near_ref[...] = lax.fori_loop(0, (item_count + (ITEMS - 1)) // ITEMS, visit, near_ref[...])
        lane = lax.broadcasted_iota(jnp.int32, (chunk, LANES), 1)
        packed = jnp.zeros((chunk, LANES), jnp.float32)
        for home in range(homes):
            packed = jnp.where(lane == home, lane_total(total_ref[home]), packed)
        packed_ref[...] = packed

    def meanwhile():
        home_columns()
        own_sweep(descreen)

    neighbour_lists(partner_ref, first_home, home_id, first_window, homes, slots, window, table_ref)
    move_lists(table_ref, lists_ref, lists_sem, meanwhile)
    intrinsic, rho, _ = type_fields(turned_ref[pl.ds(first_atom, chunk), :])
    item_count = lax.fori_loop(0, homes, list_items, 0)
    for index in range(ITEMS):
        items_ref[item_count + index] = homes << shift
    sweep(descreen, item_count)

    @pl.when(jnp.min(near_ref[...]) < short_range * short_range)
    def _():
        own_sweep(descreen_any)
        sweep(descreen_any, item_count)

    psi = (0.125 * packed_ref[...]) * rho
    shaped = born_alpha * psi - born_beta * psi * psi + born_gamma * psi * psi * psi
    radii = 1.0 / (1.0 / rho - jnp.tanh(shaped) / intrinsic)

    if chunk < LANES:
        radii = jnp.concatenate([radii, jnp.zeros((LANES - chunk, LANES), jnp.float32)], axis=0)
    turned_ref[...] = radii.T
    lane = lax.broadcasted_iota(jnp.int32, (blocks, LANES), 1)
    sent = turned_ref[pl.ds(0, blocks, stride=parts), :]
    for index in range(1, parts):
        rows = pltpu.roll(turned_ref[pl.ds(index, blocks, stride=parts), :], index * chunk, 1)
        sent = jnp.where(lane >= index * chunk, rows, sent)
    for copy in range(copies_ref.shape[0]):
        copies_ref[copy] = sent


def own_columns(rows, first, columns_ref):
    columns = turned(jnp.concatenate(rows, axis=0))
    for index in range(sum(row.shape[0] for row in rows)):
        columns_ref[first + index] = spread(columns, index)


def pair_distance(columns_ref, blocks, block, step, rows):
    dx = columns_ref[block, step] - rows[0]
    dy = columns_ref[blocks + block, step] - rows[1]
    dz = columns_ref[2 * blocks + block, step] - rows[2]
    return dx, dy, dz


def distance_kernel(
    blocks, parts, whole, table_ref, window_ref, columns_ref, squares_ref, lists_ref, lists_sem
):
    groups = columns_ref.shape[1]
    together = 4
    first_window, _, own_id, part_here = device_place(blocks, parts, whole)
    first_own, list_lane = own_id - first_window, part_here * blocks
    fields = (WINDOW_X, WINDOW_Y, WINDOW_Z)

    def home_columns():
        rows = [
            jnp.concatenate(
                [window_ref[field, pl.ds(first_own + block, 1), :] for block in range(blocks)], axis=0
            )
            for field in fields
        ]
        own_columns(rows, 0, columns_ref)

    move_lists(table_ref, lists_ref, lists_sem, home_columns)
    for block in range(blocks):

        def visit(turn, carry, block=block):
            for other in range(together):
                entry = turn * together + other
                partner = lists_ref[SUBLANES + entry, list_lane + block]
                rows = [row_of(window_ref, field, partner) for field in fields]
                for start in range(0, groups, STEP):
                    step = pl.ds(start, STEP)
                    dx, dy, dz = pair_distance(columns_ref, blocks, block, step, rows)
                    squares_ref[block, entry, step] = dx * dx + dy * dy + dz * dz
            return carry

        entries = jnp.minimum(lists_ref[0, list_lane + block], squares_ref.shape[1])
        lax.fori_loop(0, (entries + (together - 1)) // together, visit, 0)


def energy_kernel(
    parts,
    whole,
    table_ref,
    window_ref,
    squares_ref,
    places_ref,
    gathered_ref,
    own_radii_ref,
    energy_ref,
    forces_ref,
    grad_ref,
    columns_ref,
    radii_ref,
    total_ref,
    lists_ref,
    lists_sem,
):
    devices, blocks, atoms = gathered_ref.shape
    window = devices * blocks
    part_rows = window // parts
    chunk = atoms // parts
    groups = atoms // SUBLANES
    first_window, _, own_id, part_here = device_place(blocks, parts, whole)
    first_own, list_lane = own_id - first_window, part_here * blocks
    fields = [(window_ref, field) for field in (WINDOW_X, WINDOW_Y, WINDOW_Z, WINDOW_CHARGE)] + [(radii_ref, 0)]

    def unpack():
        lane = lax.broadcasted_iota(jnp.int32, (part_rows, LANES), 1)
        pieces = [
            gathered_ref[pl.ds(part, devices // parts, stride=parts)].reshape(part_rows, atoms)
            for part in range(parts)
        ]
        for place in range(parts):
            whole_rows = pieces[0] if place == 0 else pltpu.roll(pieces[0], (parts - place) * chunk, 1)
            for part in range(1, parts):
                shift = (part - place) % parts
                piece = pieces[part] if shift == 0 else pltpu.roll(pieces[part], shift * chunk, 1)
                whole_rows = jnp.where(lane >= part * chunk, piece, whole_rows)
            radii_ref[0, pl.ds(place, part_rows, stride=parts), :] = whole_rows
        radii_ref[0, window : window + SUBLANES, :] = jnp.ones((SUBLANES, LANES), jnp.float32)

    def own_rows(ref, field):
        return jnp.concatenate([ref[field, pl.ds(first_own + block, 1), :] for block in range(blocks)], axis=0)

    def pair_terms(block, step, rows, same=None, entry=None):
        charge, radius = rows[3:]
        dx, dy, dz = pair_distance(places_ref, blocks, block, step, rows)
        squared = dx * dx + dy * dy + dz * dz if entry is None else squares_ref[block, entry, step]
        if same is not None:
            squared = jnp.where(same, 1.0, squared)
            charge = jnp.where(same, 0.0, charge)
        spread_sq = columns_ref[block, step] * radius
        power = squared * pltpu.reciprocal(spread_sq, approx=True)
        quarter = 0.25 * jnp.exp(power)
        root_sq = squared - spread_sq * quarter
        inv_root = lax.rsqrt(root_sq)
        potential = charge * inv_root
        pull = (potential * pltpu.reciprocal(root_sq, approx=True)) * (1.0 - quarter)
        return (pull * dx, pull * dy, pull * dz, potential, pull * squared)

    def own_pairs():
        unpack()
        own_radii = own_rows(radii_ref, 0)
        own_radii_ref[...] = own_radii
        own_columns([-4.0 * own_radii], 0, columns_ref)
        for block in range(blocks):
            rows = [row_of(ref, field, first_own + block) for ref, field in fields]
            for start in range(0, groups, ENERGY_STEP):
                step = pl.ds(start, ENERGY_STEP)
                terms = pair_terms(block, step, rows, diagonal(ENERGY_STEP, start * SUBLANES))
                for term, value in enumerate(terms):
                    total_ref[term * blocks + block, step] = value

    move_lists(table_ref, lists_ref, lists_sem, own_pairs)
    for block in range(blocks):

        def visit(count, first, stored, index, carry, block=block):
            partners = []
            for other in range(count):
                entry = first + index * count + other
                partner = lists_ref[SUBLANES + entry, list_lane + block]
                rows = [row_of(ref, field, partner) for ref, field in fields]
                partners.append((rows, entry if stored else None))
            for start in range(0, groups, ENERGY_STEP):
                step = pl.ds(start, ENERGY_STEP)
                sums = [total_ref[term * blocks + block, step] for term in range(5)]
                for rows, entry in partners:
                    terms = pair_terms(block, step, rows, entry=entry)
                    sums = [total + value for total, value in zip(sums, terms)]
                for term, value in enumerate(sums):
                    total_ref[term * blocks + block, step] = value
            return carry

        entries = lists_ref[0, list_lane + block]
        left = jnp.minimum(entries, squares_ref.shape[1])
        first = 0
        for count in (4, 2, 1):
            turns = left // count
            lax.fori_loop(0, turns, functools.partial(visit, count, first, True), 0)
            first = first + turns * count
            left = left - turns * count
        lax.fori_loop(first, entries, functools.partial(visit, 1, 0, False), 0)
    sums = lane_sums([total_ref[index] for index in range(5 * blocks)], 5 * blocks)
    charges = own_rows(window_ref, WINDOW_CHARGE)
    own_decay = 1.0 / own_radii_ref[...]
    scale = solvent_tau * charges
    for axis in range(3):
        forces_ref[axis] = -scale * sums[axis * blocks : (axis + 1) * blocks]
    own_energy = 0.5 * scale * charges * own_decay
    energy_ref[...] = -0.5 * scale * sums[3 * blocks : 4 * blocks] - own_energy
    radial = sums[3 * blocks : 4 * blocks] - sums[4 * blocks : 5 * blocks]
    grad_ref[...] = (own_energy + 0.5 * scale * radial) * own_decay


def shards(positions, charges, types, pairs, owner_map):
    _, blocks, atoms = positions.shape
    regions = lax.axis_size("region")
    region_devices = lax.axis_size("dev")
    kept_regions, whole = window_regions(regions)
    devices = kept_regions * region_devices
    window = devices * blocks
    parts = atoms // CHUNK
    while region_devices % parts or 4 * parts * blocks > LANES:
        parts //= 2
    homes = parts * blocks
    chunk = atoms // parts

    vmem = pl.BlockSpec(memory_space=pltpu.VMEM)
    params = pltpu.CompilerParams(vmem_limit_bytes=24 * 1024 * 1024)
    copy_count = lax.axis_size(exchange_axes())
    twins = twin_count(region_devices)
    arrived = sent_to_both_twins(
        pl.pallas_call(
            functools.partial(fields_kernel, blocks, atoms),
            out_shape=jax.ShapeDtypeStruct((copy_count // twins, ROW_COUNT, blocks, atoms), jnp.float32),
            in_specs=[pl.BlockSpec(memory_space=pltpu.HBM)] * 5,
            out_specs=vmem,
            scratch_shapes=[
                pltpu.VMEM(positions.shape, positions.dtype),
                pltpu.VMEM(types.shape, types.dtype),
                pltpu.VMEM(charges.shape, charges.dtype),
                pltpu.SMEM(pairs.shape, pairs.dtype),
                pltpu.SMEM(owner_map.shape, owner_map.dtype),
                pltpu.SemaphoreType.DMA((5,)),
            ],
        )(positions, types, charges, pairs, owner_map)
    )
    arrived = [with_other_regions(part).reshape(devices // twins, ROW_COUNT * blocks, atoms) for part in arrived]
    padded = -(-window // LANES) * LANES
    table = jax.ShapeDtypeStruct((SUBLANES + padded, LANES), jnp.int32)
    fields = jax.ShapeDtypeStruct((WINDOW_COUNT, window + SUBLANES, atoms), jnp.float32)
    copies, lists, window_fields = pl.pallas_call(
        functools.partial(radii_kernel, blocks, pairs.shape[1], twins, whole),
        out_shape=(jax.ShapeDtypeStruct((copy_count, blocks, atoms), jnp.float32), table, fields),
        in_specs=[vmem] * twins,
        out_specs=(vmem, vmem, vmem),
        scratch_shapes=[
            pltpu.VMEM((4, homes, chunk // SUBLANES, SUBLANES, LANES), jnp.float32),
            pltpu.VMEM((window, atoms), jnp.float32),
            pltpu.VMEM((padded, atoms), jnp.float32),
            pltpu.VMEM((homes, chunk // SUBLANES, SUBLANES, LANES), jnp.float32),
            pltpu.VMEM((LANES, LANES), jnp.float32),
            pltpu.VMEM((chunk, LANES), jnp.float32),
            pltpu.VMEM((STEP, SUBLANES, LANES), jnp.float32),
            pltpu.SMEM(table.shape, jnp.int32),
            pltpu.SMEM((homes * (padded // max(1, LANES // chunk) + 1) + 64,), jnp.int32),
            pltpu.SemaphoreType.DMA(()),
        ],
        compiler_params=params,
    )(*arrived)
    block_out = jax.ShapeDtypeStruct((blocks, atoms), jnp.float32)
    groups = atoms // SUBLANES
    anywhere = pl.BlockSpec(memory_space=pl.ANY)
    places, squares = pl.pallas_call(
        functools.partial(distance_kernel, blocks, parts, whole),
        out_shape=(
            jax.ShapeDtypeStruct((3 * blocks, groups, SUBLANES, LANES), jnp.float32),
            jax.ShapeDtypeStruct((blocks, LIST_ROWS, groups, SUBLANES, LANES), jnp.float32),
        ),
        in_specs=[anywhere, vmem],
        out_specs=(vmem, vmem),
        scratch_shapes=[pltpu.SMEM(table.shape, jnp.int32), pltpu.SemaphoreType.DMA(())],
        compiler_params=params,
        cost_estimate=pl.CostEstimate(flops=40_000_000, bytes_accessed=10_000_000, transcendentals=0),
    )(lists, window_fields)
    window_radii = with_other_regions(sent_directly(copies))
    own_radii, energy, forces, grad = pl.pallas_call(
        functools.partial(energy_kernel, parts, whole),
        out_shape=(block_out, block_out, jax.ShapeDtypeStruct((3, blocks, atoms), jnp.float32), block_out),
        in_specs=[anywhere] + [vmem] * 4,
        out_specs=(vmem, vmem, vmem, vmem),
        scratch_shapes=[
            pltpu.VMEM((blocks, groups, SUBLANES, LANES), jnp.float32),
            pltpu.VMEM((1, window + SUBLANES, atoms), jnp.float32),
            pltpu.VMEM((5 * blocks, atoms // SUBLANES, SUBLANES, LANES), jnp.float32),
            pltpu.SMEM(table.shape, jnp.int32),
            pltpu.SemaphoreType.DMA(()),
        ],
        compiler_params=params,
    )(lists, window_fields, squares, places, window_radii)
    return own_radii, energy, forces, grad


def solution(mesh):
    placed = (
        P(None, ("region", "dev"), None),
        P(("region", "dev"), None),
        P(("region", "dev"), None),
        P(("region", "dev"), None),
        P(),
    )
    return jax.shard_map(
        shards,
        mesh=mesh,
        in_specs=placed,
        out_specs=(
            P(("region", "dev"), None),
            P(("region", "dev"), None),
            P(None, ("region", "dev"), None),
            P(("region", "dev"), None),
        ),
        check_vma=False,
    )
```

```python
import functools

import jax
import jax.numpy as jnp
from jax import lax
from jax.experimental import pallas as pl
from jax.experimental.pallas import tpu as pltpu
from jax.sharding import PartitionSpec as P

type_radii = (1.2, 1.7, 1.55, 1.52, 1.85, 1.8)
type_scales = (0.85, 0.72, 0.79, 0.85, 0.86, 0.96)
radius_offset = 0.09
born_alpha = 1.0
born_beta = 0.8
born_gamma = 4.85
solvent_tau = 1.0 - 1.0 / 78.5

ROW_X, ROW_Y, ROW_Z, ROW_TYPE, ROW_CHARGE, ROW_PARTNER, ROW_COUNT = range(7)
WINDOW_X, WINDOW_Y, WINDOW_Z, WINDOW_SCALED, WINDOW_CHARGE, WINDOW_COUNT = range(6)
LANES = 128
SUBLANES = 8
STEP = 4
ENERGY_STEP = 2
CHUNK = 32
LIST_ROWS = 32
ITEMS = 4
EMPTY_SLOT = -1.0e6
FAR_AWAY = 1.0e15

scaled_values = [scale * (radius - radius_offset) for radius, scale in zip(type_radii, type_scales)]
short_range = 1.01 * max(
    max(scaled_values) - (min(type_radii) - radius_offset),
    (max(type_radii) - radius_offset) - min(scaled_values),
    0.5,
)


def window_regions(region_count):
    return (region_count, True) if region_count <= 3 else (3, False)


def exchange_axes():
    return ("region", "dev") if window_regions(lax.axis_size("region"))[1] else ("dev",)


def sent_directly(copies):
    axes = exchange_axes()
    everyone = [list(reversed(range(lax.axis_size(axes))))]
    return lax.all_to_all(copies, axes, split_axis=0, concat_axis=0, axis_index_groups=everyone, tiled=True)


def twin_count(device_count):
    return 2 - device_count % 2


def sent_to_both_twins(copies):
    count = lax.axis_size("dev")
    twins = twin_count(count)
    axes = exchange_axes()
    regions = lax.axis_size(axes) // count
    alike = [list(reversed(range(parity, regions * count, twins))) for parity in range(twins)]
    here = lax.all_to_all(copies, axes, split_axis=0, concat_axis=0, axis_index_groups=alike, tiled=True)
    if twins == 1:
        return [here]
    return [here, lax.ppermute(here, "dev", [(i, i ^ 1) for i in range(count)])]


def with_other_regions(here):
    regions = lax.axis_size("region")
    if window_regions(regions)[1]:
        return here
    below = lax.ppermute(here, "region", [(i, i + 1) for i in range(regions - 1)])
    above = lax.ppermute(here, "region", [(i + 1, i) for i in range(regions - 1)])
    return jnp.concatenate([below, here, above], axis=0)


def by_type(types, table):
    value = jnp.full(types.shape, table[0], jnp.float32)
    for index in range(1, len(table)):
        value = jnp.where(types == index, jnp.float32(table[index]), value)
    return value


def type_fields(types):
    intrinsic = by_type(types, type_radii)
    rho = intrinsic - radius_offset
    return intrinsic, rho, by_type(types, type_scales) * rho


def turned(rows):
    count, width = rows.shape
    if count < LANES:
        rows = jnp.concatenate([rows, jnp.zeros((LANES - count, width), rows.dtype)], axis=0)
    return rows.T


def spread(columns, index):
    count = columns.shape[0]
    wide = jnp.broadcast_to(columns[:, index : index + 1], (count, LANES))
    return wide.reshape(count // SUBLANES, SUBLANES, LANES)


def row_of(ref, field, row):
    return ref[field, pl.ds(row, SUBLANES, stride=0), :][None]


def diagonal(groups, first_atom):
    shape = (groups, SUBLANES, LANES)
    row = lax.broadcasted_iota(jnp.int32, shape, 0) * SUBLANES + lax.broadcasted_iota(jnp.int32, shape, 1)
    return row + first_atom == lax.broadcasted_iota(jnp.int32, shape, 2)


def lane_total(array):
    return jnp.sum(array.reshape(-1, LANES), axis=1, keepdims=True)


def lane_sums(arrays, count):
    atoms = arrays[0].shape[0] * SUBLANES
    lane = lax.broadcasted_iota(jnp.int32, (atoms, LANES), 1)
    packed = jnp.zeros((atoms, LANES), jnp.float32)
    for index, array in enumerate(arrays):
        packed = jnp.where(lane == index, lane_total(array), packed)
    return packed.T[:count]


def fields_kernel(blocks, atoms, *refs):
    inputs, copies_ref, here, sems = refs[:5], refs[5], refs[6:11], refs[11]
    moves = [pltpu.make_async_copy(src, dst, sems.at[i]) for i, (src, dst) in enumerate(zip(inputs, here))]
    for move in moves:
        move.start()
    for move in moves:
        move.wait()
    positions_ref, types_ref, charges_ref, pairs_ref, owner_ref = here
    slot = lax.broadcasted_iota(jnp.int32, (1, atoms), 1)
    partners = []
    for block in range(blocks):
        row = jnp.full((1, atoms), EMPTY_SLOT, jnp.float32)
        for index in range(pairs_ref.shape[1]):
            cell = pairs_ref[block, index]
            partner = jnp.where(cell >= 0, owner_ref[jnp.maximum(cell, 0)] + 1, int(EMPTY_SLOT))
            row = jnp.where(slot == index, partner.astype(jnp.float32), row)
        partners.append(row)
    rows = [positions_ref[axis] for axis in range(3)]
    rows += [types_ref[...].astype(jnp.float32), charges_ref[...], jnp.concatenate(partners, axis=0)]
    for copy in range(copies_ref.shape[0]):
        for index, row in enumerate(rows):
            copies_ref[copy, index] = row


def descreen(squared, rho, scaled):
    inv_dist = lax.rsqrt(squared)
    share = scaled * inv_dist
    inner = 0.25 - share
    high = 0.25 + share
    low = jnp.maximum(rho * inv_dist, inner)
    inv_low = pltpu.reciprocal(low, approx=True)
    ratio = low * pltpu.reciprocal(high, approx=True)
    curve = (1.0 - ratio) + inner * (ratio - high * inv_low)
    return (inv_low * curve + 2.0 * jnp.log(ratio)) * inv_dist


def descreen_any(squared, rho, scaled):
    rho, scaled = 4.0 * rho, 4.0 * scaled
    inv_dist = lax.rsqrt(squared)
    distance = squared * inv_dist
    high = distance + scaled
    gap = distance - scaled
    low = jnp.maximum(rho, jnp.abs(gap))
    inv_low = 1.0 / low
    inv_high = 1.0 / high
    quarter = 0.25 * inv_dist
    curve = (squared - scaled * scaled) * quarter
    body = (0.5 * (inv_low - inv_high)) * (1.0 - (inv_low + inv_high) * curve)
    body = body + jnp.log(low * inv_high) * quarter
    body = body + jnp.where(rho < -gap, 1.0 / rho - inv_low, 0.0)
    return jnp.where(high > rho, 8.0 * body, 0.0)


def neighbour_lists(partner_ref, first_home, home_id, first_window, homes, slots, filler, table_ref):
    window = partner_ref.shape[0]
    tiles = [slice(start, start + LANES) for start in range(0, window, LANES)]
    depth = -(-slots // SUBLANES) * SUBLANES
    ids = jnp.concatenate([partner_ref[tile, :].T[:depth] for tile in tiles], axis=1)
    lists = turned(partner_ref[pl.ds(first_home, homes), :])[:depth]
    lane = lax.broadcasted_iota(jnp.int32, (depth, window), 1)
    lane_id = (lane + (first_window + 1)).astype(jnp.float32)
    rows = []
    for home in range(homes):
        own = (home_id + home + 1).astype(jnp.float32)
        linked = (ids == own) | (lane_id == lists[:, home : home + 1])
        rows.append(jnp.max(jnp.where(linked, 1.0, 0.0), axis=0, keepdims=True))
    linked = jnp.concatenate(rows, axis=0)
    before = lax.broadcasted_iota(jnp.int32, (window, window), 0)
    after = lax.broadcasted_iota(jnp.int32, (window, window), 1)
    ramp = jnp.where(before <= after, 1.0, 0.0).astype(jnp.bfloat16)
    rank = jnp.dot(linked.astype(jnp.bfloat16), ramp, preferred_element_type=jnp.float32)
    place = jnp.where(linked > 0.0, rank, 0.0)
    total = jnp.sum(linked, axis=1, keepdims=True)
    name = lax.broadcasted_iota(jnp.int32, (LIST_ROWS, window), 1).astype(jnp.float32)
    spot = lax.broadcasted_iota(jnp.int32, (LIST_ROWS, window), 0).astype(jnp.float32)
    own_lane = lax.broadcasted_iota(jnp.int32, (LIST_ROWS, LANES), 1)

    def some_rows(start):
        first = jnp.asarray(start + 1).astype(jnp.float32)
        packed = jnp.zeros((LIST_ROWS, LANES), jnp.float32)
        for home in range(homes):
            hit = place[home : home + 1] == spot + first
            found = jnp.sum(jnp.where(hit, name - float(filler), 0.0), axis=1, keepdims=True)
            packed = jnp.where(own_lane == home, found, packed)
        rows = pl.ds(pl.multiple_of(SUBLANES + start, SUBLANES), LIST_ROWS)
        table_ref[rows, :] = packed.astype(jnp.int32) + filler

    counts = jnp.zeros((SUBLANES, LANES), jnp.float32)
    lane = lax.broadcasted_iota(jnp.int32, (SUBLANES, LANES), 1)
    for home in range(homes):
        counts = jnp.where(lane == home, total[home : home + 1], counts)
    longest = jnp.max(total)
    table_ref[0:SUBLANES, :] = jnp.where(lane == LANES - 1, longest, counts).astype(jnp.int32)
    some_rows(0)

    def more_rows(turn, carry):
        some_rows(turn * LIST_ROWS)
        return carry

    lax.fori_loop(1, (longest.astype(jnp.int32) + (LIST_ROWS - 1)) // LIST_ROWS, more_rows, 0)


def move_lists(table_ref, lists_ref, sem, when_wanted):
    usual = pl.ds(0, SUBLANES + LIST_ROWS)
    move = pltpu.make_async_copy(table_ref.at[usual], lists_ref.at[usual], sem)
    move.start()
    when_wanted()
    move.wait()
    rows = lists_ref.shape[0] - (SUBLANES + LIST_ROWS)
    if rows > 0:

        @pl.when(lists_ref[0, LANES - 1] > LIST_ROWS)
        def _():
            rest = pl.ds(SUBLANES + LIST_ROWS, rows)
            more = pltpu.make_async_copy(table_ref.at[rest], lists_ref.at[rest], sem)
            more.start()
            more.wait()


def device_place(blocks, parts, whole):
    region, device = lax.axis_index("region"), lax.axis_index("dev")
    region_blocks = lax.axis_size("dev") * blocks
    first_window = 0 if whole else (region - 1) * region_blocks
    first_own = region * region_blocks + device * blocks
    part = lax.rem(device, parts)
    return first_window, first_own - part * blocks, first_own, part


def radii_kernel(
    blocks,
    slots,
    twins,
    whole,
    order,
    *refs,
):
    arrived_refs, refs = refs[:twins], refs[twins:]
    copies_ref, table_ref, window_ref, columns_ref, types_ref, partner_ref, total_ref, *refs = refs
    turned_ref, packed_ref, near_ref, lists_ref, items_ref, lists_sem = refs
    _, homes, groups, _, _ = columns_ref.shape
    chunk = groups * SUBLANES
    window = types_ref.shape[0]
    parts = homes // blocks
    together = max(1, LANES // chunk)
    first_window, home_id, _, part = device_place(blocks, parts, whole)
    first_home = pl.multiple_of(home_id - first_window, homes)
    first_atom = pl.multiple_of(part * chunk, chunk)

    tables = [window_ref.at[WINDOW_X], window_ref.at[WINDOW_Y], window_ref.at[WINDOW_Z]]
    tables += [types_ref, window_ref.at[WINDOW_CHARGE], partner_ref]
    odd = lax.rem(lax.axis_index("dev"), 2) == 1
    for place, pair in enumerate(order):
        for field, table in enumerate(tables):
            rows = [ref[place, field * blocks : (field + 1) * blocks, :] for ref in arrived_refs]
            if twins == 2:
                rows = [jnp.where(odd, rows[1], rows[0]), jnp.where(odd, rows[0], rows[1])]
            first = pair * twins * blocks
            table[first : first + twins * blocks, :] = jnp.concatenate(rows, axis=0)
    if partner_ref.shape[0] > window:
        spare = (partner_ref.shape[0] - window, LANES)
        partner_ref[window:, :] = jnp.full(spare, EMPTY_SLOT, jnp.float32)
    def scaled_radii():
        _, _, scaled = type_fields(types_ref[...])
        window_ref[WINDOW_SCALED, 0:window, :] = 0.25 * scaled
        for field in range(WINDOW_COUNT):
            filler = FAR_AWAY if field == WINDOW_X else 0.0
            window_ref[field, window : window + SUBLANES, :] = jnp.full((SUBLANES, LANES), filler, jnp.float32)

    def home_columns():
        scaled_radii()
        home_rows = [window_ref[field, pl.ds(first_home, homes), :] for field in range(3)]
        turned_ref[...] = turned(jnp.concatenate([types_ref[pl.ds(first_home, homes), :]] + home_rows, axis=0))
        columns = turned_ref[pl.ds(first_atom, chunk), :]
        _, rho, _ = type_fields(columns)
        for home in range(homes):
            columns_ref[0, home] = spread(0.25 * rho, home)
            for index in range(1, 4):
                columns_ref[index, home] = spread(columns, index * homes + home)

    def pair_distance(home, step, rows):
        dx = columns_ref[1, home, step] - rows[0]
        dy = columns_ref[2, home, step] - rows[1]
        dz = columns_ref[3, home, step] - rows[2]
        return dx * dx + dy * dy + dz * dz

    steps = [pl.ds(start, STEP) for start in range(0, groups, STEP)]

    shift = lists_ref.shape[0].bit_length()
    usual = 8

    def list_items(home, filled):
        turns = (lists_ref[0, home] + (together - 1)) // together

        def put(index, carry):
            items_ref[filled + index] = (home << shift) + index * together
            return carry

        for index in range(usual):
            put(index, 0)
        lax.fori_loop(usual, turns, put, 0)
        return filled + turns

    def own_sweep(integral):
        near_ref[...] = jnp.full(near_ref.shape, FAR_AWAY, jnp.float32)
        own_together = min(homes, 2 * together)

        def own_pairs(turn, carry):
            for index in range(own_together):
                home = turn * own_together + index
                rows = [row_of(window_ref, field, first_home + home) for field in range(4)]
                for start, step in zip(range(0, groups, STEP), steps):
                    same = diagonal(STEP, first_atom + start * SUBLANES)
                    squared = jnp.where(same, FAR_AWAY, pair_distance(home, step, rows))
                    term = integral(squared, columns_ref[0, home, step], rows[3])
                    total_ref[home, step] = jnp.where(same, 0.0, term)
                    near_ref[...] = jnp.minimum(near_ref[...], squared)
            return carry

        lax.fori_loop(0, homes // own_together, own_pairs, 0)

    def sweep(integral, item_count):
        def visit(turn, nearest):
            sums = []
            for index in range(ITEMS):
                item = items_ref[turn * ITEMS + index]
                line, entry = item >> shift, item & ((1 << shift) - 1)
                home = jnp.minimum(line, homes - 1)
                parts_of = [None] * len(steps)
                for other in range(together):
                    partner = lists_ref[SUBLANES + entry + other, line]
                    rows = [row_of(window_ref, field, partner) for field in range(4)]
                    for place, step in enumerate(steps):
                        squared = pair_distance(home, step, rows)
                        nearest = jnp.minimum(nearest, squared)
                        term = integral(squared, columns_ref[0, home, step], rows[3])
                        parts_of[place] = term if other == 0 else parts_of[place] + term
                sums.append((home, parts_of))
            for home, parts_of in sums:
                for part, step in zip(parts_of, steps):
                    total_ref[home, step] += part
            return nearest

        near_ref[...] = lax.fori_loop(0, (item_count + (ITEMS - 1)) // ITEMS, visit, near_ref[...])
        lane = lax.broadcasted_iota(jnp.int32, (chunk, LANES), 1)
        packed = jnp.zeros((chunk, LANES), jnp.float32)
        for home in range(homes):
            packed = jnp.where(lane == home, lane_total(total_ref[home]), packed)
        packed_ref[...] = packed

    def meanwhile():
        home_columns()
        own_sweep(descreen)

    neighbour_lists(partner_ref, first_home, home_id, first_window, homes, slots, window, table_ref)
    move_lists(table_ref, lists_ref, lists_sem, meanwhile)
    intrinsic, rho, _ = type_fields(turned_ref[pl.ds(first_atom, chunk), :])
    item_count = lax.fori_loop(0, homes, list_items, 0)
    for index in range(ITEMS):
        items_ref[item_count + index] = homes << shift
    sweep(descreen, item_count)

    @pl.when(jnp.min(near_ref[...]) < short_range * short_range)
    def _():
        own_sweep(descreen_any)
        sweep(descreen_any, item_count)

    psi = (0.125 * packed_ref[...]) * rho
    shaped = born_alpha * psi - born_beta * psi * psi + born_gamma * psi * psi * psi
    radii = 1.0 / (1.0 / rho - jnp.tanh(shaped) / intrinsic)

    if chunk < LANES:
        radii = jnp.concatenate([radii, jnp.zeros((LANES - chunk, LANES), jnp.float32)], axis=0)
    turned_ref[...] = radii.T
    lane = lax.broadcasted_iota(jnp.int32, (blocks, LANES), 1)
    sent = turned_ref[pl.ds(0, blocks, stride=parts), :]
    for index in range(1, parts):
        rows = pltpu.roll(turned_ref[pl.ds(index, blocks, stride=parts), :], index * chunk, 1)
        sent = jnp.where(lane >= index * chunk, rows, sent)
    for copy in range(copies_ref.shape[0]):
        copies_ref[copy] = sent


def energy_kernel(
    parts,
    whole,
    order,
    table_ref,
    window_ref,
    gathered_ref,
    own_radii_ref,
    energy_ref,
    forces_ref,
    grad_ref,
    columns_ref,
    radii_ref,
    total_ref,
    lists_ref,
    lists_sem,
):
    devices, blocks, atoms = gathered_ref.shape
    window = devices * blocks
    part_rows = window // parts
    chunk = atoms // parts
    groups = atoms // SUBLANES
    first_window, _, own_id, part_here = device_place(blocks, parts, whole)
    first_own, list_lane = own_id - first_window, part_here * blocks
    fields = [(window_ref, field) for field in (WINDOW_X, WINDOW_Y, WINDOW_Z, WINDOW_CHARGE)] + [(radii_ref, 0)]

    def unpack():
        lane = lax.broadcasted_iota(jnp.int32, (part_rows, LANES), 1)
        pieces = [
            jnp.concatenate([gathered_ref[order.index(device)] for device in range(part, devices, parts)], axis=0)
            for part in range(parts)
        ]
        for place in range(parts):
            whole_rows = pieces[0] if place == 0 else pltpu.roll(pieces[0], (parts - place) * chunk, 1)
            for part in range(1, parts):
                shift = (part - place) % parts
                piece = pieces[part] if shift == 0 else pltpu.roll(pieces[part], shift * chunk, 1)
                whole_rows = jnp.where(lane >= part * chunk, piece, whole_rows)
            radii_ref[0, pl.ds(place, part_rows, stride=parts), :] = whole_rows
        radii_ref[0, window : window + SUBLANES, :] = jnp.ones((SUBLANES, LANES), jnp.float32)

    def own_rows(ref, field):
        return jnp.concatenate([ref[field, pl.ds(first_own + block, 1), :] for block in range(blocks)], axis=0)

    def pair_terms(block, step, rows, same=None):
        x, y, z, charge, radius = rows
        dx = columns_ref[block, step] - x
        dy = columns_ref[blocks + block, step] - y
        dz = columns_ref[2 * blocks + block, step] - z
        squared = dx * dx + dy * dy + dz * dz
        if same is not None:
            squared = jnp.where(same, 1.0, squared)
            charge = jnp.where(same, 0.0, charge)
        spread_sq = columns_ref[3 * blocks + block, step] * radius
        power = squared * pltpu.reciprocal(spread_sq, approx=True)
        quarter = 0.25 * jnp.exp(power)
        root_sq = squared - spread_sq * quarter
        inv_root = lax.rsqrt(root_sq)
        potential = charge * inv_root
        pull = (potential * pltpu.reciprocal(root_sq, approx=True)) * (1.0 - quarter)
        return (pull * dx, pull * dy, pull * dz, potential, pull * squared)

    def own_pairs():
        unpack()
        own_radii = own_rows(radii_ref, 0)
        own_radii_ref[...] = own_radii
        own = [own_rows(window_ref, field) for field in (WINDOW_X, WINDOW_Y, WINDOW_Z)]
        columns = turned(jnp.concatenate(own + [-4.0 * own_radii], axis=0))
        for index in range(4 * blocks):
            columns_ref[index] = spread(columns, index)
        for block in range(blocks):
            rows = [row_of(ref, field, first_own + block) for ref, field in fields]
            for start in range(0, groups, ENERGY_STEP):
                step = pl.ds(start, ENERGY_STEP)
                terms = pair_terms(block, step, rows, diagonal(ENERGY_STEP, start * SUBLANES))
                for term, value in enumerate(terms):
                    total_ref[term * blocks + block, step] = value

    move_lists(table_ref, lists_ref, lists_sem, own_pairs)
    for block in range(blocks):

        def visit(count, first, index, carry, block=block):
            partners = []
            for other in range(count):
                partner = lists_ref[SUBLANES + first + index * count + other, list_lane + block]
                partners.append([row_of(ref, field, partner) for ref, field in fields])
            for start in range(0, groups, ENERGY_STEP):
                step = pl.ds(start, ENERGY_STEP)
                sums = [total_ref[term * blocks + block, step] for term in range(5)]
                for rows in partners:
                    sums = [total + value for total, value in zip(sums, pair_terms(block, step, rows))]
                for term, value in enumerate(sums):
                    total_ref[term * blocks + block, step] = value
            return carry

        left = lists_ref[0, list_lane + block]
        first = 0
        for count in (4, 2, 1):
            turns = left // count
            lax.fori_loop(0, turns, functools.partial(visit, count, first), 0)
            first = first + turns * count
            left = left - turns * count
    sums = lane_sums([total_ref[index] for index in range(5 * blocks)], 5 * blocks)
    charges = own_rows(window_ref, WINDOW_CHARGE)
    own_decay = 1.0 / own_radii_ref[...]
    scale = solvent_tau * charges
    for axis in range(3):
        forces_ref[axis] = -scale * sums[axis * blocks : (axis + 1) * blocks]
    own_energy = 0.5 * scale * charges * own_decay
    energy_ref[...] = -0.5 * scale * sums[3 * blocks : 4 * blocks] - own_energy
    radial = sums[3 * blocks : 4 * blocks] - sums[4 * blocks : 5 * blocks]
    grad_ref[...] = (own_energy + 0.5 * scale * radial) * own_decay


def shards(positions, charges, types, pairs, owner_map):
    _, blocks, atoms = positions.shape
    regions = lax.axis_size("region")
    region_devices = lax.axis_size("dev")
    kept_regions, whole = window_regions(regions)
    devices = kept_regions * region_devices
    window = devices * blocks
    parts = atoms // CHUNK
    while region_devices % parts or 4 * parts * blocks > LANES:
        parts //= 2
    homes = parts * blocks
    chunk = atoms // parts

    vmem = pl.BlockSpec(memory_space=pltpu.VMEM)
    params = pltpu.CompilerParams(vmem_limit_bytes=40 * 1024 * 1024)
    copy_count = lax.axis_size(exchange_axes())
    twins = twin_count(region_devices)
    arrived = sent_to_both_twins(
        pl.pallas_call(
            functools.partial(fields_kernel, blocks, atoms),
            out_shape=jax.ShapeDtypeStruct((copy_count // twins, ROW_COUNT, blocks, atoms), jnp.float32),
            in_specs=[pl.BlockSpec(memory_space=pltpu.HBM)] * 5,
            out_specs=vmem,
            scratch_shapes=[
                pltpu.VMEM(positions.shape, positions.dtype),
                pltpu.VMEM(types.shape, types.dtype),
                pltpu.VMEM(charges.shape, charges.dtype),
                pltpu.SMEM(pairs.shape, pairs.dtype),
                pltpu.SMEM(owner_map.shape, owner_map.dtype),
                pltpu.SemaphoreType.DMA((5,)),
            ],
        )(positions, types, charges, pairs, owner_map)
    )
    arrived = [with_other_regions(part).reshape(devices // twins, ROW_COUNT * blocks, atoms) for part in arrived]
    padded = -(-window // LANES) * LANES
    table = jax.ShapeDtypeStruct((SUBLANES + padded, LANES), jnp.int32)
    exchange_regions = copy_count // region_devices
    order = [
        region * copy_count + place
        for region in range(kept_regions // exchange_regions)
        for place in reversed(range(copy_count))
    ]
    pair_order = [device // twins for device in order if device % twins == 0]
    fields = jax.ShapeDtypeStruct((WINDOW_COUNT, window + SUBLANES, atoms), jnp.float32)
    copies, lists, window_fields = pl.pallas_call(
        functools.partial(radii_kernel, blocks, pairs.shape[1], twins, whole, pair_order),
        out_shape=(jax.ShapeDtypeStruct((copy_count, blocks, atoms), jnp.float32), table, fields),
        in_specs=[vmem] * twins,
        out_specs=(vmem, vmem, vmem),
        scratch_shapes=[
            pltpu.VMEM((4, homes, chunk // SUBLANES, SUBLANES, LANES), jnp.float32),
            pltpu.VMEM((window, atoms), jnp.float32),
            pltpu.VMEM((padded, atoms), jnp.float32),
            pltpu.VMEM((homes, chunk // SUBLANES, SUBLANES, LANES), jnp.float32),
            pltpu.VMEM((LANES, LANES), jnp.float32),
            pltpu.VMEM((chunk, LANES), jnp.float32),
            pltpu.VMEM((STEP, SUBLANES, LANES), jnp.float32),
            pltpu.SMEM(table.shape, jnp.int32),
            pltpu.SMEM((homes * (padded // max(1, LANES // chunk) + 1) + 64,), jnp.int32),
            pltpu.SemaphoreType.DMA(()),
        ],
        compiler_params=params,
    )(*arrived)
    block_out = jax.ShapeDtypeStruct((blocks, atoms), jnp.float32)
    window_radii = with_other_regions(sent_directly(copies))
    own_radii, energy, forces, grad = pl.pallas_call(
        functools.partial(energy_kernel, parts, whole, order),
        out_shape=(block_out, block_out, jax.ShapeDtypeStruct((3, blocks, atoms), jnp.float32), block_out),
        in_specs=[pl.BlockSpec(memory_space=pl.ANY), vmem, vmem],
        out_specs=(vmem, vmem, vmem, vmem),
        scratch_shapes=[
            pltpu.VMEM((4 * blocks, atoms // SUBLANES, SUBLANES, LANES), jnp.float32),
            pltpu.VMEM((1, window + SUBLANES, atoms), jnp.float32),
            pltpu.VMEM((5 * blocks, atoms // SUBLANES, SUBLANES, LANES), jnp.float32),
            pltpu.SMEM(table.shape, jnp.int32),
            pltpu.SemaphoreType.DMA(()),
        ],
        compiler_params=params,
    )(lists, window_fields, window_radii)
    return own_radii, energy, forces, grad


def solution(mesh):
    placed = (
        P(None, ("region", "dev"), None),
        P(("region", "dev"), None),
        P(("region", "dev"), None),
        P(("region", "dev"), None),
        P(),
    )
    return jax.shard_map(
        shards,
        mesh=mesh,
        in_specs=placed,
        out_specs=(
            P(("region", "dev"), None),
            P(("region", "dev"), None),
            P(None, ("region", "dev"), None),
            P(("region", "dev"), None),
        ),
        check_vma=False,
    )
```

```python
import functools

import jax
import jax.numpy as jnp
from jax import lax
from jax.experimental import pallas as pl
from jax.experimental.pallas import tpu as pltpu
from jax.sharding import PartitionSpec as P

type_radii = (1.2, 1.7, 1.55, 1.52, 1.85, 1.8)
type_scales = (0.85, 0.72, 0.79, 0.85, 0.86, 0.96)
radius_offset = 0.09
born_alpha = 1.0
born_beta = 0.8
born_gamma = 4.85
solvent_tau = 1.0 - 1.0 / 78.5

ROW_X, ROW_Y, ROW_Z, ROW_TYPE, ROW_CHARGE, ROW_PARTNER, ROW_COUNT = range(7)
WINDOW_X, WINDOW_Y, WINDOW_Z, WINDOW_SCALED, WINDOW_CHARGE, WINDOW_COUNT = range(6)
LANES = 128
SUBLANES = 8
STEP = 4
ENERGY_STEP = 2
CHUNK = 32
LIST_ROWS = 32
PARTNERS = 2
ITEMS = 8
EMPTY_SLOT = -1.0e6
FAR_AWAY = 1.0e15

scaled_values = [scale * (radius - radius_offset) for radius, scale in zip(type_radii, type_scales)]
short_range = 1.01 * max(
    max(scaled_values) - (min(type_radii) - radius_offset),
    (max(type_radii) - radius_offset) - min(scaled_values),
    0.5,
)


def window_regions(region_count):
    return (region_count, True) if region_count <= 3 else (3, False)


def exchange_axes():
    return ("region", "dev") if window_regions(lax.axis_size("region"))[1] else ("dev",)


def sent_directly(copies):
    return lax.all_to_all(copies, exchange_axes(), split_axis=0, concat_axis=0, tiled=True)


def twin_count(device_count):
    return 2 - device_count % 2


def sent_to_both_twins(copies):
    count = lax.axis_size("dev")
    twins = twin_count(count)
    axes = exchange_axes()
    regions = lax.axis_size(axes) // count
    alike = [list(reversed(range(parity, regions * count, twins))) for parity in range(twins)]
    here = lax.all_to_all(copies, axes, split_axis=0, concat_axis=0, axis_index_groups=alike, tiled=True)
    if twins == 1:
        return [here]
    return [here, lax.ppermute(here, "dev", [(i, i ^ 1) for i in range(count)])]


def with_other_regions(here):
    regions = lax.axis_size("region")
    if window_regions(regions)[1]:
        return here
    below = lax.ppermute(here, "region", [(i, i + 1) for i in range(regions - 1)])
    above = lax.ppermute(here, "region", [(i + 1, i) for i in range(regions - 1)])
    return jnp.concatenate([below, here, above], axis=0)


def by_type(types, table):
    value = jnp.full(types.shape, table[0], jnp.float32)
    for index in range(1, len(table)):
        value = jnp.where(types == index, jnp.float32(table[index]), value)
    return value


def type_fields(types):
    intrinsic = by_type(types, type_radii)
    rho = intrinsic - radius_offset
    return intrinsic, rho, by_type(types, type_scales) * rho


def turned(rows):
    count, width = rows.shape
    if count < LANES:
        rows = jnp.concatenate([rows, jnp.zeros((LANES - count, width), rows.dtype)], axis=0)
    return rows.T


def spread(columns, index):
    count = columns.shape[0]
    wide = jnp.broadcast_to(columns[:, index : index + 1], (count, LANES))
    return wide.reshape(count // SUBLANES, SUBLANES, LANES)


def row_of(ref, field, row):
    return ref[field, pl.ds(row, SUBLANES, stride=0), :][None]


def diagonal(groups, first_atom):
    shape = (groups, SUBLANES, LANES)
    row = lax.broadcasted_iota(jnp.int32, shape, 0) * SUBLANES + lax.broadcasted_iota(jnp.int32, shape, 1)
    return row + first_atom == lax.broadcasted_iota(jnp.int32, shape, 2)


def lane_total(array):
    return jnp.sum(array.reshape(-1, LANES), axis=1, keepdims=True)


def lane_sums(arrays, count):
    atoms = arrays[0].shape[0] * SUBLANES
    lane = lax.broadcasted_iota(jnp.int32, (atoms, LANES), 1)
    packed = jnp.zeros((atoms, LANES), jnp.float32)
    for index, array in enumerate(arrays):
        packed = jnp.where(lane == index, lane_total(array), packed)
    return packed.T[:count]


def fields_kernel(blocks, atoms, *refs):
    inputs, copies_ref, here, sems = refs[:5], refs[5], refs[6:11], refs[11]
    moves = [pltpu.make_async_copy(src, dst, sems.at[i]) for i, (src, dst) in enumerate(zip(inputs, here))]
    for move in moves:
        move.start()
    for move in moves:
        move.wait()
    positions_ref, types_ref, charges_ref, pairs_ref, owner_ref = here
    slot = lax.broadcasted_iota(jnp.int32, (1, atoms), 1)
    partners = []
    for block in range(blocks):
        row = jnp.full((1, atoms), EMPTY_SLOT, jnp.float32)
        for index in range(pairs_ref.shape[1]):
            cell = pairs_ref[block, index]
            partner = jnp.where(cell >= 0, owner_ref[jnp.maximum(cell, 0)] + 1, int(EMPTY_SLOT))
            row = jnp.where(slot == index, partner.astype(jnp.float32), row)
        partners.append(row)
    rows = [positions_ref[axis] for axis in range(3)]
    rows += [types_ref[...].astype(jnp.float32), charges_ref[...], jnp.concatenate(partners, axis=0)]
    for copy in range(copies_ref.shape[0]):
        for index, row in enumerate(rows):
            copies_ref[copy, index] = row


def descreen(squared, rho, scaled):
    inv_dist = lax.rsqrt(squared)
    share = scaled * inv_dist
    inner = 0.25 - share
    high = 0.25 + share
    low = jnp.maximum(rho * inv_dist, inner)
    inv_low = pltpu.reciprocal(low, approx=True)
    ratio = low * pltpu.reciprocal(high, approx=True)
    curve = (1.0 - ratio) + inner * (ratio - high * inv_low)
    return (inv_low * curve + 2.0 * jnp.log(ratio)) * inv_dist


def descreen_any(squared, rho, scaled):
    rho, scaled = 4.0 * rho, 4.0 * scaled
    inv_dist = lax.rsqrt(squared)
    distance = squared * inv_dist
    high = distance + scaled
    gap = distance - scaled
    low = jnp.maximum(rho, jnp.abs(gap))
    inv_low = 1.0 / low
    inv_high = 1.0 / high
    quarter = 0.25 * inv_dist
    curve = (squared - scaled * scaled) * quarter
    body = (0.5 * (inv_low - inv_high)) * (1.0 - (inv_low + inv_high) * curve)
    body = body + jnp.log(low * inv_high) * quarter
    body = body + jnp.where(rho < -gap, 1.0 / rho - inv_low, 0.0)
    return jnp.where(high > rho, 8.0 * body, 0.0)


def neighbour_lists(partner_ref, first_home, home_id, first_window, homes, slots, filler, table_ref):
    window = partner_ref.shape[0]
    tiles = [slice(start, start + LANES) for start in range(0, window, LANES)]
    depth = -(-slots // SUBLANES) * SUBLANES
    ids = jnp.concatenate([partner_ref[tile, :].T[:depth] for tile in tiles], axis=1)
    lists = turned(partner_ref[pl.ds(first_home, homes), :])[:depth]
    lane = lax.broadcasted_iota(jnp.int32, (depth, window), 1)
    lane_id = (lane + (first_window + 1)).astype(jnp.float32)
    rows = []
    for home in range(homes):
        own = (home_id + home + 1).astype(jnp.float32)
        linked = (ids == own) | (lane_id == lists[:, home : home + 1])
        rows.append(jnp.max(jnp.where(linked, 1.0, 0.0), axis=0, keepdims=True))
    linked = jnp.concatenate(rows, axis=0)
    before = lax.broadcasted_iota(jnp.int32, (window, window), 0)
    after = lax.broadcasted_iota(jnp.int32, (window, window), 1)
    ramp = jnp.where(before <= after, 1.0, 0.0).astype(jnp.bfloat16)
    rank = jnp.dot(linked.astype(jnp.bfloat16), ramp, preferred_element_type=jnp.float32)
    place = jnp.where(linked > 0.0, rank, 0.0)
    total = jnp.sum(linked, axis=1, keepdims=True)
    name = lax.broadcasted_iota(jnp.int32, (LIST_ROWS, window), 1).astype(jnp.float32)
    spot = lax.broadcasted_iota(jnp.int32, (LIST_ROWS, window), 0).astype(jnp.float32)
    own_lane = lax.broadcasted_iota(jnp.int32, (LIST_ROWS, LANES), 1)

    def some_rows(start):
        first = jnp.asarray(start + 1).astype(jnp.float32)
        packed = jnp.zeros((LIST_ROWS, LANES), jnp.float32)
        for home in range(homes):
            hit = place[home : home + 1] == spot + first
            found = jnp.sum(jnp.where(hit, name - float(filler), 0.0), axis=1, keepdims=True)
            packed = jnp.where(own_lane == home, found, packed)
        rows = pl.ds(pl.multiple_of(SUBLANES + start, SUBLANES), LIST_ROWS)
        table_ref[rows, :] = packed.astype(jnp.int32) + filler

    counts = jnp.zeros((SUBLANES, LANES), jnp.float32)
    lane = lax.broadcasted_iota(jnp.int32, (SUBLANES, LANES), 1)
    for home in range(homes):
        counts = jnp.where(lane == home, total[home : home + 1], counts)
    longest = jnp.max(total)
    table_ref[0:SUBLANES, :] = jnp.where(lane == LANES - 1, longest, counts).astype(jnp.int32)
    some_rows(0)

    def more_rows(turn, carry):
        some_rows(turn * LIST_ROWS)
        return carry

    lax.fori_loop(1, (longest.astype(jnp.int32) + (LIST_ROWS - 1)) // LIST_ROWS, more_rows, 0)


def move_lists(table_ref, lists_ref, sem, when_wanted):
    usual = pl.ds(0, SUBLANES + LIST_ROWS)
    move = pltpu.make_async_copy(table_ref.at[usual], lists_ref.at[usual], sem)
    move.start()
    when_wanted()
    move.wait()
    rows = lists_ref.shape[0] - (SUBLANES + LIST_ROWS)
    if rows > 0:

        @pl.when(lists_ref[0, LANES - 1] > LIST_ROWS)
        def _():
            rest = pl.ds(SUBLANES + LIST_ROWS, rows)
            more = pltpu.make_async_copy(table_ref.at[rest], lists_ref.at[rest], sem)
            more.start()
            more.wait()


def device_place(blocks, parts, whole):
    region, device = lax.axis_index("region"), lax.axis_index("dev")
    region_blocks = lax.axis_size("dev") * blocks
    first_window = 0 if whole else (region - 1) * region_blocks
    first_own = region * region_blocks + device * blocks
    part = lax.rem(device, parts)
    return first_window, first_own - part * blocks, first_own, part


def radii_kernel(
    blocks,
    slots,
    twins,
    whole,
    order,
    *refs,
):
    arrived_refs, refs = refs[:twins], refs[twins:]
    copies_ref, table_ref, window_ref, columns_ref, types_ref, partner_ref, total_ref, *refs = refs
    turned_ref, packed_ref, near_ref, lists_ref, items_ref, lists_sem = refs
    _, homes, groups, _, _ = columns_ref.shape
    chunk = groups * SUBLANES
    window = types_ref.shape[0]
    parts = homes // blocks
    together = PARTNERS
    first_window, home_id, _, part = device_place(blocks, parts, whole)
    first_home = pl.multiple_of(home_id - first_window, homes)
    first_atom = pl.multiple_of(part * chunk, chunk)

    tables = [window_ref.at[WINDOW_X], window_ref.at[WINDOW_Y], window_ref.at[WINDOW_Z]]
    tables += [types_ref, window_ref.at[WINDOW_CHARGE], partner_ref]
    odd = lax.rem(lax.axis_index("dev"), 2) == 1
    for place, pair in enumerate(order):
        for field, table in enumerate(tables):
            rows = [ref[place, field * blocks : (field + 1) * blocks, :] for ref in arrived_refs]
            if twins == 2:
                rows = [jnp.where(odd, rows[1], rows[0]), jnp.where(odd, rows[0], rows[1])]
            first = pair * twins * blocks
            table[first : first + twins * blocks, :] = jnp.concatenate(rows, axis=0)
    if partner_ref.shape[0] > window:
        spare = (partner_ref.shape[0] - window, LANES)
        partner_ref[window:, :] = jnp.full(spare, EMPTY_SLOT, jnp.float32)
    def scaled_radii():
        _, _, scaled = type_fields(types_ref[...])
        window_ref[WINDOW_SCALED, 0:window, :] = 0.25 * scaled
        for field in range(WINDOW_COUNT):
            filler = FAR_AWAY if field == WINDOW_X else 0.0
            window_ref[field, window : window + SUBLANES, :] = jnp.full((SUBLANES, LANES), filler, jnp.float32)

    def home_columns():
        scaled_radii()
        home_rows = [window_ref[field, pl.ds(first_home, homes), :] for field in range(3)]
        turned_ref[...] = turned(jnp.concatenate([types_ref[pl.ds(first_home, homes), :]] + home_rows, axis=0))
        columns = turned_ref[pl.ds(first_atom, chunk), :]
        _, rho, _ = type_fields(columns)
        for home in range(homes):
            columns_ref[0, home] = spread(0.25 * rho, home)
            for index in range(1, 4):
                columns_ref[index, home] = spread(columns, index * homes + home)

    def pair_distance(home, step, rows):
        dx = columns_ref[1, home, step] - rows[0]
        dy = columns_ref[2, home, step] - rows[1]
        dz = columns_ref[3, home, step] - rows[2]
        return dx * dx + dy * dy + dz * dz

    steps = [pl.ds(start, STEP) for start in range(0, groups, STEP)]

    shift = lists_ref.shape[0].bit_length()
    usual = 16 // PARTNERS + 6

    def list_items(home, filled):
        turns = (lists_ref[0, home] + (together - 1)) // together

        def put(index, carry):
            items_ref[filled + index] = (home << shift) + index * together
            return carry

        for index in range(usual):
            put(index, 0)
        lax.fori_loop(usual, turns, put, 0)
        return filled + turns

    def own_sweep(integral):
        near_ref[...] = jnp.full(near_ref.shape, FAR_AWAY, jnp.float32)
        own_together = min(homes, 2 * LANES // chunk)

        def own_pairs(turn, carry):
            for index in range(own_together):
                home = turn * own_together + index
                rows = [row_of(window_ref, field, first_home + home) for field in range(4)]
                for start, step in zip(range(0, groups, STEP), steps):
                    same = diagonal(STEP, first_atom + start * SUBLANES)
                    squared = jnp.where(same, FAR_AWAY, pair_distance(home, step, rows))
                    term = integral(squared, columns_ref[0, home, step], rows[3])
                    total_ref[home, step] = jnp.where(same, 0.0, term)
                    near_ref[...] = jnp.minimum(near_ref[...], squared)
            return carry

        lax.fori_loop(0, homes // own_together, own_pairs, 0)

    def sweep(integral, item_count):
        def visit(turn, nearest):
            sums = []
            for index in range(ITEMS):
                item = items_ref[turn * ITEMS + index]
                line, entry = item >> shift, item & ((1 << shift) - 1)
                home = jnp.minimum(line, homes - 1)
                parts_of = [None] * len(steps)
                for other in range(together):
                    partner = lists_ref[SUBLANES + entry + other, line]
                    rows = [row_of(window_ref, field, partner) for field in range(4)]
                    for place, step in enumerate(steps):
                        squared = pair_distance(home, step, rows)
                        nearest = jnp.minimum(nearest, squared)
                        term = integral(squared, columns_ref[0, home, step], rows[3])
                        parts_of[place] = term if other == 0 else parts_of[place] + term
                sums.append((home, parts_of))
            for home, parts_of in sums:
                for part, step in zip(parts_of, steps):
                    total_ref[home, step] += part
            return nearest

        near_ref[...] = lax.fori_loop(0, (item_count + (ITEMS - 1)) // ITEMS, visit, near_ref[...])
        lane = lax.broadcasted_iota(jnp.int32, (chunk, LANES), 1)
        packed = jnp.zeros((chunk, LANES), jnp.float32)
        for home in range(homes):
            packed = jnp.where(lane == home, lane_total(total_ref[home]), packed)
        packed_ref[...] = packed

    def meanwhile():
        home_columns()
        own_sweep(descreen)

    neighbour_lists(partner_ref, first_home, home_id, first_window, homes, slots, window, table_ref)
    move_lists(table_ref, lists_ref, lists_sem, meanwhile)
    intrinsic, rho, _ = type_fields(turned_ref[pl.ds(first_atom, chunk), :])
    item_count = lax.fori_loop(0, homes, list_items, 0)
    for index in range(ITEMS):
        items_ref[item_count + index] = homes << shift
    sweep(descreen, item_count)

    @pl.when(jnp.min(near_ref[...]) < short_range * short_range)
    def _():
        own_sweep(descreen_any)
        sweep(descreen_any, item_count)

    psi = (0.125 * packed_ref[...]) * rho
    shaped = born_alpha * psi - born_beta * psi * psi + born_gamma * psi * psi * psi
    radii = 1.0 / (1.0 / rho - jnp.tanh(shaped) / intrinsic)

    if chunk < LANES:
        radii = jnp.concatenate([radii, jnp.zeros((LANES - chunk, LANES), jnp.float32)], axis=0)
    turned_ref[...] = radii.T
    lane = lax.broadcasted_iota(jnp.int32, (blocks, LANES), 1)
    sent = turned_ref[pl.ds(0, blocks, stride=parts), :]
    for index in range(1, parts):
        rows = pltpu.roll(turned_ref[pl.ds(index, blocks, stride=parts), :], index * chunk, 1)
        sent = jnp.where(lane >= index * chunk, rows, sent)
    for copy in range(copies_ref.shape[0]):
        copies_ref[copy] = sent


def energy_kernel(
    parts,
    whole,
    table_ref,
    window_ref,
    gathered_ref,
    own_radii_ref,
    energy_ref,
    forces_ref,
    grad_ref,
    columns_ref,
    radii_ref,
    total_ref,
    lists_ref,
    lists_sem,
):
    devices, blocks, atoms = gathered_ref.shape
    window = devices * blocks
    part_rows = window // parts
    chunk = atoms // parts
    groups = atoms // SUBLANES
    first_window, _, own_id, part_here = device_place(blocks, parts, whole)
    first_own, list_lane = own_id - first_window, part_here * blocks
    fields = [(window_ref, field) for field in (WINDOW_X, WINDOW_Y, WINDOW_Z, WINDOW_CHARGE)] + [(radii_ref, 0)]

    def unpack():
        lane = lax.broadcasted_iota(jnp.int32, (part_rows, LANES), 1)
        pieces = [
            gathered_ref[pl.ds(part, devices // parts, stride=parts)].reshape(part_rows, atoms)
            for part in range(parts)
        ]
        for place in range(parts):
            whole_rows = pieces[0] if place == 0 else pltpu.roll(pieces[0], (parts - place) * chunk, 1)
            for part in range(1, parts):
                shift = (part - place) % parts
                piece = pieces[part] if shift == 0 else pltpu.roll(pieces[part], shift * chunk, 1)
                whole_rows = jnp.where(lane >= part * chunk, piece, whole_rows)
            radii_ref[0, pl.ds(place, part_rows, stride=parts), :] = whole_rows
        radii_ref[0, window : window + SUBLANES, :] = jnp.ones((SUBLANES, LANES), jnp.float32)

    def own_rows(ref, field):
        return jnp.concatenate([ref[field, pl.ds(first_own + block, 1), :] for block in range(blocks)], axis=0)

    def home_columns(block, start):
        return [columns_ref[field * blocks + block, pl.ds(start, ENERGY_STEP)] for field in range(4)]

    def pair_terms(home, rows, same=None):
        x, y, z, charge, radius = rows
        dx = home[0] - x
        dy = home[1] - y
        dz = home[2] - z
        squared = dx * dx + dy * dy + dz * dz
        if same is not None:
            squared = jnp.where(same, 1.0, squared)
            charge = jnp.where(same, 0.0, charge)
        spread_sq = home[3] * radius
        power = squared * pltpu.reciprocal(spread_sq, approx=True)
        quarter = 0.25 * jnp.exp(power)
        root_sq = squared - spread_sq * quarter
        inv_root = lax.rsqrt(root_sq)
        potential = charge * inv_root
        pull = (potential * pltpu.reciprocal(root_sq, approx=True)) * (1.0 - quarter)
        return (pull * dx, pull * dy, pull * dz, potential, pull * squared)

    def own_pairs():
        unpack()
        own_radii = own_rows(radii_ref, 0)
        own_radii_ref[...] = own_radii
        own = [own_rows(window_ref, field) for field in (WINDOW_X, WINDOW_Y, WINDOW_Z)]
        columns = turned(jnp.concatenate(own + [-4.0 * own_radii], axis=0))
        for index in range(4 * blocks):
            columns_ref[index] = spread(columns, index)
        for block in range(blocks):
            rows = [row_of(ref, field, first_own + block) for ref, field in fields]
            for start in range(0, groups, ENERGY_STEP):
                step = pl.ds(start, ENERGY_STEP)
                terms = pair_terms(home_columns(block, start), rows, diagonal(ENERGY_STEP, start * SUBLANES))
                for term, value in enumerate(terms):
                    total_ref[term * blocks + block, step] = value

    move_lists(table_ref, lists_ref, lists_sem, own_pairs)
    for block in range(blocks):

        def visit(count, first, index, carry, block=block):
            partners = []
            for other in range(count):
                partner = lists_ref[SUBLANES + first + index * count + other, list_lane + block]
                partners.append([row_of(ref, field, partner) for ref, field in fields])
            for start in range(0, groups, ENERGY_STEP):
                step = pl.ds(start, ENERGY_STEP)
                home = home_columns(block, start)
                sums = [total_ref[term * blocks + block, step] for term in range(5)]
                for rows in partners:
                    sums = [total + value for total, value in zip(sums, pair_terms(home, rows))]
                for term, value in enumerate(sums):
                    total_ref[term * blocks + block, step] = value
            return carry

        left = lists_ref[0, list_lane + block]
        first = 0
        for count in (4, 2, 1):
            turns = left // count
            lax.fori_loop(0, turns, functools.partial(visit, count, first), 0)
            first = first + turns * count
            left = left - turns * count
    sums = lane_sums([total_ref[index] for index in range(5 * blocks)], 5 * blocks)
    charges = own_rows(window_ref, WINDOW_CHARGE)
    own_decay = 1.0 / own_radii_ref[...]
    scale = solvent_tau * charges
    for axis in range(3):
        forces_ref[axis] = -scale * sums[axis * blocks : (axis + 1) * blocks]
    own_energy = 0.5 * scale * charges * own_decay
    energy_ref[...] = -0.5 * scale * sums[3 * blocks : 4 * blocks] - own_energy
    radial = sums[3 * blocks : 4 * blocks] - sums[4 * blocks : 5 * blocks]
    grad_ref[...] = (own_energy + 0.5 * scale * radial) * own_decay


def shards(positions, charges, types, pairs, owner_map):
    _, blocks, atoms = positions.shape
    regions = lax.axis_size("region")
    region_devices = lax.axis_size("dev")
    kept_regions, whole = window_regions(regions)
    devices = kept_regions * region_devices
    window = devices * blocks
    parts = atoms // CHUNK
    while region_devices % parts or 4 * parts * blocks > LANES:
        parts //= 2
    homes = parts * blocks
    chunk = atoms // parts

    vmem = pl.BlockSpec(memory_space=pltpu.VMEM)
    params = pltpu.CompilerParams(vmem_limit_bytes=40 * 1024 * 1024)
    copy_count = lax.axis_size(exchange_axes())
    twins = twin_count(region_devices)
    arrived = sent_to_both_twins(
        pl.pallas_call(
            functools.partial(fields_kernel, blocks, atoms),
            out_shape=jax.ShapeDtypeStruct((copy_count // twins, ROW_COUNT, blocks, atoms), jnp.float32),
            in_specs=[pl.BlockSpec(memory_space=pltpu.HBM)] * 5,
            out_specs=vmem,
            scratch_shapes=[
                pltpu.VMEM(positions.shape, positions.dtype),
                pltpu.VMEM(types.shape, types.dtype),
                pltpu.VMEM(charges.shape, charges.dtype),
                pltpu.SMEM(pairs.shape, pairs.dtype),
                pltpu.SMEM(owner_map.shape, owner_map.dtype),
                pltpu.SemaphoreType.DMA((5,)),
            ],
        )(positions, types, charges, pairs, owner_map)
    )
    arrived = [with_other_regions(part).reshape(devices // twins, ROW_COUNT * blocks, atoms) for part in arrived]
    padded = -(-window // LANES) * LANES
    table = jax.ShapeDtypeStruct((SUBLANES + padded, LANES), jnp.int32)
    pairs_sent = copy_count // twins
    pair_order = [
        first + place for first in range(0, devices // twins, pairs_sent) for place in reversed(range(pairs_sent))
    ]
    fields = jax.ShapeDtypeStruct((WINDOW_COUNT, window + SUBLANES, atoms), jnp.float32)
    copies, lists, window_fields = pl.pallas_call(
        functools.partial(radii_kernel, blocks, pairs.shape[1], twins, whole, pair_order),
        out_shape=(jax.ShapeDtypeStruct((copy_count, blocks, atoms), jnp.float32), table, fields),
        in_specs=[vmem] * twins,
        out_specs=(vmem, vmem, vmem),
        scratch_shapes=[
            pltpu.VMEM((4, homes, chunk // SUBLANES, SUBLANES, LANES), jnp.float32),
            pltpu.VMEM((window, atoms), jnp.float32),
            pltpu.VMEM((padded, atoms), jnp.float32),
            pltpu.VMEM((homes, chunk // SUBLANES, SUBLANES, LANES), jnp.float32),
            pltpu.VMEM((LANES, LANES), jnp.float32),
            pltpu.VMEM((chunk, LANES), jnp.float32),
            pltpu.VMEM((STEP, SUBLANES, LANES), jnp.float32),
            pltpu.SMEM(table.shape, jnp.int32),
            pltpu.SMEM((homes * (padded // PARTNERS + 1) + 64,), jnp.int32),
            pltpu.SemaphoreType.DMA(()),
        ],
        compiler_params=params,
    )(*arrived)
    block_out = jax.ShapeDtypeStruct((blocks, atoms), jnp.float32)
    window_radii = with_other_regions(sent_directly(copies))
    own_radii, energy, forces, grad = pl.pallas_call(
        functools.partial(energy_kernel, parts, whole),
        out_shape=(block_out, block_out, jax.ShapeDtypeStruct((3, blocks, atoms), jnp.float32), block_out),
        in_specs=[pl.BlockSpec(memory_space=pl.ANY), vmem, vmem],
        out_specs=(vmem, vmem, vmem, vmem),
        scratch_shapes=[
            pltpu.VMEM((4 * blocks, atoms // SUBLANES, SUBLANES, LANES), jnp.float32),
            pltpu.VMEM((1, window + SUBLANES, atoms), jnp.float32),
            pltpu.VMEM((5 * blocks, atoms // SUBLANES, SUBLANES, LANES), jnp.float32),
            pltpu.SMEM(table.shape, jnp.int32),
            pltpu.SemaphoreType.DMA(()),
        ],
        compiler_params=params,
    )(lists, window_fields, window_radii)
    return own_radii, energy, forces, grad


def solution(mesh):
    placed = (
        P(None, ("region", "dev"), None),
        P(("region", "dev"), None),
        P(("region", "dev"), None),
        P(("region", "dev"), None),
        P(),
    )
    return jax.shard_map(
        shards,
        mesh=mesh,
        in_specs=placed,
        out_specs=(
            P(("region", "dev"), None),
            P(("region", "dev"), None),
            P(None, ("region", "dev"), None),
            P(("region", "dev"), None),
        ),
        check_vma=False,
    )
```

```python
import functools

import jax
import jax.numpy as jnp
from jax import lax
from jax.experimental import pallas as pl
from jax.experimental.pallas import tpu as pltpu
from jax.sharding import PartitionSpec as P

type_radii = (1.2, 1.7, 1.55, 1.52, 1.85, 1.8)
type_scales = (0.85, 0.72, 0.79, 0.85, 0.86, 0.96)
radius_offset = 0.09
born_alpha = 1.0
born_beta = 0.8
born_gamma = 4.85
solvent_tau = 1.0 - 1.0 / 78.5

ROW_X, ROW_Y, ROW_Z, ROW_TYPE, ROW_CHARGE, ROW_PARTNER, ROW_COUNT = range(7)
WINDOW_X, WINDOW_Y, WINDOW_Z, WINDOW_SCALED, WINDOW_CHARGE, WINDOW_COUNT = range(6)
LANES = 128
SUBLANES = 8
STEP = 2
ENERGY_STEP = 4
CHUNK = 32
LIST_ROWS = 32
PARTNERS = 2
ITEMS = 8
EMPTY_SLOT = -1.0e6
FAR_AWAY = 1.0e15

scaled_values = [scale * (radius - radius_offset) for radius, scale in zip(type_radii, type_scales)]
short_range = 1.01 * max(
    max(scaled_values) - (min(type_radii) - radius_offset),
    (max(type_radii) - radius_offset) - min(scaled_values),
    0.5,
)


def window_regions(region_count):
    return (region_count, True) if region_count <= 3 else (3, False)


def exchange_axes():
    return ("region", "dev") if window_regions(lax.axis_size("region"))[1] else ("dev",)


def sent_directly(copies):
    return lax.all_to_all(copies, exchange_axes(), split_axis=0, concat_axis=0, tiled=True)


def twin_count(device_count):
    return 2 - device_count % 2


def sent_to_both_twins(copies):
    count = lax.axis_size("dev")
    twins = twin_count(count)
    axes = exchange_axes()
    regions = lax.axis_size(axes) // count
    alike = [list(reversed(range(parity, regions * count, twins))) for parity in range(twins)]
    here = lax.all_to_all(copies, axes, split_axis=0, concat_axis=0, axis_index_groups=alike, tiled=True)
    if twins == 1:
        return [here]
    return [here, lax.ppermute(here, "dev", [(i, i ^ 1) for i in range(count)])]


def with_other_regions(here):
    regions = lax.axis_size("region")
    if window_regions(regions)[1]:
        return here
    below = lax.ppermute(here, "region", [(i, i + 1) for i in range(regions - 1)])
    above = lax.ppermute(here, "region", [(i + 1, i) for i in range(regions - 1)])
    return jnp.concatenate([below, here, above], axis=0)


def by_type(types, table):
    value = jnp.full(types.shape, table[0], jnp.float32)
    for index in range(1, len(table)):
        value = jnp.where(types == index, jnp.float32(table[index]), value)
    return value


def type_fields(types):
    intrinsic = by_type(types, type_radii)
    rho = intrinsic - radius_offset
    return intrinsic, rho, by_type(types, type_scales) * rho


def turned(rows):
    count, width = rows.shape
    if count < LANES:
        rows = jnp.concatenate([rows, jnp.zeros((LANES - count, width), rows.dtype)], axis=0)
    return rows.T


def spread(columns, index):
    count = columns.shape[0]
    wide = jnp.broadcast_to(columns[:, index : index + 1], (count, LANES))
    return wide.reshape(count // SUBLANES, SUBLANES, LANES)


def row_of(ref, field, row):
    return ref[field, pl.ds(row, SUBLANES, stride=0), :][None]


def diagonal(groups, first_atom):
    shape = (groups, SUBLANES, LANES)
    row = lax.broadcasted_iota(jnp.int32, shape, 0) * SUBLANES + lax.broadcasted_iota(jnp.int32, shape, 1)
    return row + first_atom == lax.broadcasted_iota(jnp.int32, shape, 2)


def lane_total(array):
    return jnp.sum(array.reshape(-1, LANES), axis=1, keepdims=True)


def lane_sums(arrays, count):
    atoms = arrays[0].shape[0] * SUBLANES
    lane = lax.broadcasted_iota(jnp.int32, (atoms, LANES), 1)
    packed = jnp.zeros((atoms, LANES), jnp.float32)
    for index, array in enumerate(arrays):
        packed = jnp.where(lane == index, lane_total(array), packed)
    return packed.T[:count]


def fields_kernel(blocks, atoms, *refs):
    inputs, copies_ref, here, sems = refs[:5], refs[5], refs[6:11], refs[11]
    moves = [pltpu.make_async_copy(src, dst, sems.at[i]) for i, (src, dst) in enumerate(zip(inputs, here))]
    for move in moves:
        move.start()
    for move in moves:
        move.wait()
    positions_ref, types_ref, charges_ref, pairs_ref, owner_ref = here
    slot = lax.broadcasted_iota(jnp.int32, (1, atoms), 1)
    partners = []
    for block in range(blocks):
        row = jnp.full((1, atoms), EMPTY_SLOT, jnp.float32)
        for index in range(pairs_ref.shape[1]):
            cell = pairs_ref[block, index]
            partner = jnp.where(cell >= 0, owner_ref[jnp.maximum(cell, 0)] + 1, int(EMPTY_SLOT))
            row = jnp.where(slot == index, partner.astype(jnp.float32), row)
        partners.append(row)
    rows = [positions_ref[axis] for axis in range(3)]
    rows += [types_ref[...].astype(jnp.float32), charges_ref[...], jnp.concatenate(partners, axis=0)]
    for copy in range(copies_ref.shape[0]):
        for index, row in enumerate(rows):
            copies_ref[copy, index] = row


def descreen(squared, rho, scaled):
    inv_dist = lax.rsqrt(squared)
    share = scaled * inv_dist
    inner = 0.25 - share
    high = 0.25 + share
    low = jnp.maximum(rho * inv_dist, inner)
    inv_low = pltpu.reciprocal(low, approx=True)
    ratio = low * pltpu.reciprocal(high, approx=True)
    curve = (1.0 - ratio) + inner * (ratio - high * inv_low)
    return (inv_low * curve + 2.0 * jnp.log(ratio)) * inv_dist


def descreen_any(squared, rho, scaled):
    rho, scaled = 4.0 * rho, 4.0 * scaled
    inv_dist = lax.rsqrt(squared)
    distance = squared * inv_dist
    high = distance + scaled
    gap = distance - scaled
    low = jnp.maximum(rho, jnp.abs(gap))
    inv_low = 1.0 / low
    inv_high = 1.0 / high
    quarter = 0.25 * inv_dist
    curve = (squared - scaled * scaled) * quarter
    body = (0.5 * (inv_low - inv_high)) * (1.0 - (inv_low + inv_high) * curve)
    body = body + jnp.log(low * inv_high) * quarter
    body = body + jnp.where(rho < -gap, 1.0 / rho - inv_low, 0.0)
    return jnp.where(high > rho, 8.0 * body, 0.0)


def neighbour_lists(partner_ref, first_home, home_id, first_window, homes, slots, filler, table_ref):
    window = partner_ref.shape[0]
    tiles = [slice(start, start + LANES) for start in range(0, window, LANES)]
    depth = -(-slots // SUBLANES) * SUBLANES
    ids = jnp.concatenate([partner_ref[tile, :].T[:depth] for tile in tiles], axis=1)
    lists = turned(partner_ref[pl.ds(first_home, homes), :])[:depth]
    lane = lax.broadcasted_iota(jnp.int32, (depth, window), 1)
    lane_id = (lane + (first_window + 1)).astype(jnp.float32)
    rows = []
    for home in range(homes):
        own = (home_id + home + 1).astype(jnp.float32)
        linked = (ids == own) | (lane_id == lists[:, home : home + 1])
        rows.append(jnp.max(jnp.where(linked, 1.0, 0.0), axis=0, keepdims=True))
    linked = jnp.concatenate(rows, axis=0)
    before = lax.broadcasted_iota(jnp.int32, (window, window), 0)
    after = lax.broadcasted_iota(jnp.int32, (window, window), 1)
    ramp = jnp.where(before <= after, 1.0, 0.0).astype(jnp.bfloat16)
    rank = jnp.dot(linked.astype(jnp.bfloat16), ramp, preferred_element_type=jnp.float32)
    place = jnp.where(linked > 0.0, rank, 0.0)
    total = jnp.sum(linked, axis=1, keepdims=True)
    name = lax.broadcasted_iota(jnp.int32, (LIST_ROWS, window), 1).astype(jnp.float32)
    spot = lax.broadcasted_iota(jnp.int32, (LIST_ROWS, window), 0).astype(jnp.float32)
    own_lane = lax.broadcasted_iota(jnp.int32, (LIST_ROWS, LANES), 1)

    def some_rows(start):
        first = jnp.asarray(start + 1).astype(jnp.float32)
        packed = jnp.zeros((LIST_ROWS, LANES), jnp.float32)
        for home in range(homes):
            hit = place[home : home + 1] == spot + first
            found = jnp.sum(jnp.where(hit, name - float(filler), 0.0), axis=1, keepdims=True)
            packed = jnp.where(own_lane == home, found, packed)
        rows = pl.ds(pl.multiple_of(SUBLANES + start, SUBLANES), LIST_ROWS)
        table_ref[rows, :] = packed.astype(jnp.int32) + filler

    counts = jnp.zeros((SUBLANES, LANES), jnp.float32)
    lane = lax.broadcasted_iota(jnp.int32, (SUBLANES, LANES), 1)
    for home in range(homes):
        counts = jnp.where(lane == home, total[home : home + 1], counts)
    longest = jnp.max(total)
    table_ref[0:SUBLANES, :] = jnp.where(lane == LANES - 1, longest, counts).astype(jnp.int32)
    some_rows(0)

    def more_rows(turn, carry):
        some_rows(turn * LIST_ROWS)
        return carry

    lax.fori_loop(1, (longest.astype(jnp.int32) + (LIST_ROWS - 1)) // LIST_ROWS, more_rows, 0)


def move_lists(table_ref, lists_ref, sem, when_wanted):
    usual = pl.ds(0, SUBLANES + LIST_ROWS)
    move = pltpu.make_async_copy(table_ref.at[usual], lists_ref.at[usual], sem)
    move.start()
    when_wanted()
    move.wait()
    rows = lists_ref.shape[0] - (SUBLANES + LIST_ROWS)
    if rows > 0:

        @pl.when(lists_ref[0, LANES - 1] > LIST_ROWS)
        def _():
            rest = pl.ds(SUBLANES + LIST_ROWS, rows)
            more = pltpu.make_async_copy(table_ref.at[rest], lists_ref.at[rest], sem)
            more.start()
            more.wait()


def device_place(blocks, parts, whole):
    region, device = lax.axis_index("region"), lax.axis_index("dev")
    region_blocks = lax.axis_size("dev") * blocks
    first_window = 0 if whole else (region - 1) * region_blocks
    first_own = region * region_blocks + device * blocks
    part = lax.rem(device, parts)
    return first_window, first_own - part * blocks, first_own, part


def radii_kernel(
    blocks,
    slots,
    twins,
    whole,
    order,
    *refs,
):
    arrived_refs, refs = refs[:twins], refs[twins:]
    copies_ref, table_ref, window_ref, columns_ref, types_ref, partner_ref, total_ref, *refs = refs
    turned_ref, packed_ref, near_ref, lists_ref, items_ref, lists_sem = refs
    _, homes, groups, _, _ = columns_ref.shape
    chunk = groups * SUBLANES
    window = types_ref.shape[0]
    parts = homes // blocks
    together = PARTNERS
    first_window, home_id, _, part = device_place(blocks, parts, whole)
    first_home = pl.multiple_of(home_id - first_window, homes)
    first_atom = pl.multiple_of(part * chunk, chunk)

    tables = [window_ref.at[WINDOW_X], window_ref.at[WINDOW_Y], window_ref.at[WINDOW_Z]]
    tables += [types_ref, window_ref.at[WINDOW_CHARGE], partner_ref]
    odd = lax.rem(lax.axis_index("dev"), 2) == 1
    for place, pair in enumerate(order):
        for field, table in enumerate(tables):
            rows = [ref[place, field * blocks : (field + 1) * blocks, :] for ref in arrived_refs]
            if twins == 2:
                rows = [jnp.where(odd, rows[1], rows[0]), jnp.where(odd, rows[0], rows[1])]
            first = pair * twins * blocks
            table[first : first + twins * blocks, :] = jnp.concatenate(rows, axis=0)
    if partner_ref.shape[0] > window:
        spare = (partner_ref.shape[0] - window, LANES)
        partner_ref[window:, :] = jnp.full(spare, EMPTY_SLOT, jnp.float32)
    def scaled_radii():
        _, _, scaled = type_fields(types_ref[...])
        window_ref[WINDOW_SCALED, 0:window, :] = 0.25 * scaled
        for field in range(WINDOW_COUNT):
            filler = FAR_AWAY if field == WINDOW_X else 0.0
            window_ref[field, window : window + SUBLANES, :] = jnp.full((SUBLANES, LANES), filler, jnp.float32)

    def home_columns():
        scaled_radii()
        home_rows = [window_ref[field, pl.ds(first_home, homes), :] for field in range(3)]
        turned_ref[...] = turned(jnp.concatenate([types_ref[pl.ds(first_home, homes), :]] + home_rows, axis=0))
        columns = turned_ref[pl.ds(first_atom, chunk), :]
        _, rho, _ = type_fields(columns)
        for home in range(homes):
            columns_ref[0, home] = spread(0.25 * rho, home)
            for index in range(1, 4):
                columns_ref[index, home] = spread(columns, index * homes + home)

    def pair_distance(home, step, rows):
        dx = columns_ref[1, home, step] - rows[0]
        dy = columns_ref[2, home, step] - rows[1]
        dz = columns_ref[3, home, step] - rows[2]
        return dx * dx + dy * dy + dz * dz

    steps = [pl.ds(start, STEP) for start in range(0, groups, STEP)]

    shift = lists_ref.shape[0].bit_length()
    usual = 16 // PARTNERS + 6

    def list_items(home, filled):
        turns = (lists_ref[0, home] + (together - 1)) // together

        def put(index, carry):
            items_ref[filled + index] = (home << shift) + index * together
            return carry

        for index in range(usual):
            put(index, 0)
        lax.fori_loop(usual, turns, put, 0)
        return filled + turns

    def own_sweep(integral):
        near_ref[...] = jnp.full(near_ref.shape, FAR_AWAY, jnp.float32)
        own_together = min(homes, 2 * LANES // chunk)

        def own_pairs(turn, carry):
            for index in range(own_together):
                home = turn * own_together + index
                rows = [row_of(window_ref, field, first_home + home) for field in range(4)]
                for start, step in zip(range(0, groups, STEP), steps):
                    same = diagonal(STEP, first_atom + start * SUBLANES)
                    squared = jnp.where(same, FAR_AWAY, pair_distance(home, step, rows))
                    term = integral(squared, columns_ref[0, home, step], rows[3])
                    total_ref[home, step] = jnp.where(same, 0.0, term)
                    near_ref[...] = jnp.minimum(near_ref[...], squared)
            return carry

        lax.fori_loop(0, homes // own_together, own_pairs, 0)

    def sweep(integral, item_count):
        def visit(turn, nearest):
            sums = []
            for index in range(ITEMS):
                item = items_ref[turn * ITEMS + index]
                line, entry = item >> shift, item & ((1 << shift) - 1)
                home = jnp.minimum(line, homes - 1)
                parts_of = [None] * len(steps)
                for other in range(together):
                    partner = lists_ref[SUBLANES + entry + other, line]
                    rows = [row_of(window_ref, field, partner) for field in range(4)]
                    for place, step in enumerate(steps):
                        squared = pair_distance(home, step, rows)
                        nearest = jnp.minimum(nearest, squared)
                        term = integral(squared, columns_ref[0, home, step], rows[3])
                        parts_of[place] = term if other == 0 else parts_of[place] + term
                sums.append((home, parts_of))
            for home, parts_of in sums:
                for part, step in zip(parts_of, steps):
                    total_ref[home, step] += part
            return nearest

        near_ref[...] = lax.fori_loop(0, (item_count + (ITEMS - 1)) // ITEMS, visit, near_ref[...])
        lane = lax.broadcasted_iota(jnp.int32, (chunk, LANES), 1)
        packed = jnp.zeros((chunk, LANES), jnp.float32)
        for home in range(homes):
            packed = jnp.where(lane == home, lane_total(total_ref[home]), packed)
        packed_ref[...] = packed

    def meanwhile():
        home_columns()
        own_sweep(descreen)

    neighbour_lists(partner_ref, first_home, home_id, first_window, homes, slots, window, table_ref)
    move_lists(table_ref, lists_ref, lists_sem, meanwhile)
    intrinsic, rho, _ = type_fields(turned_ref[pl.ds(first_atom, chunk), :])
    item_count = lax.fori_loop(0, homes, list_items, 0)
    for index in range(ITEMS):
        items_ref[item_count + index] = homes << shift
    sweep(descreen, item_count)

    @pl.when(jnp.min(near_ref[...]) < short_range * short_range)
    def _():
        own_sweep(descreen_any)
        sweep(descreen_any, item_count)

    psi = (0.125 * packed_ref[...]) * rho
    shaped = born_alpha * psi - born_beta * psi * psi + born_gamma * psi * psi * psi
    radii = 1.0 / (1.0 / rho - jnp.tanh(shaped) / intrinsic)

    if chunk < LANES:
        radii = jnp.concatenate([radii, jnp.zeros((LANES - chunk, LANES), jnp.float32)], axis=0)
    turned_ref[...] = radii.T
    lane = lax.broadcasted_iota(jnp.int32, (blocks, LANES), 1)
    sent = turned_ref[pl.ds(0, blocks, stride=parts), :]
    for index in range(1, parts):
        rows = pltpu.roll(turned_ref[pl.ds(index, blocks, stride=parts), :], index * chunk, 1)
        sent = jnp.where(lane >= index * chunk, rows, sent)
    for copy in range(copies_ref.shape[0]):
        copies_ref[copy] = sent


def energy_kernel(
    parts,
    whole,
    table_ref,
    window_ref,
    gathered_ref,
    own_radii_ref,
    energy_ref,
    forces_ref,
    grad_ref,
    columns_ref,
    radii_ref,
    total_ref,
    lists_ref,
    lists_sem,
):
    devices, blocks, atoms = gathered_ref.shape
    window = devices * blocks
    part_rows = window // parts
    chunk = atoms // parts
    groups = atoms // SUBLANES
    first_window, _, own_id, part_here = device_place(blocks, parts, whole)
    first_own, list_lane = own_id - first_window, part_here * blocks
    fields = [(window_ref, field) for field in (WINDOW_X, WINDOW_Y, WINDOW_Z, WINDOW_CHARGE)] + [(radii_ref, 0)]

    def unpack():
        lane = lax.broadcasted_iota(jnp.int32, (part_rows, LANES), 1)
        pieces = [
            gathered_ref[pl.ds(part, devices // parts, stride=parts)].reshape(part_rows, atoms)
            for part in range(parts)
        ]
        for place in range(parts):
            whole_rows = pieces[0] if place == 0 else pltpu.roll(pieces[0], (parts - place) * chunk, 1)
            for part in range(1, parts):
                shift = (part - place) % parts
                piece = pieces[part] if shift == 0 else pltpu.roll(pieces[part], shift * chunk, 1)
                whole_rows = jnp.where(lane >= part * chunk, piece, whole_rows)
            radii_ref[0, pl.ds(place, part_rows, stride=parts), :] = whole_rows
        radii_ref[0, window : window + SUBLANES, :] = jnp.ones((SUBLANES, LANES), jnp.float32)

    def own_rows(ref, field):
        return jnp.concatenate([ref[field, pl.ds(first_own + block, 1), :] for block in range(blocks)], axis=0)

    def home_columns(block, start):
        return [columns_ref[field * blocks + block, pl.ds(start, ENERGY_STEP)] for field in range(4)]

    def pair_terms(home, rows, same=None):
        x, y, z, charge, radius = rows
        dx = home[0] - x
        dy = home[1] - y
        dz = home[2] - z
        squared = dx * dx + dy * dy + dz * dz
        if same is not None:
            squared = jnp.where(same, 1.0, squared)
            charge = jnp.where(same, 0.0, charge)
        spread_sq = home[3] * radius
        power = squared * pltpu.reciprocal(spread_sq, approx=True)
        quarter = 0.25 * jnp.exp(power)
        root_sq = squared - spread_sq * quarter
        inv_root = lax.rsqrt(root_sq)
        potential = charge * inv_root
        pull = (potential * pltpu.reciprocal(root_sq, approx=True)) * (1.0 - quarter)
        return (pull * dx, pull * dy, pull * dz, potential, pull * squared)

    def own_pairs():
        unpack()
        own_radii = own_rows(radii_ref, 0)
        own_radii_ref[...] = own_radii
        own = [own_rows(window_ref, field) for field in (WINDOW_X, WINDOW_Y, WINDOW_Z)]
        columns = turned(jnp.concatenate(own + [-4.0 * own_radii], axis=0))
        for index in range(4 * blocks):
            columns_ref[index] = spread(columns, index)
        for block in range(blocks):
            rows = [row_of(ref, field, first_own + block) for ref, field in fields]
            for start in range(0, groups, ENERGY_STEP):
                step = pl.ds(start, ENERGY_STEP)
                terms = pair_terms(home_columns(block, start), rows, diagonal(ENERGY_STEP, start * SUBLANES))
                for term, value in enumerate(terms):
                    total_ref[term * blocks + block, step] = value

    move_lists(table_ref, lists_ref, lists_sem, own_pairs)
    for block in range(blocks):

        def visit(count, first, index, carry, block=block):
            partners = []
            for other in range(count):
                partner = lists_ref[SUBLANES + first + index * count + other, list_lane + block]
                partners.append([row_of(ref, field, partner) for ref, field in fields])
            for start in range(0, groups, ENERGY_STEP):
                step = pl.ds(start, ENERGY_STEP)
                home = home_columns(block, start)
                sums = [total_ref[term * blocks + block, step] for term in range(5)]
                for rows in partners:
                    sums = [total + value for total, value in zip(sums, pair_terms(home, rows))]
                for term, value in enumerate(sums):
                    total_ref[term * blocks + block, step] = value
            return carry

        left = lists_ref[0, list_lane + block]
        first = 0
        for count in (4, 2, 1):
            turns = left // count
            lax.fori_loop(0, turns, functools.partial(visit, count, first), 0)
            first = first + turns * count
            left = left - turns * count
    sums = lane_sums([total_ref[index] for index in range(5 * blocks)], 5 * blocks)
    charges = own_rows(window_ref, WINDOW_CHARGE)
    own_decay = 1.0 / own_radii_ref[...]
    scale = solvent_tau * charges
    for axis in range(3):
        forces_ref[axis] = -scale * sums[axis * blocks : (axis + 1) * blocks]
    own_energy = 0.5 * scale * charges * own_decay
    energy_ref[...] = -0.5 * scale * sums[3 * blocks : 4 * blocks] - own_energy
    radial = sums[3 * blocks : 4 * blocks] - sums[4 * blocks : 5 * blocks]
    grad_ref[...] = (own_energy + 0.5 * scale * radial) * own_decay


def shards(positions, charges, types, pairs, owner_map):
    _, blocks, atoms = positions.shape
    regions = lax.axis_size("region")
    region_devices = lax.axis_size("dev")
    kept_regions, whole = window_regions(regions)
    devices = kept_regions * region_devices
    window = devices * blocks
    parts = atoms // CHUNK
    while region_devices % parts or 4 * parts * blocks > LANES:
        parts //= 2
    homes = parts * blocks
    chunk = atoms // parts

    vmem = pl.BlockSpec(memory_space=pltpu.VMEM)
    params = pltpu.CompilerParams(vmem_limit_bytes=40 * 1024 * 1024)
    copy_count = lax.axis_size(exchange_axes())
    twins = twin_count(region_devices)
    arrived = sent_to_both_twins(
        pl.pallas_call(
            functools.partial(fields_kernel, blocks, atoms),
            out_shape=jax.ShapeDtypeStruct((copy_count // twins, ROW_COUNT, blocks, atoms), jnp.float32),
            in_specs=[pl.BlockSpec(memory_space=pltpu.HBM)] * 5,
            out_specs=vmem,
            scratch_shapes=[
                pltpu.VMEM(positions.shape, positions.dtype),
                pltpu.VMEM(types.shape, types.dtype),
                pltpu.VMEM(charges.shape, charges.dtype),
                pltpu.SMEM(pairs.shape, pairs.dtype),
                pltpu.SMEM(owner_map.shape, owner_map.dtype),
                pltpu.SemaphoreType.DMA((5,)),
            ],
        )(positions, types, charges, pairs, owner_map)
    )
    arrived = [with_other_regions(part).reshape(devices // twins, ROW_COUNT * blocks, atoms) for part in arrived]
    padded = -(-window // LANES) * LANES
    table = jax.ShapeDtypeStruct((SUBLANES + padded, LANES), jnp.int32)
    pairs_sent = copy_count // twins
    pair_order = [
        first + place for first in range(0, devices // twins, pairs_sent) for place in reversed(range(pairs_sent))
    ]
    fields = jax.ShapeDtypeStruct((WINDOW_COUNT, window + SUBLANES, atoms), jnp.float32)
    copies, lists, window_fields = pl.pallas_call(
        functools.partial(radii_kernel, blocks, pairs.shape[1], twins, whole, pair_order),
        out_shape=(jax.ShapeDtypeStruct((copy_count, blocks, atoms), jnp.float32), table, fields),
        in_specs=[vmem] * twins,
        out_specs=(vmem, vmem, vmem),
        scratch_shapes=[
            pltpu.VMEM((4, homes, chunk // SUBLANES, SUBLANES, LANES), jnp.float32),
            pltpu.VMEM((window, atoms), jnp.float32),
            pltpu.VMEM((padded, atoms), jnp.float32),
            pltpu.VMEM((homes, chunk // SUBLANES, SUBLANES, LANES), jnp.float32),
            pltpu.VMEM((LANES, LANES), jnp.float32),
            pltpu.VMEM((chunk, LANES), jnp.float32),
            pltpu.VMEM((STEP, SUBLANES, LANES), jnp.float32),
            pltpu.SMEM(table.shape, jnp.int32),
            pltpu.SMEM((homes * (padded // PARTNERS + 1) + 64,), jnp.int32),
            pltpu.SemaphoreType.DMA(()),
        ],
        compiler_params=params,
    )(*arrived)
    block_out = jax.ShapeDtypeStruct((blocks, atoms), jnp.float32)
    window_radii = with_other_regions(sent_directly(copies))
    own_radii, energy, forces, grad = pl.pallas_call(
        functools.partial(energy_kernel, parts, whole),
        out_shape=(block_out, block_out, jax.ShapeDtypeStruct((3, blocks, atoms), jnp.float32), block_out),
        in_specs=[pl.BlockSpec(memory_space=pl.ANY), vmem, vmem],
        out_specs=(vmem, vmem, vmem, vmem),
        scratch_shapes=[
            pltpu.VMEM((4 * blocks, atoms // SUBLANES, SUBLANES, LANES), jnp.float32),
            pltpu.VMEM((1, window + SUBLANES, atoms), jnp.float32),
            pltpu.VMEM((5 * blocks, atoms // SUBLANES, SUBLANES, LANES), jnp.float32),
            pltpu.SMEM(table.shape, jnp.int32),
            pltpu.SemaphoreType.DMA(()),
        ],
        compiler_params=params,
    )(lists, window_fields, window_radii)
    return own_radii, energy, forces, grad


def solution(mesh):
    placed = (
        P(None, ("region", "dev"), None),
        P(("region", "dev"), None),
        P(("region", "dev"), None),
        P(("region", "dev"), None),
        P(),
    )
    return jax.shard_map(
        shards,
        mesh=mesh,
        in_specs=placed,
        out_specs=(
            P(("region", "dev"), None),
            P(("region", "dev"), None),
            P(None, ("region", "dev"), None),
            P(("region", "dev"), None),
        ),
        check_vma=False,
    )
```

```python
import functools

import jax
import jax.numpy as jnp
from jax import lax
from jax.experimental import pallas as pl
from jax.experimental.pallas import tpu as pltpu
from jax.sharding import PartitionSpec as P

type_radii = (1.2, 1.7, 1.55, 1.52, 1.85, 1.8)
type_scales = (0.85, 0.72, 0.79, 0.85, 0.86, 0.96)
radius_offset = 0.09
born_alpha = 1.0
born_beta = 0.8
born_gamma = 4.85
solvent_tau = 1.0 - 1.0 / 78.5

ROW_X, ROW_Y, ROW_Z, ROW_TYPE, ROW_CHARGE, ROW_PARTNER, ROW_COUNT = range(7)
WINDOW_X, WINDOW_Y, WINDOW_Z, WINDOW_SCALED, WINDOW_CHARGE, WINDOW_COUNT = range(6)
LANES = 128
SUBLANES = 8
STEP = 2
ENERGY_STEP = 4
CHUNK = 32
LIST_ROWS = 32
PARTNERS = 2
ITEMS = 8
EMPTY_SLOT = -1.0e6
FAR_AWAY = 1.0e15

scaled_values = [scale * (radius - radius_offset) for radius, scale in zip(type_radii, type_scales)]
short_range = 1.01 * max(
    max(scaled_values) - (min(type_radii) - radius_offset),
    (max(type_radii) - radius_offset) - min(scaled_values),
    0.5,
)


def window_regions(region_count):
    return (region_count, True) if region_count <= 3 else (3, False)


def exchange_axes():
    return ("region", "dev") if window_regions(lax.axis_size("region"))[1] else ("dev",)


def sent_directly(copies):
    return lax.all_to_all(copies, exchange_axes(), split_axis=0, concat_axis=0, tiled=True)


def twin_count(device_count):
    return 2 - device_count % 2


def pair_ranks(regions, device_count):
    pairs = device_count // twin_count(device_count)
    near = 2 - pairs % 2
    return [
        region * pairs + far * near + line
        for region in reversed(range(regions))
        for line in reversed(range(near))
        for far in reversed(range(pairs // near))
    ]


def sent_to_both_twins(copies):
    count = lax.axis_size("dev")
    twins = twin_count(count)
    axes = exchange_axes()
    regions = lax.axis_size(axes) // count
    alike = [[pair * twins + parity for pair in pair_ranks(regions, count)] for parity in range(twins)]
    here = lax.all_to_all(copies, axes, split_axis=0, concat_axis=0, axis_index_groups=alike, tiled=True)
    if twins == 1:
        return [here]
    return [here, lax.ppermute(here, "dev", [(i, i ^ 1) for i in range(count)])]


def with_other_regions(here):
    regions = lax.axis_size("region")
    if window_regions(regions)[1]:
        return here
    below = lax.ppermute(here, "region", [(i, i + 1) for i in range(regions - 1)])
    above = lax.ppermute(here, "region", [(i + 1, i) for i in range(regions - 1)])
    return jnp.concatenate([below, here, above], axis=0)


def by_type(types, table):
    value = jnp.full(types.shape, table[0], jnp.float32)
    for index in range(1, len(table)):
        value = jnp.where(types == index, jnp.float32(table[index]), value)
    return value


def type_fields(types):
    intrinsic = by_type(types, type_radii)
    rho = intrinsic - radius_offset
    return intrinsic, rho, by_type(types, type_scales) * rho


def turned(rows):
    count, width = rows.shape
    if count < LANES:
        rows = jnp.concatenate([rows, jnp.zeros((LANES - count, width), rows.dtype)], axis=0)
    return rows.T


def spread(columns, index):
    count = columns.shape[0]
    wide = jnp.broadcast_to(columns[:, index : index + 1], (count, LANES))
    return wide.reshape(count // SUBLANES, SUBLANES, LANES)


def row_of(ref, field, row):
    return ref[field, pl.ds(row, SUBLANES, stride=0), :][None]


def diagonal(groups, first_atom):
    shape = (groups, SUBLANES, LANES)
    row = lax.broadcasted_iota(jnp.int32, shape, 0) * SUBLANES + lax.broadcasted_iota(jnp.int32, shape, 1)
    return row + first_atom == lax.broadcasted_iota(jnp.int32, shape, 2)


def lane_total(array):
    return jnp.sum(array.reshape(-1, LANES), axis=1, keepdims=True)


def lane_sums(arrays, count):
    atoms = arrays[0].shape[0] * SUBLANES
    lane = lax.broadcasted_iota(jnp.int32, (atoms, LANES), 1)
    packed = jnp.zeros((atoms, LANES), jnp.float32)
    for index, array in enumerate(arrays):
        packed = jnp.where(lane == index, lane_total(array), packed)
    return packed.T[:count]


def fields_kernel(blocks, atoms, *refs):
    inputs, copies_ref, here, sems = refs[:5], refs[5], refs[6:11], refs[11]
    moves = [pltpu.make_async_copy(src, dst, sems.at[i]) for i, (src, dst) in enumerate(zip(inputs, here))]
    for move in moves:
        move.start()
    for move in moves:
        move.wait()
    positions_ref, types_ref, charges_ref, pairs_ref, owner_ref = here
    slot = lax.broadcasted_iota(jnp.int32, (1, atoms), 1)
    partners = []
    for block in range(blocks):
        row = jnp.full((1, atoms), EMPTY_SLOT, jnp.float32)
        for index in range(pairs_ref.shape[1]):
            cell = pairs_ref[block, index]
            partner = jnp.where(cell >= 0, owner_ref[jnp.maximum(cell, 0)] + 1, int(EMPTY_SLOT))
            row = jnp.where(slot == index, partner.astype(jnp.float32), row)
        partners.append(row)
    rows = [positions_ref[axis] for axis in range(3)]
    rows += [types_ref[...].astype(jnp.float32), charges_ref[...], jnp.concatenate(partners, axis=0)]
    for copy in range(copies_ref.shape[0]):
        for index, row in enumerate(rows):
            copies_ref[copy, index] = row


def descreen(squared, rho, scaled):
    inv_dist = lax.rsqrt(squared)
    share = scaled * inv_dist
    inner = 0.25 - share
    high = 0.25 + share
    low = jnp.maximum(rho * inv_dist, inner)
    inv_low = pltpu.reciprocal(low, approx=True)
    ratio = low * pltpu.reciprocal(high, approx=True)
    curve = (1.0 - ratio) + inner * (ratio - high * inv_low)
    return (inv_low * curve + 2.0 * jnp.log(ratio)) * inv_dist


def descreen_any(squared, rho, scaled):
    rho, scaled = 4.0 * rho, 4.0 * scaled
    inv_dist = lax.rsqrt(squared)
    distance = squared * inv_dist
    high = distance + scaled
    gap = distance - scaled
    low = jnp.maximum(rho, jnp.abs(gap))
    inv_low = 1.0 / low
    inv_high = 1.0 / high
    quarter = 0.25 * inv_dist
    curve = (squared - scaled * scaled) * quarter
    body = (0.5 * (inv_low - inv_high)) * (1.0 - (inv_low + inv_high) * curve)
    body = body + jnp.log(low * inv_high) * quarter
    body = body + jnp.where(rho < -gap, 1.0 / rho - inv_low, 0.0)
    return jnp.where(high > rho, 8.0 * body, 0.0)


def neighbour_lists(partner_ref, first_home, home_id, first_window, homes, slots, filler, table_ref):
    window = partner_ref.shape[0]
    tiles = [slice(start, start + LANES) for start in range(0, window, LANES)]
    depth = -(-slots // SUBLANES) * SUBLANES
    ids = jnp.concatenate([partner_ref[tile, :].T[:depth] for tile in tiles], axis=1)
    lists = turned(partner_ref[pl.ds(first_home, homes), :])[:depth]
    lane = lax.broadcasted_iota(jnp.int32, (depth, window), 1)
    lane_id = (lane + (first_window + 1)).astype(jnp.float32)
    rows = []
    for home in range(homes):
        own = (home_id + home + 1).astype(jnp.float32)
        linked = (ids == own) | (lane_id == lists[:, home : home + 1])
        rows.append(jnp.max(jnp.where(linked, 1.0, 0.0), axis=0, keepdims=True))
    linked = jnp.concatenate(rows, axis=0)
    before = lax.broadcasted_iota(jnp.int32, (window, window), 0)
    after = lax.broadcasted_iota(jnp.int32, (window, window), 1)
    ramp = jnp.where(before <= after, 1.0, 0.0).astype(jnp.bfloat16)
    rank = jnp.dot(linked.astype(jnp.bfloat16), ramp, preferred_element_type=jnp.float32)
    place = jnp.where(linked > 0.0, rank, 0.0)
    total = jnp.sum(linked, axis=1, keepdims=True)
    name = lax.broadcasted_iota(jnp.int32, (LIST_ROWS, window), 1).astype(jnp.float32)
    spot = lax.broadcasted_iota(jnp.int32, (LIST_ROWS, window), 0).astype(jnp.float32)
    own_lane = lax.broadcasted_iota(jnp.int32, (LIST_ROWS, LANES), 1)

    def some_rows(start):
        first = jnp.asarray(start + 1).astype(jnp.float32)
        packed = jnp.zeros((LIST_ROWS, LANES), jnp.float32)
        for home in range(homes):
            hit = place[home : home + 1] == spot + first
            found = jnp.sum(jnp.where(hit, name - float(filler), 0.0), axis=1, keepdims=True)
            packed = jnp.where(own_lane == home, found, packed)
        rows = pl.ds(pl.multiple_of(SUBLANES + start, SUBLANES), LIST_ROWS)
        table_ref[rows, :] = packed.astype(jnp.int32) + filler

    counts = jnp.zeros((SUBLANES, LANES), jnp.float32)
    lane = lax.broadcasted_iota(jnp.int32, (SUBLANES, LANES), 1)
    for home in range(homes):
        counts = jnp.where(lane == home, total[home : home + 1], counts)
    longest = jnp.max(total)
    table_ref[0:SUBLANES, :] = jnp.where(lane == LANES - 1, longest, counts).astype(jnp.int32)
    some_rows(0)

    def more_rows(turn, carry):
        some_rows(turn * LIST_ROWS)
        return carry

    lax.fori_loop(1, (longest.astype(jnp.int32) + (LIST_ROWS - 1)) // LIST_ROWS, more_rows, 0)


def move_lists(table_ref, lists_ref, sem, when_wanted):
    usual = pl.ds(0, SUBLANES + LIST_ROWS)
    move = pltpu.make_async_copy(table_ref.at[usual], lists_ref.at[usual], sem)
    move.start()
    when_wanted()
    move.wait()
    rows = lists_ref.shape[0] - (SUBLANES + LIST_ROWS)
    if rows > 0:

        @pl.when(lists_ref[0, LANES - 1] > LIST_ROWS)
        def _():
            rest = pl.ds(SUBLANES + LIST_ROWS, rows)
            more = pltpu.make_async_copy(table_ref.at[rest], lists_ref.at[rest], sem)
            more.start()
            more.wait()


def device_place(blocks, parts, whole):
    region, device = lax.axis_index("region"), lax.axis_index("dev")
    region_blocks = lax.axis_size("dev") * blocks
    first_window = 0 if whole else (region - 1) * region_blocks
    first_own = region * region_blocks + device * blocks
    part = lax.rem(device, parts)
    return first_window, first_own - part * blocks, first_own, part


def radii_kernel(
    blocks,
    slots,
    twins,
    whole,
    order,
    *refs,
):
    arrived_refs, refs = refs[:twins], refs[twins:]
    copies_ref, table_ref, window_ref, columns_ref, types_ref, partner_ref, total_ref, *refs = refs
    turned_ref, packed_ref, near_ref, lists_ref, items_ref, lists_sem = refs
    _, homes, groups, _, _ = columns_ref.shape
    chunk = groups * SUBLANES
    window = types_ref.shape[0]
    parts = homes // blocks
    together = PARTNERS
    first_window, home_id, _, part = device_place(blocks, parts, whole)
    first_home = pl.multiple_of(home_id - first_window, homes)
    first_atom = pl.multiple_of(part * chunk, chunk)

    tables = [window_ref.at[WINDOW_X], window_ref.at[WINDOW_Y], window_ref.at[WINDOW_Z]]
    tables += [types_ref, window_ref.at[WINDOW_CHARGE], partner_ref]
    odd = lax.rem(lax.axis_index("dev"), 2) == 1
    for place, pair in enumerate(order):
        for field, table in enumerate(tables):
            rows = [ref[place, field * blocks : (field + 1) * blocks, :] for ref in arrived_refs]
            if twins == 2:
                rows = [jnp.where(odd, rows[1], rows[0]), jnp.where(odd, rows[0], rows[1])]
            first = pair * twins * blocks
            table[first : first + twins * blocks, :] = jnp.concatenate(rows, axis=0)
    if partner_ref.shape[0] > window:
        spare = (partner_ref.shape[0] - window, LANES)
        partner_ref[window:, :] = jnp.full(spare, EMPTY_SLOT, jnp.float32)
    def scaled_radii():
        _, _, scaled = type_fields(types_ref[...])
        window_ref[WINDOW_SCALED, 0:window, :] = 0.25 * scaled
        for field in range(WINDOW_COUNT):
            filler = FAR_AWAY if field == WINDOW_X else 0.0
            window_ref[field, window : window + SUBLANES, :] = jnp.full((SUBLANES, LANES), filler, jnp.float32)

    def home_columns():
        scaled_radii()
        home_rows = [window_ref[field, pl.ds(first_home, homes), :] for field in range(3)]
        turned_ref[...] = turned(jnp.concatenate([types_ref[pl.ds(first_home, homes), :]] + home_rows, axis=0))
        columns = turned_ref[pl.ds(first_atom, chunk), :]
        _, rho, _ = type_fields(columns)
        for home in range(homes):
            columns_ref[0, home] = spread(0.25 * rho, home)
            for index in range(1, 4):
                columns_ref[index, home] = spread(columns, index * homes + home)

    def pair_distance(home, step, rows):
        dx = columns_ref[1, home, step] - rows[0]
        dy = columns_ref[2, home, step] - rows[1]
        dz = columns_ref[3, home, step] - rows[2]
        return dx * dx + dy * dy + dz * dz

    steps = [pl.ds(start, STEP) for start in range(0, groups, STEP)]

    shift = lists_ref.shape[0].bit_length()
    usual = 16 // PARTNERS + 6

    def list_items(home, filled):
        turns = (lists_ref[0, home] + (together - 1)) // together

        def put(index, carry):
            items_ref[filled + index] = (home << shift) + index * together
            return carry

        for index in range(usual):
            put(index, 0)
        lax.fori_loop(usual, turns, put, 0)
        return filled + turns

    def own_sweep(integral):
        near_ref[...] = jnp.full(near_ref.shape, FAR_AWAY, jnp.float32)
        own_together = min(homes, 2 * LANES // chunk)

        def own_pairs(turn, carry):
            for index in range(own_together):
                home = turn * own_together + index
                rows = [row_of(window_ref, field, first_home + home) for field in range(4)]
                for start, step in zip(range(0, groups, STEP), steps):
                    same = diagonal(STEP, first_atom + start * SUBLANES)
                    squared = jnp.where(same, FAR_AWAY, pair_distance(home, step, rows))
                    term = integral(squared, columns_ref[0, home, step], rows[3])
                    total_ref[home, step] = jnp.where(same, 0.0, term)
                    near_ref[...] = jnp.minimum(near_ref[...], squared)
            return carry

        lax.fori_loop(0, homes // own_together, own_pairs, 0)

    def sweep(integral, item_count):
        def visit(turn, nearest):
            sums = []
            for index in range(ITEMS):
                item = items_ref[turn * ITEMS + index]
                line, entry = item >> shift, item & ((1 << shift) - 1)
                home = jnp.minimum(line, homes - 1)
                parts_of = [None] * len(steps)
                for other in range(together):
                    partner = lists_ref[SUBLANES + entry + other, line]
                    rows = [row_of(window_ref, field, partner) for field in range(4)]
                    for place, step in enumerate(steps):
                        squared = pair_distance(home, step, rows)
                        nearest = jnp.minimum(nearest, squared)
                        term = integral(squared, columns_ref[0, home, step], rows[3])
                        parts_of[place] = term if other == 0 else parts_of[place] + term
                sums.append((home, parts_of))
            for home, parts_of in sums:
                for part, step in zip(parts_of, steps):
                    total_ref[home, step] += part
            return nearest

        near_ref[...] = lax.fori_loop(0, (item_count + (ITEMS - 1)) // ITEMS, visit, near_ref[...])
        lane = lax.broadcasted_iota(jnp.int32, (chunk, LANES), 1)
        packed = jnp.zeros((chunk, LANES), jnp.float32)
        for home in range(homes):
            packed = jnp.where(lane == home, lane_total(total_ref[home]), packed)
        packed_ref[...] = packed

    def meanwhile():
        home_columns()
        own_sweep(descreen)

    neighbour_lists(partner_ref, first_home, home_id, first_window, homes, slots, window, table_ref)
    move_lists(table_ref, lists_ref, lists_sem, meanwhile)
    intrinsic, rho, _ = type_fields(turned_ref[pl.ds(first_atom, chunk), :])
    item_count = lax.fori_loop(0, homes, list_items, 0)
    for index in range(ITEMS):
        items_ref[item_count + index] = homes << shift
    sweep(descreen, item_count)

    @pl.when(jnp.min(near_ref[...]) < short_range * short_range)
    def _():
        own_sweep(descreen_any)
        sweep(descreen_any, item_count)

    psi = (0.125 * packed_ref[...]) * rho
    shaped = born_alpha * psi - born_beta * psi * psi + born_gamma * psi * psi * psi
    radii = 1.0 / (1.0 / rho - jnp.tanh(shaped) / intrinsic)

    if chunk < LANES:
        radii = jnp.concatenate([radii, jnp.zeros((LANES - chunk, LANES), jnp.float32)], axis=0)
    turned_ref[...] = radii.T
    lane = lax.broadcasted_iota(jnp.int32, (blocks, LANES), 1)
    sent = turned_ref[pl.ds(0, blocks, stride=parts), :]
    for index in range(1, parts):
        rows = pltpu.roll(turned_ref[pl.ds(index, blocks, stride=parts), :], index * chunk, 1)
        sent = jnp.where(lane >= index * chunk, rows, sent)
    for copy in range(copies_ref.shape[0]):
        copies_ref[copy] = sent


def energy_kernel(
    parts,
    whole,
    table_ref,
    window_ref,
    gathered_ref,
    own_radii_ref,
    energy_ref,
    forces_ref,
    grad_ref,
    columns_ref,
    radii_ref,
    total_ref,
    lists_ref,
    lists_sem,
):
    devices, blocks, atoms = gathered_ref.shape
    window = devices * blocks
    part_rows = window // parts
    chunk = atoms // parts
    groups = atoms // SUBLANES
    first_window, _, own_id, part_here = device_place(blocks, parts, whole)
    first_own, list_lane = own_id - first_window, part_here * blocks
    fields = [(window_ref, field) for field in (WINDOW_X, WINDOW_Y, WINDOW_Z, WINDOW_CHARGE)] + [(radii_ref, 0)]

    def unpack():
        lane = lax.broadcasted_iota(jnp.int32, (part_rows, LANES), 1)
        pieces = [
            gathered_ref[pl.ds(part, devices // parts, stride=parts)].reshape(part_rows, atoms)
            for part in range(parts)
        ]
        for place in range(parts):
            whole_rows = pieces[0] if place == 0 else pltpu.roll(pieces[0], (parts - place) * chunk, 1)
            for part in range(1, parts):
                shift = (part - place) % parts
                piece = pieces[part] if shift == 0 else pltpu.roll(pieces[part], shift * chunk, 1)
                whole_rows = jnp.where(lane >= part * chunk, piece, whole_rows)
            radii_ref[0, pl.ds(place, part_rows, stride=parts), :] = whole_rows
        radii_ref[0, window : window + SUBLANES, :] = jnp.ones((SUBLANES, LANES), jnp.float32)

    def own_rows(ref, field):
        return jnp.concatenate([ref[field, pl.ds(first_own + block, 1), :] for block in range(blocks)], axis=0)

    def home_columns(block, start):
        return [columns_ref[field * blocks + block, pl.ds(start, ENERGY_STEP)] for field in range(4)]

    def pair_terms(home, rows, same=None):
        x, y, z, charge, radius = rows
        dx = home[0] - x
        dy = home[1] - y
        dz = home[2] - z
        squared = dx * dx + dy * dy + dz * dz
        if same is not None:
            squared = jnp.where(same, 1.0, squared)
            charge = jnp.where(same, 0.0, charge)
        spread_sq = home[3] * radius
        power = squared * pltpu.reciprocal(spread_sq, approx=True)
        quarter = 0.25 * jnp.exp(power)
        root_sq = squared - spread_sq * quarter
        inv_root = lax.rsqrt(root_sq)
        potential = charge * inv_root
        pull = (potential * pltpu.reciprocal(root_sq, approx=True)) * (1.0 - quarter)
        return (pull * dx, pull * dy, pull * dz, potential, pull * squared)

    def own_pairs():
        unpack()
        own_radii = own_rows(radii_ref, 0)
        own_radii_ref[...] = own_radii
        own = [own_rows(window_ref, field) for field in (WINDOW_X, WINDOW_Y, WINDOW_Z)]
        columns = turned(jnp.concatenate(own + [-4.0 * own_radii], axis=0))
        for index in range(4 * blocks):
            columns_ref[index] = spread(columns, index)
        for block in range(blocks):
            rows = [row_of(ref, field, first_own + block) for ref, field in fields]
            for start in range(0, groups, ENERGY_STEP):
                step = pl.ds(start, ENERGY_STEP)
                terms = pair_terms(home_columns(block, start), rows, diagonal(ENERGY_STEP, start * SUBLANES))
                for term, value in enumerate(terms):
                    total_ref[term * blocks + block, step] = value

    move_lists(table_ref, lists_ref, lists_sem, own_pairs)
    for block in range(blocks):

        def visit(count, first, index, carry, block=block):
            partners = []
            for other in range(count):
                partner = lists_ref[SUBLANES + first + index * count + other, list_lane + block]
                partners.append([row_of(ref, field, partner) for ref, field in fields])
            for start in range(0, groups, ENERGY_STEP):
                step = pl.ds(start, ENERGY_STEP)
                home = home_columns(block, start)
                sums = [total_ref[term * blocks + block, step] for term in range(5)]
                for rows in partners:
                    sums = [total + value for total, value in zip(sums, pair_terms(home, rows))]
                for term, value in enumerate(sums):
                    total_ref[term * blocks + block, step] = value
            return carry

        left = lists_ref[0, list_lane + block]
        first = 0
        for count in (4, 2, 1):
            turns = left // count
            lax.fori_loop(0, turns, functools.partial(visit, count, first), 0)
            first = first + turns * count
            left = left - turns * count
    sums = lane_sums([total_ref[index] for index in range(5 * blocks)], 5 * blocks)
    charges = own_rows(window_ref, WINDOW_CHARGE)
    own_decay = 1.0 / own_radii_ref[...]
    scale = solvent_tau * charges
    for axis in range(3):
        forces_ref[axis] = -scale * sums[axis * blocks : (axis + 1) * blocks]
    own_energy = 0.5 * scale * charges * own_decay
    energy_ref[...] = -0.5 * scale * sums[3 * blocks : 4 * blocks] - own_energy
    radial = sums[3 * blocks : 4 * blocks] - sums[4 * blocks : 5 * blocks]
    grad_ref[...] = (own_energy + 0.5 * scale * radial) * own_decay


def shards(positions, charges, types, pairs, owner_map):
    _, blocks, atoms = positions.shape
    regions = lax.axis_size("region")
    region_devices = lax.axis_size("dev")
    kept_regions, whole = window_regions(regions)
    devices = kept_regions * region_devices
    window = devices * blocks
    parts = atoms // CHUNK
    while region_devices % parts or 4 * parts * blocks > LANES:
        parts //= 2
    homes = parts * blocks
    chunk = atoms // parts

    vmem = pl.BlockSpec(memory_space=pltpu.VMEM)
    params = pltpu.CompilerParams(vmem_limit_bytes=40 * 1024 * 1024)
    copy_count = lax.axis_size(exchange_axes())
    twins = twin_count(region_devices)
    arrived = sent_to_both_twins(
        pl.pallas_call(
            functools.partial(fields_kernel, blocks, atoms),
            out_shape=jax.ShapeDtypeStruct((copy_count // twins, ROW_COUNT, blocks, atoms), jnp.float32),
            in_specs=[pl.BlockSpec(memory_space=pltpu.HBM)] * 5,
            out_specs=vmem,
            scratch_shapes=[
                pltpu.VMEM(positions.shape, positions.dtype),
                pltpu.VMEM(types.shape, types.dtype),
                pltpu.VMEM(charges.shape, charges.dtype),
                pltpu.SMEM(pairs.shape, pairs.dtype),
                pltpu.SMEM(owner_map.shape, owner_map.dtype),
                pltpu.SemaphoreType.DMA((5,)),
            ],
        )(positions, types, charges, pairs, owner_map)
    )
    arrived = [with_other_regions(part).reshape(devices // twins, ROW_COUNT * blocks, atoms) for part in arrived]
    padded = -(-window // LANES) * LANES
    table = jax.ShapeDtypeStruct((SUBLANES + padded, LANES), jnp.int32)
    pairs_sent = copy_count // twins
    ranks = pair_ranks(copy_count // region_devices, region_devices)
    pair_order = [first + pair for first in range(0, devices // twins, pairs_sent) for pair in ranks]
    fields = jax.ShapeDtypeStruct((WINDOW_COUNT, window + SUBLANES, atoms), jnp.float32)
    copies, lists, window_fields = pl.pallas_call(
        functools.partial(radii_kernel, blocks, pairs.shape[1], twins, whole, pair_order),
        out_shape=(jax.ShapeDtypeStruct((copy_count, blocks, atoms), jnp.float32), table, fields),
        in_specs=[vmem] * twins,
        out_specs=(vmem, vmem, vmem),
        scratch_shapes=[
            pltpu.VMEM((4, homes, chunk // SUBLANES, SUBLANES, LANES), jnp.float32),
            pltpu.VMEM((window, atoms), jnp.float32),
            pltpu.VMEM((padded, atoms), jnp.float32),
            pltpu.VMEM((homes, chunk // SUBLANES, SUBLANES, LANES), jnp.float32),
            pltpu.VMEM((LANES, LANES), jnp.float32),
            pltpu.VMEM((chunk, LANES), jnp.float32),
            pltpu.VMEM((STEP, SUBLANES, LANES), jnp.float32),
            pltpu.SMEM(table.shape, jnp.int32),
            pltpu.SMEM((homes * (padded // PARTNERS + 1) + 64,), jnp.int32),
            pltpu.SemaphoreType.DMA(()),
        ],
        compiler_params=params,
    )(*arrived)
    block_out = jax.ShapeDtypeStruct((blocks, atoms), jnp.float32)
    window_radii = with_other_regions(sent_directly(copies))
    own_radii, energy, forces, grad = pl.pallas_call(
        functools.partial(energy_kernel, parts, whole),
        out_shape=(block_out, block_out, jax.ShapeDtypeStruct((3, blocks, atoms), jnp.float32), block_out),
        in_specs=[pl.BlockSpec(memory_space=pl.ANY), vmem, vmem],
        out_specs=(vmem, vmem, vmem, vmem),
        scratch_shapes=[
            pltpu.VMEM((4 * blocks, atoms // SUBLANES, SUBLANES, LANES), jnp.float32),
            pltpu.VMEM((1, window + SUBLANES, atoms), jnp.float32),
            pltpu.VMEM((5 * blocks, atoms // SUBLANES, SUBLANES, LANES), jnp.float32),
            pltpu.SMEM(table.shape, jnp.int32),
            pltpu.SemaphoreType.DMA(()),
        ],
        compiler_params=params,
    )(lists, window_fields, window_radii)
    return own_radii, energy, forces, grad


def solution(mesh):
    placed = (
        P(None, ("region", "dev"), None),
        P(("region", "dev"), None),
        P(("region", "dev"), None),
        P(("region", "dev"), None),
        P(),
    )
    return jax.shard_map(
        shards,
        mesh=mesh,
        in_specs=placed,
        out_specs=(
            P(("region", "dev"), None),
            P(("region", "dev"), None),
            P(None, ("region", "dev"), None),
            P(("region", "dev"), None),
        ),
        check_vma=False,
    )
```

```python
import functools

import jax
import jax.numpy as jnp
from jax import lax
from jax.experimental import pallas as pl
from jax.experimental.pallas import tpu as pltpu
from jax.sharding import PartitionSpec as P

type_radii = (1.2, 1.7, 1.55, 1.52, 1.85, 1.8)
type_scales = (0.85, 0.72, 0.79, 0.85, 0.86, 0.96)
radius_offset = 0.09
born_alpha = 1.0
born_beta = 0.8
born_gamma = 4.85
solvent_tau = 1.0 - 1.0 / 78.5

ROW_X, ROW_Y, ROW_Z, ROW_TYPE, ROW_CHARGE, ROW_PARTNER, ROW_COUNT = range(7)
WINDOW_X, WINDOW_Y, WINDOW_Z, WINDOW_SCALED, WINDOW_CHARGE, WINDOW_COUNT = range(6)
LANES = 128
SUBLANES = 8
STEP = 2
ENERGY_STEP = 4
CHUNK = 32
LIST_ROWS = 32
PARTNERS = 2
ITEMS = 8
EMPTY_SLOT = -1.0e6
FAR_AWAY = 1.0e15

scaled_values = [scale * (radius - radius_offset) for radius, scale in zip(type_radii, type_scales)]
short_range = 1.01 * max(
    max(scaled_values) - (min(type_radii) - radius_offset),
    (max(type_radii) - radius_offset) - min(scaled_values),
    0.5,
)


def window_regions(region_count):
    return (region_count, True) if region_count <= 3 else (3, False)


def exchange_axes():
    return ("region", "dev") if window_regions(lax.axis_size("region"))[1] else ("dev",)


def sent_directly(copies):
    return lax.all_to_all(copies, exchange_axes(), split_axis=0, concat_axis=0, tiled=True)


def twin_count(device_count):
    return 2 - device_count % 2


def sent_to_both_twins(copies):
    count = lax.axis_size("dev")
    twins = twin_count(count)
    axes = exchange_axes()
    regions = lax.axis_size(axes) // count
    alike = [list(reversed(range(parity, regions * count, twins))) for parity in range(twins)]
    here = lax.all_to_all(copies, axes, split_axis=0, concat_axis=0, axis_index_groups=alike, tiled=True)
    if twins == 1:
        return [here]
    return [here, lax.ppermute(here, "dev", [(i, i ^ 1) for i in range(count)])]


def with_other_regions(here):
    regions = lax.axis_size("region")
    if window_regions(regions)[1]:
        return here
    below = lax.ppermute(here, "region", [(i, i + 1) for i in range(regions - 1)])
    above = lax.ppermute(here, "region", [(i + 1, i) for i in range(regions - 1)])
    return jnp.concatenate([below, here, above], axis=0)


def by_type(types, table):
    value = jnp.full(types.shape, table[0], jnp.float32)
    for index in range(1, len(table)):
        value = jnp.where(types == index, jnp.float32(table[index]), value)
    return value


def type_fields(types):
    intrinsic = by_type(types, type_radii)
    rho = intrinsic - radius_offset
    return intrinsic, rho, by_type(types, type_scales) * rho


def turned(rows):
    count, width = rows.shape
    if count < LANES:
        rows = jnp.concatenate([rows, jnp.zeros((LANES - count, width), rows.dtype)], axis=0)
    return rows.T


def spread(columns, index):
    count = columns.shape[0]
    wide = jnp.broadcast_to(columns[:, index : index + 1], (count, LANES))
    return wide.reshape(count // SUBLANES, SUBLANES, LANES)


def row_of(ref, field, row):
    return ref[field, pl.ds(row, SUBLANES, stride=0), :][None]


def diagonal(groups, first_atom):
    shape = (groups, SUBLANES, LANES)
    row = lax.broadcasted_iota(jnp.int32, shape, 0) * SUBLANES + lax.broadcasted_iota(jnp.int32, shape, 1)
    return row + first_atom == lax.broadcasted_iota(jnp.int32, shape, 2)


def lane_total(array):
    return jnp.sum(array.reshape(-1, LANES), axis=1, keepdims=True)


def lane_sums(arrays, count):
    atoms = arrays[0].shape[0] * SUBLANES
    lane = lax.broadcasted_iota(jnp.int32, (atoms, LANES), 1)
    packed = jnp.zeros((atoms, LANES), jnp.float32)
    for index, array in enumerate(arrays):
        packed = jnp.where(lane == index, lane_total(array), packed)
    return packed.T[:count]


def fields_kernel(blocks, atoms, *refs):
    inputs, copies_ref, here, sems = refs[:5], refs[5], refs[6:11], refs[11]
    moves = [pltpu.make_async_copy(src, dst, sems.at[i]) for i, (src, dst) in enumerate(zip(inputs, here))]
    for move in moves:
        move.start()
    for move in moves:
        move.wait()
    positions_ref, types_ref, charges_ref, pairs_ref, owner_ref = here
    slot = lax.broadcasted_iota(jnp.int32, (1, atoms), 1)
    partners = []
    for block in range(blocks):
        row = jnp.full((1, atoms), EMPTY_SLOT, jnp.float32)
        for index in range(pairs_ref.shape[1]):
            cell = pairs_ref[block, index]
            partner = jnp.where(cell >= 0, owner_ref[jnp.maximum(cell, 0)] + 1, int(EMPTY_SLOT))
            row = jnp.where(slot == index, partner.astype(jnp.float32), row)
        partners.append(row)
    rows = [positions_ref[axis] for axis in range(3)]
    rows += [types_ref[...].astype(jnp.float32), charges_ref[...], jnp.concatenate(partners, axis=0)]
    for copy in range(copies_ref.shape[0]):
        for index, row in enumerate(rows):
            copies_ref[copy, index] = row


def descreen(squared, rho, scaled):
    inv_dist = lax.rsqrt(squared)
    share = scaled * inv_dist
    inner = 0.25 - share
    high = 0.25 + share
    low = jnp.maximum(rho * inv_dist, inner)
    inv_low = pltpu.reciprocal(low, approx=True)
    ratio = low * pltpu.reciprocal(high, approx=True)
    curve = (1.0 - ratio) + inner * (ratio - high * inv_low)
    return (inv_low * curve + 2.0 * jnp.log(ratio)) * inv_dist


def descreen_any(squared, rho, scaled):
    rho, scaled = 4.0 * rho, 4.0 * scaled
    inv_dist = lax.rsqrt(squared)
    distance = squared * inv_dist
    high = distance + scaled
    gap = distance - scaled
    low = jnp.maximum(rho, jnp.abs(gap))
    inv_low = 1.0 / low
    inv_high = 1.0 / high
    quarter = 0.25 * inv_dist
    curve = (squared - scaled * scaled) * quarter
    body = (0.5 * (inv_low - inv_high)) * (1.0 - (inv_low + inv_high) * curve)
    body = body + jnp.log(low * inv_high) * quarter
    body = body + jnp.where(rho < -gap, 1.0 / rho - inv_low, 0.0)
    return jnp.where(high > rho, 8.0 * body, 0.0)


def neighbour_lists(partner_ref, first_home, home_id, first_window, homes, slots, filler, table_ref):
    window = partner_ref.shape[0]
    tiles = [slice(start, start + LANES) for start in range(0, window, LANES)]
    depth = -(-slots // SUBLANES) * SUBLANES
    ids = jnp.concatenate([partner_ref[tile, :].T[:depth] for tile in tiles], axis=1)
    lists = turned(partner_ref[pl.ds(first_home, homes), :])[:depth]
    lane = lax.broadcasted_iota(jnp.int32, (depth, window), 1)
    lane_id = (lane + (first_window + 1)).astype(jnp.float32)
    rows = []
    for home in range(homes):
        own = (home_id + home + 1).astype(jnp.float32)
        linked = (ids == own) | (lane_id == lists[:, home : home + 1])
        rows.append(jnp.max(jnp.where(linked, 1.0, 0.0), axis=0, keepdims=True))
    linked = jnp.concatenate(rows, axis=0)
    before = lax.broadcasted_iota(jnp.int32, (window, window), 0)
    after = lax.broadcasted_iota(jnp.int32, (window, window), 1)
    ramp = jnp.where(before <= after, 1.0, 0.0).astype(jnp.bfloat16)
    rank = jnp.dot(linked.astype(jnp.bfloat16), ramp, preferred_element_type=jnp.float32)
    place = jnp.where(linked > 0.0, rank, 0.0)
    total = jnp.sum(linked, axis=1, keepdims=True)
    name = lax.broadcasted_iota(jnp.int32, (LIST_ROWS, window), 1).astype(jnp.float32)
    spot = lax.broadcasted_iota(jnp.int32, (LIST_ROWS, window), 0).astype(jnp.float32)
    own_lane = lax.broadcasted_iota(jnp.int32, (LIST_ROWS, LANES), 1)

    def some_rows(start):
        first = jnp.asarray(start + 1).astype(jnp.float32)
        packed = jnp.zeros((LIST_ROWS, LANES), jnp.float32)
        for home in range(homes):
            hit = place[home : home + 1] == spot + first
            found = jnp.sum(jnp.where(hit, name - float(filler), 0.0), axis=1, keepdims=True)
            packed = jnp.where(own_lane == home, found, packed)
        rows = pl.ds(pl.multiple_of(SUBLANES + start, SUBLANES), LIST_ROWS)
        table_ref[rows, :] = packed.astype(jnp.int32) + filler

    counts = jnp.zeros((SUBLANES, LANES), jnp.float32)
    lane = lax.broadcasted_iota(jnp.int32, (SUBLANES, LANES), 1)
    for home in range(homes):
        counts = jnp.where(lane == home, total[home : home + 1], counts)
    longest = jnp.max(total)
    table_ref[0:SUBLANES, :] = jnp.where(lane == LANES - 1, longest, counts).astype(jnp.int32)
    some_rows(0)

    def more_rows(turn, carry):
        some_rows(turn * LIST_ROWS)
        return carry

    lax.fori_loop(1, (longest.astype(jnp.int32) + (LIST_ROWS - 1)) // LIST_ROWS, more_rows, 0)


def move_lists(table_ref, lists_ref, sem, when_wanted):
    usual = pl.ds(0, SUBLANES + LIST_ROWS)
    move = pltpu.make_async_copy(table_ref.at[usual], lists_ref.at[usual], sem)
    move.start()
    when_wanted()
    move.wait()
    rows = lists_ref.shape[0] - (SUBLANES + LIST_ROWS)
    if rows > 0:

        @pl.when(lists_ref[0, LANES - 1] > LIST_ROWS)
        def _():
            rest = pl.ds(SUBLANES + LIST_ROWS, rows)
            more = pltpu.make_async_copy(table_ref.at[rest], lists_ref.at[rest], sem)
            more.start()
            more.wait()


def device_place(blocks, parts, whole):
    region, device = lax.axis_index("region"), lax.axis_index("dev")
    region_blocks = lax.axis_size("dev") * blocks
    first_window = 0 if whole else (region - 1) * region_blocks
    first_own = region * region_blocks + device * blocks
    part = lax.rem(device, parts)
    return first_window, first_own - part * blocks, first_own, part


def radii_kernel(
    blocks,
    slots,
    twins,
    whole,
    order,
    *refs,
):
    arrived_refs, refs = refs[:twins], refs[twins:]
    copies_ref, table_ref, window_ref, columns_ref, types_ref, partner_ref, total_ref, *refs = refs
    turned_ref, packed_ref, near_ref, lists_ref, items_ref, lists_sem = refs
    _, homes, groups, _, _ = columns_ref.shape
    chunk = groups * SUBLANES
    window = types_ref.shape[0]
    parts = homes // blocks
    together = PARTNERS
    first_window, home_id, _, part = device_place(blocks, parts, whole)
    first_home = pl.multiple_of(home_id - first_window, homes)
    first_atom = pl.multiple_of(part * chunk, chunk)

    tables = [window_ref.at[WINDOW_X], window_ref.at[WINDOW_Y], window_ref.at[WINDOW_Z]]
    tables += [types_ref, window_ref.at[WINDOW_CHARGE], partner_ref]
    odd = lax.rem(lax.axis_index("dev"), 2) == 1
    for place, pair in enumerate(order):
        for field, table in enumerate(tables):
            rows = [ref[place, field * blocks : (field + 1) * blocks, :] for ref in arrived_refs]
            if twins == 2:
                rows = [jnp.where(odd, rows[1], rows[0]), jnp.where(odd, rows[0], rows[1])]
            first = pair * twins * blocks
            table[first : first + twins * blocks, :] = jnp.concatenate(rows, axis=0)
    if partner_ref.shape[0] > window:
        spare = (partner_ref.shape[0] - window, LANES)
        partner_ref[window:, :] = jnp.full(spare, EMPTY_SLOT, jnp.float32)
    def scaled_radii():
        _, _, scaled = type_fields(types_ref[...])
        window_ref[WINDOW_SCALED, 0:window, :] = 0.25 * scaled
        for field in range(WINDOW_COUNT):
            filler = FAR_AWAY if field == WINDOW_X else 0.0
            window_ref[field, window : window + SUBLANES, :] = jnp.full((SUBLANES, LANES), filler, jnp.float32)

    def home_columns():
        scaled_radii()
        home_rows = [window_ref[field, pl.ds(first_home, homes), :] for field in range(3)]
        turned_ref[...] = turned(jnp.concatenate([types_ref[pl.ds(first_home, homes), :]] + home_rows, axis=0))
        columns = turned_ref[pl.ds(first_atom, chunk), :]
        _, rho, _ = type_fields(columns)
        for home in range(homes):
            columns_ref[0, home] = spread(0.25 * rho, home)
            for index in range(1, 4):
                columns_ref[index, home] = spread(columns, index * homes + home)

    def pair_distance(home, step, rows):
        dx = columns_ref[1, home, step] - rows[0]
        dy = columns_ref[2, home, step] - rows[1]
        dz = columns_ref[3, home, step] - rows[2]
        return dx * dx + dy * dy + dz * dz

    steps = [pl.ds(start, STEP) for start in range(0, groups, STEP)]

    shift = lists_ref.shape[0].bit_length()
    usual = 16 // PARTNERS + 6

    def list_items(home, filled):
        turns = (lists_ref[0, home] + (together - 1)) // together

        def put(index, carry):
            items_ref[filled + index] = (home << shift) + index * together
            return carry

        for index in range(usual):
            put(index, 0)
        lax.fori_loop(usual, turns, put, 0)
        return filled + turns

    def own_sweep(integral):
        near_ref[...] = jnp.full(near_ref.shape, FAR_AWAY, jnp.float32)
        own_together = min(homes, 2 * LANES // chunk)

        def own_pairs(turn, carry):
            for index in range(own_together):
                home = turn * own_together + index
                rows = [row_of(window_ref, field, first_home + home) for field in range(4)]
                for start, step in zip(range(0, groups, STEP), steps):
                    same = diagonal(STEP, first_atom + start * SUBLANES)
                    squared = jnp.where(same, FAR_AWAY, pair_distance(home, step, rows))
                    term = integral(squared, columns_ref[0, home, step], rows[3])
                    total_ref[home, step] = jnp.where(same, 0.0, term)
                    near_ref[...] = jnp.minimum(near_ref[...], squared)
            return carry

        lax.fori_loop(0, homes // own_together, own_pairs, 0)

    def sweep(integral, item_count):
        def visit(turn, nearest):
            sums = []
            for index in range(ITEMS):
                item = items_ref[turn * ITEMS + index]
                line, entry = item >> shift, item & ((1 << shift) - 1)
                home = jnp.minimum(line, homes - 1)
                parts_of = [None] * len(steps)
                for other in range(together):
                    partner = lists_ref[SUBLANES + entry + other, line]
                    rows = [row_of(window_ref, field, partner) for field in range(4)]
                    for place, step in enumerate(steps):
                        squared = pair_distance(home, step, rows)
                        nearest = jnp.minimum(nearest, squared)
                        term = integral(squared, columns_ref[0, home, step], rows[3])
                        parts_of[place] = term if other == 0 else parts_of[place] + term
                sums.append((home, parts_of))
            for home, parts_of in sums:
                for part, step in zip(parts_of, steps):
                    total_ref[home, step] += part
            return nearest

        near_ref[...] = lax.fori_loop(0, (item_count + (ITEMS - 1)) // ITEMS, visit, near_ref[...])
        lane = lax.broadcasted_iota(jnp.int32, (chunk, LANES), 1)
        packed = jnp.zeros((chunk, LANES), jnp.float32)
        for home in range(homes):
            packed = jnp.where(lane == home, lane_total(total_ref[home]), packed)
        packed_ref[...] = packed

    def meanwhile():
        home_columns()
        own_sweep(descreen)

    neighbour_lists(partner_ref, first_home, home_id, first_window, homes, slots, window, table_ref)
    move_lists(table_ref, lists_ref, lists_sem, meanwhile)
    intrinsic, rho, _ = type_fields(turned_ref[pl.ds(first_atom, chunk), :])
    item_count = lax.fori_loop(0, homes, list_items, 0)
    for index in range(ITEMS):
        items_ref[item_count + index] = homes << shift
    sweep(descreen, item_count)

    @pl.when(jnp.min(near_ref[...]) < short_range * short_range)
    def _():
        own_sweep(descreen_any)
        sweep(descreen_any, item_count)

    psi = (0.125 * packed_ref[...]) * rho
    shaped = born_alpha * psi - born_beta * psi * psi + born_gamma * psi * psi * psi
    radii = 1.0 / (1.0 / rho - jnp.tanh(shaped) / intrinsic)

    if chunk < LANES:
        radii = jnp.concatenate([radii, jnp.zeros((LANES - chunk, LANES), jnp.float32)], axis=0)
    turned_ref[...] = radii.T
    lane = lax.broadcasted_iota(jnp.int32, (blocks, LANES), 1)
    sent = turned_ref[pl.ds(0, blocks, stride=parts), :]
    for index in range(1, parts):
        rows = pltpu.roll(turned_ref[pl.ds(index, blocks, stride=parts), :], index * chunk, 1)
        sent = jnp.where(lane >= index * chunk, rows, sent)
    for copy in range(copies_ref.shape[0]):
        copies_ref[copy] = sent


def energy_kernel(
    parts,
    whole,
    table_ref,
    window_ref,
    gathered_ref,
    own_radii_ref,
    energy_ref,
    forces_ref,
    grad_ref,
    columns_ref,
    radii_ref,
    total_ref,
    lists_ref,
    lists_sem,
):
    devices, blocks, atoms = gathered_ref.shape
    window = devices * blocks
    part_rows = window // parts
    chunk = atoms // parts
    groups = atoms // SUBLANES
    first_window, _, own_id, part_here = device_place(blocks, parts, whole)
    first_own, list_lane = own_id - first_window, part_here * blocks
    fields = [(window_ref, field) for field in (WINDOW_X, WINDOW_Y, WINDOW_Z, WINDOW_CHARGE)] + [(radii_ref, 0)]

    def unpack():
        lane = lax.broadcasted_iota(jnp.int32, (part_rows, LANES), 1)
        pieces = [
            gathered_ref[pl.ds(part, devices // parts, stride=parts)].reshape(part_rows, atoms)
            for part in range(parts)
        ]
        for place in range(parts):
            whole_rows = pieces[0] if place == 0 else pltpu.roll(pieces[0], (parts - place) * chunk, 1)
            for part in range(1, parts):
                shift = (part - place) % parts
                piece = pieces[part] if shift == 0 else pltpu.roll(pieces[part], shift * chunk, 1)
                whole_rows = jnp.where(lane >= part * chunk, piece, whole_rows)
            radii_ref[0, pl.ds(place, part_rows, stride=parts), :] = whole_rows
        radii_ref[0, window : window + SUBLANES, :] = jnp.ones((SUBLANES, LANES), jnp.float32)

    def own_rows(ref, field):
        return jnp.concatenate([ref[field, pl.ds(first_own + block, 1), :] for block in range(blocks)], axis=0)

    def home_columns(block, start):
        return [columns_ref[field * blocks + block, pl.ds(start, ENERGY_STEP)] for field in range(4)]

    def pair_terms(home, rows, same=None):
        x, y, z, charge, radius = rows
        dx = home[0] - x
        dy = home[1] - y
        dz = home[2] - z
        squared = dx * dx + dy * dy + dz * dz
        if same is not None:
            squared = jnp.where(same, 1.0, squared)
            charge = jnp.where(same, 0.0, charge)
        spread_sq = home[3] * radius
        power = squared * pltpu.reciprocal(spread_sq, approx=True)
        quarter = 0.25 * jnp.exp(power)
        root_sq = squared - spread_sq * quarter
        inv_root = lax.rsqrt(root_sq)
        potential = charge * inv_root
        pull = (potential * pltpu.reciprocal(root_sq, approx=True)) * (1.0 - quarter)
        return (pull * dx, pull * dy, pull * dz, potential, pull * squared)

    def own_pairs():
        unpack()
        own_radii = own_rows(radii_ref, 0)
        own_radii_ref[...] = own_radii
        own = [own_rows(window_ref, field) for field in (WINDOW_X, WINDOW_Y, WINDOW_Z)]
        columns = turned(jnp.concatenate(own + [-4.0 * own_radii], axis=0))
        for index in range(4 * blocks):
            columns_ref[index] = spread(columns, index)
        for block in range(blocks):
            rows = [row_of(ref, field, first_own + block) for ref, field in fields]
            for start in range(0, groups, ENERGY_STEP):
                step = pl.ds(start, ENERGY_STEP)
                terms = pair_terms(home_columns(block, start), rows, diagonal(ENERGY_STEP, start * SUBLANES))
                for term, value in enumerate(terms):
                    total_ref[term * blocks + block, step] = value

    move_lists(table_ref, lists_ref, lists_sem, own_pairs)
    for block in range(blocks):

        def visit(count, first, index, carry, block=block):
            partners = []
            for other in range(count):
                partner = lists_ref[SUBLANES + first + index * count + other, list_lane + block]
                partners.append([row_of(ref, field, partner) for ref, field in fields])
            for start in range(0, groups, ENERGY_STEP):
                step = pl.ds(start, ENERGY_STEP)
                home = home_columns(block, start)
                sums = [total_ref[term * blocks + block, step] for term in range(5)]
                for rows in partners:
                    sums = [total + value for total, value in zip(sums, pair_terms(home, rows))]
                for term, value in enumerate(sums):
                    total_ref[term * blocks + block, step] = value
            return carry

        left = lists_ref[0, list_lane + block]
        first = 0
        for count in (8, 4, 2, 1):
            turns = left // count
            lax.fori_loop(0, turns, functools.partial(visit, count, first), 0)
            first = first + turns * count
            left = left - turns * count
    sums = lane_sums([total_ref[index] for index in range(5 * blocks)], 5 * blocks)
    charges = own_rows(window_ref, WINDOW_CHARGE)
    own_decay = 1.0 / own_radii_ref[...]
    scale = solvent_tau * charges
    for axis in range(3):
        forces_ref[axis] = -scale * sums[axis * blocks : (axis + 1) * blocks]
    own_energy = 0.5 * scale * charges * own_decay
    energy_ref[...] = -0.5 * scale * sums[3 * blocks : 4 * blocks] - own_energy
    radial = sums[3 * blocks : 4 * blocks] - sums[4 * blocks : 5 * blocks]
    grad_ref[...] = (own_energy + 0.5 * scale * radial) * own_decay


def shards(positions, charges, types, pairs, owner_map):
    _, blocks, atoms = positions.shape
    regions = lax.axis_size("region")
    region_devices = lax.axis_size("dev")
    kept_regions, whole = window_regions(regions)
    devices = kept_regions * region_devices
    window = devices * blocks
    parts = atoms // CHUNK
    while region_devices % parts or 4 * parts * blocks > LANES:
        parts //= 2
    homes = parts * blocks
    chunk = atoms // parts

    vmem = pl.BlockSpec(memory_space=pltpu.VMEM)
    params = pltpu.CompilerParams(vmem_limit_bytes=40 * 1024 * 1024)
    copy_count = lax.axis_size(exchange_axes())
    twins = twin_count(region_devices)
    arrived = sent_to_both_twins(
        pl.pallas_call(
            functools.partial(fields_kernel, blocks, atoms),
            out_shape=jax.ShapeDtypeStruct((copy_count // twins, ROW_COUNT, blocks, atoms), jnp.float32),
            in_specs=[pl.BlockSpec(memory_space=pltpu.HBM)] * 5,
            out_specs=vmem,
            scratch_shapes=[
                pltpu.VMEM(positions.shape, positions.dtype),
                pltpu.VMEM(types.shape, types.dtype),
                pltpu.VMEM(charges.shape, charges.dtype),
                pltpu.SMEM(pairs.shape, pairs.dtype),
                pltpu.SMEM(owner_map.shape, owner_map.dtype),
                pltpu.SemaphoreType.DMA((5,)),
            ],
        )(positions, types, charges, pairs, owner_map)
    )
    arrived = [with_other_regions(part).reshape(devices // twins, ROW_COUNT * blocks, atoms) for part in arrived]
    padded = -(-window // LANES) * LANES
    table = jax.ShapeDtypeStruct((SUBLANES + padded, LANES), jnp.int32)
    pairs_sent = copy_count // twins
    pair_order = [
        first + place for first in range(0, devices // twins, pairs_sent) for place in reversed(range(pairs_sent))
    ]
    fields = jax.ShapeDtypeStruct((WINDOW_COUNT, window + SUBLANES, atoms), jnp.float32)
    copies, lists, window_fields = pl.pallas_call(
        functools.partial(radii_kernel, blocks, pairs.shape[1], twins, whole, pair_order),
        out_shape=(jax.ShapeDtypeStruct((copy_count, blocks, atoms), jnp.float32), table, fields),
        in_specs=[vmem] * twins,
        out_specs=(vmem, vmem, vmem),
        scratch_shapes=[
            pltpu.VMEM((4, homes, chunk // SUBLANES, SUBLANES, LANES), jnp.float32),
            pltpu.VMEM((window, atoms), jnp.float32),
            pltpu.VMEM((padded, atoms), jnp.float32),
            pltpu.VMEM((homes, chunk // SUBLANES, SUBLANES, LANES), jnp.float32),
            pltpu.VMEM((LANES, LANES), jnp.float32),
            pltpu.VMEM((chunk, LANES), jnp.float32),
            pltpu.VMEM((STEP, SUBLANES, LANES), jnp.float32),
            pltpu.SMEM(table.shape, jnp.int32),
            pltpu.SMEM((homes * (padded // PARTNERS + 1) + 64,), jnp.int32),
            pltpu.SemaphoreType.DMA(()),
        ],
        compiler_params=params,
    )(*arrived)
    block_out = jax.ShapeDtypeStruct((blocks, atoms), jnp.float32)
    window_radii = with_other_regions(sent_directly(copies))
    own_radii, energy, forces, grad = pl.pallas_call(
        functools.partial(energy_kernel, parts, whole),
        out_shape=(block_out, block_out, jax.ShapeDtypeStruct((3, blocks, atoms), jnp.float32), block_out),
        in_specs=[pl.BlockSpec(memory_space=pl.ANY), vmem, vmem],
        out_specs=(vmem, vmem, vmem, vmem),
        scratch_shapes=[
            pltpu.VMEM((4 * blocks, atoms // SUBLANES, SUBLANES, LANES), jnp.float32),
            pltpu.VMEM((1, window + SUBLANES, atoms), jnp.float32),
            pltpu.VMEM((5 * blocks, atoms // SUBLANES, SUBLANES, LANES), jnp.float32),
            pltpu.SMEM(table.shape, jnp.int32),
            pltpu.SemaphoreType.DMA(()),
        ],
        compiler_params=params,
    )(lists, window_fields, window_radii)
    return own_radii, energy, forces, grad


def solution(mesh):
    placed = (
        P(None, ("region", "dev"), None),
        P(("region", "dev"), None),
        P(("region", "dev"), None),
        P(("region", "dev"), None),
        P(),
    )
    return jax.shard_map(
        shards,
        mesh=mesh,
        in_specs=placed,
        out_specs=(
            P(("region", "dev"), None),
            P(("region", "dev"), None),
            P(None, ("region", "dev"), None),
            P(("region", "dev"), None),
        ),
        check_vma=False,
    )
```
